32 devices in a mesh: ctx: 16 (over z, y, core), fsdp: 2 (over x).
Axes of the slice: x: 2, y: 2, z: 4, core: 2. Of those that a mesh axis runs over, the one named last changes fastest.
Arguments:
- tokens: bfloat16 [4096, 1024], P(('ctx', 'fsdp')), may hold values from -6 to 6
- cotangent: bfloat16 [4096, 1024], P(('ctx', 'fsdp')), may hold values from -6 to 6
- lengths: int32 [2, 2], P('fsdp'), may hold values from 256 to 1024, as said below
- stretch_ids: int32 [16, 2, 2], P(None, 'fsdp'), may hold values from 0 to 31, as said below
- w_query: bfloat16 [2, 1024, 2048], P(None, 'fsdp'), may hold values from -0.1875 to 0.1875
- key_projection_weight: bfloat16 [2, 1024, 1024], P(None, 'fsdp'), may hold values from -0.1875 to 0.1875
- value_projection_weight: bfloat16 [2, 1024, 1024], P(None, 'fsdp'), may hold values from -0.1875 to 0.1875
- w_out: bfloat16 [2, 2048, 1024], P(None, 'fsdp'), may hold values from -1 to 1
- w_gate: bfloat16 [2, 1024, 3072], P(None, 'fsdp'), may hold values from -0.1875 to 0.1875
- w_up: bfloat16 [2, 1024, 3072], P(None, 'fsdp'), may hold values from -0.1875 to 0.1875
- w_down: bfloat16 [2, 3072, 1024], P(None, 'fsdp'), may hold values from -0.109375 to 0.109375
- g_attn: bfloat16 [2, 1024], P(None, 'fsdp'), may hold values from 0.5 to 1.5
- g_mlp: bfloat16 [2, 1024], P(None, 'fsdp'), may hold values from 0.5 to 1.5
- g_query: bfloat16 [2, 128], P(None, 'fsdp'), may hold values from 0.099609375 to 1.8984375
- g_key: bfloat16 [2, 128], P(None, 'fsdp'), may hold values from 0.099609375 to 1.8984375
Outputs:
- output: bfloat16 [4096, 1024], P(('ctx', 'fsdp'))
- grad_tokens: float32 [4096, 1024], P(('ctx', 'fsdp'))
- grad_query: float32 [2, 1024, 2048], P(None, ('ctx', 'fsdp'))
- grad_key: float32 [2, 1024, 1024], P(None, ('ctx', 'fsdp'))
- grad_value: float32 [2, 1024, 1024], P(None, ('ctx', 'fsdp'))
- grad_out: float32 [2, 2048, 1024], P(None, ('ctx', 'fsdp'))
- grad_gate: float32 [2, 1024, 3072], P(None, ('ctx', 'fsdp'))
- grad_up: float32 [2, 1024, 3072], P(None, ('ctx', 'fsdp'))
- grad_down: float32 [2, 3072, 1024], P(None, ('ctx', 'fsdp'))
- grad_attn_gain: float32 [2, 1024], P(None, ('ctx', 'fsdp'))
- grad_mlp_gain: float32 [2, 1024], P(None, ('ctx', 'fsdp'))
- grad_query_gain: float32 [2, 128], P(None, ('ctx', 'fsdp'))
- grad_key_gain: float32 [2, 128], P(None, ('ctx', 'fsdp'))
The draws below stay inside these ranges and needn't reach their ends.
Inputs may be any that keep to these rules, and one draw needn't show every extreme that they name: `lengths`: in each fsdp group at least one of its two slots is full. `stretch_ids`: in each fsdp group every number 0 to 31 occurs once; number s * 16 + j is stretch j of slot s; ctx device c holds two stretches of slot c // 8, numbers j and 15 - j of that slot, the smaller first.
All inputs are finite; a program needn't handle non-finite values.
Results may differ from the reference program's by a relative error of at most 0.033.
Values may be sent and summed in bfloat16 or wider, within the bound.
A program may use at most 384 MiB of HBM per device.

```python
import math
import jax
import jax.numpy as jnp
from jax import lax

MODEL_WIDTH = 1024
QUERY_HEADS = 16
KEY_VALUE_HEADS = 8
HEAD_SIZE = 128
FF = 3072
DECODER_LAYERS = 2
STRETCH = 64
SLOT_LEN = 1024
SLOTS = 4
TOKENS = 4096
N_CTX = 16
N_FSDP = 2


def draw_lengths(key, part):
    low_end = SLOT_LEN // 4
    drawn = jax.random.randint(jax.random.fold_in(key, 1), (SLOTS // 2, 2), low_end, SLOT_LEN + 1)
    which_full = jax.random.randint(jax.random.fold_in(key, 2), (SLOTS // 2, 1), 0, 2)
    full_mark = jnp.arange(2, dtype=jnp.int32)[None, :] == which_full
    return jnp.where(full_mark, SLOT_LEN, drawn).astype(jnp.int32)


def draw_stretch_ids(key, part):
    ctx_count = SLOT_LEN // STRETCH
    half_pairs = ctx_count // 2
    columns = []
    for group_index in range(SLOTS // 2):
        slot_rows = []
        for slot_index in range(2):
            pair_inner = jax.random.permutation(jax.random.fold_in(key, 10 + 2 * group_index + slot_index), half_pairs).astype(jnp.int32)
            lower_stretch = slot_index * ctx_count + pair_inner
            upper_stretch = slot_index * ctx_count + ctx_count - 1 - pair_inner
            slot_rows.append(jnp.stack([lower_stretch, upper_stretch], axis=-1))
        columns.append(jnp.concatenate(slot_rows, axis=0))
    return jnp.stack(columns, axis=1).astype(jnp.int32)


def level_of(rng, dims, shards, least, high):
    level, own = 1.0, jax.random.fold_in(rng, 6)
    for axis_at, blocks in shards:
        heights = jnp.exp(jax.random.uniform(jax.random.fold_in(own, axis_at), (blocks,), jnp.float32, least / len(shards), high / len(shards)))
        level = level * jnp.repeat(heights, dims[axis_at] // blocks).reshape([-1 if axis == axis_at else 1 for axis in range(len(dims))])
    return level


def normal_values(own_key, extent, scale, most, shards=(), kind=jnp.bfloat16):
    values = jax.random.normal(own_key, extent, jnp.float32) * scale
    if len(shards) > 0:
        values = level_of(own_key, extent, shards, -0.22, 0.18) * values
    return jnp.clip(values, min=-most, max=most).astype(kind)


def setup_inputs(seed: int = 0) -> dict:
    seeds = jax.random.split(jax.random.key(seed), 16)
    tokens = normal_values(seeds[0], (TOKENS, MODEL_WIDTH), 1.0, 6.0, ((0, 32),))
    cotangent = normal_values(seeds[1], (TOKENS, MODEL_WIDTH), 1.0, 6.0, ((0, 32),))
    lengths = draw_lengths(jax.random.fold_in(seeds[15], 71), 0)
    stretch_ids = draw_stretch_ids(jax.random.fold_in(seeds[15], 71), 0)
    w_query = normal_values(seeds[4], (DECODER_LAYERS, MODEL_WIDTH, QUERY_HEADS * HEAD_SIZE), MODEL_WIDTH ** -0.5, 0.1875, ((1, 2),))
    key_projection_weight = normal_values(seeds[5], (DECODER_LAYERS, MODEL_WIDTH, KEY_VALUE_HEADS * HEAD_SIZE), MODEL_WIDTH ** -0.5, 0.1875, ((1, 2),))
    value_projection_weight = normal_values(seeds[6], (DECODER_LAYERS, MODEL_WIDTH, KEY_VALUE_HEADS * HEAD_SIZE), MODEL_WIDTH ** -0.5, 0.1875, ((1, 2),))
    w_out = normal_values(seeds[7], (DECODER_LAYERS, QUERY_HEADS * HEAD_SIZE, MODEL_WIDTH), 32 ** -0.5, 1.0, ((1, 2),))
    w_gate = normal_values(seeds[8], (DECODER_LAYERS, MODEL_WIDTH, FF), MODEL_WIDTH ** -0.5, 0.1875, ((1, 2),))
    w_up = normal_values(seeds[9], (DECODER_LAYERS, MODEL_WIDTH, FF), MODEL_WIDTH ** -0.5, 0.1875, ((1, 2),))
    w_down = normal_values(seeds[10], (DECODER_LAYERS, FF, MODEL_WIDTH), FF ** -0.5, 0.109375, ((1, 2),))
    g_attn = jnp.clip(1.0 + 0.1 * jax.random.normal(seeds[11], (DECODER_LAYERS, MODEL_WIDTH), jnp.float32), 0.5, 1.5).astype(jnp.bfloat16)
    g_mlp = jnp.clip(1.0 + 0.1 * jax.random.normal(seeds[12], (DECODER_LAYERS, MODEL_WIDTH), jnp.float32), 0.5, 1.5).astype(jnp.bfloat16)
    g_query = jnp.clip(1.0 + 0.18 * jax.random.normal(seeds[13], (DECODER_LAYERS, HEAD_SIZE), jnp.float32), 0.099609375, 1.8984375).astype(jnp.bfloat16)
    g_key = jnp.clip(1.0 + 0.18 * jax.random.normal(seeds[14], (DECODER_LAYERS, HEAD_SIZE), jnp.float32), 0.099609375, 1.8984375).astype(jnp.bfloat16)
    return dict(tokens=tokens, cotangent=cotangent, lengths=lengths, stretch_ids=stretch_ids, w_query=w_query, key_projection_weight=key_projection_weight, value_projection_weight=value_projection_weight, w_out=w_out, w_gate=w_gate, w_up=w_up, w_down=w_down, g_attn=g_attn, g_mlp=g_mlp, g_query=g_query, g_key=g_key)


@jax.custom_vjp
def lowered_value(v):
    return lax.optimization_barrier(v.astype(jnp.bfloat16)).astype(jnp.float32)

@jax.custom_vjp
def lowered_backward(v):
    return v

def low_keep(v):
    return (lowered_value(v), None)

def low_pass(kept, grad):
    return (grad,)

def back_keep(v):
    return (v, None)

def back_low(kept, grad):
    return (lowered_value(grad),)
lowered_value.defvjp(low_keep, low_pass)
lowered_backward.defvjp(back_keep, back_low)
norm_epsilon = 1e-06
rope_base = 1000000.0
masked_logits = -1e+30
highest_precision = lax.Precision.HIGHEST

def token_places(stretch_table, slot_lengths):
    ctx_count = stretch_table.shape[0]
    stretch_order = stretch_table.reshape(-1)
    within = jnp.arange(STRETCH, dtype=jnp.int32)
    places = (stretch_order % ctx_count * STRETCH)[:, None] + within[None, :]
    slot_ids = jnp.broadcast_to((stretch_order // ctx_count)[:, None], places.shape).reshape(-1)
    places = places.reshape(-1)
    limits = jnp.where(slot_ids == 0, slot_lengths[0], slot_lengths[1])
    return (places, slot_ids, places < limits)

def rotary_tables(places):
    half_dim = HEAD_SIZE // 2
    spread = jnp.arange(half_dim, dtype=jnp.int32).astype(jnp.float32) * (2.0 / HEAD_SIZE)
    inverse = jnp.exp(spread * -math.log(rope_base))
    angles = places.astype(jnp.float32)[:, None] * inverse[None, :]
    return (jnp.concatenate([jnp.cos(angles)] * 2, axis=-1), jnp.concatenate([jnp.sin(angles)] * 2, axis=-1))

def rotate(values, cosine_table, sine_table):
    half_dim = values.shape[-1] // 2
    turned = jnp.concatenate([-values[..., half_dim:], values[..., :half_dim]], axis=-1)
    return values * cosine_table[:, None, :] + turned * sine_table[:, None, :]

def rms_norm(values, gain_vec):
    return values * lax.rsqrt(lax.optimization_barrier(jnp.mean(values * values, axis=-1, keepdims=True)) + norm_epsilon) * gain_vec

def matrix_product(left_side, right_side):
    return jnp.dot(left_side, right_side, preferred_element_type=jnp.float32, precision=highest_precision)

def attend(queries, key_head_list, value_head_list, places, slot_ids, live_mask):
    total_rows = queries.shape[0]
    block_row_list = math.gcd(total_rows, 512)
    group_count = QUERY_HEADS // KEY_VALUE_HEADS
    score_scale = HEAD_SIZE ** (-0.5)

    def one_block(pieces):
        query_tile_block, place_block, slot_block = pieces
        grouped_rows = query_tile_block.reshape(block_row_list, KEY_VALUE_HEADS, group_count, HEAD_SIZE)
        scores = jnp.einsum('qhgd,khd->hgqk', grouped_rows, key_head_list, precision=highest_precision) * score_scale
        scores = lowered_backward(scores)
        allowed = (slot_ids[None, :] == slot_block[:, None]) & (places[None, :] <= place_block[:, None]) & live_mask[None, :]
        scores = jnp.where(allowed, scores, masked_logits)
        highest = lax.optimization_barrier(jnp.max(scores, axis=-1, keepdims=True))
        expo = jnp.where(allowed, jnp.exp(scores - highest), 0.0)
        prob_block = lowered_value(expo / lax.optimization_barrier(jnp.sum(expo, axis=-1, keepdims=True)))
        attended = jnp.einsum('hgqk,khd->qhgd', prob_block, value_head_list, precision=highest_precision)
        return attended.reshape(block_row_list, QUERY_HEADS * HEAD_SIZE)
    blocks = lax.map(jax.checkpoint(one_block), (queries.reshape(-1, block_row_list, QUERY_HEADS, HEAD_SIZE), places.reshape(-1, block_row_list), slot_ids.reshape(-1, block_row_list)))
    return blocks.reshape(total_rows, QUERY_HEADS * HEAD_SIZE)

def block_forward(stream, layer_params, places, slot_ids, live_mask, cosine_table, sine_table):
    query_weight, key_matrix, value_matrix, out_weight, gate_weight, up_weight, down_weight, attn_gain, mlp_gain, query_gain, key_gain = layer_params
    total_rows = stream.shape[0]
    normalized = lowered_value(rms_norm(stream, attn_gain))
    queries = lowered_backward(matrix_product(normalized, query_weight)).reshape(total_rows, QUERY_HEADS, HEAD_SIZE)
    key_head_list = lowered_backward(matrix_product(normalized, key_matrix)).reshape(total_rows, KEY_VALUE_HEADS, HEAD_SIZE)
    value_head_list = lowered_backward(lowered_value(matrix_product(normalized, value_matrix))).reshape(total_rows, KEY_VALUE_HEADS, HEAD_SIZE)
    queries = lowered_value(rotate(rms_norm(queries, query_gain), cosine_table, sine_table))
    key_head_list = lowered_value(rotate(rms_norm(key_head_list, key_gain), cosine_table, sine_table))
    attended = lowered_backward(lowered_value(attend(queries, key_head_list, value_head_list, places, slot_ids, live_mask)))
    middle = stream + lowered_backward(matrix_product(attended, out_weight))
    normed_mid = lowered_value(rms_norm(middle, mlp_gain))
    gate_act = lowered_backward(matrix_product(normed_mid, gate_weight))
    upward = lowered_backward(matrix_product(normed_mid, up_weight))
    hidden = lowered_value(jax.nn.silu(gate_act) * upward)
    return middle + lowered_backward(matrix_product(hidden, down_weight))

def reference(tokens, cotangent, lengths, stretch_ids, w_query, key_projection_weight, value_projection_weight, w_out, w_gate, w_up, w_down, g_attn, g_mlp, g_query, g_key):
    params = tuple((array_in.astype(jnp.float32) for array_in in (w_query, key_projection_weight, value_projection_weight, w_out, w_gate, w_up, w_down, g_attn, g_mlp, g_query, g_key)))
    inputs = tokens.astype(jnp.float32)
    group_tables = []
    for group_index in range(N_FSDP):
        places, slot_ids, live_mask = token_places(stretch_ids[:, group_index, :], lengths[group_index])
        cosine_table, sine_table = rotary_tables(places)
        group_tables.append((places, slot_ids, live_mask, cosine_table, sine_table))

    def forward(inputs, params):
        arranged = inputs.reshape(N_CTX, N_FSDP, -1, MODEL_WIDTH)
        results = []
        for group_index in range(N_FSDP):
            places, slot_ids, live_mask, cosine_table, sine_table = group_tables[group_index]
            stream = arranged[:, group_index].reshape(-1, MODEL_WIDTH)
            for layer_index in range(DECODER_LAYERS):
                layer_params = tuple((param[layer_index] for param in params))
                stream = block_forward(stream, layer_params, places, slot_ids, live_mask, cosine_table, sine_table)
            results.append((stream * live_mask[:, None].astype(jnp.float32)).reshape(N_CTX, -1, MODEL_WIDTH))
        return jnp.stack(results, axis=1).reshape(-1, MODEL_WIDTH)
    result, pullback = jax.vjp(forward, inputs, params)
    grad_inputs, grad_params = pullback(cotangent.astype(jnp.float32))
    return (result.astype(jnp.bfloat16), grad_inputs) + tuple(grad_params)
```

```python
import math

import jax
import jax.numpy as jnp
from jax import lax
from jax.experimental import pallas as pl
from jax.experimental.pallas import tpu as pltpu
from jax.sharding import PartitionSpec as P

QUERY_HEADS = 16
KEY_VALUE_HEADS = 8
HEAD_SIZE = 128
DECODER_LAYERS = 2
STRETCH = 64


norm_epsilon = 1e-06
rope_base = 1000000.0
masked_logits = -1e30

MESH = pl.DeviceIdType.MESH
TILES = 15
GRADS = 12
AHEAD = 3


def grad_index(t):
    return jnp.maximum(t - 3, jnp.where(t < 3, 0, 1))


def act_index(t):
    return jnp.minimum(t, 5) + jnp.where(t >= 11, 1, 0)


def is_new(t):
    return (t == 0) | (t == 3) | ((t >= 5) & (t < TILES))


def rs_kernel(
    acts, grads, out, abuf, afwd, gbuf, ysend, yrecv, own, zsend, zrecv, zown,
    a_local, a_xs, a_xr, a_cs, a_cr, g_local, g_xs, g_xr, g_cs, g_cr, g_fs, g_fr,
    y_s, y_r, z_s, z_r,
):
    c = lax.axis_index("ctx")
    x = lax.axis_index("fsdp")
    core = c % 2
    y = c // 2 % 2
    z = c // 4
    sibling = (c + 1 - 2 * core, x)
    across = (c, 1 - x)
    aside = (c + 2 - 4 * y, x)

    def along(o):
        return ((z + o) % 4 * 4 + c % 4, x)

    barrier = pltpu.get_barrier_semaphore()
    for other in (sibling, across, aside, along(1), along(2), along(3)):
        pl.semaphore_signal(barrier, inc=1, device_id=other, device_id_type=MESH)
    pl.semaphore_wait(barrier, 6)

    def remote(src, dst, s, r, dev):
        return pltpu.make_async_remote_copy(
            src_ref=src, dst_ref=dst, send_sem=s, recv_sem=r, device_id=dev, device_id_type=MESH
        )

    spans = (pl.ds(0, 3), pl.ds(3, 4))

    def act_local(g):
        return pltpu.make_async_copy(
            acts.at[x, core, spans[g]], abuf.at[spans[g], :, pl.ds(0, 128)], a_local.at[g]
        )

    def act_across(g):
        return (
            remote(
                acts.at[1 - x, core, spans[g]], abuf.at[spans[g], :, pl.ds(128, 128)],
                a_xs.at[g, 0], a_xr.at[g, 0], across,
            ),
            remote(
                acts.at[1 - x, 1 - core, spans[g]], afwd.at[spans[g]],
                a_xs.at[g, 1], a_xr.at[g, 1], across,
            ),
        )

    def act_sibling(g):
        return remote(
            acts.at[x, 1 - core, spans[g]], abuf.at[spans[g], :, pl.ds(256, 128)],
            a_cs.at[g, 0], a_cr.at[g, 0], sibling,
        )

    def act_forward(g):
        return remote(
            afwd.at[spans[g]], abuf.at[spans[g], :, pl.ds(384, 128)],
            a_cs.at[g, 1], a_cr.at[g, 1], sibling,
        )

    def grad_local(i):
        return pltpu.make_async_copy(grads.at[i], gbuf.at[i, pl.ds(0, 128)], g_local.at[i])

    def grad_across(i):
        return remote(grads.at[i], gbuf.at[i, pl.ds(128, 128)], g_xs.at[i], g_xr.at[i], across)

    def grad_sibling(i):
        return remote(grads.at[i], gbuf.at[i, pl.ds(256, 128)], g_cs.at[i], g_cr.at[i], sibling)

    def grad_forward(i):
        return remote(
            gbuf.at[i, pl.ds(128, 128)], gbuf.at[i, pl.ds(384, 128)], g_fs.at[i], g_fr.at[i], sibling
        )

    def y_copy(t):
        return remote(ysend.at[t], yrecv.at[t], y_s.at[t], y_r.at[t], aside)

    def z_copy(t, o):
        return remote(
            zsend.at[t, o - 1], zrecv.at[t, 3 - o], z_s.at[t, o - 1], z_r.at[t, 3 - o], along(o)
        )

    def start_acts(g):
        for copy in act_across(g):
            copy.start()
        act_sibling(g).start()
        act_local(g).start()

    def start_grad(i):
        grad_across(i).start()
        grad_sibling(i).start()
        grad_local(i).start()

    start_acts(0)
    start_grad(0)
    start_acts(1)
    for i in range(1, AHEAD):
        start_grad(i)

    def forward_acts(g):
        act_across(g)[1].wait_recv()
        act_forward(g).start()

    def await_acts(g):
        act_local(g).wait()
        act_across(g)[0].wait_recv()
        act_sibling(g).wait_recv()
        act_forward(g).wait_recv()

    def step(s, carry):
        t = s - 5

        @pl.when(t >= 0)
        def finish():
            total = zown[t % 4]
            for o in (1, 2, 3):
                z_copy(t, o).wait_recv()
            for o in range(3):
                total += zrecv[t, o].astype(jnp.float32)
            out[t] = total

        u = s - 3

        @pl.when((u >= 0) & (u < TILES))
        def spread():
            y_copy(u).wait_recv()

            def part(index):
                rows = pl.ds(pl.multiple_of(index * 32, 32), 32)
                return own[u % 4, rows, :] + yrecv[u, rows, :].astype(jnp.float32)

            for o in (2, 1, 3):
                zsend[u, o - 1] = part((z + o) % 4).astype(jnp.bfloat16)
                z_copy(u, o).start()
            zown[u % 4] = part(z)

        v = s - 1

        @pl.when((v >= 0) & (v < TILES))
        def compute():
            gi = grad_index(v)
            ai = act_index(v)

            @pl.when(v == 0)
            def first_acts():
                await_acts(0)

            @pl.when(v == 3)
            def second_acts():
                await_acts(1)

            @pl.when(is_new(v))
            def fresh():
                grad_local(gi).wait()
                grad_sibling(gi).wait_recv()
                grad_forward(gi).wait_recv()

            for half in range(2):
                cols = pl.ds(half * 512, 512)
                right = gbuf[gi, :, cols]
                theirs = pl.ds(pl.multiple_of((1 - y) * 128, 128), 128)
                mine = pl.ds(pl.multiple_of(y * 128, 128), 128)
                ysend[v, :, cols] = jnp.dot(
                    abuf[ai, theirs, :], right, preferred_element_type=jnp.float32
                ).astype(jnp.bfloat16)
                own[v % 4, :, cols] = jnp.dot(
                    abuf[ai, mine, :], right, preferred_element_type=jnp.float32
                )
            y_copy(v).start()

        @pl.when(is_new(s))
        def forward():
            i = grad_index(s)

            @pl.when(s == 0)
            def first_forward():
                forward_acts(0)

            @pl.when(s == 3)
            def second_forward():
                forward_acts(1)

            grad_across(i).wait_recv()
            grad_forward(i).start()

            @pl.when(i + AHEAD < GRADS)
            def more():
                start_grad(i + AHEAD)

        return carry

    lax.fori_loop(0, TILES + 5, step, 0)

    for g in range(2):
        for copy in act_across(g):
            copy.wait_send()
        act_sibling(g).wait_send()
        act_forward(g).wait_send()

    def drain_grads(i, carry):
        grad_across(i).wait_send()
        grad_sibling(i).wait_send()
        grad_forward(i).wait_send()
        return carry

    lax.fori_loop(0, GRADS, drain_grads, 0)

    def drain_tiles(t, carry):
        y_copy(t).wait_send()
        for o in (1, 2, 3):
            z_copy(t, o).wait_send()
        return carry

    lax.fori_loop(0, TILES, drain_tiles, 0)


def reduce_layer(acts, grads, collective_id):
    dma = pltpu.SemaphoreType.DMA
    low, wide = jnp.bfloat16, jnp.float32
    return pl.pallas_call(
        rs_kernel,
        out_shape=jax.ShapeDtypeStruct((TILES, 32, 1024), wide),
        in_specs=[pl.BlockSpec(memory_space=pl.ANY)] * 2,
        out_specs=pl.BlockSpec(memory_space=pltpu.VMEM),
        scratch_shapes=[
            pltpu.VMEM((7, 256, 512), low),
            pltpu.VMEM((7, 256, 128), low),
            pltpu.VMEM((GRADS, 512, 1024), low),
            pltpu.VMEM((TILES, 128, 1024), low),
            pltpu.VMEM((TILES, 128, 1024), low),
            pltpu.VMEM((4, 128, 1024), wide),
            pltpu.VMEM((TILES, 3, 32, 1024), low),
            pltpu.VMEM((TILES, 3, 32, 1024), low),
            pltpu.VMEM((4, 32, 1024), wide),
            dma((2,)), dma((2, 2)), dma((2, 2)), dma((2, 2)), dma((2, 2)),
            dma((GRADS,)), dma((GRADS,)), dma((GRADS,)), dma((GRADS,)), dma((GRADS,)),
            dma((GRADS,)), dma((GRADS,)),
            dma((TILES,)), dma((TILES,)), dma((TILES, 3)), dma((TILES, 3)),
        ],
        compiler_params=pltpu.CompilerParams(
            collective_id=collective_id, has_side_effects=True, vmem_limit_bytes=48 * 2**20
        ),
        name="weight_gradient_reduce",
    )(acts, grads)


def act_blocks(values):
    turned = values.T.reshape(4, 2, 2, 2, -1, 32, values.shape[0])
    return turned.transpose(3, 2, 4, 1, 0, 5, 6).reshape(2, 2, -1, 256, values.shape[0])


def grad_blocks(values):
    return values.reshape(values.shape[0], -1, 1024).transpose(1, 0, 2)


def side_by_side(tiles):
    return tiles.transpose(1, 0, 2).reshape(tiles.shape[1], -1)


def reduce_weights(acts, grads, collective_id):
    tiles = reduce_layer(
        jnp.concatenate([act_blocks(member) for member in acts], axis=2),
        jnp.concatenate([grad_blocks(member) for member in grads], axis=0),
        collective_id,
    )
    return (
        side_by_side(tiles[11:13]),
        tiles[13],
        tiles[14],
        tiles[3:5].reshape(64, 1024),
        side_by_side(tiles[5:8]),
        side_by_side(tiles[8:11]),
        tiles[0:3].reshape(96, 1024),
    )


def from_partner(shard, axis, apart):
    return lax.ppermute(shard, axis, [(i, i ^ 1 << apart) for i in range(lax.axis_size(axis))])


def token_places(stretch_table, slot_lengths):
    ctx_count = stretch_table.shape[0]
    stretch_order = stretch_table.reshape(-1)
    within = jnp.arange(STRETCH, dtype=jnp.int32)
    places = (stretch_order % ctx_count * STRETCH)[:, None] + within[None, :]
    slot_ids = jnp.broadcast_to((stretch_order // ctx_count)[:, None], places.shape).reshape(-1)
    places = places.reshape(-1)
    limits = jnp.where(slot_ids == 0, slot_lengths[0], slot_lengths[1])
    return (places, slot_ids, places < limits)


def rotary_tables(places):
    half_dim = HEAD_SIZE // 2
    spread = jnp.arange(half_dim, dtype=jnp.int32).astype(jnp.float32) * (2.0 / HEAD_SIZE)
    inverse = jnp.exp(spread * -math.log(rope_base))
    angles = places.astype(jnp.float32)[:, None] * inverse[None, :]
    return (
        jnp.concatenate([jnp.cos(angles)] * 2, axis=-1),
        jnp.concatenate([jnp.sin(angles)] * 2, axis=-1),
    )


def rotate(values, cosine_table, sine_table):
    half_dim = values.shape[-1] // 2
    turned = jnp.concatenate([-values[..., half_dim:], values[..., :half_dim]], axis=-1)
    return values * cosine_table[:, None, :] + turned * sine_table[:, None, :]


def unrotate(upstream, cosine_table, sine_table):
    half_dim = upstream.shape[-1] // 2
    scaled_sine = upstream * sine_table[:, None, :]
    turned_back = jnp.concatenate(
        [scaled_sine[..., half_dim:], -scaled_sine[..., :half_dim]], axis=-1
    )
    return upstream * cosine_table[:, None, :] + turned_back


def norm_forward(values, gain_vec):
    scale_inv = lax.rsqrt(jnp.mean(values * values, axis=-1, keepdims=True) + norm_epsilon)
    return (values * scale_inv * gain_vec, scale_inv)


def norm_backward(values, scale_inv, gain_vec, upstream):
    weighted = upstream * gain_vec
    grad_input = scale_inv * weighted - values * scale_inv**3 * jnp.mean(
        weighted * values, axis=-1, keepdims=True
    )
    gain_term = jnp.sum((upstream * values * scale_inv).reshape(-1, values.shape[-1]), axis=0)
    return (grad_input, gain_term)


def upper_bit(local_index, bit_number):
    return local_index // 2**bit_number % 2 == 1


def joined_rows(mine, received, upper_side):
    first_rows = jnp.where(upper_side, received, mine)
    second_rows = jnp.where(upper_side, mine, received)
    return jnp.concatenate([first_rows, second_rows], axis=0)


def half_gather(pair, local_index):
    gathered_rows = pair
    for bit_number in range(lax.axis_size("ctx").bit_length() - 2):
        received = from_partner(gathered_rows, "ctx", bit_number)
        gathered_rows = joined_rows(gathered_rows, received, upper_bit(local_index, bit_number))
    return gathered_rows


def half_reduce(term, local_index):
    for bit_number in reversed(range(lax.axis_size("ctx").bit_length() - 2)):
        span = term.shape[0] // 2
        lower_rows = term[:span]
        upper_rows = term[span:]
        upper_side = upper_bit(local_index, bit_number)
        kept_rows = jnp.where(upper_side, upper_rows, lower_rows)
        sent_rows = jnp.where(upper_side, lower_rows, upper_rows)
        term = kept_rows + from_partner(sent_rows, "ctx", bit_number)
    return term


def over_keys(update, carried, count_rows):
    block_length = math.gcd(count_rows, 512)

    def inner_step(current, block_index):
        return (update(current, block_index * block_length, block_length), None)

    carried, unused = lax.scan(
        inner_step, carried, jnp.arange(count_rows // block_length, dtype=jnp.int32)
    )
    return carried


def allowed_mask(key_meta, query_meta, row_start, block_length):
    key_places = lax.dynamic_slice_in_dim(key_meta[0], row_start, block_length)
    key_slots = lax.dynamic_slice_in_dim(key_meta[1], row_start, block_length)
    key_live = lax.dynamic_slice_in_dim(key_meta[2], row_start, block_length)
    allowed = (
        (key_slots[None, :] == query_meta[1][:, None])
        & (key_places[None, :] <= query_meta[0][:, None])
        & key_live[None, :]
    )
    return allowed[None, None]


def forward_update(
    current, query_head_group, key_tile_block, value_tile_block, allowed, score_scale
):
    running_max, running_sum, running_acc = current
    block_length = key_tile_block.shape[0]
    key_head_list = key_tile_block.reshape(block_length, KEY_VALUE_HEADS, HEAD_SIZE)
    value_head_list = value_tile_block.reshape(block_length, KEY_VALUE_HEADS, HEAD_SIZE)
    scores = (
        jnp.einsum(
            "qhgd,khd->hgqk", query_head_group, key_head_list, preferred_element_type=jnp.float32
        )
        * score_scale
    )
    scores = jnp.where(allowed, scores, masked_logits)
    new_max = jnp.maximum(running_max, jnp.max(scores, axis=-1))
    factor = jnp.exp(running_max - new_max)
    prob_block = jnp.where(allowed, jnp.exp(scores - new_max[..., None]), 0.0)
    new_sum = running_sum * factor + jnp.sum(prob_block, axis=-1)
    new_acc = running_acc * factor[..., None] + jnp.einsum(
        "hgqk,khd->hgqd",
        prob_block.astype(jnp.bfloat16),
        value_head_list,
        preferred_element_type=jnp.float32,
    )
    return (new_max, new_sum, new_acc)


def score_parts(
    query_head_group,
    output_grad_group,
    key_tile_block,
    value_tile_block,
    allowed,
    log_total,
    row_delta,
    score_scale,
):
    block_length = key_tile_block.shape[0]
    key_head_list = key_tile_block.reshape(block_length, KEY_VALUE_HEADS, HEAD_SIZE)
    value_head_list = value_tile_block.reshape(block_length, KEY_VALUE_HEADS, HEAD_SIZE)
    scores = (
        jnp.einsum(
            "qhgd,khd->hgqk", query_head_group, key_head_list, preferred_element_type=jnp.float32
        )
        * score_scale
    )
    prob_block = jnp.where(allowed, jnp.exp(scores - log_total[..., None]), 0.0)
    dprob = jnp.einsum(
        "qhgd,khd->hgqk", output_grad_group, value_head_list, preferred_element_type=jnp.float32
    )
    dscore_low = (prob_block * (dprob - row_delta[..., None])).astype(jnp.bfloat16)
    return (prob_block, dscore_low, key_head_list)


def attention_inputs(stream, gathered, cosine_table, sine_table):
    count_rows = stream.shape[0]
    normalized, inv_attn = norm_forward(stream, gathered[7].astype(jnp.float32))
    normed_low = normalized.astype(jnp.bfloat16)
    query_heads = jnp.dot(normed_low, gathered[0], preferred_element_type=jnp.float32).reshape(
        count_rows, QUERY_HEADS, HEAD_SIZE
    )
    key_head_list = jnp.dot(normed_low, gathered[1], preferred_element_type=jnp.float32).reshape(
        count_rows, KEY_VALUE_HEADS, HEAD_SIZE
    )
    value_low = jnp.dot(normed_low, gathered[2], preferred_element_type=jnp.float32).astype(
        jnp.bfloat16
    )
    query_normed, inv_query = norm_forward(query_heads, gathered[9].astype(jnp.float32))
    key_normed, inv_key = norm_forward(key_head_list, gathered[10].astype(jnp.float32))
    query_lowered = rotate(query_normed, cosine_table, sine_table).astype(jnp.bfloat16)
    key_low = (
        rotate(key_normed, cosine_table, sine_table)
        .astype(jnp.bfloat16)
        .reshape(count_rows, KEY_VALUE_HEADS * HEAD_SIZE)
    )
    return {
        "normed_low": normed_low,
        "inv_attn": inv_attn,
        "query_heads": query_heads,
        "inv_query": inv_query,
        "key_heads": key_head_list,
        "inv_key": inv_key,
        "query_low": query_lowered,
        "key_low": key_low,
        "value_low": value_low,
    }


def block_rest(stream, gathered, attn_low):
    middle = stream + jnp.dot(attn_low, gathered[3], preferred_element_type=jnp.float32)
    normed_mid, inv_mid = norm_forward(middle, gathered[8].astype(jnp.float32))
    normed_mid_low = normed_mid.astype(jnp.bfloat16)
    gate_act = jnp.dot(normed_mid_low, gathered[4], preferred_element_type=jnp.float32)
    upward = jnp.dot(normed_mid_low, gathered[5], preferred_element_type=jnp.float32)
    hidden_low = (jax.nn.silu(gate_act) * upward).astype(jnp.bfloat16)
    result = middle + jnp.dot(hidden_low, gathered[6], preferred_element_type=jnp.float32)
    return {
        "middle": middle,
        "inv_mid": inv_mid,
        "normed_mid_low": normed_mid_low,
        "gate_act": gate_act,
        "upward": upward,
        "hidden_low": hidden_low,
        "result": result,
    }


def per_device(
    tokens,
    cotangent,
    lengths,
    stretch_ids,
    w_query,
    key_projection_weight,
    value_projection_weight,
    w_out,
    w_gate,
    w_up,
    w_down,
    g_attn,
    g_mlp,
    g_query,
    g_key,
):
    count_rows = tokens.shape[0]
    ctx_count = lax.axis_size("ctx")
    half_count = ctx_count // 2
    key_value_width = KEY_VALUE_HEADS * HEAD_SIZE
    key_meta = token_places(stretch_ids[:, 0, :], lengths[0])
    ctx_index = lax.axis_index("ctx")
    local_index = ctx_index % half_count
    base_row = ctx_index // half_count * half_count * count_rows
    half_row_set = half_count * count_rows
    offset_mine = ctx_index * count_rows
    query_meta = tuple(
        (lax.dynamic_slice_in_dim(meta_array, offset_mine, count_rows) for meta_array in key_meta)
    )
    live_mine = query_meta[2].astype(jnp.float32)[:, None]
    cosine_table, sine_table = rotary_tables(query_meta[0])
    group_count = QUERY_HEADS // KEY_VALUE_HEADS
    score_scale = HEAD_SIZE ** (-0.5)

    def attend_forward(query_head_group, key_source, value_source, current):

        def update(carried, local_row, block_length):
            key_tile_block = lax.dynamic_slice_in_dim(key_source, local_row, block_length)
            value_tile_block = lax.dynamic_slice_in_dim(value_source, local_row, block_length)
            allowed = allowed_mask(key_meta, query_meta, base_row + local_row, block_length)
            return forward_update(
                carried, query_head_group, key_tile_block, value_tile_block, allowed, score_scale
            )

        return over_keys(update, current, key_source.shape[0])

    saved = []
    stream = tokens.astype(jnp.float32)
    for layer_index in range(DECODER_LAYERS):
        gathered = (
            lax.all_gather(w_query[layer_index], "fsdp", axis=0, tiled=True),
            lax.all_gather(key_projection_weight[layer_index], "fsdp", axis=0, tiled=True),
            lax.all_gather(value_projection_weight[layer_index], "fsdp", axis=0, tiled=True),
            lax.all_gather(w_out[layer_index], "fsdp", axis=0, tiled=True),
            lax.all_gather(w_gate[layer_index], "fsdp", axis=0, tiled=True),
            lax.all_gather(w_up[layer_index], "fsdp", axis=0, tiled=True),
            lax.all_gather(w_down[layer_index], "fsdp", axis=0, tiled=True),
            lax.all_gather(g_attn[layer_index], "fsdp", axis=0, tiled=True),
            lax.all_gather(g_mlp[layer_index], "fsdp", axis=0, tiled=True),
            lax.all_gather(g_query[layer_index], "fsdp", axis=0, tiled=True),
            lax.all_gather(g_key[layer_index], "fsdp", axis=0, tiled=True),
        )
        present_inputs = attention_inputs(stream, gathered, cosine_table, sine_table)
        query_head_group = present_inputs["query_low"].reshape(
            count_rows, KEY_VALUE_HEADS, group_count, HEAD_SIZE
        )
        start_state = (
            jnp.full((KEY_VALUE_HEADS, group_count, count_rows), masked_logits, jnp.float32),
            jnp.zeros((KEY_VALUE_HEADS, group_count, count_rows), jnp.float32),
            jnp.zeros((KEY_VALUE_HEADS, group_count, count_rows, HEAD_SIZE), jnp.float32),
        )
        pair_all = half_gather(
            jnp.concatenate([present_inputs["key_low"], present_inputs["value_low"]], axis=-1),
            local_index,
        )
        key_all = pair_all[:, :key_value_width]
        value_all = pair_all[:, key_value_width:]
        final_state = attend_forward(query_head_group, key_all, value_all, start_state)
        attended = final_state[2] / final_state[1][..., None]
        log_total = final_state[0] + jnp.log(final_state[1])
        attn_low = (
            jnp.transpose(attended, (2, 0, 1, 3))
            .reshape(count_rows, QUERY_HEADS * HEAD_SIZE)
            .astype(jnp.bfloat16)
        )
        rest = block_rest(stream, gathered, attn_low)
        kept = (gathered, key_all, value_all, present_inputs, rest)
        saved.append((stream, attended, log_total, kept))
        stream = rest["result"]
    output_low = (stream * live_mine).astype(jnp.bfloat16)
    grad_stream = cotangent.astype(jnp.float32) * live_mine
    layer_grads = [None] * DECODER_LAYERS
    for layer_index in reversed(range(DECODER_LAYERS)):
        stream_in, attended, log_total, kept = saved[layer_index]
        attn_low = (
            jnp.transpose(attended, (2, 0, 1, 3))
            .reshape(count_rows, QUERY_HEADS * HEAD_SIZE)
            .astype(jnp.bfloat16)
        )
        gathered, key_all, value_all, present_inputs, rest = kept
        ffn_grad_low = grad_stream.astype(jnp.bfloat16)
        hidden_grad = jnp.einsum(
            "td,fd->tf", ffn_grad_low, gathered[6], preferred_element_type=jnp.float32
        )
        gate_act = rest["gate_act"]
        sigmoid_gate = jax.nn.sigmoid(gate_act)
        gate_grad_low = (
            hidden_grad * rest["upward"] * sigmoid_gate * (1.0 + gate_act * (1.0 - sigmoid_gate))
        ).astype(jnp.bfloat16)
        up_grad_low = (hidden_grad * gate_act * sigmoid_gate).astype(jnp.bfloat16)
        normed_mid_grad = jnp.einsum(
            "tf,df->td", gate_grad_low, gathered[4], preferred_element_type=jnp.float32
        ) + jnp.einsum("tf,df->td", up_grad_low, gathered[5], preferred_element_type=jnp.float32)
        mid_norm_grad, mlp_gain_term = norm_backward(
            rest["middle"], rest["inv_mid"], gathered[8].astype(jnp.float32), normed_mid_grad
        )
        middle_grad = grad_stream + mid_norm_grad
        attn_grad_low = middle_grad.astype(jnp.bfloat16)
        output_gradient_lowered = jnp.einsum(
            "td,qd->tq", attn_grad_low, gathered[3], preferred_element_type=jnp.float32
        ).astype(jnp.bfloat16)
        output_grad_group = output_gradient_lowered.reshape(
            count_rows, KEY_VALUE_HEADS, group_count, HEAD_SIZE
        )
        row_delta = jnp.sum(
            jnp.transpose(output_grad_group.astype(jnp.float32), (1, 2, 0, 3)) * attended, axis=-1
        )
        query_head_group = present_inputs["query_low"].reshape(
            count_rows, KEY_VALUE_HEADS, group_count, HEAD_SIZE
        )
        key_block_size = math.gcd(half_row_set, 512)

        def backward_step(query_acc, block_index):
            row_start = block_index * key_block_size
            key_tile_block = lax.dynamic_slice_in_dim(key_all, row_start, key_block_size)
            value_tile_block = lax.dynamic_slice_in_dim(value_all, row_start, key_block_size)
            allowed = allowed_mask(key_meta, query_meta, base_row + row_start, key_block_size)
            prob_block, dscore_low, key_head_list = score_parts(
                query_head_group,
                output_grad_group,
                key_tile_block,
                value_tile_block,
                allowed,
                log_total,
                row_delta,
                score_scale,
            )
            query_next = (query_acc, jnp.zeros((key_block_size, 2 * key_value_width), jnp.float32))[
                0
            ] + jnp.einsum(
                "hgqk,khd->qhgd", dscore_low, key_head_list, preferred_element_type=jnp.float32
            ) * score_scale
            value_grad = jnp.einsum(
                "hgqk,qhgd->khd",
                prob_block.astype(jnp.bfloat16),
                output_grad_group,
                preferred_element_type=jnp.float32,
            )
            key_grad = (
                jnp.einsum(
                    "hgqk,qhgd->khd",
                    dscore_low,
                    query_head_group,
                    preferred_element_type=jnp.float32,
                )
                * score_scale
            )
            block_rows = jnp.concatenate(
                [
                    key_grad.reshape(key_block_size, key_value_width),
                    value_grad.reshape(key_block_size, key_value_width),
                ],
                axis=-1,
            )
            return (query_next, block_rows)

        query_grad, key_value_rows = lax.scan(
            backward_step,
            jnp.zeros((count_rows, KEY_VALUE_HEADS, group_count, HEAD_SIZE), jnp.float32),
            jnp.arange(half_row_set // key_block_size, dtype=jnp.int32),
        )
        key_value_term = key_value_rows.reshape(half_row_set, 2 * key_value_width)
        key_value_gradient = half_reduce(key_value_term, local_index)
        key_gradient_rows = key_value_gradient[:, :key_value_width].reshape(
            count_rows, KEY_VALUE_HEADS, HEAD_SIZE
        )
        value_grad_low = key_value_gradient[:, key_value_width:].astype(jnp.bfloat16)
        query_pre, query_gain_term = norm_backward(
            present_inputs["query_heads"],
            present_inputs["inv_query"],
            gathered[9].astype(jnp.float32),
            unrotate(
                query_grad.reshape(count_rows, QUERY_HEADS, HEAD_SIZE), cosine_table, sine_table
            ),
        )
        key_pre, key_gain_term = norm_backward(
            present_inputs["key_heads"],
            present_inputs["inv_key"],
            gathered[10].astype(jnp.float32),
            unrotate(key_gradient_rows, cosine_table, sine_table),
        )
        query_grad_low = query_pre.reshape(count_rows, QUERY_HEADS * HEAD_SIZE).astype(jnp.bfloat16)
        key_grad_low = key_pre.reshape(count_rows, key_value_width).astype(jnp.bfloat16)
        normed_low = present_inputs["normed_low"]
        normed_grad = jnp.einsum(
            "tq,dq->td", query_grad_low, gathered[0], preferred_element_type=jnp.float32
        )
        normed_grad = normed_grad + jnp.einsum(
            "tq,dq->td", key_grad_low, gathered[1], preferred_element_type=jnp.float32
        )
        normed_grad = normed_grad + jnp.einsum(
            "tq,dq->td", value_grad_low, gathered[2], preferred_element_type=jnp.float32
        )
        in_norm_grad, attn_gain_term = norm_backward(
            stream_in, present_inputs["inv_attn"], gathered[7].astype(jnp.float32), normed_grad
        )
        grad_stream = middle_grad + in_norm_grad
        gain_sums = tuple(
            (
                lax.psum_scatter(term, ("ctx", "fsdp"), scatter_dimension=0, tiled=True)
                for term in (attn_gain_term, mlp_gain_term, query_gain_term, key_gain_term)
            )
        )
        if half_count == KEY_VALUE_HEADS:
            weight_sums = reduce_weights(
                (rest["hidden_low"], attn_low, rest["normed_mid_low"], normed_low),
                (
                    ffn_grad_low,
                    attn_grad_low,
                    gate_grad_low,
                    up_grad_low,
                    query_grad_low,
                    key_grad_low,
                    value_grad_low,
                ),
                layer_index + 1,
            )
        else:
            weight_sums = tuple(
                (
                    lax.psum_scatter(
                        jnp.einsum("td,tq->dq", left, right, preferred_element_type=jnp.float32),
                        ("ctx", "fsdp"),
                        scatter_dimension=0,
                        tiled=True,
                    )
                    for left, right in (
                        (normed_low, query_grad_low),
                        (normed_low, key_grad_low),
                        (normed_low, value_grad_low),
                        (attn_low, attn_grad_low),
                        (rest["normed_mid_low"], gate_grad_low),
                        (rest["normed_mid_low"], up_grad_low),
                        (rest["hidden_low"], ffn_grad_low),
                    )
                )
            )
        layer_grads[layer_index] = weight_sums + gain_sums
    stacked = tuple(
        (jnp.stack([layer_sums[member] for layer_sums in layer_grads]) for member in range(11))
    )
    return (output_low, grad_stream) + stacked


def solution(mesh):
    in_specs = (
        P(("ctx", "fsdp"), None),
        P(("ctx", "fsdp"), None),
        P("fsdp", None),
        P(None, "fsdp", None),
        P(None, "fsdp", None),
        P(None, "fsdp", None),
        P(None, "fsdp", None),
        P(None, "fsdp", None),
        P(None, "fsdp", None),
        P(None, "fsdp", None),
        P(None, "fsdp", None),
        P(None, "fsdp"),
        P(None, "fsdp"),
        P(None, "fsdp"),
        P(None, "fsdp"),
    )
    out_specs = (
        P(("ctx", "fsdp"), None),
        P(("ctx", "fsdp"), None),
        P(None, ("ctx", "fsdp"), None),
        P(None, ("ctx", "fsdp"), None),
        P(None, ("ctx", "fsdp"), None),
        P(None, ("ctx", "fsdp"), None),
        P(None, ("ctx", "fsdp"), None),
        P(None, ("ctx", "fsdp"), None),
        P(None, ("ctx", "fsdp"), None),
        P(None, ("ctx", "fsdp")),
        P(None, ("ctx", "fsdp")),
        P(None, ("ctx", "fsdp")),
        P(None, ("ctx", "fsdp")),
    )
    return jax.shard_map(
        per_device, mesh=mesh, in_specs=in_specs, out_specs=out_specs, check_vma=False
    )
```

```python
import functools
import math

import jax
import jax.numpy as jnp
from jax import lax
from jax.experimental import pallas as pl
from jax.experimental.pallas import tpu as pltpu
from jax.sharding import PartitionSpec as P

QUERY_HEADS = 16
KEY_VALUE_HEADS = 8
HEAD_SIZE = 128
DECODER_LAYERS = 2
STRETCH = 64


norm_epsilon = 1e-06
rope_base = 1000000.0
masked_logits = -1e30

MESH = pl.DeviceIdType.MESH

TILES = 15
GRADS = 12
AHEAD = 3


def grad_index(t):
    return jnp.maximum(t - 3, jnp.where(t < 3, 0, 1))


def act_index(t):
    return jnp.minimum(t, 5) + jnp.where(t >= 11, 1, 0)


def is_new(t):
    return (t == 0) | (t == 3) | ((t >= 5) & (t < TILES))


def rs_kernel(
    acts, grads, gains, out, gain_out, abuf, afwd, gbuf, ysend, yrecv, own, zsend, zrecv, zown,
    a_local, a_xs, a_xr, a_cs, a_cr, g_local, g_xs, g_xr, g_cs, g_cr, g_fs, g_fr,
    y_s, y_r, z_s, z_r, gain_part, gain_recv, gain_s, gain_r,
):
    c = lax.axis_index("ctx")
    x = lax.axis_index("fsdp")
    core = c % 2
    y = c // 2 % 2
    z = c // 4
    sibling = (c + 1 - 2 * core, x)
    across = (c, 1 - x)
    aside = (c + 2 - 4 * y, x)

    def along(o):
        return ((z + o) % 4 * 4 + c % 4, x)

    barrier = pltpu.get_barrier_semaphore()
    for other in (sibling, across, aside, along(1), along(2), along(3)):
        pl.semaphore_signal(barrier, inc=1, device_id=other, device_id_type=MESH)
    pl.semaphore_wait(barrier, 6)

    def remote(src, dst, s, r, dev):
        return pltpu.make_async_remote_copy(
            src_ref=src, dst_ref=dst, send_sem=s, recv_sem=r, device_id=dev, device_id_type=MESH
        )

    spans = (pl.ds(0, 3), pl.ds(3, 4))

    def act_local(g):
        return pltpu.make_async_copy(
            acts.at[x, core, spans[g]], abuf.at[spans[g], :, pl.ds(0, 128)], a_local.at[g]
        )

    def act_across(g, other):
        if other:
            return remote(
                acts.at[1 - x, 1 - core, spans[g]], afwd.at[spans[g]],
                a_xs.at[g, 1], a_xr.at[g, 1], across,
            )
        return remote(
            acts.at[1 - x, core, spans[g]], abuf.at[spans[g], :, pl.ds(128, 128)],
            a_xs.at[g, 0], a_xr.at[g, 0], across,
        )

    def act_sibling(g):
        return remote(
            acts.at[x, 1 - core, spans[g]], abuf.at[spans[g], :, pl.ds(256, 128)],
            a_cs.at[g, 0], a_cr.at[g, 0], sibling,
        )

    def act_forward(g):
        return remote(
            afwd.at[spans[g]], abuf.at[spans[g], :, pl.ds(384, 128)],
            a_cs.at[g, 1], a_cr.at[g, 1], sibling,
        )

    def grad_local(i):
        return pltpu.make_async_copy(grads.at[i], gbuf.at[i, pl.ds(0, 128)], g_local.at[i])

    def grad_across(i):
        return remote(grads.at[i], gbuf.at[i, pl.ds(128, 128)], g_xs.at[i], g_xr.at[i], across)

    def grad_sibling(i):
        return remote(grads.at[i], gbuf.at[i, pl.ds(256, 128)], g_cs.at[i], g_cr.at[i], sibling)

    def grad_forward(i):
        return remote(
            gbuf.at[i, pl.ds(128, 128)], gbuf.at[i, pl.ds(384, 128)], g_fs.at[i], g_fr.at[i], sibling
        )

    def y_copy(t):
        return remote(ysend.at[t], yrecv.at[t], y_s.at[t], y_r.at[t], aside)

    def z_copy(t, o):
        return remote(
            zsend.at[t, o - 1], zrecv.at[t, 3 - o], z_s.at[t, o - 1], z_r.at[t, 3 - o], along(o)
        )

    def start_acts(g):
        act_across(g, 0).start()
        act_across(g, 1).start()
        act_sibling(g).start()
        act_local(g).start()

    def start_grad(i):
        grad_across(i).start()
        grad_sibling(i).start()
        grad_local(i).start()

    def gain_copy(i):
        return remote(
            gains if i == 0 else gain_part.at[i - 1],
            gain_recv.at[i],
            gain_s.at[i],
            gain_r.at[i],
            (across, sibling, aside)[i],
        )

    def gain_along(o):
        return remote(
            gain_part.at[2], gain_recv.at[6 - o], gain_s.at[2 + o], gain_r.at[6 - o], along(o)
        )

    gain_copy(0).start()
    start_acts(0)
    start_grad(0)
    start_acts(1)
    for i in range(1, AHEAD):
        start_grad(i)

    def forward_acts(g):
        act_across(g, 1).wait_recv()
        act_forward(g).start()

    def await_acts(g):
        act_local(g).wait()
        act_across(g, 0).wait_recv()
        act_sibling(g).wait_recv()
        act_forward(g).wait_recv()

    def step(s, carry):
        for i in range(3):

            @pl.when(s == 2 * i + 2)
            def gain_stage(i=i):
                gain_copy(i).wait_recv()
                gain_part[i] = (gains[...] if i == 0 else gain_part[i - 1]) + gain_recv[i]
                if i < 2:
                    gain_copy(i + 1).start()
                else:
                    for o in (1, 2, 3):
                        gain_along(o).start()

        @pl.when(s == 10)
        def gain_total():
            for o in (1, 2, 3):
                gain_along(o).wait_recv()
            gain_out[...] = gain_part[2] + gain_recv[3] + gain_recv[4] + gain_recv[5]

        t = s - 5

        @pl.when(t >= 0)
        def finish():
            total = zown[t % 4]
            for o in (1, 2, 3):
                z_copy(t, o).wait_recv()
            for o in range(3):
                total += zrecv[t, o].astype(jnp.float32)
            out[t] = total

        u = s - 3

        @pl.when((u >= 0) & (u < TILES))
        def spread():
            y_copy(u).wait_recv()

            def part(index):
                rows = pl.ds(pl.multiple_of(index * 32, 32), 32)
                return own[u % 4, rows, :] + yrecv[u, rows, :].astype(jnp.float32)

            for o in (2, 1, 3):
                zsend[u, o - 1] = part((z + o) % 4).astype(jnp.bfloat16)
                z_copy(u, o).start()
            zown[u % 4] = part(z)

        v = s - 1

        @pl.when((v >= 0) & (v < TILES))
        def compute():
            gi = grad_index(v)
            ai = act_index(v)

            @pl.when(v == 0)
            def first_acts():
                await_acts(0)

            @pl.when(v == 3)
            def second_acts():
                await_acts(1)

            @pl.when(is_new(v))
            def fresh():
                grad_local(gi).wait()
                grad_sibling(gi).wait_recv()
                grad_forward(gi).wait_recv()

            for half in range(2):
                cols = pl.ds(half * 512, 512)
                right = gbuf[gi, :, cols]
                theirs = pl.ds(pl.multiple_of((1 - y) * 128, 128), 128)
                mine = pl.ds(pl.multiple_of(y * 128, 128), 128)
                ysend[v, :, cols] = jnp.dot(
                    abuf[ai, theirs, :], right, preferred_element_type=jnp.float32
                ).astype(jnp.bfloat16)
                own[v % 4, :, cols] = jnp.dot(
                    abuf[ai, mine, :], right, preferred_element_type=jnp.float32
                )
            y_copy(v).start()

        @pl.when(is_new(s))
        def forward():
            i = grad_index(s)

            @pl.when(s == 0)
            def first_forward():
                forward_acts(0)

            @pl.when(s == 3)
            def second_forward():
                forward_acts(1)

            grad_across(i).wait_recv()
            grad_forward(i).start()

            @pl.when(i + AHEAD < GRADS)
            def more():
                start_grad(i + AHEAD)

        return carry

    lax.fori_loop(0, TILES + 5, step, 0)

    for i in range(3):
        gain_copy(i).wait_send()
        gain_along(i + 1).wait_send()
    for g in range(2):
        act_across(g, 0).wait_send()
        act_across(g, 1).wait_send()
        act_sibling(g).wait_send()
        act_forward(g).wait_send()

    def drain_grads(i, carry):
        grad_across(i).wait_send()
        grad_sibling(i).wait_send()
        grad_forward(i).wait_send()
        return carry

    lax.fori_loop(0, GRADS, drain_grads, 0)

    def drain_tiles(t, carry):
        y_copy(t).wait_send()
        for o in (1, 2, 3):
            z_copy(t, o).wait_send()
        return carry

    lax.fori_loop(0, TILES, drain_tiles, 0)


def reduce_layer(acts, grads, gains, collective_id):
    dma = pltpu.SemaphoreType.DMA
    low, wide = jnp.bfloat16, jnp.float32
    return pl.pallas_call(
        rs_kernel,
        out_shape=[
            jax.ShapeDtypeStruct((TILES, 32, 1024), wide),
            jax.ShapeDtypeStruct(gains.shape, wide),
        ],
        in_specs=[pl.BlockSpec(memory_space=pl.ANY)] * 2
        + [pl.BlockSpec(memory_space=pltpu.VMEM)],
        out_specs=[pl.BlockSpec(memory_space=pltpu.VMEM)] * 2,
        scratch_shapes=[
            pltpu.VMEM((7, 256, 512), low),
            pltpu.VMEM((7, 256, 128), low),
            pltpu.VMEM((GRADS, 512, 1024), low),
            pltpu.VMEM((TILES, 128, 1024), low),
            pltpu.VMEM((TILES, 128, 1024), low),
            pltpu.VMEM((4, 128, 1024), wide),
            pltpu.VMEM((TILES, 3, 32, 1024), low),
            pltpu.VMEM((TILES, 3, 32, 1024), low),
            pltpu.VMEM((4, 32, 1024), wide),
            dma((2,)), dma((2, 2)), dma((2, 2)), dma((2, 2)), dma((2, 2)),
            dma((GRADS,)), dma((GRADS,)), dma((GRADS,)), dma((GRADS,)), dma((GRADS,)),
            dma((GRADS,)), dma((GRADS,)),
            dma((TILES,)), dma((TILES,)), dma((TILES, 3)), dma((TILES, 3)),
            pltpu.VMEM((3,) + gains.shape, wide), pltpu.VMEM((6,) + gains.shape, wide),
            dma((6,)), dma((6,)),
        ],
        compiler_params=pltpu.CompilerParams(
            collective_id=collective_id, has_side_effects=True, vmem_limit_bytes=48 * 2**20
        ),
        name="weight_gradient_reduce",
    )(acts, grads, gains)


GATHER_PLAN = ((0, 0, 0), (1, 0, 2048), (2, 0, 3072), (3, 1, 0), (4, 2, 0), (5, 2, 3072), (6, 3, 0))
MEMBERS = 7


def gather_kernel(layers, *refs):
    sources = refs[:MEMBERS]
    gains = refs[MEMBERS]
    outs = refs[MEMBERS + 1 : MEMBERS + 1 + 4 * len(layers)]
    gains_out = refs[MEMBERS + 1 + 4 * len(layers)]
    (l_sem, l_rec, x_s, x_r, y_s, y_r, z_s, z_r, yd_s, yd_r, zd_s, zd_r, c_s, c_r, g_sem) = refs[
        MEMBERS + 2 + 4 * len(layers) :
    ]
    c = lax.axis_index("ctx")
    x = lax.axis_index("fsdp")
    core = c % 2
    y = c // 2 % 2
    near = c // 4 % 2
    sibling = (c + 1 - 2 * core, x)
    across = (c, 1 - x)
    aside = (c + 2 - 4 * y, x)
    along = (c + 4 - 8 * near, x)

    barrier = pltpu.get_barrier_semaphore()
    for other in (sibling, across, aside, along):
        pl.semaphore_signal(barrier, inc=1, device_id=other, device_id_type=MESH)
    pl.semaphore_wait(barrier, 4)

    def remote(src, dst, s, r, dev):
        return pltpu.make_async_remote_copy(
            src_ref=src, dst_ref=dst, send_sem=s, recv_sem=r, device_id=dev, device_id_type=MESH
        )

    here = near * 2 + y
    by_y = near * 2 + 1 - y
    by_z = (1 - near) * 2 + y
    corner = (1 - near) * 2 + 1 - y
    steps = [(n, m) for n in range(len(layers)) for m in range(MEMBERS)]
    count = len(steps)

    def geometry(i):
        n, m = steps[i]
        source, target, column = GATHER_PLAN[m]
        half = sources[source].shape[1]
        part = half // 8
        width = sources[source].shape[2]
        return n, sources[source], outs[4 * n + target], half, part, width, column

    def window(i, owner_x, owner_core, piece, share=None):
        n, src, out, half, part, width, column = geometry(i)
        start = owner_x * half + (piece * 2 + owner_core) * part
        rows = part
        if share is not None:
            rows = part // 2
            start = start + share * rows
        return out.at[pl.ds(pl.multiple_of(start, 16), rows), pl.ds(column, width)]

    def local(i):
        n, src, out, half, part, width, column = geometry(i)
        rows = pl.ds(pl.multiple_of(x * half, 16), half)
        return remote(
            src.at[layers[n]], out.at[rows, pl.ds(column, width)], l_sem.at[i], l_rec.at[i], sibling
        )

    def x_copy(i):
        n, src, out, half, part, width, column = geometry(i)
        rows = pl.ds(pl.multiple_of((here * 2 + core) * part, 16), part)
        return remote(
            src.at[layers[n], rows], window(i, x, core, here), x_s.at[i], x_r.at[i], across
        )

    def same(i, piece, s, r, dev, share=None):
        view = window(i, 1 - x, core, piece, share)
        return remote(view, view, s, r, dev)

    def y_copy(i):
        return same(i, here, y_s.at[i], y_r.at[i], aside)

    def z_copy(i):
        return same(i, here, z_s.at[i], z_r.at[i], along)

    def y_corner(i):
        return same(i, by_z, yd_s.at[i], yd_r.at[i], aside, 1)

    def z_corner(i):
        return same(i, by_y, zd_s.at[i], zd_r.at[i], along, 0)

    def core_copy(i, which):
        piece = (here, by_y, by_z, corner)[which]
        return same(i, piece, c_s.at[i, which], c_r.at[i, which], sibling)

    gain_local = pltpu.make_async_copy(gains, gains_out.at[x], g_sem.at[0])
    gain_remote = remote(gains, gains_out.at[x], g_sem.at[1], g_sem.at[2], across)
    gain_local.start()
    gain_remote.start()

    ahead = 3
    for i in range(min(ahead, count)):
        x_copy(i).start()
        local(i).start()
    for s in range(count + 3):
        if s < count:
            x_copy(s).wait_recv()
            y_copy(s).start()
            z_copy(s).start()
            core_copy(s, 0).start()
            if s + ahead < count:
                x_copy(s + ahead).start()
                local(s + ahead).start()
        i = s - 1
        if 0 <= i < count:
            y_copy(i).wait_recv()
            z_corner(i).start()
            core_copy(i, 1).start()
            z_copy(i).wait_recv()
            y_corner(i).start()
            core_copy(i, 2).start()
        i = s - 3
        if 0 <= i < count:
            y_corner(i).wait_recv()
            z_corner(i).wait_recv()
            core_copy(i, 3).start()
    gain_local.wait()
    gain_remote.wait()
    for i in range(count):
        local(i).wait()
        for copy in (x_copy(i), y_copy(i), z_copy(i), y_corner(i), z_corner(i)):
            copy.wait_send()
        for which in range(4):
            core_copy(i, which).wait()


def gather_weights(weights, gains, layers, collective_id):
    dma = pltpu.SemaphoreType.DMA
    count = MEMBERS * len(layers)
    low = jnp.bfloat16
    shapes = [(1024, 4096), (2048, 1024), (1024, 6144), (3072, 1024)] * len(layers)
    return pl.pallas_call(
        functools.partial(gather_kernel, layers),
        out_shape=[jax.ShapeDtypeStruct(s, low) for s in shapes]
        + [jax.ShapeDtypeStruct((2,) + gains.shape, low)],
        in_specs=[pl.BlockSpec(memory_space=pl.ANY)] * (MEMBERS + 1),
        out_specs=[pl.BlockSpec(memory_space=pl.ANY)] * (len(shapes) + 1),
        scratch_shapes=[dma((count,))] * 12 + [dma((count, 4))] * 2 + [dma((3,))],
        compiler_params=pltpu.CompilerParams(collective_id=collective_id, has_side_effects=True),
        name="weight_gather",
    )(*weights, gains)


PEERS = KEY_VALUE_HEADS
SCALE = HEAD_SIZE ** (-0.5)
NT = (((1,), (1,)), ((), ()))


def peer_tools():
    c = lax.axis_index("ctx")
    x = lax.axis_index("fsdp")
    me = c % PEERS

    def peer(r):
        return (c - me + r, x)

    def remote(src, dst, s, r, dev):
        return pltpu.make_async_remote_copy(
            src_ref=src, dst_ref=dst, send_sem=s, recv_sem=r, device_id=dev, device_id_type=MESH
        )

    barrier = pltpu.get_barrier_semaphore()

    def greet(o, carry):
        pl.semaphore_signal(
            barrier, inc=1, device_id=peer((me + o) % PEERS), device_id_type=MESH
        )
        return carry

    lax.fori_loop(1, PEERS, greet, 0)
    return me, peer, remote, barrier


def head_columns(first, index):
    return pl.ds(pl.multiple_of(first + index * HEAD_SIZE, HEAD_SIZE), HEAD_SIZE)


def attend_kernel(
    pre, cosine, sine, gains, key_place, query_cap, out, kept, kept_out, kept_log,
    send, osend, orecv, vt, q_s, q_r, k_s, k_r, o_s, o_r,
):
    me, peer, remote, barrier = peer_tools()
    cos = cosine[...]
    sin = sine[...]

    def turned(first, index, gain):
        v = pre[:, head_columns(first, index)]
        r = lax.rsqrt(jnp.mean(v * v, axis=-1, keepdims=True) + norm_epsilon)
        n = v * r * gain
        return (n * cos + pltpu.roll(n, HEAD_SIZE // 2, 1) * sin).astype(jnp.bfloat16)

    def key_copy(r, slot):
        return remote(
            send.at[r, pl.ds(2, 2)], kept.at[slot, pl.ds(2, 2)], k_s.at[r], k_r.at[slot], peer(r)
        )

    def query_copy(r, slot):
        return remote(
            send.at[r, pl.ds(0, 2)], kept.at[slot, pl.ds(0, 2)], q_s.at[r], q_r.at[slot], peer(r)
        )

    def out_copy(r, slot):
        return remote(osend.at[r], orecv.at[slot], o_s.at[r], o_r.at[slot], peer(r))

    def make_keys(o, carry):
        r = (me + o) % PEERS
        key = turned(2048, r, gains[1:2, :])
        value = pre[:, head_columns(3072, r)].astype(jnp.bfloat16)

        @pl.when(o < PEERS)
        def away():
            send[r, 2] = key
            send[r, 3] = value

        @pl.when(o == PEERS)
        def home():
            kept[me, 2] = key
            kept[me, 3] = value

        @pl.when(o == 1)
        def entered():
            pl.semaphore_wait(barrier, PEERS - 1)

        @pl.when(o < PEERS)
        def push():
            key_copy(r, me).start()

        return carry

    def make_queries(o, carry):
        r = (me + o) % PEERS
        first = turned(0, 2 * r, gains[0:1, :])
        second = turned(0, 2 * r + 1, gains[0:1, :])

        @pl.when(o < PEERS)
        def away():
            send[r, 0] = first
            send[r, 1] = second
            query_copy(r, me).start()

        @pl.when(o == PEERS)
        def home():
            kept[me, 0] = first
            kept[me, 1] = second

        return carry

    lax.fori_loop(1, PEERS + 1, make_keys, 0)
    lax.fori_loop(1, PEERS + 1, make_queries, 0)

    def await_keys(o, carry):
        key_copy(me, (me + o) % PEERS).wait_recv()
        return carry

    lax.fori_loop(1, PEERS, await_keys, 0)

    def turn_values(j, carry):
        vt[j] = kept[j, 3].astype(jnp.float32).T.astype(jnp.bfloat16)
        return carry

    lax.fori_loop(0, PEERS, turn_values, 0)

    def block(o, carry):
        j = (me + o) % PEERS

        @pl.when(o > 0)
        def arrived():
            query_copy(me, j).wait_recv()

        queries = kept[j, 0:2].reshape(2 * 128, HEAD_SIZE)
        keys = kept[:, 2].reshape(PEERS * 128, HEAD_SIZE)
        scores = lax.dot_general(keys, queries, NT, preferred_element_type=jnp.float32) * SCALE
        allowed = key_place[...] <= query_cap[j]
        scores = jnp.where(allowed, scores, masked_logits)
        highest = jnp.max(scores, axis=0, keepdims=True)
        expo = jnp.exp(scores - highest)
        total = jnp.sum(expo, axis=0, keepdims=True)
        low = expo.astype(jnp.bfloat16)
        turned_out = jnp.zeros((HEAD_SIZE, 256), jnp.float32)
        for i in range(PEERS):
            turned_out += jnp.dot(
                vt[i], low[i * 128 : (i + 1) * 128], preferred_element_type=jnp.float32
            )
        turned_out = turned_out / total
        kept_out[j] = turned_out
        kept_log[j] = jnp.broadcast_to(highest + jnp.log(total), (8, 256))
        attended = turned_out.T.astype(jnp.bfloat16).reshape(2, 128, HEAD_SIZE)

        @pl.when(o == 0)
        def home():
            orecv[me] = attended

        @pl.when(o > 0)
        def away():
            osend[j] = attended
            out_copy(j, me).start()

        return carry

    lax.fori_loop(0, PEERS, block, 0)

    def collect(o, carry):
        h = (me + o) % PEERS

        @pl.when(o > 0)
        def arrived():
            out_copy(me, h).wait_recv()

        out[:, head_columns(0, 2 * h)] = orecv[h, 0]
        out[:, head_columns(0, 2 * h + 1)] = orecv[h, 1]
        return carry

    lax.fori_loop(0, PEERS, collect, 0)

    def drain(o, carry):
        r = (me + o) % PEERS
        key_copy(r, me).wait_send()
        query_copy(r, me).wait_send()
        out_copy(r, me).wait_send()
        return carry

    lax.fori_loop(1, PEERS, drain, 0)


def attend(pre, cosine, sine, gains, key_place, query_cap, collective_id):
    dma = pltpu.SemaphoreType.DMA
    low, wide = jnp.bfloat16, jnp.float32
    return pl.pallas_call(
        attend_kernel,
        out_shape=[
            jax.ShapeDtypeStruct((128, 2048), low),
            jax.ShapeDtypeStruct((PEERS, 4, 128, HEAD_SIZE), low),
            jax.ShapeDtypeStruct((PEERS, HEAD_SIZE, 256), wide),
            jax.ShapeDtypeStruct((PEERS, 8, 256), wide),
        ],
        in_specs=[pl.BlockSpec(memory_space=pltpu.VMEM)] * 6,
        out_specs=[pl.BlockSpec(memory_space=pltpu.VMEM)] * 4,
        scratch_shapes=[
            pltpu.VMEM((PEERS, 4, 128, HEAD_SIZE), low),
            pltpu.VMEM((PEERS, 2, 128, HEAD_SIZE), low),
            pltpu.VMEM((PEERS, 2, 128, HEAD_SIZE), low),
            pltpu.VMEM((PEERS, HEAD_SIZE, 128), low),
        ]
        + [dma((PEERS,))] * 6,
        compiler_params=pltpu.CompilerParams(
            collective_id=collective_id, has_side_effects=True, vmem_limit_bytes=40 * 2**20
        ),
        name="attend",
    )(pre, cosine, sine, gains, key_place, query_cap)


def attend_back_kernel(
    upstream, kept, kept_out, kept_log, pre, cosine, sine, gains, key_place, query_cap,
    out, gain_out,
    dsend, drecv, qsend, qrecv, ksend, krecv, kt, key_sum, value_sum,
    d_s, d_r, q_s, q_r, k_s, k_r,
):
    me, peer, remote, barrier = peer_tools()
    cos = cosine[...]
    sin = sine[...]

    def grad_copy(r, slot):
        return remote(dsend.at[r], drecv.at[slot], d_s.at[r], d_r.at[slot], peer(r))

    def query_copy(r, slot):
        return remote(qsend.at[r], qrecv.at[slot], q_s.at[r], q_r.at[slot], peer(r))

    def key_copy(r, slot):
        return remote(ksend.at[r], krecv.at[slot], k_s.at[r], k_r.at[slot], peer(r))

    pl.semaphore_wait(barrier, PEERS - 1)

    def push(o, carry):
        r = (me + o) % PEERS
        dsend[r, 0] = upstream[:, head_columns(0, 2 * r)]
        dsend[r, 1] = upstream[:, head_columns(0, 2 * r + 1)]
        grad_copy(r, me).start()
        return carry

    lax.fori_loop(1, PEERS, push, 0)
    drecv[me, 0] = upstream[:, head_columns(0, 2 * me)]
    drecv[me, 1] = upstream[:, head_columns(0, 2 * me + 1)]

    def turn_keys(j, carry):
        kt[j] = kept[j, 2].astype(jnp.float32).T.astype(jnp.bfloat16)
        return carry

    lax.fori_loop(0, PEERS, turn_keys, 0)
    key_sum[...] = jnp.zeros_like(key_sum)
    value_sum[...] = jnp.zeros_like(value_sum)

    def block(o, carry):
        j = (me + o) % PEERS

        @pl.when(o > 0)
        def arrived():
            grad_copy(me, j).wait_recv()

        grads = drecv[j].reshape(2 * 128, HEAD_SIZE)
        delta = jnp.sum(grads.astype(jnp.float32).T * kept_out[j], axis=0, keepdims=True)
        queries = kept[j, 0:2].reshape(2 * 128, HEAD_SIZE)
        keys = kept[:, 2].reshape(PEERS * 128, HEAD_SIZE)
        values = kept[:, 3].reshape(PEERS * 128, HEAD_SIZE)
        scores = lax.dot_general(keys, queries, NT, preferred_element_type=jnp.float32) * SCALE
        allowed = key_place[...] <= query_cap[j]
        scores = jnp.where(allowed, scores, masked_logits)
        prob = jnp.exp(scores - kept_log[j, 0:1, :])
        dprob = lax.dot_general(values, grads, NT, preferred_element_type=jnp.float32)
        dscore = (prob * (dprob - delta)).astype(jnp.bfloat16)
        value_sum[...] += jnp.dot(
            prob.astype(jnp.bfloat16), grads, preferred_element_type=jnp.float32
        )
        key_sum[...] += jnp.dot(dscore, queries, preferred_element_type=jnp.float32)
        turned = jnp.zeros((HEAD_SIZE, 256), jnp.float32)
        for i in range(PEERS):
            turned += jnp.dot(
                kt[i], dscore[i * 128 : (i + 1) * 128], preferred_element_type=jnp.float32
            )
        query_grad = (turned * SCALE).T.astype(jnp.bfloat16).reshape(2, 128, HEAD_SIZE)

        @pl.when(o == 0)
        def home():
            qrecv[me] = query_grad

        @pl.when(o > 0)
        def away():
            qsend[j] = query_grad
            query_copy(j, me).start()

        return carry

    lax.fori_loop(0, PEERS, block, 0)

    def push_keys(o, carry):
        j = (me + o) % PEERS
        rows = pl.ds(pl.multiple_of(j * 128, 128), 128)
        key = (key_sum[rows, :] * SCALE).astype(jnp.bfloat16)
        value = value_sum[rows, :].astype(jnp.bfloat16)

        @pl.when(o < PEERS)
        def away():
            ksend[j, 0] = key
            ksend[j, 1] = value
            key_copy(j, me).start()

        @pl.when(o == PEERS)
        def home():
            krecv[me, 0] = key
            krecv[me, 1] = value

        return carry

    lax.fori_loop(1, PEERS + 1, push_keys, 0)

    def back(grad, first, index, gain):
        g = grad.astype(jnp.float32)
        dy = g * cos - pltpu.roll(g, HEAD_SIZE // 2, 1) * sin
        v = pre[:, head_columns(first, index)]
        r = lax.rsqrt(jnp.mean(v * v, axis=-1, keepdims=True) + norm_epsilon)
        u = dy * gain
        result = r * u - v * (r * r * r) * jnp.mean(u * v, axis=-1, keepdims=True)
        return result.astype(jnp.bfloat16), jnp.sum(dy * v * r, axis=0, keepdims=True)

    def finish_queries(o, total):
        h = (me + o) % PEERS

        @pl.when(o > 0)
        def arrived():
            query_copy(me, h).wait_recv()

        for i in range(2):
            low, term = back(qrecv[h, i], 0, 2 * h + i, gains[0:1, :])
            out[:, head_columns(0, 2 * h + i)] = low
            total += term
        return total

    zero = jnp.zeros((1, HEAD_SIZE), jnp.float32)
    query_total = lax.fori_loop(0, PEERS, finish_queries, zero)

    def finish_keys(o, total):
        h = (me + o) % PEERS

        @pl.when(o > 0)
        def arrived():
            key_copy(me, h).wait_recv()

        low, term = back(krecv[h, 0], 2048, h, gains[1:2, :])
        out[:, head_columns(2048, h)] = low
        out[:, head_columns(3072, h)] = krecv[h, 1]
        return total + term

    key_total = lax.fori_loop(0, PEERS, finish_keys, zero)
    gain_out[...] = jnp.concatenate(
        [query_total, key_total, jnp.zeros((6, HEAD_SIZE), jnp.float32)], axis=0
    )

    def drain(o, carry):
        r = (me + o) % PEERS
        grad_copy(r, me).wait_send()
        query_copy(r, me).wait_send()
        key_copy(r, me).wait_send()
        return carry

    lax.fori_loop(1, PEERS, drain, 0)


def attend_back(
    upstream, kept, kept_out, kept_log, pre, cosine, sine, gains, key_place, query_cap, collective_id
):
    dma = pltpu.SemaphoreType.DMA
    low, wide = jnp.bfloat16, jnp.float32
    pair = pltpu.VMEM((PEERS, 2, 128, HEAD_SIZE), low)
    return pl.pallas_call(
        attend_back_kernel,
        out_shape=[
            jax.ShapeDtypeStruct((128, 4096), low),
            jax.ShapeDtypeStruct((8, HEAD_SIZE), wide),
        ],
        in_specs=[pl.BlockSpec(memory_space=pltpu.VMEM)] * 10,
        out_specs=[pl.BlockSpec(memory_space=pltpu.VMEM)] * 2,
        scratch_shapes=[pair] * 6
        + [
            pltpu.VMEM((PEERS, HEAD_SIZE, 128), low),
            pltpu.VMEM((PEERS * 128, HEAD_SIZE), wide),
            pltpu.VMEM((PEERS * 128, HEAD_SIZE), wide),
        ]
        + [dma((PEERS,))] * 6,
        compiler_params=pltpu.CompilerParams(
            collective_id=collective_id, has_side_effects=True, vmem_limit_bytes=48 * 2**20
        ),
        name="attend_back",
    )(upstream, kept, kept_out, kept_log, pre, cosine, sine, gains, key_place, query_cap)


def from_partner(shard, axis, apart):
    return lax.ppermute(shard, axis, [(i, i ^ 1 << apart) for i in range(lax.axis_size(axis))])


def token_places(stretch_table, slot_lengths):
    ctx_count = stretch_table.shape[0]
    stretch_order = stretch_table.reshape(-1)
    within = jnp.arange(STRETCH, dtype=jnp.int32)
    places = (stretch_order % ctx_count * STRETCH)[:, None] + within[None, :]
    slot_ids = jnp.broadcast_to((stretch_order // ctx_count)[:, None], places.shape).reshape(-1)
    places = places.reshape(-1)
    limits = jnp.where(slot_ids == 0, slot_lengths[0], slot_lengths[1])
    return (places, slot_ids, places < limits)


def rotary_tables(places):
    half_dim = HEAD_SIZE // 2
    spread = jnp.arange(half_dim, dtype=jnp.int32).astype(jnp.float32) * (2.0 / HEAD_SIZE)
    inverse = jnp.exp(spread * -math.log(rope_base))
    angles = places.astype(jnp.float32)[:, None] * inverse[None, :]
    return (
        jnp.concatenate([jnp.cos(angles)] * 2, axis=-1),
        jnp.concatenate([jnp.sin(angles)] * 2, axis=-1),
    )


def rotate(values, cosine_table, sine_table):
    half_dim = values.shape[-1] // 2
    turned = jnp.concatenate([-values[..., half_dim:], values[..., :half_dim]], axis=-1)
    return values * cosine_table[:, None, :] + turned * sine_table[:, None, :]


def unrotate(upstream, cosine_table, sine_table):
    half_dim = upstream.shape[-1] // 2
    scaled_sine = upstream * sine_table[:, None, :]
    turned_back = jnp.concatenate(
        [scaled_sine[..., half_dim:], -scaled_sine[..., :half_dim]], axis=-1
    )
    return upstream * cosine_table[:, None, :] + turned_back


def norm_forward(values, gain_vec):
    scale_inv = lax.rsqrt(jnp.mean(values * values, axis=-1, keepdims=True) + norm_epsilon)
    return (values * scale_inv * gain_vec, scale_inv)


def norm_backward(values, scale_inv, gain_vec, upstream):
    weighted = upstream * gain_vec
    grad_input = scale_inv * weighted - values * scale_inv**3 * jnp.mean(
        weighted * values, axis=-1, keepdims=True
    )
    gain_term = jnp.sum((upstream * values * scale_inv).reshape(-1, values.shape[-1]), axis=0)
    return (grad_input, gain_term)


def upper_bit(local_index, bit_number):
    return local_index // 2**bit_number % 2 == 1


def joined_rows(mine, received, upper_side):
    first_rows = jnp.where(upper_side, received, mine)
    second_rows = jnp.where(upper_side, mine, received)
    return jnp.concatenate([first_rows, second_rows], axis=0)


def half_gather(pair, local_index):
    gathered_rows = pair
    for bit_number in range(lax.axis_size("ctx").bit_length() - 2):
        received = from_partner(gathered_rows, "ctx", bit_number)
        gathered_rows = joined_rows(gathered_rows, received, upper_bit(local_index, bit_number))
    return gathered_rows


def half_reduce(term, local_index):
    for bit_number in reversed(range(lax.axis_size("ctx").bit_length() - 2)):
        span = term.shape[0] // 2
        lower_rows = term[:span]
        upper_rows = term[span:]
        upper_side = upper_bit(local_index, bit_number)
        kept_rows = jnp.where(upper_side, upper_rows, lower_rows)
        sent_rows = jnp.where(upper_side, lower_rows, upper_rows)
        term = kept_rows + from_partner(sent_rows, "ctx", bit_number)
    return term


def over_keys(update, carried, count_rows):
    block_length = math.gcd(count_rows, 512)

    def inner_step(current, block_index):
        return (update(current, block_index * block_length, block_length), None)

    carried, unused = lax.scan(
        inner_step, carried, jnp.arange(count_rows // block_length, dtype=jnp.int32)
    )
    return carried


def allowed_mask(key_meta, query_meta, row_start, block_length):
    key_places = lax.dynamic_slice_in_dim(key_meta[0], row_start, block_length)
    key_slots = lax.dynamic_slice_in_dim(key_meta[1], row_start, block_length)
    key_live = lax.dynamic_slice_in_dim(key_meta[2], row_start, block_length)
    allowed = (
        (key_slots[None, :] == query_meta[1][:, None])
        & (key_places[None, :] <= query_meta[0][:, None])
        & key_live[None, :]
    )
    return allowed[None, None]


def forward_update(
    current, query_head_group, key_tile_block, value_tile_block, allowed, score_scale
):
    running_max, running_sum, running_acc = current
    block_length = key_tile_block.shape[0]
    key_head_list = key_tile_block.reshape(block_length, KEY_VALUE_HEADS, HEAD_SIZE)
    value_head_list = value_tile_block.reshape(block_length, KEY_VALUE_HEADS, HEAD_SIZE)
    scores = (
        jnp.einsum(
            "qhgd,khd->hgqk", query_head_group, key_head_list, preferred_element_type=jnp.float32
        )
        * score_scale
    )
    scores = jnp.where(allowed, scores, masked_logits)
    new_max = jnp.maximum(running_max, jnp.max(scores, axis=-1))
    factor = jnp.exp(running_max - new_max)
    prob_block = jnp.where(allowed, jnp.exp(scores - new_max[..., None]), 0.0)
    new_sum = running_sum * factor + jnp.sum(prob_block, axis=-1)
    new_acc = running_acc * factor[..., None] + jnp.einsum(
        "hgqk,khd->hgqd",
        prob_block.astype(jnp.bfloat16),
        value_head_list,
        preferred_element_type=jnp.float32,
    )
    return (new_max, new_sum, new_acc)


def score_parts(
    query_head_group,
    output_grad_group,
    key_tile_block,
    value_tile_block,
    allowed,
    log_total,
    row_delta,
    score_scale,
):
    block_length = key_tile_block.shape[0]
    key_head_list = key_tile_block.reshape(block_length, KEY_VALUE_HEADS, HEAD_SIZE)
    value_head_list = value_tile_block.reshape(block_length, KEY_VALUE_HEADS, HEAD_SIZE)
    scores = (
        jnp.einsum(
            "qhgd,khd->hgqk", query_head_group, key_head_list, preferred_element_type=jnp.float32
        )
        * score_scale
    )
    prob_block = jnp.where(allowed, jnp.exp(scores - log_total[..., None]), 0.0)
    dprob = jnp.einsum(
        "qhgd,khd->hgqk", output_grad_group, value_head_list, preferred_element_type=jnp.float32
    )
    dscore_low = (prob_block * (dprob - row_delta[..., None])).astype(jnp.bfloat16)
    return (prob_block, dscore_low, key_head_list)


def attention_inputs(stream, gathered, cosine_table, sine_table):
    count_rows = stream.shape[0]
    normalized, inv_attn = norm_forward(stream, gathered[7].astype(jnp.float32))
    normed_low = normalized.astype(jnp.bfloat16)
    query_heads = jnp.dot(normed_low, gathered[0], preferred_element_type=jnp.float32).reshape(
        count_rows, QUERY_HEADS, HEAD_SIZE
    )
    key_head_list = jnp.dot(normed_low, gathered[1], preferred_element_type=jnp.float32).reshape(
        count_rows, KEY_VALUE_HEADS, HEAD_SIZE
    )
    value_low = jnp.dot(normed_low, gathered[2], preferred_element_type=jnp.float32).astype(
        jnp.bfloat16
    )
    query_normed, inv_query = norm_forward(query_heads, gathered[9].astype(jnp.float32))
    key_normed, inv_key = norm_forward(key_head_list, gathered[10].astype(jnp.float32))
    query_lowered = rotate(query_normed, cosine_table, sine_table).astype(jnp.bfloat16)
    key_low = (
        rotate(key_normed, cosine_table, sine_table)
        .astype(jnp.bfloat16)
        .reshape(count_rows, KEY_VALUE_HEADS * HEAD_SIZE)
    )
    return {
        "normed_low": normed_low,
        "inv_attn": inv_attn,
        "query_heads": query_heads,
        "inv_query": inv_query,
        "key_heads": key_head_list,
        "inv_key": inv_key,
        "query_low": query_lowered,
        "key_low": key_low,
        "value_low": value_low,
    }


def block_rest(stream, gathered, attn_low):
    middle = stream + jnp.dot(attn_low, gathered[3], preferred_element_type=jnp.float32)
    normed_mid, inv_mid = norm_forward(middle, gathered[8].astype(jnp.float32))
    normed_mid_low = normed_mid.astype(jnp.bfloat16)
    gate_act = jnp.dot(normed_mid_low, gathered[4], preferred_element_type=jnp.float32)
    upward = jnp.dot(normed_mid_low, gathered[5], preferred_element_type=jnp.float32)
    hidden_low = (jax.nn.silu(gate_act) * upward).astype(jnp.bfloat16)
    result = middle + jnp.dot(hidden_low, gathered[6], preferred_element_type=jnp.float32)
    return {
        "middle": middle,
        "inv_mid": inv_mid,
        "normed_mid_low": normed_mid_low,
        "gate_act": gate_act,
        "upward": upward,
        "hidden_low": hidden_low,
        "result": result,
    }


def general_device(
    tokens,
    cotangent,
    lengths,
    stretch_ids,
    w_query,
    key_projection_weight,
    value_projection_weight,
    w_out,
    w_gate,
    w_up,
    w_down,
    g_attn,
    g_mlp,
    g_query,
    g_key,
):
    count_rows = tokens.shape[0]
    ctx_count = lax.axis_size("ctx")
    half_count = ctx_count // 2
    key_value_width = KEY_VALUE_HEADS * HEAD_SIZE
    key_meta = token_places(stretch_ids[:, 0, :], lengths[0])
    ctx_index = lax.axis_index("ctx")
    local_index = ctx_index % half_count
    base_row = ctx_index // half_count * half_count * count_rows
    half_row_set = half_count * count_rows
    offset_mine = ctx_index * count_rows
    query_meta = tuple(
        (lax.dynamic_slice_in_dim(meta_array, offset_mine, count_rows) for meta_array in key_meta)
    )
    live_mine = query_meta[2].astype(jnp.float32)[:, None]
    cosine_table, sine_table = rotary_tables(query_meta[0])
    group_count = QUERY_HEADS // KEY_VALUE_HEADS
    score_scale = HEAD_SIZE ** (-0.5)

    def attend_forward(query_head_group, key_source, value_source, current):

        def update(carried, local_row, block_length):
            key_tile_block = lax.dynamic_slice_in_dim(key_source, local_row, block_length)
            value_tile_block = lax.dynamic_slice_in_dim(value_source, local_row, block_length)
            allowed = allowed_mask(key_meta, query_meta, base_row + local_row, block_length)
            return forward_update(
                carried, query_head_group, key_tile_block, value_tile_block, allowed, score_scale
            )

        return over_keys(update, current, key_source.shape[0])

    saved = []
    stream = tokens.astype(jnp.float32)
    for layer_index in range(DECODER_LAYERS):
        gathered = (
            lax.all_gather(w_query[layer_index], "fsdp", axis=0, tiled=True),
            lax.all_gather(key_projection_weight[layer_index], "fsdp", axis=0, tiled=True),
            lax.all_gather(value_projection_weight[layer_index], "fsdp", axis=0, tiled=True),
            lax.all_gather(w_out[layer_index], "fsdp", axis=0, tiled=True),
            lax.all_gather(w_gate[layer_index], "fsdp", axis=0, tiled=True),
            lax.all_gather(w_up[layer_index], "fsdp", axis=0, tiled=True),
            lax.all_gather(w_down[layer_index], "fsdp", axis=0, tiled=True),
            lax.all_gather(g_attn[layer_index], "fsdp", axis=0, tiled=True),
            lax.all_gather(g_mlp[layer_index], "fsdp", axis=0, tiled=True),
            lax.all_gather(g_query[layer_index], "fsdp", axis=0, tiled=True),
            lax.all_gather(g_key[layer_index], "fsdp", axis=0, tiled=True),
        )
        present_inputs = attention_inputs(stream, gathered, cosine_table, sine_table)
        query_head_group = present_inputs["query_low"].reshape(
            count_rows, KEY_VALUE_HEADS, group_count, HEAD_SIZE
        )
        start_state = (
            jnp.full((KEY_VALUE_HEADS, group_count, count_rows), masked_logits, jnp.float32),
            jnp.zeros((KEY_VALUE_HEADS, group_count, count_rows), jnp.float32),
            jnp.zeros((KEY_VALUE_HEADS, group_count, count_rows, HEAD_SIZE), jnp.float32),
        )
        pair_all = half_gather(
            jnp.concatenate([present_inputs["key_low"], present_inputs["value_low"]], axis=-1),
            local_index,
        )
        key_all = pair_all[:, :key_value_width]
        value_all = pair_all[:, key_value_width:]
        final_state = attend_forward(query_head_group, key_all, value_all, start_state)
        attended = final_state[2] / final_state[1][..., None]
        log_total = final_state[0] + jnp.log(final_state[1])
        attn_low = (
            jnp.transpose(attended, (2, 0, 1, 3))
            .reshape(count_rows, QUERY_HEADS * HEAD_SIZE)
            .astype(jnp.bfloat16)
        )
        rest = block_rest(stream, gathered, attn_low)
        kept = (gathered, key_all, value_all, present_inputs, rest)
        saved.append((stream, attended, log_total, kept))
        stream = rest["result"]
    output_low = (stream * live_mine).astype(jnp.bfloat16)
    grad_stream = cotangent.astype(jnp.float32) * live_mine
    layer_grads = [None] * DECODER_LAYERS
    for layer_index in reversed(range(DECODER_LAYERS)):
        stream_in, attended, log_total, kept = saved[layer_index]
        attn_low = (
            jnp.transpose(attended, (2, 0, 1, 3))
            .reshape(count_rows, QUERY_HEADS * HEAD_SIZE)
            .astype(jnp.bfloat16)
        )
        gathered, key_all, value_all, present_inputs, rest = kept
        ffn_grad_low = grad_stream.astype(jnp.bfloat16)
        grad_down = jnp.einsum(
            "tf,td->fd", rest["hidden_low"], ffn_grad_low, preferred_element_type=jnp.float32
        )
        hidden_grad = jnp.einsum(
            "td,fd->tf", ffn_grad_low, gathered[6], preferred_element_type=jnp.float32
        )
        gate_act = rest["gate_act"]
        sigmoid_gate = jax.nn.sigmoid(gate_act)
        gate_grad_low = (
            hidden_grad * rest["upward"] * sigmoid_gate * (1.0 + gate_act * (1.0 - sigmoid_gate))
        ).astype(jnp.bfloat16)
        up_grad_low = (hidden_grad * gate_act * sigmoid_gate).astype(jnp.bfloat16)
        grad_gate = jnp.einsum(
            "td,tf->df", rest["normed_mid_low"], gate_grad_low, preferred_element_type=jnp.float32
        )
        grad_up = jnp.einsum(
            "td,tf->df", rest["normed_mid_low"], up_grad_low, preferred_element_type=jnp.float32
        )
        normed_mid_grad = jnp.einsum(
            "tf,df->td", gate_grad_low, gathered[4], preferred_element_type=jnp.float32
        ) + jnp.einsum("tf,df->td", up_grad_low, gathered[5], preferred_element_type=jnp.float32)
        mid_norm_grad, mlp_gain_term = norm_backward(
            rest["middle"], rest["inv_mid"], gathered[8].astype(jnp.float32), normed_mid_grad
        )
        middle_grad = grad_stream + mid_norm_grad
        attn_grad_low = middle_grad.astype(jnp.bfloat16)
        grad_out = jnp.einsum(
            "tq,td->qd", attn_low, attn_grad_low, preferred_element_type=jnp.float32
        )
        output_gradient_lowered = jnp.einsum(
            "td,qd->tq", attn_grad_low, gathered[3], preferred_element_type=jnp.float32
        ).astype(jnp.bfloat16)
        output_grad_group = output_gradient_lowered.reshape(
            count_rows, KEY_VALUE_HEADS, group_count, HEAD_SIZE
        )
        row_delta = jnp.sum(
            jnp.transpose(output_grad_group.astype(jnp.float32), (1, 2, 0, 3)) * attended, axis=-1
        )
        query_head_group = present_inputs["query_low"].reshape(
            count_rows, KEY_VALUE_HEADS, group_count, HEAD_SIZE
        )
        key_block_size = math.gcd(half_row_set, 512)

        def backward_step(query_acc, block_index):
            row_start = block_index * key_block_size
            key_tile_block = lax.dynamic_slice_in_dim(key_all, row_start, key_block_size)
            value_tile_block = lax.dynamic_slice_in_dim(value_all, row_start, key_block_size)
            allowed = allowed_mask(key_meta, query_meta, base_row + row_start, key_block_size)
            prob_block, dscore_low, key_head_list = score_parts(
                query_head_group,
                output_grad_group,
                key_tile_block,
                value_tile_block,
                allowed,
                log_total,
                row_delta,
                score_scale,
            )
            query_next = (query_acc, jnp.zeros((key_block_size, 2 * key_value_width), jnp.float32))[
                0
            ] + jnp.einsum(
                "hgqk,khd->qhgd", dscore_low, key_head_list, preferred_element_type=jnp.float32
            ) * score_scale
            value_grad = jnp.einsum(
                "hgqk,qhgd->khd",
                prob_block.astype(jnp.bfloat16),
                output_grad_group,
                preferred_element_type=jnp.float32,
            )
            key_grad = (
                jnp.einsum(
                    "hgqk,qhgd->khd",
                    dscore_low,
                    query_head_group,
                    preferred_element_type=jnp.float32,
                )
                * score_scale
            )
            block_rows = jnp.concatenate(
                [
                    key_grad.reshape(key_block_size, key_value_width),
                    value_grad.reshape(key_block_size, key_value_width),
                ],
                axis=-1,
            )
            return (query_next, block_rows)

        query_grad, key_value_rows = lax.scan(
            backward_step,
            jnp.zeros((count_rows, KEY_VALUE_HEADS, group_count, HEAD_SIZE), jnp.float32),
            jnp.arange(half_row_set // key_block_size, dtype=jnp.int32),
        )
        key_value_term = key_value_rows.reshape(half_row_set, 2 * key_value_width)
        key_value_gradient = half_reduce(key_value_term, local_index)
        key_gradient_rows = key_value_gradient[:, :key_value_width].reshape(
            count_rows, KEY_VALUE_HEADS, HEAD_SIZE
        )
        value_grad_low = key_value_gradient[:, key_value_width:].astype(jnp.bfloat16)
        query_pre, query_gain_term = norm_backward(
            present_inputs["query_heads"],
            present_inputs["inv_query"],
            gathered[9].astype(jnp.float32),
            unrotate(
                query_grad.reshape(count_rows, QUERY_HEADS, HEAD_SIZE), cosine_table, sine_table
            ),
        )
        key_pre, key_gain_term = norm_backward(
            present_inputs["key_heads"],
            present_inputs["inv_key"],
            gathered[10].astype(jnp.float32),
            unrotate(key_gradient_rows, cosine_table, sine_table),
        )
        query_grad_low = query_pre.reshape(count_rows, QUERY_HEADS * HEAD_SIZE).astype(jnp.bfloat16)
        key_grad_low = key_pre.reshape(count_rows, key_value_width).astype(jnp.bfloat16)
        normed_low = present_inputs["normed_low"]
        grad_query = jnp.einsum(
            "td,tq->dq", normed_low, query_grad_low, preferred_element_type=jnp.float32
        )
        grad_key = jnp.einsum(
            "td,tq->dq", normed_low, key_grad_low, preferred_element_type=jnp.float32
        )
        grad_value = jnp.einsum(
            "td,tq->dq", normed_low, value_grad_low, preferred_element_type=jnp.float32
        )
        normed_grad = jnp.einsum(
            "tq,dq->td", query_grad_low, gathered[0], preferred_element_type=jnp.float32
        )
        normed_grad = normed_grad + jnp.einsum(
            "tq,dq->td", key_grad_low, gathered[1], preferred_element_type=jnp.float32
        )
        normed_grad = normed_grad + jnp.einsum(
            "tq,dq->td", value_grad_low, gathered[2], preferred_element_type=jnp.float32
        )
        in_norm_grad, attn_gain_term = norm_backward(
            stream_in, present_inputs["inv_attn"], gathered[7].astype(jnp.float32), normed_grad
        )
        grad_stream = middle_grad + in_norm_grad
        layer_grads[layer_index] = (
            lax.psum_scatter(grad_query, ("ctx", "fsdp"), scatter_dimension=0, tiled=True),
            lax.psum_scatter(grad_key, ("ctx", "fsdp"), scatter_dimension=0, tiled=True),
            lax.psum_scatter(grad_value, ("ctx", "fsdp"), scatter_dimension=0, tiled=True),
            lax.psum_scatter(grad_out, ("ctx", "fsdp"), scatter_dimension=0, tiled=True),
            lax.psum_scatter(grad_gate, ("ctx", "fsdp"), scatter_dimension=0, tiled=True),
            lax.psum_scatter(grad_up, ("ctx", "fsdp"), scatter_dimension=0, tiled=True),
            lax.psum_scatter(grad_down, ("ctx", "fsdp"), scatter_dimension=0, tiled=True),
            lax.psum_scatter(attn_gain_term, ("ctx", "fsdp"), scatter_dimension=0, tiled=True),
            lax.psum_scatter(mlp_gain_term, ("ctx", "fsdp"), scatter_dimension=0, tiled=True),
            lax.psum_scatter(query_gain_term, ("ctx", "fsdp"), scatter_dimension=0, tiled=True),
            lax.psum_scatter(key_gain_term, ("ctx", "fsdp"), scatter_dimension=0, tiled=True),
        )
    stacked = tuple(
        (jnp.stack([layer_sums[member] for layer_sums in layer_grads]) for member in range(11))
    )
    return (output_low, grad_stream) + stacked


def act_blocks(values):
    turned = values.T.reshape(4, 2, 2, 2, -1, 32, values.shape[0])
    return turned.transpose(3, 2, 4, 1, 0, 5, 6).reshape(2, 2, -1, 256, values.shape[0])


def grad_blocks(values):
    return values.reshape(values.shape[0], -1, 1024).transpose(1, 0, 2)


def side_by_side(tiles):
    return tiles.transpose(1, 0, 2).reshape(tiles.shape[1], -1)


def product(left, right):
    return jnp.dot(left, right, preferred_element_type=jnp.float32)


def product_turned(left, right):
    return lax.dot_general(left, right, NT, preferred_element_type=jnp.float32)


def fast_device(
    tokens,
    cotangent,
    lengths,
    stretch_ids,
    w_query,
    key_projection_weight,
    value_projection_weight,
    w_out,
    w_gate,
    w_up,
    w_down,
    g_attn,
    g_mlp,
    g_query,
    g_key,
):
    count_rows, width = tokens.shape
    ctx_index = lax.axis_index("ctx")
    places, slot_ids, live = token_places(stretch_ids[:, 0, :], lengths[0])
    group_rows = PEERS * count_rows
    base_row = ctx_index // PEERS * group_rows
    my_row = ctx_index * count_rows
    slot_places = lax.dynamic_slice_in_dim(places, base_row, group_rows)
    limit = lax.dynamic_slice_in_dim(lengths[0], ctx_index // PEERS, 1)
    caps = jnp.minimum(slot_places, limit - 1).reshape(PEERS, 1, count_rows)
    query_cap = jnp.concatenate([caps, caps], axis=2)
    key_place = slot_places[:, None]
    live_mine = lax.dynamic_slice_in_dim(live, my_row, count_rows).astype(jnp.float32)[:, None]
    cosine, sine = rotary_tables(lax.dynamic_slice_in_dim(places, my_row, count_rows))
    half = HEAD_SIZE // 2
    sine = jnp.concatenate([-sine[:, :half], sine[:, half:]], axis=1)

    packed = jnp.concatenate([member.reshape(-1) for member in (g_attn, g_mlp, g_query, g_key)])
    packed = jnp.pad(packed, (0, 4096 - packed.shape[0])).reshape(32, 128)
    gathered = gather_weights(
        (w_query, key_projection_weight, value_projection_weight, w_out, w_gate, w_up, w_down),
        packed,
        tuple(range(DECODER_LAYERS)),
        1,
    )
    flat = gathered[-1].reshape(2, -1).astype(jnp.float32)
    gains = []
    offset = 0
    for member in (g_attn, g_mlp, g_query, g_key):
        span = member.shape[1]
        sides = flat[:, offset : offset + DECODER_LAYERS * span].reshape(2, DECODER_LAYERS, span)
        gains.append(sides.transpose(1, 0, 2).reshape(DECODER_LAYERS, 2 * span))
        offset += DECODER_LAYERS * span

    stream = tokens.astype(jnp.float32)
    saved = []
    for layer in range(DECODER_LAYERS):
        into, out_weight, wide_weight, down = gathered[4 * layer : 4 * layer + 4]
        head_gains = jnp.concatenate([gains[2][layer : layer + 1], gains[3][layer : layer + 1]], 0)
        normed, inv_attn = norm_forward(stream, gains[0][layer])
        normed_low = normed.astype(jnp.bfloat16)
        pre = product(normed_low, into)
        attn_low, kept, kept_out, kept_log = attend(
            pre, cosine, sine, head_gains, key_place, query_cap, 2 + layer
        )
        middle = stream + product(attn_low, out_weight)
        normed_mid, inv_mid = norm_forward(middle, gains[1][layer])
        mid_low = normed_mid.astype(jnp.bfloat16)
        both = product(mid_low, wide_weight)
        ff = both.shape[1] // 2
        gate, up = both[:, :ff], both[:, ff:]
        hidden_low = (jax.nn.silu(gate) * up).astype(jnp.bfloat16)
        saved.append(
            (stream, inv_attn, normed_low, pre, attn_low, kept, kept_out, kept_log,
             middle, inv_mid, mid_low, gate, up, hidden_low, head_gains)
        )
        stream = middle + product(hidden_low, down)
    output_low = (stream * live_mine).astype(jnp.bfloat16)

    grad_stream = cotangent.astype(jnp.float32) * live_mine
    layer_grads = [None] * DECODER_LAYERS
    place = ctx_index * 2 + lax.axis_index("fsdp")
    for layer in reversed(range(DECODER_LAYERS)):
        into, out_weight, wide_weight, down = gathered[4 * layer : 4 * layer + 4]
        (stream_in, inv_attn, normed_low, pre, attn_low, kept, kept_out, kept_log,
         middle, inv_mid, mid_low, gate, up, hidden_low, head_gains) = saved[layer]
        down_low = grad_stream.astype(jnp.bfloat16)
        hidden_grad = product_turned(down_low, down)
        sigmoid_gate = jax.nn.sigmoid(gate)
        gate_low = (hidden_grad * up * sigmoid_gate * (1.0 + gate * (1.0 - sigmoid_gate))).astype(
            jnp.bfloat16
        )
        up_low = (hidden_grad * gate * sigmoid_gate).astype(jnp.bfloat16)
        both_low = jnp.concatenate([gate_low, up_low], axis=1)
        mid_grad = product_turned(both_low, wide_weight)
        mid_norm_grad, mlp_term = norm_backward(middle, inv_mid, gains[1][layer], mid_grad)
        middle_grad = grad_stream + mid_norm_grad
        out_low = middle_grad.astype(jnp.bfloat16)
        attn_grad = product_turned(out_low, out_weight).astype(jnp.bfloat16)
        pre_grad, head_terms = attend_back(
            attn_grad, kept, kept_out, kept_log, pre, cosine, sine, head_gains,
            key_place, query_cap, 2 + DECODER_LAYERS + layer,
        )
        normed_grad = product_turned(pre_grad, into)
        in_norm_grad, attn_term = norm_backward(stream_in, inv_attn, gains[0][layer], normed_grad)
        grad_stream = middle_grad + in_norm_grad
        terms = jnp.concatenate(
            [attn_term.reshape(-1, 128), mlp_term.reshape(-1, 128), head_terms], axis=0
        )
        tiles, sums = reduce_layer(
            jnp.concatenate(
                [act_blocks(member) for member in (hidden_low, attn_low, mid_low, normed_low)],
                axis=2,
            ),
            jnp.concatenate(
                [grad_blocks(member) for member in (down_low, out_low, both_low, pre_grad)], axis=0
            ),
            terms,
            2 + 2 * DECODER_LAYERS + layer,
        )

        def share(first, rows, span):
            flat_sum = sums[first : first + rows].reshape(-1)
            return lax.dynamic_slice_in_dim(flat_sum, place * span, span)

        layer_grads[layer] = (
            side_by_side(tiles[11:13]),
            tiles[13],
            tiles[14],
            tiles[3:5].reshape(64, 1024),
            side_by_side(tiles[5:8]),
            side_by_side(tiles[8:11]),
            tiles[0:3].reshape(96, 1024),
            share(0, 8, 32),
            share(8, 8, 32),
            share(16, 1, 4),
            share(17, 1, 4),
        )
    stacked = tuple(
        (jnp.stack([layer_sums[member] for layer_sums in layer_grads]) for member in range(11))
    )
    return (output_low, grad_stream) + stacked


def solution(mesh):
    plain = mesh.shape["ctx"] == 2 * KEY_VALUE_HEADS and mesh.shape["fsdp"] == 2
    device = fast_device if plain else general_device
    in_specs = (
        P(("ctx", "fsdp"), None),
        P(("ctx", "fsdp"), None),
        P("fsdp", None),
        P(None, "fsdp", None),
        P(None, "fsdp", None),
        P(None, "fsdp", None),
        P(None, "fsdp", None),
        P(None, "fsdp", None),
        P(None, "fsdp", None),
        P(None, "fsdp", None),
        P(None, "fsdp", None),
        P(None, "fsdp"),
        P(None, "fsdp"),
        P(None, "fsdp"),
        P(None, "fsdp"),
    )
    out_specs = (
        P(("ctx", "fsdp"), None),
        P(("ctx", "fsdp"), None),
        P(None, ("ctx", "fsdp"), None),
        P(None, ("ctx", "fsdp"), None),
        P(None, ("ctx", "fsdp"), None),
        P(None, ("ctx", "fsdp"), None),
        P(None, ("ctx", "fsdp"), None),
        P(None, ("ctx", "fsdp"), None),
        P(None, ("ctx", "fsdp"), None),
        P(None, ("ctx", "fsdp")),
        P(None, ("ctx", "fsdp")),
        P(None, ("ctx", "fsdp")),
        P(None, ("ctx", "fsdp")),
    )
    return jax.shard_map(
        device, mesh=mesh, in_specs=in_specs, out_specs=out_specs, check_vma=False
    )
```

```python
import functools
import math

import jax
import jax.numpy as jnp
from jax import lax
from jax.experimental import pallas as pl
from jax.experimental.pallas import tpu as pltpu
from jax.sharding import PartitionSpec as P

QUERY_HEADS = 16
KEY_VALUE_HEADS = 8
HEAD_SIZE = 128
DECODER_LAYERS = 2
STRETCH = 64


norm_epsilon = 1e-06
rope_base = 1000000.0
masked_logits = -1e30

MESH = pl.DeviceIdType.MESH


TILES = 15
GRADS = 12
ACTS = 7
AHEAD = 3
ACT_SPANS = ((0, 3), (3, 1), (4, 2), (6, 1))


def grad_index(t):
    return jnp.where(t < 3, 0, jnp.where(t < 9, t - 2, jnp.where(t < 11, 7, t - 3)))


def act_index(t):
    return jnp.where(t < 3, t, jnp.where(t < 9, 3, jnp.where(t < 11, t - 5, 6)))


def is_new(t):
    return (t == 0) | ((t >= 3) & (t < 10)) | (t >= 11)


def make_remote(src, dst, s, r, dev):
    return pltpu.make_async_remote_copy(
        src_ref=src, dst_ref=dst, send_sem=s, recv_sem=r, device_id=dev, device_id_type=MESH
    )


class Reducer:
    def __init__(self, acts, grads, results, scratch, layers):
        self.acts, self.grads, self.results, self.layers = acts, grads, results, layers
        self.count = len(layers)
        (self.gheld, self.abuf, self.afwd, self.gtile, self.ysend, self.yrecv, self.own,
         self.zsend, self.zrecv, self.zown,
         self.a_local, self.a_xs, self.a_xr, self.a_cs, self.a_cr,
         self.g_local, self.g_xs, self.g_xr, self.g_cs, self.g_cr, self.g_fs, self.g_fr,
         self.y_s, self.y_r, self.z_s, self.z_r) = scratch
        c = lax.axis_index("ctx")
        x = lax.axis_index("fsdp")
        self.c, self.x = c, x
        self.core = c % 2
        self.y = c // 2 % 2
        self.z = c // 4
        self.sibling = (c + 1 - 2 * self.core, x)
        self.across = (c, 1 - x)
        self.aside = (c + 2 - 4 * self.y, x)

    def along(self, o):
        return ((self.z + o) % 4 * 4 + self.c % 4, self.x)

    def partners(self):
        return (self.sibling, self.across, self.aside) + tuple(self.along(o) for o in (1, 2, 3))

    def act(self, n, k, what):
        first, blocks = ACT_SPANS[k]
        src = self.acts[n][k]
        span = pl.ds(first, blocks)
        x, core = self.x, self.core

        def held(place):
            return self.abuf.at[n, :, :, span, :, pl.ds(128 * place, 128)]

        if what == "local":
            return pltpu.make_async_copy(
                src.at[:, :, core, x], held(0), self.a_local.at[n, k]
            )
        if what == "across":
            return make_remote(
                src.at[:, :, core, 1 - x], held(1), self.a_xs.at[n, k, 0], self.a_xr.at[n, k, 0],
                self.across,
            )
        if what == "relay":
            return make_remote(
                src.at[:, :, 1 - core, 1 - x], self.afwd.at[n, :, :, span],
                self.a_xs.at[n, k, 1], self.a_xr.at[n, k, 1], self.across,
            )
        if what == "sibling":
            return make_remote(
                src.at[:, :, 1 - core, x], held(2), self.a_cs.at[n, k, 0], self.a_cr.at[n, k, 0],
                self.sibling,
            )
        return make_remote(
            self.afwd.at[n, :, :, span], held(3), self.a_cs.at[n, k, 1], self.a_cr.at[n, k, 1],
            self.sibling,
        )

    def start_acts(self, n, ks):
        for what in ("across", "relay", "sibling", "local"):
            for k in ks:
                self.act(n, k, what).start()

    def forward_acts(self, n, ks):
        for k in ks:
            self.act(n, k, "relay").wait_recv()
            self.act(n, k, "forward").start()

    def await_acts(self, n, ks):
        for k in ks:
            self.act(n, k, "local").wait()
            for what in ("across", "sibling", "forward"):
                self.act(n, k, what).wait_recv()

    def grad_across(self, i, src=None):
        rows = self.gheld.at[i, pl.ds(0, 128)]
        return make_remote(
            rows if src is None else src, rows, self.g_xs.at[i], self.g_xr.at[i], self.across
        )

    def grad_sibling(self, i, src=None):
        rows = self.gheld.at[i, pl.ds(128, 128)]
        return make_remote(
            rows if src is None else src, rows, self.g_cs.at[i], self.g_cr.at[i], self.sibling
        )

    def grad_forward(self, i):
        return make_remote(
            self.gheld.at[i, pl.ds(0, 128)], self.gheld.at[i, pl.ds(256, 128)],
            self.g_fs.at[i], self.g_fr.at[i], self.sibling,
        )

    def grad_own(self, i, src=None):
        rows = self.gtile.at[pl.ds(0, 128)]
        return pltpu.make_async_copy(rows if src is None else src, rows, self.g_local.at[0])

    def grad_load(self, i):
        return pltpu.make_async_copy(
            self.gheld.at[i], self.gtile.at[pl.ds(128, 384)], self.g_local.at[1]
        )

    def with_source(self, i, act):
        at = 0
        for n in range(self.count):
            for ref, blocks in self.grads[n]:
                first = at

                @pl.when((i >= first) & (i < first + blocks))
                def use(ref=ref, first=first):
                    act(ref.at[:, pl.ds(pl.multiple_of((i - first) * 1024, 1024), 1024)])

                at += blocks

    def start_grad(self, i):
        def go(src):
            self.grad_across(i, src).start()
            self.grad_sibling(i, src).start()

        self.with_source(i, go)

    def y_copy(self, t):
        return make_remote(
            self.ysend.at[t], self.yrecv.at[t], self.y_s.at[t], self.y_r.at[t], self.aside
        )

    def z_copy(self, t, o):
        return make_remote(
            self.zsend.at[t, o - 1], self.zrecv.at[t, 3 - o], self.z_s.at[t, o - 1],
            self.z_r.at[t, 3 - o], self.along(o),
        )

    def begin(self):
        self.start_acts(0, (0,))
        self.start_grad(0)
        self.start_acts(0, (1, 2, 3))
        for i in range(1, AHEAD):
            self.start_grad(i)

    def store(self, t, total):
        n = t // TILES
        tile = t % TILES
        query, key, value, out, gate, up, down = self.results
        by_rows = ((0, 3, down), (9, 2, out))
        by_columns = ((3, 3, gate), (6, 3, up), (11, 2, query), (13, 1, key), (14, 1, value))
        if self.count == 1:
            layer = self.layers[0]
        else:
            layer = jnp.where(n == 0, self.layers[0], self.layers[1])
        for first, blocks, ref in by_rows:

            @pl.when((tile >= first) & (tile < first + blocks))
            def rows(first=first, ref=ref):
                ref[layer, pl.ds(pl.multiple_of((tile - first) * 32, 32), 32), :] = total

        for first, blocks, ref in by_columns:

            @pl.when((tile >= first) & (tile < first + blocks))
            def columns(first=first, ref=ref):
                ref[layer, :, pl.ds(pl.multiple_of((tile - first) * 1024, 1024), 1024)] = total

    def step(self, s):
        tiles = TILES * self.count
        t = s - 5

        @pl.when((t >= 0) & (t < tiles))
        def finish():
            total = self.zown[t % 4]
            for o in (1, 2, 3):
                self.z_copy(t, o).wait_recv()
            for o in range(3):
                total += self.zrecv[t, o].astype(jnp.float32)
            self.store(t, total)

        u = s - 3

        @pl.when((u >= 0) & (u < tiles))
        def spread():
            self.y_copy(u).wait_recv()

            def part(index):
                rows = pl.ds(pl.multiple_of(index * 32, 32), 32)
                return self.own[u % 4, rows, :] + self.yrecv[u, rows, :].astype(jnp.float32)

            for o in (2, 1, 3):
                self.zsend[u, o - 1] = part((self.z + o) % 4).astype(jnp.bfloat16)
                self.z_copy(u, o).start()
            self.zown[u % 4] = part(self.z)

        v = s - 1

        @pl.when((v >= 0) & (v < tiles))
        def compute():
            n = v // TILES
            tile = v % TILES
            gi = n * GRADS + grad_index(tile)
            ai = act_index(tile)
            for layer in range(self.count):

                @pl.when(v == TILES * layer)
                def first_acts(layer=layer):
                    self.await_acts(layer, (0,))

                @pl.when(v == TILES * layer + 3)
                def second_acts(layer=layer):
                    self.await_acts(layer, (1, 2, 3))

            @pl.when(is_new(tile))
            def fresh():
                self.with_source(gi, lambda src: self.grad_own(gi, src).start())
                self.grad_sibling(gi).wait_recv()
                self.grad_forward(gi).wait_recv()
                self.grad_load(gi).start()
                self.grad_own(gi).wait()
                self.grad_load(gi).wait()

            for half in range(2):
                cols = pl.ds(half * 512, 512)
                right = self.gtile[:, cols]
                theirs = self.abuf[n, :, 1 - self.y, ai].reshape(128, 512)
                mine = self.abuf[n, :, self.y, ai].reshape(128, 512)
                self.ysend[v, :, cols] = jnp.dot(
                    theirs, right, preferred_element_type=jnp.float32
                ).astype(jnp.bfloat16)
                self.own[v % 4, :, cols] = jnp.dot(mine, right, preferred_element_type=jnp.float32)
            self.y_copy(v).start()

        @pl.when((s < tiles) & is_new(s % TILES))
        def forward():
            i = s // TILES * GRADS + grad_index(s % TILES)
            for layer in range(self.count):

                @pl.when(s == TILES * layer)
                def first_forward(layer=layer):
                    self.forward_acts(layer, (0,))

                @pl.when(s == TILES * layer + 3)
                def second_forward(layer=layer):
                    self.forward_acts(layer, (1, 2, 3))

            self.grad_across(i).wait_recv()
            self.grad_forward(i).start()
            for layer in range(1, self.count):

                @pl.when(i == GRADS * layer - AHEAD)
                def next_acts(layer=layer):
                    self.start_acts(layer, (0,))

                @pl.when(i == GRADS * layer - AHEAD + 1)
                def other_acts(layer=layer):
                    self.start_acts(layer, (1, 2, 3))

            @pl.when(i + AHEAD < GRADS * self.count)
            def more():
                self.start_grad(i + AHEAD)

    def steps(self):
        return TILES * self.count + 5

    def drain(self):
        for n in range(self.count):
            for k in range(4):
                for what in ("across", "relay", "sibling", "forward"):
                    self.act(n, k, what).wait_send()

        def drain_grads(i, carry):
            self.grad_across(i).wait_send()
            self.grad_sibling(i).wait_send()
            self.grad_forward(i).wait_send()
            return carry

        lax.fori_loop(0, GRADS * self.count, drain_grads, 0)

        def drain_tiles(t, carry):
            self.y_copy(t).wait_send()
            for o in (1, 2, 3):
                self.z_copy(t, o).wait_send()
            return carry

        lax.fori_loop(0, TILES * self.count, drain_tiles, 0)


class GainSum:
    def __init__(self, reducer, source, out, scratch):
        self.reducer, self.source, self.out = reducer, source, out
        self.part, self.recv, self.s, self.r = scratch

    def hop(self, i):
        red = self.reducer
        return make_remote(
            self.source if i == 0 else self.part.at[i - 1], self.recv.at[i], self.s.at[i],
            self.r.at[i], (red.across, red.sibling, red.aside)[i],
        )

    def along(self, o):
        return make_remote(
            self.part.at[2], self.recv.at[6 - o], self.s.at[2 + o], self.r.at[6 - o],
            self.reducer.along(o),
        )

    def step(self, s, first):
        @pl.when(s == first)
        def begin():
            self.hop(0).start()

        for i in range(3):

            @pl.when(s == first + 1 + i)
            def stage(i=i):
                self.hop(i).wait_recv()
                self.part[i] = (self.source[...] if i == 0 else self.part[i - 1]) + self.recv[i]
                if i < 2:
                    self.hop(i + 1).start()
                else:
                    for o in (1, 2, 3):
                        self.along(o).start()

        @pl.when(s == first + 5)
        def total():
            for o in (1, 2, 3):
                self.along(o).wait_recv()
            self.out[...] = self.part[2] + self.recv[3] + self.recv[4] + self.recv[5]

    def drain(self):
        for i in range(3):
            self.hop(i).wait_send()
            self.along(i + 1).wait_send()


def reduce_scratch(count):
    dma = pltpu.SemaphoreType.DMA
    low, wide = jnp.bfloat16, jnp.float32
    tiles, grads = TILES * count, GRADS * count
    return [
        pltpu.VMEM((count, 4, 2, ACTS, 32, 512), low),
        pltpu.VMEM((count, 4, 2, ACTS, 32, 128), low),
        pltpu.VMEM((512, 1024), low),
        pltpu.VMEM((tiles, 128, 1024), low),
        pltpu.VMEM((tiles, 128, 1024), low),
        pltpu.VMEM((4, 128, 1024), wide),
        pltpu.VMEM((tiles, 3, 32, 1024), low),
        pltpu.VMEM((tiles, 3, 32, 1024), low),
        pltpu.VMEM((4, 32, 1024), wide),
        dma((count, 4)), dma((count, 4, 2)), dma((count, 4, 2)), dma((count, 4, 2)),
        dma((count, 4, 2)),
        dma((2,)), dma((grads,)), dma((grads,)), dma((grads,)), dma((grads,)), dma((grads,)),
        dma((grads,)),
        dma((tiles,)), dma((tiles,)), dma((tiles, 3)), dma((tiles, 3)),
    ]


def gain_scratch(rows):
    dma = pltpu.SemaphoreType.DMA
    return [
        pltpu.VMEM((3, rows, 128), jnp.float32),
        pltpu.VMEM((6, rows, 128), jnp.float32),
        dma((6,)),
        dma((6,)),
    ]


RESULTS = ((32, 2048), (32, 1024), (32, 1024), (64, 1024), (32, 3072), (32, 3072), (96, 1024))


def reduce_kernel(layers, *refs):
    count = len(layers)
    acts = [refs[4 * n : 4 * n + 4] for n in range(count)]
    refs = refs[4 * count :]
    grads = []
    for n in range(count):
        down, both, out, pre = refs[4 * n : 4 * n + 4]
        grads.append(((down, 1), (both, 6), (out, 1), (pre, 4)))
    refs = refs[4 * count :]
    gains = refs[0]
    results = refs[1:8]
    gain_out = refs[8]
    held = refs[9]
    sizes = len(reduce_scratch(count))
    reducer = Reducer(acts, grads, results, (held,) + tuple(refs[10 : 10 + sizes]), layers)
    gain_sum = GainSum(reducer, gains, gain_out, refs[10 + sizes :])
    barrier = pltpu.get_barrier_semaphore()
    for other in reducer.partners():
        pl.semaphore_signal(barrier, inc=1, device_id=other, device_id_type=MESH)
    pl.semaphore_wait(barrier, 6)
    reducer.begin()

    def step(s, carry):
        gain_sum.step(s, 2)
        reducer.step(s)
        return carry

    lax.fori_loop(0, reducer.steps(), step, 0)
    reducer.drain()
    gain_sum.drain()


def reduce_layers(acts, grads, gains, layers, collective_id):
    count = len(layers)
    wide = jnp.float32
    return pl.pallas_call(
        functools.partial(reduce_kernel, layers),
        out_shape=[jax.ShapeDtypeStruct((count,) + shape, wide) for shape in RESULTS]
        + [
            jax.ShapeDtypeStruct(gains.shape, wide),
            jax.ShapeDtypeStruct((GRADS * count, 384, 1024), jnp.bfloat16),
        ],
        in_specs=[pl.BlockSpec(memory_space=pl.ANY)] * (8 * count)
        + [pl.BlockSpec(memory_space=pltpu.VMEM)],
        out_specs=[pl.BlockSpec(memory_space=pltpu.VMEM)] * 8
        + [pl.BlockSpec(memory_space=pl.ANY)],
        scratch_shapes=reduce_scratch(count) + gain_scratch(gains.shape[0]),
        compiler_params=pltpu.CompilerParams(
            collective_id=collective_id, has_side_effects=True, vmem_limit_bytes=56 * 2**20
        ),
        name="weight_gradient_reduce",
    )(*acts, *grads, gains)


GATHER_PLAN = ((0, 0, 0), (1, 0, 2048), (2, 0, 3072), (3, 1, 0), (4, 2, 0), (5, 2, 3072), (6, 3, 0))
MEMBERS = 7


def gather_kernel(layers, *refs):
    sources = refs[:MEMBERS]
    gains = refs[MEMBERS]
    outs = refs[MEMBERS + 1 : MEMBERS + 1 + 4 * len(layers)]
    gains_out = refs[MEMBERS + 1 + 4 * len(layers)]
    (l_sem, l_rec, x_s, x_r, y_s, y_r, z_s, z_r, yd_s, yd_r, zd_s, zd_r, c_s, c_r, g_sem) = refs[
        MEMBERS + 2 + 4 * len(layers) :
    ]
    c = lax.axis_index("ctx")
    x = lax.axis_index("fsdp")
    core = c % 2
    y = c // 2 % 2
    near = c // 4 % 2
    sibling = (c + 1 - 2 * core, x)
    across = (c, 1 - x)
    aside = (c + 2 - 4 * y, x)
    along = (c + 4 - 8 * near, x)

    barrier = pltpu.get_barrier_semaphore()
    for other in (sibling, across, aside, along):
        pl.semaphore_signal(barrier, inc=1, device_id=other, device_id_type=MESH)
    pl.semaphore_wait(barrier, 4)

    def remote(src, dst, s, r, dev):
        return pltpu.make_async_remote_copy(
            src_ref=src, dst_ref=dst, send_sem=s, recv_sem=r, device_id=dev, device_id_type=MESH
        )

    here = near * 2 + y
    by_y = near * 2 + 1 - y
    by_z = (1 - near) * 2 + y
    corner = (1 - near) * 2 + 1 - y
    steps = [(n, m) for n in range(len(layers)) for m in range(MEMBERS)]
    count = len(steps)

    def geometry(i):
        n, m = steps[i]
        source, target, column = GATHER_PLAN[m]
        half = sources[source].shape[1]
        part = half // 8
        width = sources[source].shape[2]
        return n, sources[source], outs[4 * n + target], half, part, width, column

    def window(i, owner_x, owner_core, piece, share=None):
        n, src, out, half, part, width, column = geometry(i)
        start = owner_x * half + (piece * 2 + owner_core) * part
        rows = part
        if share is not None:
            rows = part // 2
            start = start + share * rows
        return out.at[pl.ds(pl.multiple_of(start, 16), rows), pl.ds(column, width)]

    def local(i):
        n, src, out, half, part, width, column = geometry(i)
        rows = pl.ds(pl.multiple_of(x * half, 16), half)
        return remote(
            src.at[layers[n]], out.at[rows, pl.ds(column, width)], l_sem.at[i], l_rec.at[i], sibling
        )

    def x_copy(i):
        n, src, out, half, part, width, column = geometry(i)
        rows = pl.ds(pl.multiple_of((here * 2 + core) * part, 16), part)
        return remote(
            src.at[layers[n], rows], window(i, x, core, here), x_s.at[i], x_r.at[i], across
        )

    def same(i, piece, s, r, dev, share=None):
        view = window(i, 1 - x, core, piece, share)
        return remote(view, view, s, r, dev)

    def y_copy(i):
        return same(i, here, y_s.at[i], y_r.at[i], aside)

    def z_copy(i):
        return same(i, here, z_s.at[i], z_r.at[i], along)

    def y_corner(i):
        return same(i, by_z, yd_s.at[i], yd_r.at[i], aside, 1)

    def z_corner(i):
        return same(i, by_y, zd_s.at[i], zd_r.at[i], along, 0)

    def core_copy(i, which):
        piece = (here, by_y, by_z, corner)[which]
        return same(i, piece, c_s.at[i, which], c_r.at[i, which], sibling)

    gain_local = pltpu.make_async_copy(gains, gains_out.at[x], g_sem.at[0])
    gain_remote = remote(gains, gains_out.at[x], g_sem.at[1], g_sem.at[2], across)
    gain_local.start()
    gain_remote.start()

    ahead = 3
    for i in range(min(ahead, count)):
        x_copy(i).start()
        local(i).start()
    for s in range(count + 3):
        if s < count:
            x_copy(s).wait_recv()
            y_copy(s).start()
            z_copy(s).start()
            core_copy(s, 0).start()
            if s + ahead < count:
                x_copy(s + ahead).start()
                local(s + ahead).start()
        i = s - 1
        if 0 <= i < count:
            y_copy(i).wait_recv()
            z_corner(i).start()
            core_copy(i, 1).start()
            z_copy(i).wait_recv()
            y_corner(i).start()
            core_copy(i, 2).start()
        i = s - 3
        if 0 <= i < count:
            y_corner(i).wait_recv()
            z_corner(i).wait_recv()
            core_copy(i, 3).start()
    gain_local.wait()
    gain_remote.wait()
    for i in range(count):
        local(i).wait()
        for copy in (x_copy(i), y_copy(i), z_copy(i), y_corner(i), z_corner(i)):
            copy.wait_send()
        for which in range(4):
            core_copy(i, which).wait()


def gather_weights(weights, gains, layers, collective_id):
    dma = pltpu.SemaphoreType.DMA
    count = MEMBERS * len(layers)
    low = jnp.bfloat16
    shapes = [(1024, 4096), (2048, 1024), (1024, 6144), (3072, 1024)] * len(layers)
    return pl.pallas_call(
        functools.partial(gather_kernel, layers),
        out_shape=[jax.ShapeDtypeStruct(s, low) for s in shapes]
        + [jax.ShapeDtypeStruct((2,) + gains.shape, low)],
        in_specs=[pl.BlockSpec(memory_space=pl.ANY)] * (MEMBERS + 1),
        out_specs=[pl.BlockSpec(memory_space=pl.ANY)] * (len(shapes) + 1),
        scratch_shapes=[dma((count,))] * 12 + [dma((count, 4))] * 2 + [dma((3,))],
        compiler_params=pltpu.CompilerParams(collective_id=collective_id, has_side_effects=True),
        name="weight_gather",
    )(*weights, gains)


PEERS = KEY_VALUE_HEADS
SCALE = HEAD_SIZE ** (-0.5)
NT = (((1,), (1,)), ((), ()))


def peer_tools():
    c = lax.axis_index("ctx")
    x = lax.axis_index("fsdp")
    me = c % PEERS

    def peer(r):
        return (c - me + r, x)

    def remote(src, dst, s, r, dev):
        return pltpu.make_async_remote_copy(
            src_ref=src, dst_ref=dst, send_sem=s, recv_sem=r, device_id=dev, device_id_type=MESH
        )

    barrier = pltpu.get_barrier_semaphore()

    def greet(o, carry):
        pl.semaphore_signal(
            barrier, inc=1, device_id=peer((me + o) % PEERS), device_id_type=MESH
        )
        return carry

    lax.fori_loop(1, PEERS, greet, 0)
    return me, peer, remote, barrier


def head_columns(first, index):
    return pl.ds(pl.multiple_of(first + index * HEAD_SIZE, HEAD_SIZE), HEAD_SIZE)


def attend_kernel(
    pre, cosine, sine, gains, key_place, query_cap, out, kept, kept_out, kept_log,
    send, osend, orecv, vt, q_s, q_r, k_s, k_r, o_s, o_r,
):
    me, peer, remote, barrier = peer_tools()
    cos = cosine[...]
    sin = sine[...]

    def turned(first, index, gain):
        v = pre[:, head_columns(first, index)]
        r = lax.rsqrt(jnp.mean(v * v, axis=-1, keepdims=True) + norm_epsilon)
        n = v * r * gain
        return (n * cos + pltpu.roll(n, HEAD_SIZE // 2, 1) * sin).astype(jnp.bfloat16)

    def key_copy(r, slot):
        return remote(
            send.at[r, pl.ds(2, 2)], kept.at[slot, pl.ds(2, 2)], k_s.at[r], k_r.at[slot], peer(r)
        )

    def query_copy(r, slot):
        return remote(
            send.at[r, pl.ds(0, 2)], kept.at[slot, pl.ds(0, 2)], q_s.at[r], q_r.at[slot], peer(r)
        )

    def out_copy(r, slot):
        return remote(osend.at[r], orecv.at[slot], o_s.at[r], o_r.at[slot], peer(r))

    def make_keys(o, carry):
        r = (me + o) % PEERS
        key = turned(2048, r, gains[1:2, :])
        value = pre[:, head_columns(3072, r)].astype(jnp.bfloat16)

        @pl.when(o < PEERS)
        def away():
            send[r, 2] = key
            send[r, 3] = value

        @pl.when(o == PEERS)
        def home():
            kept[me, 2] = key
            kept[me, 3] = value

        @pl.when(o == 1)
        def entered():
            pl.semaphore_wait(barrier, PEERS - 1)

        @pl.when(o < PEERS)
        def push():
            key_copy(r, me).start()

        return carry

    def make_queries(o, carry):
        r = (me + o) % PEERS
        first = turned(0, 2 * r, gains[0:1, :])
        second = turned(0, 2 * r + 1, gains[0:1, :])

        @pl.when(o < PEERS)
        def away():
            send[r, 0] = first
            send[r, 1] = second
            query_copy(r, me).start()

        @pl.when(o == PEERS)
        def home():
            kept[me, 0] = first
            kept[me, 1] = second

        return carry

    lax.fori_loop(1, PEERS + 1, make_keys, 0)
    lax.fori_loop(1, PEERS + 1, make_queries, 0)

    def await_keys(o, carry):
        key_copy(me, (me + o) % PEERS).wait_recv()
        return carry

    lax.fori_loop(1, PEERS, await_keys, 0)

    def turn_values(j, carry):
        vt[j] = kept[j, 3].astype(jnp.float32).T.astype(jnp.bfloat16)
        return carry

    lax.fori_loop(0, PEERS, turn_values, 0)

    def block(o, carry):
        j = (me + o) % PEERS

        @pl.when(o > 0)
        def arrived():
            query_copy(me, j).wait_recv()

        queries = kept[j, 0:2].reshape(2 * 128, HEAD_SIZE)
        keys = kept[:, 2].reshape(PEERS * 128, HEAD_SIZE)
        scores = lax.dot_general(keys, queries, NT, preferred_element_type=jnp.float32) * SCALE
        allowed = key_place[...] <= query_cap[j]
        scores = jnp.where(allowed, scores, masked_logits)
        highest = jnp.max(scores, axis=0, keepdims=True)
        expo = jnp.exp(scores - highest)
        total = jnp.sum(expo, axis=0, keepdims=True)
        low = expo.astype(jnp.bfloat16)
        turned_out = jnp.zeros((HEAD_SIZE, 256), jnp.float32)
        for i in range(PEERS):
            turned_out += jnp.dot(
                vt[i], low[i * 128 : (i + 1) * 128], preferred_element_type=jnp.float32
            )
        turned_out = turned_out / total
        kept_out[j] = turned_out
        kept_log[j] = jnp.broadcast_to(highest + jnp.log(total), (8, 256))
        attended = turned_out.T.astype(jnp.bfloat16).reshape(2, 128, HEAD_SIZE)

        @pl.when(o == 0)
        def home():
            orecv[me] = attended

        @pl.when(o > 0)
        def away():
            osend[j] = attended
            out_copy(j, me).start()

        return carry

    lax.fori_loop(0, PEERS, block, 0)

    def collect(o, carry):
        h = (me + o) % PEERS

        @pl.when(o > 0)
        def arrived():
            out_copy(me, h).wait_recv()

        out[:, head_columns(0, 2 * h)] = orecv[h, 0]
        out[:, head_columns(0, 2 * h + 1)] = orecv[h, 1]
        return carry

    lax.fori_loop(0, PEERS, collect, 0)

    def drain(o, carry):
        r = (me + o) % PEERS
        key_copy(r, me).wait_send()
        query_copy(r, me).wait_send()
        out_copy(r, me).wait_send()
        return carry

    lax.fori_loop(1, PEERS, drain, 0)


def attend(pre, cosine, sine, gains, key_place, query_cap, collective_id):
    dma = pltpu.SemaphoreType.DMA
    low, wide = jnp.bfloat16, jnp.float32
    return pl.pallas_call(
        attend_kernel,
        out_shape=[
            jax.ShapeDtypeStruct((128, 2048), low),
            jax.ShapeDtypeStruct((PEERS, 4, 128, HEAD_SIZE), low),
            jax.ShapeDtypeStruct((PEERS, HEAD_SIZE, 256), wide),
            jax.ShapeDtypeStruct((PEERS, 8, 256), wide),
        ],
        in_specs=[pl.BlockSpec(memory_space=pltpu.VMEM)] * 6,
        out_specs=[pl.BlockSpec(memory_space=pltpu.VMEM)] * 4,
        scratch_shapes=[
            pltpu.VMEM((PEERS, 4, 128, HEAD_SIZE), low),
            pltpu.VMEM((PEERS, 2, 128, HEAD_SIZE), low),
            pltpu.VMEM((PEERS, 2, 128, HEAD_SIZE), low),
            pltpu.VMEM((PEERS, HEAD_SIZE, 128), low),
        ]
        + [dma((PEERS,))] * 6,
        compiler_params=pltpu.CompilerParams(
            collective_id=collective_id, has_side_effects=True, vmem_limit_bytes=40 * 2**20
        ),
        name="attend",
    )(pre, cosine, sine, gains, key_place, query_cap)


def attend_back_kernel(
    upstream, kept, kept_out, kept_log, pre, cosine, sine, gains, key_place, query_cap,
    out, gain_out,
    dsend, drecv, qsend, qrecv, ksend, krecv, kt, key_sum, value_sum,
    d_s, d_r, q_s, q_r, k_s, k_r,
):
    me, peer, remote, barrier = peer_tools()
    cos = cosine[...]
    sin = sine[...]

    def grad_copy(r, slot):
        return remote(dsend.at[r], drecv.at[slot], d_s.at[r], d_r.at[slot], peer(r))

    def query_copy(r, slot):
        return remote(qsend.at[r], qrecv.at[slot], q_s.at[r], q_r.at[slot], peer(r))

    def key_copy(r, slot):
        return remote(ksend.at[r], krecv.at[slot], k_s.at[r], k_r.at[slot], peer(r))

    pl.semaphore_wait(barrier, PEERS - 1)

    def push(o, carry):
        r = (me + o) % PEERS
        dsend[r, 0] = upstream[:, head_columns(0, 2 * r)]
        dsend[r, 1] = upstream[:, head_columns(0, 2 * r + 1)]
        grad_copy(r, me).start()
        return carry

    lax.fori_loop(1, PEERS, push, 0)
    drecv[me, 0] = upstream[:, head_columns(0, 2 * me)]
    drecv[me, 1] = upstream[:, head_columns(0, 2 * me + 1)]

    def turn_keys(j, carry):
        kt[j] = kept[j, 2].astype(jnp.float32).T.astype(jnp.bfloat16)
        return carry

    lax.fori_loop(0, PEERS, turn_keys, 0)
    key_sum[...] = jnp.zeros_like(key_sum)
    value_sum[...] = jnp.zeros_like(value_sum)

    def block(o, carry):
        j = (me + o) % PEERS

        @pl.when(o > 0)
        def arrived():
            grad_copy(me, j).wait_recv()

        grads = drecv[j].reshape(2 * 128, HEAD_SIZE)
        delta = jnp.sum(grads.astype(jnp.float32).T * kept_out[j], axis=0, keepdims=True)
        queries = kept[j, 0:2].reshape(2 * 128, HEAD_SIZE)
        keys = kept[:, 2].reshape(PEERS * 128, HEAD_SIZE)
        values = kept[:, 3].reshape(PEERS * 128, HEAD_SIZE)
        scores = lax.dot_general(keys, queries, NT, preferred_element_type=jnp.float32) * SCALE
        allowed = key_place[...] <= query_cap[j]
        scores = jnp.where(allowed, scores, masked_logits)
        prob = jnp.exp(scores - kept_log[j, 0:1, :])
        dprob = lax.dot_general(values, grads, NT, preferred_element_type=jnp.float32)
        dscore = (prob * (dprob - delta)).astype(jnp.bfloat16)
        value_sum[...] += jnp.dot(
            prob.astype(jnp.bfloat16), grads, preferred_element_type=jnp.float32
        )
        key_sum[...] += jnp.dot(dscore, queries, preferred_element_type=jnp.float32)
        turned = jnp.zeros((HEAD_SIZE, 256), jnp.float32)
        for i in range(PEERS):
            turned += jnp.dot(
                kt[i], dscore[i * 128 : (i + 1) * 128], preferred_element_type=jnp.float32
            )
        query_grad = (turned * SCALE).T.astype(jnp.bfloat16).reshape(2, 128, HEAD_SIZE)

        @pl.when(o == 0)
        def home():
            qrecv[me] = query_grad

        @pl.when(o > 0)
        def away():
            qsend[j] = query_grad
            query_copy(j, me).start()

        return carry

    lax.fori_loop(0, PEERS, block, 0)

    def push_keys(o, carry):
        j = (me + o) % PEERS
        rows = pl.ds(pl.multiple_of(j * 128, 128), 128)
        key = (key_sum[rows, :] * SCALE).astype(jnp.bfloat16)
        value = value_sum[rows, :].astype(jnp.bfloat16)

        @pl.when(o < PEERS)
        def away():
            ksend[j, 0] = key
            ksend[j, 1] = value
            key_copy(j, me).start()

        @pl.when(o == PEERS)
        def home():
            krecv[me, 0] = key
            krecv[me, 1] = value

        return carry

    lax.fori_loop(1, PEERS + 1, push_keys, 0)

    def back(grad, first, index, gain):
        g = grad.astype(jnp.float32)
        dy = g * cos - pltpu.roll(g, HEAD_SIZE // 2, 1) * sin
        v = pre[:, head_columns(first, index)]
        r = lax.rsqrt(jnp.mean(v * v, axis=-1, keepdims=True) + norm_epsilon)
        u = dy * gain
        result = r * u - v * (r * r * r) * jnp.mean(u * v, axis=-1, keepdims=True)
        return result.astype(jnp.bfloat16), jnp.sum(dy * v * r, axis=0, keepdims=True)

    def finish_queries(o, total):
        h = (me + o) % PEERS

        @pl.when(o > 0)
        def arrived():
            query_copy(me, h).wait_recv()

        for i in range(2):
            low, term = back(qrecv[h, i], 0, 2 * h + i, gains[0:1, :])
            out[:, head_columns(0, 2 * h + i)] = low
            total += term
        return total

    zero = jnp.zeros((1, HEAD_SIZE), jnp.float32)
    query_total = lax.fori_loop(0, PEERS, finish_queries, zero)

    def finish_keys(o, total):
        h = (me + o) % PEERS

        @pl.when(o > 0)
        def arrived():
            key_copy(me, h).wait_recv()

        low, term = back(krecv[h, 0], 2048, h, gains[1:2, :])
        out[:, head_columns(2048, h)] = low
        out[:, head_columns(3072, h)] = krecv[h, 1]
        return total + term

    key_total = lax.fori_loop(0, PEERS, finish_keys, zero)
    gain_out[...] = jnp.concatenate(
        [query_total, key_total, jnp.zeros((6, HEAD_SIZE), jnp.float32)], axis=0
    )

    def drain(o, carry):
        r = (me + o) % PEERS
        grad_copy(r, me).wait_send()
        query_copy(r, me).wait_send()
        key_copy(r, me).wait_send()
        return carry

    lax.fori_loop(1, PEERS, drain, 0)


def attend_back(
    upstream, kept, kept_out, kept_log, pre, cosine, sine, gains, key_place, query_cap, collective_id
):
    dma = pltpu.SemaphoreType.DMA
    low, wide = jnp.bfloat16, jnp.float32
    pair = pltpu.VMEM((PEERS, 2, 128, HEAD_SIZE), low)
    return pl.pallas_call(
        attend_back_kernel,
        out_shape=[
            jax.ShapeDtypeStruct((128, 4096), low),
            jax.ShapeDtypeStruct((8, HEAD_SIZE), wide),
        ],
        in_specs=[pl.BlockSpec(memory_space=pltpu.VMEM)] * 10,
        out_specs=[pl.BlockSpec(memory_space=pltpu.VMEM)] * 2,
        scratch_shapes=[pair] * 6
        + [
            pltpu.VMEM((PEERS, HEAD_SIZE, 128), low),
            pltpu.VMEM((PEERS * 128, HEAD_SIZE), wide),
            pltpu.VMEM((PEERS * 128, HEAD_SIZE), wide),
        ]
        + [dma((PEERS,))] * 6,
        compiler_params=pltpu.CompilerParams(
            collective_id=collective_id, has_side_effects=True, vmem_limit_bytes=48 * 2**20
        ),
        name="attend_back",
    )(upstream, kept, kept_out, kept_log, pre, cosine, sine, gains, key_place, query_cap)


def from_partner(shard, axis, apart):
    return lax.ppermute(shard, axis, [(i, i ^ 1 << apart) for i in range(lax.axis_size(axis))])


def token_places(stretch_table, slot_lengths):
    ctx_count = stretch_table.shape[0]
    stretch_order = stretch_table.reshape(-1)
    within = jnp.arange(STRETCH, dtype=jnp.int32)
    places = (stretch_order % ctx_count * STRETCH)[:, None] + within[None, :]
    slot_ids = jnp.broadcast_to((stretch_order // ctx_count)[:, None], places.shape).reshape(-1)
    places = places.reshape(-1)
    limits = jnp.where(slot_ids == 0, slot_lengths[0], slot_lengths[1])
    return (places, slot_ids, places < limits)


def rotary_tables(places):
    half_dim = HEAD_SIZE // 2
    spread = jnp.arange(half_dim, dtype=jnp.int32).astype(jnp.float32) * (2.0 / HEAD_SIZE)
    inverse = jnp.exp(spread * -math.log(rope_base))
    angles = places.astype(jnp.float32)[:, None] * inverse[None, :]
    return (
        jnp.concatenate([jnp.cos(angles)] * 2, axis=-1),
        jnp.concatenate([jnp.sin(angles)] * 2, axis=-1),
    )


def rotate(values, cosine_table, sine_table):
    half_dim = values.shape[-1] // 2
    turned = jnp.concatenate([-values[..., half_dim:], values[..., :half_dim]], axis=-1)
    return values * cosine_table[:, None, :] + turned * sine_table[:, None, :]


def unrotate(upstream, cosine_table, sine_table):
    half_dim = upstream.shape[-1] // 2
    scaled_sine = upstream * sine_table[:, None, :]
    turned_back = jnp.concatenate(
        [scaled_sine[..., half_dim:], -scaled_sine[..., :half_dim]], axis=-1
    )
    return upstream * cosine_table[:, None, :] + turned_back


def norm_forward(values, gain_vec):
    scale_inv = lax.rsqrt(jnp.mean(values * values, axis=-1, keepdims=True) + norm_epsilon)
    return (values * scale_inv * gain_vec, scale_inv)


def norm_backward(values, scale_inv, gain_vec, upstream):
    weighted = upstream * gain_vec
    grad_input = scale_inv * weighted - values * scale_inv**3 * jnp.mean(
        weighted * values, axis=-1, keepdims=True
    )
    gain_term = jnp.sum((upstream * values * scale_inv).reshape(-1, values.shape[-1]), axis=0)
    return (grad_input, gain_term)


def upper_bit(local_index, bit_number):
    return local_index // 2**bit_number % 2 == 1


def joined_rows(mine, received, upper_side):
    first_rows = jnp.where(upper_side, received, mine)
    second_rows = jnp.where(upper_side, mine, received)
    return jnp.concatenate([first_rows, second_rows], axis=0)


def half_gather(pair, local_index):
    gathered_rows = pair
    for bit_number in range(lax.axis_size("ctx").bit_length() - 2):
        received = from_partner(gathered_rows, "ctx", bit_number)
        gathered_rows = joined_rows(gathered_rows, received, upper_bit(local_index, bit_number))
    return gathered_rows


def half_reduce(term, local_index):
    for bit_number in reversed(range(lax.axis_size("ctx").bit_length() - 2)):
        span = term.shape[0] // 2
        lower_rows = term[:span]
        upper_rows = term[span:]
        upper_side = upper_bit(local_index, bit_number)
        kept_rows = jnp.where(upper_side, upper_rows, lower_rows)
        sent_rows = jnp.where(upper_side, lower_rows, upper_rows)
        term = kept_rows + from_partner(sent_rows, "ctx", bit_number)
    return term


def over_keys(update, carried, count_rows):
    block_length = math.gcd(count_rows, 512)

    def inner_step(current, block_index):
        return (update(current, block_index * block_length, block_length), None)

    carried, unused = lax.scan(
        inner_step, carried, jnp.arange(count_rows // block_length, dtype=jnp.int32)
    )
    return carried


def allowed_mask(key_meta, query_meta, row_start, block_length):
    key_places = lax.dynamic_slice_in_dim(key_meta[0], row_start, block_length)
    key_slots = lax.dynamic_slice_in_dim(key_meta[1], row_start, block_length)
    key_live = lax.dynamic_slice_in_dim(key_meta[2], row_start, block_length)
    allowed = (
        (key_slots[None, :] == query_meta[1][:, None])
        & (key_places[None, :] <= query_meta[0][:, None])
        & key_live[None, :]
    )
    return allowed[None, None]


def forward_update(
    current, query_head_group, key_tile_block, value_tile_block, allowed, score_scale
):
    running_max, running_sum, running_acc = current
    block_length = key_tile_block.shape[0]
    key_head_list = key_tile_block.reshape(block_length, KEY_VALUE_HEADS, HEAD_SIZE)
    value_head_list = value_tile_block.reshape(block_length, KEY_VALUE_HEADS, HEAD_SIZE)
    scores = (
        jnp.einsum(
            "qhgd,khd->hgqk", query_head_group, key_head_list, preferred_element_type=jnp.float32
        )
        * score_scale
    )
    scores = jnp.where(allowed, scores, masked_logits)
    new_max = jnp.maximum(running_max, jnp.max(scores, axis=-1))
    factor = jnp.exp(running_max - new_max)
    prob_block = jnp.where(allowed, jnp.exp(scores - new_max[..., None]), 0.0)
    new_sum = running_sum * factor + jnp.sum(prob_block, axis=-1)
    new_acc = running_acc * factor[..., None] + jnp.einsum(
        "hgqk,khd->hgqd",
        prob_block.astype(jnp.bfloat16),
        value_head_list,
        preferred_element_type=jnp.float32,
    )
    return (new_max, new_sum, new_acc)


def score_parts(
    query_head_group,
    output_grad_group,
    key_tile_block,
    value_tile_block,
    allowed,
    log_total,
    row_delta,
    score_scale,
):
    block_length = key_tile_block.shape[0]
    key_head_list = key_tile_block.reshape(block_length, KEY_VALUE_HEADS, HEAD_SIZE)
    value_head_list = value_tile_block.reshape(block_length, KEY_VALUE_HEADS, HEAD_SIZE)
    scores = (
        jnp.einsum(
            "qhgd,khd->hgqk", query_head_group, key_head_list, preferred_element_type=jnp.float32
        )
        * score_scale
    )
    prob_block = jnp.where(allowed, jnp.exp(scores - log_total[..., None]), 0.0)
    dprob = jnp.einsum(
        "qhgd,khd->hgqk", output_grad_group, value_head_list, preferred_element_type=jnp.float32
    )
    dscore_low = (prob_block * (dprob - row_delta[..., None])).astype(jnp.bfloat16)
    return (prob_block, dscore_low, key_head_list)


def attention_inputs(stream, gathered, cosine_table, sine_table):
    count_rows = stream.shape[0]
    normalized, inv_attn = norm_forward(stream, gathered[7].astype(jnp.float32))
    normed_low = normalized.astype(jnp.bfloat16)
    query_heads = jnp.dot(normed_low, gathered[0], preferred_element_type=jnp.float32).reshape(
        count_rows, QUERY_HEADS, HEAD_SIZE
    )
    key_head_list = jnp.dot(normed_low, gathered[1], preferred_element_type=jnp.float32).reshape(
        count_rows, KEY_VALUE_HEADS, HEAD_SIZE
    )
    value_low = jnp.dot(normed_low, gathered[2], preferred_element_type=jnp.float32).astype(
        jnp.bfloat16
    )
    query_normed, inv_query = norm_forward(query_heads, gathered[9].astype(jnp.float32))
    key_normed, inv_key = norm_forward(key_head_list, gathered[10].astype(jnp.float32))
    query_lowered = rotate(query_normed, cosine_table, sine_table).astype(jnp.bfloat16)
    key_low = (
        rotate(key_normed, cosine_table, sine_table)
        .astype(jnp.bfloat16)
        .reshape(count_rows, KEY_VALUE_HEADS * HEAD_SIZE)
    )
    return {
        "normed_low": normed_low,
        "inv_attn": inv_attn,
        "query_heads": query_heads,
        "inv_query": inv_query,
        "key_heads": key_head_list,
        "inv_key": inv_key,
        "query_low": query_lowered,
        "key_low": key_low,
        "value_low": value_low,
    }


def block_rest(stream, gathered, attn_low):
    middle = stream + jnp.dot(attn_low, gathered[3], preferred_element_type=jnp.float32)
    normed_mid, inv_mid = norm_forward(middle, gathered[8].astype(jnp.float32))
    normed_mid_low = normed_mid.astype(jnp.bfloat16)
    gate_act = jnp.dot(normed_mid_low, gathered[4], preferred_element_type=jnp.float32)
    upward = jnp.dot(normed_mid_low, gathered[5], preferred_element_type=jnp.float32)
    hidden_low = (jax.nn.silu(gate_act) * upward).astype(jnp.bfloat16)
    result = middle + jnp.dot(hidden_low, gathered[6], preferred_element_type=jnp.float32)
    return {
        "middle": middle,
        "inv_mid": inv_mid,
        "normed_mid_low": normed_mid_low,
        "gate_act": gate_act,
        "upward": upward,
        "hidden_low": hidden_low,
        "result": result,
    }


def general_device(
    tokens,
    cotangent,
    lengths,
    stretch_ids,
    w_query,
    key_projection_weight,
    value_projection_weight,
    w_out,
    w_gate,
    w_up,
    w_down,
    g_attn,
    g_mlp,
    g_query,
    g_key,
):
    count_rows = tokens.shape[0]
    ctx_count = lax.axis_size("ctx")
    half_count = ctx_count // 2
    key_value_width = KEY_VALUE_HEADS * HEAD_SIZE
    key_meta = token_places(stretch_ids[:, 0, :], lengths[0])
    ctx_index = lax.axis_index("ctx")
    local_index = ctx_index % half_count
    base_row = ctx_index // half_count * half_count * count_rows
    half_row_set = half_count * count_rows
    offset_mine = ctx_index * count_rows
    query_meta = tuple(
        (lax.dynamic_slice_in_dim(meta_array, offset_mine, count_rows) for meta_array in key_meta)
    )
    live_mine = query_meta[2].astype(jnp.float32)[:, None]
    cosine_table, sine_table = rotary_tables(query_meta[0])
    group_count = QUERY_HEADS // KEY_VALUE_HEADS
    score_scale = HEAD_SIZE ** (-0.5)

    def attend_forward(query_head_group, key_source, value_source, current):

        def update(carried, local_row, block_length):
            key_tile_block = lax.dynamic_slice_in_dim(key_source, local_row, block_length)
            value_tile_block = lax.dynamic_slice_in_dim(value_source, local_row, block_length)
            allowed = allowed_mask(key_meta, query_meta, base_row + local_row, block_length)
            return forward_update(
                carried, query_head_group, key_tile_block, value_tile_block, allowed, score_scale
            )

        return over_keys(update, current, key_source.shape[0])

    saved = []
    stream = tokens.astype(jnp.float32)
    for layer_index in range(DECODER_LAYERS):
        gathered = (
            lax.all_gather(w_query[layer_index], "fsdp", axis=0, tiled=True),
            lax.all_gather(key_projection_weight[layer_index], "fsdp", axis=0, tiled=True),
            lax.all_gather(value_projection_weight[layer_index], "fsdp", axis=0, tiled=True),
            lax.all_gather(w_out[layer_index], "fsdp", axis=0, tiled=True),
            lax.all_gather(w_gate[layer_index], "fsdp", axis=0, tiled=True),
            lax.all_gather(w_up[layer_index], "fsdp", axis=0, tiled=True),
            lax.all_gather(w_down[layer_index], "fsdp", axis=0, tiled=True),
            lax.all_gather(g_attn[layer_index], "fsdp", axis=0, tiled=True),
            lax.all_gather(g_mlp[layer_index], "fsdp", axis=0, tiled=True),
            lax.all_gather(g_query[layer_index], "fsdp", axis=0, tiled=True),
            lax.all_gather(g_key[layer_index], "fsdp", axis=0, tiled=True),
        )
        present_inputs = attention_inputs(stream, gathered, cosine_table, sine_table)
        query_head_group = present_inputs["query_low"].reshape(
            count_rows, KEY_VALUE_HEADS, group_count, HEAD_SIZE
        )
        start_state = (
            jnp.full((KEY_VALUE_HEADS, group_count, count_rows), masked_logits, jnp.float32),
            jnp.zeros((KEY_VALUE_HEADS, group_count, count_rows), jnp.float32),
            jnp.zeros((KEY_VALUE_HEADS, group_count, count_rows, HEAD_SIZE), jnp.float32),
        )
        pair_all = half_gather(
            jnp.concatenate([present_inputs["key_low"], present_inputs["value_low"]], axis=-1),
            local_index,
        )
        key_all = pair_all[:, :key_value_width]
        value_all = pair_all[:, key_value_width:]
        final_state = attend_forward(query_head_group, key_all, value_all, start_state)
        attended = final_state[2] / final_state[1][..., None]
        log_total = final_state[0] + jnp.log(final_state[1])
        attn_low = (
            jnp.transpose(attended, (2, 0, 1, 3))
            .reshape(count_rows, QUERY_HEADS * HEAD_SIZE)
            .astype(jnp.bfloat16)
        )
        rest = block_rest(stream, gathered, attn_low)
        kept = (gathered, key_all, value_all, present_inputs, rest)
        saved.append((stream, attended, log_total, kept))
        stream = rest["result"]
    output_low = (stream * live_mine).astype(jnp.bfloat16)
    grad_stream = cotangent.astype(jnp.float32) * live_mine
    layer_grads = [None] * DECODER_LAYERS
    for layer_index in reversed(range(DECODER_LAYERS)):
        stream_in, attended, log_total, kept = saved[layer_index]
        attn_low = (
            jnp.transpose(attended, (2, 0, 1, 3))
            .reshape(count_rows, QUERY_HEADS * HEAD_SIZE)
            .astype(jnp.bfloat16)
        )
        gathered, key_all, value_all, present_inputs, rest = kept
        ffn_grad_low = grad_stream.astype(jnp.bfloat16)
        grad_down = jnp.einsum(
            "tf,td->fd", rest["hidden_low"], ffn_grad_low, preferred_element_type=jnp.float32
        )
        hidden_grad = jnp.einsum(
            "td,fd->tf", ffn_grad_low, gathered[6], preferred_element_type=jnp.float32
        )
        gate_act = rest["gate_act"]
        sigmoid_gate = jax.nn.sigmoid(gate_act)
        gate_grad_low = (
            hidden_grad * rest["upward"] * sigmoid_gate * (1.0 + gate_act * (1.0 - sigmoid_gate))
        ).astype(jnp.bfloat16)
        up_grad_low = (hidden_grad * gate_act * sigmoid_gate).astype(jnp.bfloat16)
        grad_gate = jnp.einsum(
            "td,tf->df", rest["normed_mid_low"], gate_grad_low, preferred_element_type=jnp.float32
        )
        grad_up = jnp.einsum(
            "td,tf->df", rest["normed_mid_low"], up_grad_low, preferred_element_type=jnp.float32
        )
        normed_mid_grad = jnp.einsum(
            "tf,df->td", gate_grad_low, gathered[4], preferred_element_type=jnp.float32
        ) + jnp.einsum("tf,df->td", up_grad_low, gathered[5], preferred_element_type=jnp.float32)
        mid_norm_grad, mlp_gain_term = norm_backward(
            rest["middle"], rest["inv_mid"], gathered[8].astype(jnp.float32), normed_mid_grad
        )
        middle_grad = grad_stream + mid_norm_grad
        attn_grad_low = middle_grad.astype(jnp.bfloat16)
        grad_out = jnp.einsum(
            "tq,td->qd", attn_low, attn_grad_low, preferred_element_type=jnp.float32
        )
        output_gradient_lowered = jnp.einsum(
            "td,qd->tq", attn_grad_low, gathered[3], preferred_element_type=jnp.float32
        ).astype(jnp.bfloat16)
        output_grad_group = output_gradient_lowered.reshape(
            count_rows, KEY_VALUE_HEADS, group_count, HEAD_SIZE
        )
        row_delta = jnp.sum(
            jnp.transpose(output_grad_group.astype(jnp.float32), (1, 2, 0, 3)) * attended, axis=-1
        )
        query_head_group = present_inputs["query_low"].reshape(
            count_rows, KEY_VALUE_HEADS, group_count, HEAD_SIZE
        )
        key_block_size = math.gcd(half_row_set, 512)

        def backward_step(query_acc, block_index):
            row_start = block_index * key_block_size
            key_tile_block = lax.dynamic_slice_in_dim(key_all, row_start, key_block_size)
            value_tile_block = lax.dynamic_slice_in_dim(value_all, row_start, key_block_size)
            allowed = allowed_mask(key_meta, query_meta, base_row + row_start, key_block_size)
            prob_block, dscore_low, key_head_list = score_parts(
                query_head_group,
                output_grad_group,
                key_tile_block,
                value_tile_block,
                allowed,
                log_total,
                row_delta,
                score_scale,
            )
            query_next = (query_acc, jnp.zeros((key_block_size, 2 * key_value_width), jnp.float32))[
                0
            ] + jnp.einsum(
                "hgqk,khd->qhgd", dscore_low, key_head_list, preferred_element_type=jnp.float32
            ) * score_scale
            value_grad = jnp.einsum(
                "hgqk,qhgd->khd",
                prob_block.astype(jnp.bfloat16),
                output_grad_group,
                preferred_element_type=jnp.float32,
            )
            key_grad = (
                jnp.einsum(
                    "hgqk,qhgd->khd",
                    dscore_low,
                    query_head_group,
                    preferred_element_type=jnp.float32,
                )
                * score_scale
            )
            block_rows = jnp.concatenate(
                [
                    key_grad.reshape(key_block_size, key_value_width),
                    value_grad.reshape(key_block_size, key_value_width),
                ],
                axis=-1,
            )
            return (query_next, block_rows)

        query_grad, key_value_rows = lax.scan(
            backward_step,
            jnp.zeros((count_rows, KEY_VALUE_HEADS, group_count, HEAD_SIZE), jnp.float32),
            jnp.arange(half_row_set // key_block_size, dtype=jnp.int32),
        )
        key_value_term = key_value_rows.reshape(half_row_set, 2 * key_value_width)
        key_value_gradient = half_reduce(key_value_term, local_index)
        key_gradient_rows = key_value_gradient[:, :key_value_width].reshape(
            count_rows, KEY_VALUE_HEADS, HEAD_SIZE
        )
        value_grad_low = key_value_gradient[:, key_value_width:].astype(jnp.bfloat16)
        query_pre, query_gain_term = norm_backward(
            present_inputs["query_heads"],
            present_inputs["inv_query"],
            gathered[9].astype(jnp.float32),
            unrotate(
                query_grad.reshape(count_rows, QUERY_HEADS, HEAD_SIZE), cosine_table, sine_table
            ),
        )
        key_pre, key_gain_term = norm_backward(
            present_inputs["key_heads"],
            present_inputs["inv_key"],
            gathered[10].astype(jnp.float32),
            unrotate(key_gradient_rows, cosine_table, sine_table),
        )
        query_grad_low = query_pre.reshape(count_rows, QUERY_HEADS * HEAD_SIZE).astype(jnp.bfloat16)
        key_grad_low = key_pre.reshape(count_rows, key_value_width).astype(jnp.bfloat16)
        normed_low = present_inputs["normed_low"]
        grad_query = jnp.einsum(
            "td,tq->dq", normed_low, query_grad_low, preferred_element_type=jnp.float32
        )
        grad_key = jnp.einsum(
            "td,tq->dq", normed_low, key_grad_low, preferred_element_type=jnp.float32
        )
        grad_value = jnp.einsum(
            "td,tq->dq", normed_low, value_grad_low, preferred_element_type=jnp.float32
        )
        normed_grad = jnp.einsum(
            "tq,dq->td", query_grad_low, gathered[0], preferred_element_type=jnp.float32
        )
        normed_grad = normed_grad + jnp.einsum(
            "tq,dq->td", key_grad_low, gathered[1], preferred_element_type=jnp.float32
        )
        normed_grad = normed_grad + jnp.einsum(
            "tq,dq->td", value_grad_low, gathered[2], preferred_element_type=jnp.float32
        )
        in_norm_grad, attn_gain_term = norm_backward(
            stream_in, present_inputs["inv_attn"], gathered[7].astype(jnp.float32), normed_grad
        )
        grad_stream = middle_grad + in_norm_grad
        layer_grads[layer_index] = (
            lax.psum_scatter(grad_query, ("ctx", "fsdp"), scatter_dimension=0, tiled=True),
            lax.psum_scatter(grad_key, ("ctx", "fsdp"), scatter_dimension=0, tiled=True),
            lax.psum_scatter(grad_value, ("ctx", "fsdp"), scatter_dimension=0, tiled=True),
            lax.psum_scatter(grad_out, ("ctx", "fsdp"), scatter_dimension=0, tiled=True),
            lax.psum_scatter(grad_gate, ("ctx", "fsdp"), scatter_dimension=0, tiled=True),
            lax.psum_scatter(grad_up, ("ctx", "fsdp"), scatter_dimension=0, tiled=True),
            lax.psum_scatter(grad_down, ("ctx", "fsdp"), scatter_dimension=0, tiled=True),
            lax.psum_scatter(attn_gain_term, ("ctx", "fsdp"), scatter_dimension=0, tiled=True),
            lax.psum_scatter(mlp_gain_term, ("ctx", "fsdp"), scatter_dimension=0, tiled=True),
            lax.psum_scatter(query_gain_term, ("ctx", "fsdp"), scatter_dimension=0, tiled=True),
            lax.psum_scatter(key_gain_term, ("ctx", "fsdp"), scatter_dimension=0, tiled=True),
        )
    stacked = tuple(
        (jnp.stack([layer_sums[member] for layer_sums in layer_grads]) for member in range(11))
    )
    return (output_low, grad_stream) + stacked


def act_rows(values):
    return values.T.reshape(4, 2, 2, 2, -1, 32, values.shape[0])


def product(left, right):
    return jnp.dot(left, right, preferred_element_type=jnp.float32)


def product_turned(left, right):
    return lax.dot_general(left, right, NT, preferred_element_type=jnp.float32)


def fast_device(
    tokens,
    cotangent,
    lengths,
    stretch_ids,
    w_query,
    key_projection_weight,
    value_projection_weight,
    w_out,
    w_gate,
    w_up,
    w_down,
    g_attn,
    g_mlp,
    g_query,
    g_key,
):
    count_rows, width = tokens.shape
    ctx_index = lax.axis_index("ctx")
    places, slot_ids, live = token_places(stretch_ids[:, 0, :], lengths[0])
    group_rows = PEERS * count_rows
    base_row = ctx_index // PEERS * group_rows
    my_row = ctx_index * count_rows
    slot_places = lax.dynamic_slice_in_dim(places, base_row, group_rows)
    limit = lax.dynamic_slice_in_dim(lengths[0], ctx_index // PEERS, 1)
    caps = jnp.minimum(slot_places, limit - 1).reshape(PEERS, 1, count_rows)
    query_cap = jnp.concatenate([caps, caps], axis=2)
    key_place = slot_places[:, None]
    live_mine = lax.dynamic_slice_in_dim(live, my_row, count_rows).astype(jnp.float32)[:, None]
    cosine, sine = rotary_tables(lax.dynamic_slice_in_dim(places, my_row, count_rows))
    half = HEAD_SIZE // 2
    sine = jnp.concatenate([-sine[:, :half], sine[:, half:]], axis=1)

    packed = jnp.concatenate([member.reshape(-1) for member in (g_attn, g_mlp, g_query, g_key)])
    packed = jnp.pad(packed, (0, 4096 - packed.shape[0])).reshape(32, 128)
    gathered = gather_weights(
        (w_query, key_projection_weight, value_projection_weight, w_out, w_gate, w_up, w_down),
        packed,
        tuple(range(DECODER_LAYERS)),
        1,
    )
    flat = gathered[-1].reshape(2, -1).astype(jnp.float32)
    gains = []
    offset = 0
    for member in (g_attn, g_mlp, g_query, g_key):
        span = member.shape[1]
        sides = flat[:, offset : offset + DECODER_LAYERS * span].reshape(2, DECODER_LAYERS, span)
        gains.append(sides.transpose(1, 0, 2).reshape(DECODER_LAYERS, 2 * span))
        offset += DECODER_LAYERS * span

    stream = tokens.astype(jnp.float32)
    saved = []
    for layer in range(DECODER_LAYERS):
        into, out_weight, wide_weight, down = gathered[4 * layer : 4 * layer + 4]
        head_gains = jnp.concatenate([gains[2][layer : layer + 1], gains[3][layer : layer + 1]], 0)
        normed, inv_attn = norm_forward(stream, gains[0][layer])
        normed_low = normed.astype(jnp.bfloat16)
        pre = product(normed_low, into)
        attn_low, kept, kept_out, kept_log = attend(
            pre, cosine, sine, head_gains, key_place, query_cap, 2 + layer
        )
        middle = stream + product(attn_low, out_weight)
        normed_mid, inv_mid = norm_forward(middle, gains[1][layer])
        mid_low = normed_mid.astype(jnp.bfloat16)
        both = product(mid_low, wide_weight)
        ff = both.shape[1] // 2
        gate, up = both[:, :ff], both[:, ff:]
        hidden_low = (jax.nn.silu(gate) * up).astype(jnp.bfloat16)
        saved.append(
            (stream, inv_attn, normed_low, pre, attn_low, kept, kept_out, kept_log,
             middle, inv_mid, mid_low, gate, up, hidden_low, head_gains)
        )
        stream = middle + product(hidden_low, down)
    output_low = (stream * live_mine).astype(jnp.bfloat16)

    grad_stream = cotangent.astype(jnp.float32) * live_mine
    reduce_acts, reduce_grads, terms = [], [], [None] * DECODER_LAYERS
    place = ctx_index * 2 + lax.axis_index("fsdp")
    for layer in reversed(range(DECODER_LAYERS)):
        into, out_weight, wide_weight, down = gathered[4 * layer : 4 * layer + 4]
        (stream_in, inv_attn, normed_low, pre, attn_low, kept, kept_out, kept_log,
         middle, inv_mid, mid_low, gate, up, hidden_low, head_gains) = saved[layer]
        down_low = grad_stream.astype(jnp.bfloat16)
        hidden_grad = product_turned(down_low, down)
        sigmoid_gate = jax.nn.sigmoid(gate)
        gate_low = (hidden_grad * up * sigmoid_gate * (1.0 + gate * (1.0 - sigmoid_gate))).astype(
            jnp.bfloat16
        )
        up_low = (hidden_grad * gate * sigmoid_gate).astype(jnp.bfloat16)
        both_low = jnp.concatenate([gate_low, up_low], axis=1)
        mid_grad = product_turned(both_low, wide_weight)
        mid_norm_grad, mlp_term = norm_backward(middle, inv_mid, gains[1][layer], mid_grad)
        middle_grad = grad_stream + mid_norm_grad
        out_low = middle_grad.astype(jnp.bfloat16)
        attn_grad = product_turned(out_low, out_weight).astype(jnp.bfloat16)
        pre_grad, head_terms = attend_back(
            attn_grad, kept, kept_out, kept_log, pre, cosine, sine, head_gains,
            key_place, query_cap, 2 + DECODER_LAYERS + layer,
        )
        normed_grad = product_turned(pre_grad, into)
        in_norm_grad, attn_term = norm_backward(stream_in, inv_attn, gains[0][layer], normed_grad)
        grad_stream = middle_grad + in_norm_grad
        terms[layer] = jnp.concatenate(
            [attn_term.reshape(-1, 128), mlp_term.reshape(-1, 128), head_terms], axis=0
        )
        reduce_acts += [act_rows(member) for member in (hidden_low, mid_low, attn_low, normed_low)]
        reduce_grads += [down_low, both_low, out_low, pre_grad]
    *weight_sums, sums, unused = reduce_layers(
        reduce_acts,
        reduce_grads,
        jnp.concatenate(terms, axis=0),
        tuple(reversed(range(DECODER_LAYERS))),
        2 + 2 * DECODER_LAYERS,
    )
    sums = sums.reshape(DECODER_LAYERS, -1)

    def share(first, span):
        return lax.dynamic_slice_in_dim(sums, first + place * span, span, axis=1)

    return (output_low, grad_stream) + tuple(weight_sums) + (
        share(0, 32), share(1024, 32), share(2048, 4), share(2176, 4)
    )


def solution(mesh):
    plain = mesh.shape["ctx"] == 2 * KEY_VALUE_HEADS and mesh.shape["fsdp"] == 2
    device = fast_device if plain else general_device
    in_specs = (
        P(("ctx", "fsdp"), None),
        P(("ctx", "fsdp"), None),
        P("fsdp", None),
        P(None, "fsdp", None),
        P(None, "fsdp", None),
        P(None, "fsdp", None),
        P(None, "fsdp", None),
        P(None, "fsdp", None),
        P(None, "fsdp", None),
        P(None, "fsdp", None),
        P(None, "fsdp", None),
        P(None, "fsdp"),
        P(None, "fsdp"),
        P(None, "fsdp"),
        P(None, "fsdp"),
    )
    out_specs = (
        P(("ctx", "fsdp"), None),
        P(("ctx", "fsdp"), None),
        P(None, ("ctx", "fsdp"), None),
        P(None, ("ctx", "fsdp"), None),
        P(None, ("ctx", "fsdp"), None),
        P(None, ("ctx", "fsdp"), None),
        P(None, ("ctx", "fsdp"), None),
        P(None, ("ctx", "fsdp"), None),
        P(None, ("ctx", "fsdp"), None),
        P(None, ("ctx", "fsdp")),
        P(None, ("ctx", "fsdp")),
        P(None, ("ctx", "fsdp")),
        P(None, ("ctx", "fsdp")),
    )
    return jax.shard_map(
        device, mesh=mesh, in_specs=in_specs, out_specs=out_specs, check_vma=False
    )
```

```python
import functools
import math

import jax
import jax.numpy as jnp
from jax import lax
from jax.experimental import pallas as pl
from jax.experimental.pallas import tpu as pltpu
from jax.sharding import PartitionSpec as P

QUERY_HEADS = 16
KEY_VALUE_HEADS = 8
HEAD_SIZE = 128
DECODER_LAYERS = 2
STRETCH = 64


norm_epsilon = 1e-06
rope_base = 1000000.0
masked_logits = -1e30

MESH = pl.DeviceIdType.MESH


TILES = 15
GRADS = 12
ACTS = 7
AHEAD = 2
SLOTS = 8
ACT_SPANS = ((0, 3), (3, 1), (4, 2), (6, 1))


def grad_index(t):
    return jnp.where(t < 3, 0, jnp.where(t < 9, t - 2, jnp.where(t < 11, 7, t - 3)))


def act_index(t):
    return jnp.where(t < 3, t, jnp.where(t < 9, 3, jnp.where(t < 11, t - 5, 6)))


def is_new(t):
    return (t == 0) | ((t >= 3) & (t < 10)) | (t >= 11)


def make_remote(src, dst, s, r, dev):
    return pltpu.make_async_remote_copy(
        src_ref=src, dst_ref=dst, send_sem=s, recv_sem=r, device_id=dev, device_id_type=MESH
    )


class Reducer:
    def __init__(self, acts, grads, results, scratch, layers):
        self.acts, self.grads, self.results, self.layers = acts, grads, results, layers
        self.count = len(layers)
        (self.gheld, self.abuf, self.afwd, self.gtile, self.ysend, self.yrecv, self.own,
         self.zsend, self.zrecv, self.zown,
         self.a_local, self.a_xs, self.a_xr, self.a_cs, self.a_cr,
         self.g_local, self.g_xs, self.g_xr, self.g_cs, self.g_cr, self.g_fs, self.g_fr,
         self.y_s, self.y_r, self.z_s, self.z_r) = scratch
        c = lax.axis_index("ctx")
        x = lax.axis_index("fsdp")
        self.c, self.x = c, x
        self.core = c % 2
        self.y = c // 2 % 2
        self.z = c // 4
        self.sibling = (c + 1 - 2 * self.core, x)
        self.across = (c, 1 - x)
        self.aside = (c + 2 - 4 * self.y, x)

    def along(self, o):
        return ((self.z + o) % 4 * 4 + self.c % 4, self.x)

    def partners(self):
        return (self.sibling, self.across, self.aside) + tuple(self.along(o) for o in (1, 2, 3))

    def act(self, n, k, what):
        first, blocks = ACT_SPANS[k]
        src = self.acts[n][k]
        span = pl.ds(first, blocks)
        x, core = self.x, self.core

        def held(place):
            return self.abuf.at[n, :, :, span, :, pl.ds(128 * place, 128)]

        if what == "local":
            return pltpu.make_async_copy(
                src.at[:, :, core, x], held(0), self.a_local.at[n, k]
            )
        if what == "across":
            return make_remote(
                src.at[:, :, core, 1 - x], held(1), self.a_xs.at[n, k, 0], self.a_xr.at[n, k, 0],
                self.across,
            )
        if what == "relay":
            return make_remote(
                src.at[:, :, 1 - core, 1 - x], self.afwd.at[n, :, :, span],
                self.a_xs.at[n, k, 1], self.a_xr.at[n, k, 1], self.across,
            )
        if what == "sibling":
            return make_remote(
                src.at[:, :, 1 - core, x], held(2), self.a_cs.at[n, k, 0], self.a_cr.at[n, k, 0],
                self.sibling,
            )
        return make_remote(
            self.afwd.at[n, :, :, span], held(3), self.a_cs.at[n, k, 1], self.a_cr.at[n, k, 1],
            self.sibling,
        )

    def start_acts(self, n, ks):
        for what in ("across", "relay", "sibling", "local"):
            for k in ks:
                self.act(n, k, what).start()

    def forward_acts(self, n, ks):
        for k in ks:
            self.act(n, k, "relay").wait_recv()
            self.act(n, k, "forward").start()

    def await_acts(self, n, ks):
        for k in ks:
            self.act(n, k, "local").wait()
            for what in ("across", "sibling", "forward"):
                self.act(n, k, what).wait_recv()

    def grad_across(self, i, src=None):
        rows = self.gheld.at[i, pl.ds(0, 128)]
        return make_remote(
            rows if src is None else src, rows, self.g_xs.at[i], self.g_xr.at[i], self.across
        )

    def grad_sibling(self, i, src=None):
        rows = self.gheld.at[i, pl.ds(128, 128)]
        return make_remote(
            rows if src is None else src, rows, self.g_cs.at[i], self.g_cr.at[i], self.sibling
        )

    def grad_forward(self, i):
        return make_remote(
            self.gheld.at[i, pl.ds(0, 128)], self.gheld.at[i, pl.ds(256, 128)],
            self.g_fs.at[i], self.g_fr.at[i], self.sibling,
        )

    def grad_own(self, i, src=None):
        rows = self.gtile.at[i % 2, pl.ds(0, 128)]
        return pltpu.make_async_copy(rows if src is None else src, rows, self.g_local.at[i % 2, 0])

    def grad_load(self, i):
        return pltpu.make_async_copy(
            self.gheld.at[i], self.gtile.at[i % 2, pl.ds(128, 384)], self.g_local.at[i % 2, 1]
        )

    def with_source(self, i, act):
        n = i // GRADS
        g = i % GRADS
        first = 0
        for ref, blocks in self.grads:

            @pl.when((g >= first) & (g < first + blocks))
            def use(ref=ref, first=first):
                act(ref.at[n, :, pl.ds(pl.multiple_of((g - first) * 1024, 1024), 1024)])

            first += blocks

    def start_grad(self, i):
        def go(src):
            self.grad_across(i, src).start()
            self.grad_sibling(i, src).start()

        self.with_source(i, go)

    def y_copy(self, t):
        return make_remote(
            self.ysend.at[t % SLOTS], self.yrecv.at[t], self.y_s.at[t], self.y_r.at[t], self.aside
        )

    def z_copy(self, t, o):
        return make_remote(
            self.zsend.at[t % SLOTS, o - 1], self.zrecv.at[t, 3 - o], self.z_s.at[t, o - 1],
            self.z_r.at[t, 3 - o], self.along(o),
        )

    def begin(self):
        self.start_acts(0, (0,))
        self.start_grad(0)
        self.start_acts(0, (1, 2, 3))

    def begin_more(self):
        for i in range(1, AHEAD):
            self.start_grad(i)

    def store(self, t, total):
        n = t // TILES
        tile = t % TILES
        query, key, value, out, gate, up, down = self.results
        by_rows = ((0, 3, down), (9, 2, out))
        by_columns = ((3, 3, gate), (6, 3, up), (11, 2, query), (13, 1, key), (14, 1, value))
        if self.count == 1:
            layer = self.layers[0]
        else:
            layer = jnp.where(n == 0, self.layers[0], self.layers[1])
        for first, blocks, ref in by_rows:

            @pl.when((tile >= first) & (tile < first + blocks))
            def rows(first=first, ref=ref):
                ref[layer, pl.ds(pl.multiple_of((tile - first) * 32, 32), 32), :] = total

        for first, blocks, ref in by_columns:

            @pl.when((tile >= first) & (tile < first + blocks))
            def columns(first=first, ref=ref):
                ref[layer, :, pl.ds(pl.multiple_of((tile - first) * 1024, 1024), 1024)] = total

    def step(self, s):
        tiles = TILES * self.count
        t = s - 6

        @pl.when((t >= 0) & (t < tiles))
        def finish():
            total = self.zown[t % 4]
            for o in (1, 2, 3):
                self.z_copy(t, o).wait_recv()
            for o in range(3):
                total += self.zrecv[t, o].astype(jnp.float32)
            self.store(t, total)

        u = s - 4

        @pl.when((u >= 0) & (u < tiles))
        def spread():
            self.y_copy(u).wait_recv()

            def part(index):
                rows = pl.ds(pl.multiple_of(index * 32, 32), 32)
                return self.own[u % 4, rows, :] + self.yrecv[u, rows, :].astype(jnp.float32)

            @pl.when(u >= SLOTS)
            def settle():
                for o in (1, 2, 3):
                    self.z_copy(u - SLOTS, o).wait_send()

            for o in (2, 1, 3):
                self.zsend[u % SLOTS, o - 1] = part((self.z + o) % 4).astype(jnp.bfloat16)
                self.z_copy(u, o).start()
            self.zown[u % 4] = part(self.z)

        v = s - 2

        @pl.when((v >= 0) & (v < tiles))
        def compute():
            n = v // TILES
            tile = v % TILES
            gi = n * GRADS + grad_index(tile)
            ai = act_index(tile)
            for layer in range(self.count):

                @pl.when(v == TILES * layer)
                def first_acts(layer=layer):
                    self.await_acts(layer, (0,))

                @pl.when(v == TILES * layer + 3)
                def second_acts(layer=layer):
                    self.await_acts(layer, (1, 2, 3))

            @pl.when(is_new(tile))
            def fresh():
                self.grad_own(gi).wait()
                self.grad_load(gi).wait()

            @pl.when(v >= SLOTS)
            def settle():
                self.y_copy(v - SLOTS).wait_send()

            left = jnp.concatenate(
                [
                    self.abuf[n, :, 1 - self.y, ai].reshape(128, 512),
                    self.abuf[n, :, self.y, ai].reshape(128, 512),
                ],
                axis=0,
            )
            for part in range(4):
                cols = pl.ds(part * 256, 256)
                result = jnp.dot(left, self.gtile[gi % 2, :, cols], preferred_element_type=jnp.float32)
                self.ysend[v % SLOTS, :, cols] = result[:128].astype(jnp.bfloat16)
                self.own[v % 4, :, cols] = result[128:]
            self.y_copy(v).start()

        w = s - 1

        @pl.when((w >= 0) & (w < tiles) & is_new(w % TILES))
        def collect():
            gi = w // TILES * GRADS + grad_index(w % TILES)
            self.with_source(gi, lambda src: self.grad_own(gi, src).start())
            self.grad_sibling(gi).wait_recv()
            self.grad_forward(gi).wait_recv()
            self.grad_load(gi).start()

        @pl.when((s >= 0) & (s < tiles) & is_new(s % TILES))
        def forward():
            i = s // TILES * GRADS + grad_index(s % TILES)
            for layer in range(self.count):

                @pl.when(s == TILES * layer)
                def first_forward(layer=layer):
                    self.forward_acts(layer, (0,))

                @pl.when(s == TILES * layer + 3)
                def second_forward(layer=layer):
                    self.forward_acts(layer, (1, 2, 3))

            self.grad_across(i).wait_recv()
            self.grad_forward(i).start()
            for layer in range(1, self.count):

                @pl.when(i == GRADS * layer - AHEAD)
                def next_acts(layer=layer):
                    self.start_acts(layer, (0,))

                @pl.when(i == GRADS * layer - AHEAD + 1)
                def other_acts(layer=layer):
                    self.start_acts(layer, (1, 2, 3))

            @pl.when(i + AHEAD < GRADS * self.count)
            def more():
                self.start_grad(i + AHEAD)

    def steps(self):
        return TILES * self.count + 6

    def drain(self):
        for n in range(self.count):
            for k in range(4):
                for what in ("across", "relay", "sibling", "forward"):
                    self.act(n, k, what).wait_send()

        def drain_grads(i, carry):
            self.grad_across(i).wait_send()
            self.grad_sibling(i).wait_send()
            self.grad_forward(i).wait_send()
            return carry

        lax.fori_loop(0, GRADS * self.count, drain_grads, 0)

        def drain_tiles(t, carry):
            self.y_copy(t).wait_send()
            for o in (1, 2, 3):
                self.z_copy(t, o).wait_send()
            return carry

        lax.fori_loop(TILES * self.count - SLOTS, TILES * self.count, drain_tiles, 0)


class GainSum:
    def __init__(self, reducer, source, out, scratch):
        self.reducer, self.source, self.out = reducer, source, out
        self.part, self.recv, self.s, self.r = scratch

    def hop(self, i):
        red = self.reducer
        return make_remote(
            self.source if i == 0 else self.part.at[i - 1], self.recv.at[i], self.s.at[i],
            self.r.at[i], (red.across, red.sibling, red.aside)[i],
        )

    def along(self, o):
        return make_remote(
            self.part.at[2], self.recv.at[6 - o], self.s.at[2 + o], self.r.at[6 - o],
            self.reducer.along(o),
        )

    def step(self, s, first):
        @pl.when(s == first)
        def begin():
            self.hop(0).start()

        for i in range(3):

            @pl.when(s == first + 1 + i)
            def stage(i=i):
                self.hop(i).wait_recv()
                self.part[i] = (self.source[...] if i == 0 else self.part[i - 1]) + self.recv[i]
                if i < 2:
                    self.hop(i + 1).start()
                else:
                    for o in (1, 2, 3):
                        self.along(o).start()

        @pl.when(s == first + 5)
        def total():
            for o in (1, 2, 3):
                self.along(o).wait_recv()
            self.out[...] = self.part[2] + self.recv[3] + self.recv[4] + self.recv[5]

    def drain(self):
        for i in range(3):
            self.hop(i).wait_send()
            self.along(i + 1).wait_send()


def reduce_scratch(count):
    dma = pltpu.SemaphoreType.DMA
    low, wide = jnp.bfloat16, jnp.float32
    tiles, grads = TILES * count, GRADS * count
    return [
        pltpu.VMEM((count, 4, 2, ACTS, 32, 512), low),
        pltpu.VMEM((count, 4, 2, ACTS, 32, 128), low),
        pltpu.VMEM((2, 512, 1024), low),
        pltpu.VMEM((SLOTS, 128, 1024), low),
        pltpu.VMEM((tiles, 128, 1024), low),
        pltpu.VMEM((4, 128, 1024), wide),
        pltpu.VMEM((SLOTS, 3, 32, 1024), low),
        pltpu.VMEM((tiles, 3, 32, 1024), low),
        pltpu.VMEM((4, 32, 1024), wide),
        dma((count, 4)), dma((count, 4, 2)), dma((count, 4, 2)), dma((count, 4, 2)),
        dma((count, 4, 2)),
        dma((2, 2)), dma((grads,)), dma((grads,)), dma((grads,)), dma((grads,)), dma((grads,)),
        dma((grads,)),
        dma((tiles,)), dma((tiles,)), dma((tiles, 3)), dma((tiles, 3)),
    ]


def gain_scratch(rows):
    dma = pltpu.SemaphoreType.DMA
    return [
        pltpu.VMEM((3, rows, 128), jnp.float32),
        pltpu.VMEM((6, rows, 128), jnp.float32),
        dma((6,)),
        dma((6,)),
    ]


RESULTS = ((32, 2048), (32, 1024), (32, 1024), (64, 1024), (32, 3072), (32, 3072), (96, 1024))


GATHER_PLAN = ((0, 0, 0), (1, 0, 2048), (2, 0, 3072), (3, 1, 0), (4, 2, 0), (5, 2, 3072), (6, 3, 0))
MEMBERS = 7


def gather_kernel(layers, *refs):
    sources = refs[:MEMBERS]
    gains = refs[MEMBERS]
    outs = refs[MEMBERS + 1 : MEMBERS + 5]
    gains_out = refs[MEMBERS + 5]
    (l_sem, l_rec, x_s, x_r, y_s, y_r, z_s, z_r, yd_s, yd_r, zd_s, zd_r, c_s, c_r, g_sem) = refs[
        MEMBERS + 6 :
    ]
    c = lax.axis_index("ctx")
    x = lax.axis_index("fsdp")
    core = c % 2
    y = c // 2 % 2
    near = c // 4 % 2
    sibling = (c + 1 - 2 * core, x)
    across = (c, 1 - x)
    aside = (c + 2 - 4 * y, x)
    along = (c + 4 - 8 * near, x)

    barrier = pltpu.get_barrier_semaphore()
    for other in (sibling, across, aside, along):
        pl.semaphore_signal(barrier, inc=1, device_id=other, device_id_type=MESH)
    pl.semaphore_wait(barrier, 4)

    def remote(src, dst, s, r, dev):
        return pltpu.make_async_remote_copy(
            src_ref=src, dst_ref=dst, send_sem=s, recv_sem=r, device_id=dev, device_id_type=MESH
        )

    here = near * 2 + y
    by_y = near * 2 + 1 - y
    by_z = (1 - near) * 2 + y
    corner = (1 - near) * 2 + 1 - y
    steps = [(n, m) for n in range(len(layers)) for m in range(MEMBERS)]
    count = len(steps)

    def geometry(i):
        n, m = steps[i]
        source, target, column = GATHER_PLAN[m]
        half = sources[source].shape[1]
        part = half // 8
        width = sources[source].shape[2]
        return n, sources[source], outs[target].at[n], half, part, width, column

    def window(i, owner_x, owner_core, piece, share=None):
        n, src, out, half, part, width, column = geometry(i)
        start = owner_x * half + (piece * 2 + owner_core) * part
        rows = part
        if share is not None:
            rows = part // 2
            start = start + share * rows
        return out.at[pl.ds(pl.multiple_of(start, 16), rows), pl.ds(column, width)]

    def local(i):
        n, src, out, half, part, width, column = geometry(i)
        rows = pl.ds(pl.multiple_of(x * half, 16), half)
        return remote(
            src.at[layers[n]], out.at[rows, pl.ds(column, width)], l_sem.at[i], l_rec.at[i], sibling
        )

    def x_copy(i):
        n, src, out, half, part, width, column = geometry(i)
        rows = pl.ds(pl.multiple_of((here * 2 + core) * part, 16), part)
        return remote(
            src.at[layers[n], rows], window(i, x, core, here), x_s.at[i], x_r.at[i], across
        )

    def same(i, piece, s, r, dev, share=None):
        view = window(i, 1 - x, core, piece, share)
        return remote(view, view, s, r, dev)

    def y_copy(i):
        return same(i, here, y_s.at[i], y_r.at[i], aside)

    def z_copy(i):
        return same(i, here, z_s.at[i], z_r.at[i], along)

    def y_corner(i):
        return same(i, by_z, yd_s.at[i], yd_r.at[i], aside, 1)

    def z_corner(i):
        return same(i, by_y, zd_s.at[i], zd_r.at[i], along, 0)

    def core_copy(i, which):
        piece = (here, by_y, by_z, corner)[which]
        return same(i, piece, c_s.at[i, which], c_r.at[i, which], sibling)

    gain_local = pltpu.make_async_copy(gains, gains_out.at[x], g_sem.at[0])
    gain_remote = remote(gains, gains_out.at[x], g_sem.at[1], g_sem.at[2], across)
    gain_local.start()
    gain_remote.start()

    ahead = 3
    for i in range(min(ahead, count)):
        x_copy(i).start()
        local(i).start()
    for s in range(count + 3):
        if s < count:
            x_copy(s).wait_recv()
            y_copy(s).start()
            z_copy(s).start()
            core_copy(s, 0).start()
            if s + ahead < count:
                x_copy(s + ahead).start()
                local(s + ahead).start()
        i = s - 1
        if 0 <= i < count:
            y_copy(i).wait_recv()
            z_corner(i).start()
            core_copy(i, 1).start()
            z_copy(i).wait_recv()
            y_corner(i).start()
            core_copy(i, 2).start()
        i = s - 3
        if 0 <= i < count:
            y_corner(i).wait_recv()
            z_corner(i).wait_recv()
            core_copy(i, 3).start()
    gain_local.wait()
    gain_remote.wait()
    for i in range(count):
        local(i).wait()
        for copy in (x_copy(i), y_copy(i), z_copy(i), y_corner(i), z_corner(i)):
            copy.wait_send()
        for which in range(4):
            core_copy(i, which).wait()


def gather_weights(weights, gains, layers, collective_id):
    dma = pltpu.SemaphoreType.DMA
    count = MEMBERS * len(layers)
    low = jnp.bfloat16
    shapes = [(1024, 4096), (2048, 1024), (1024, 6144), (3072, 1024)]
    return pl.pallas_call(
        functools.partial(gather_kernel, layers),
        out_shape=[jax.ShapeDtypeStruct((len(layers),) + s, low) for s in shapes]
        + [jax.ShapeDtypeStruct((2,) + gains.shape, low)],
        in_specs=[pl.BlockSpec(memory_space=pl.ANY)] * (MEMBERS + 1),
        out_specs=[pl.BlockSpec(memory_space=pl.ANY)] * (len(shapes) + 1),
        scratch_shapes=[dma((count,))] * 12 + [dma((count, 4))] * 2 + [dma((3,))],
        compiler_params=pltpu.CompilerParams(collective_id=collective_id, has_side_effects=True),
        name="weight_gather",
    )(*weights, gains)


PEERS = KEY_VALUE_HEADS
SCALE = HEAD_SIZE ** (-0.5)
NT = (((1,), (1,)), ((), ()))


def peer_tools():
    c = lax.axis_index("ctx")
    x = lax.axis_index("fsdp")
    me = c % PEERS

    def peer(r):
        return (c - me + r, x)

    def remote(src, dst, s, r, dev):
        return pltpu.make_async_remote_copy(
            src_ref=src, dst_ref=dst, send_sem=s, recv_sem=r, device_id=dev, device_id_type=MESH
        )

    barrier = pltpu.get_barrier_semaphore()

    def greet(o, carry):
        pl.semaphore_signal(
            barrier, inc=1, device_id=peer((me + o) % PEERS), device_id_type=MESH
        )
        return carry

    lax.fori_loop(1, PEERS, greet, 0)
    return me, peer, remote, barrier


def head_columns(first, index):
    return pl.ds(pl.multiple_of(first + index * HEAD_SIZE, HEAD_SIZE), HEAD_SIZE)


def attend_kernel(
    pre, cosine, sine, gains, key_place, query_cap, out, kept, kept_out, kept_log,
    send, osend, orecv, vt, q_s, q_r, k_s, k_r, o_s, o_r,
):
    me, peer, remote, barrier = peer_tools()
    cos = cosine[...]
    sin = sine[...]

    def turned(first, index, gain):
        v = pre[:, head_columns(first, index)]
        r = lax.rsqrt(jnp.mean(v * v, axis=-1, keepdims=True) + norm_epsilon)
        n = v * r * gain
        return (n * cos + pltpu.roll(n, HEAD_SIZE // 2, 1) * sin).astype(jnp.bfloat16)

    def key_copy(r, slot):
        return remote(
            send.at[r, pl.ds(2, 2)], kept.at[slot, pl.ds(2, 2)], k_s.at[r], k_r.at[slot], peer(r)
        )

    def query_copy(r, slot):
        return remote(
            send.at[r, pl.ds(0, 2)], kept.at[slot, pl.ds(0, 2)], q_s.at[r], q_r.at[slot], peer(r)
        )

    def out_copy(r, slot):
        return remote(osend.at[r], orecv.at[slot], o_s.at[r], o_r.at[slot], peer(r))

    def make_keys(o, carry):
        r = (me + o) % PEERS
        key = turned(2048, r, gains[1:2, :])
        value = pre[:, head_columns(3072, r)].astype(jnp.bfloat16)

        @pl.when(o < PEERS)
        def away():
            send[r, 2] = key
            send[r, 3] = value

        @pl.when(o == PEERS)
        def home():
            kept[me, 2] = key
            kept[me, 3] = value

        @pl.when(o == 1)
        def entered():
            pl.semaphore_wait(barrier, PEERS - 1)

        @pl.when(o < PEERS)
        def push():
            key_copy(r, me).start()

        return carry

    def make_queries(o, carry):
        r = (me + o) % PEERS
        first = turned(0, 2 * r, gains[0:1, :])
        second = turned(0, 2 * r + 1, gains[0:1, :])

        @pl.when(o < PEERS)
        def away():
            send[r, 0] = first
            send[r, 1] = second
            query_copy(r, me).start()

        @pl.when(o == PEERS)
        def home():
            kept[me, 0] = first
            kept[me, 1] = second

        return carry

    lax.fori_loop(1, PEERS + 1, make_keys, 0)
    lax.fori_loop(1, PEERS + 1, make_queries, 0)

    def await_keys(o, carry):
        key_copy(me, (me + o) % PEERS).wait_recv()
        return carry

    lax.fori_loop(1, PEERS, await_keys, 0)

    def turn_values(j, carry):
        vt[j] = kept[j, 3].astype(jnp.float32).T.astype(jnp.bfloat16)
        return carry

    lax.fori_loop(0, PEERS, turn_values, 0)

    def block(o, carry):
        j = (me + o) % PEERS

        @pl.when(o > 0)
        def arrived():
            query_copy(me, j).wait_recv()

        queries = kept[j, 0:2].reshape(2 * 128, HEAD_SIZE)
        keys = kept[:, 2].reshape(PEERS * 128, HEAD_SIZE)
        scores = lax.dot_general(keys, queries, NT, preferred_element_type=jnp.float32) * SCALE
        allowed = key_place[...] <= query_cap[j]
        scores = jnp.where(allowed, scores, masked_logits)
        highest = jnp.max(scores, axis=0, keepdims=True)
        expo = jnp.exp(scores - highest)
        total = jnp.sum(expo, axis=0, keepdims=True)
        low = expo.astype(jnp.bfloat16)
        turned_out = jnp.zeros((HEAD_SIZE, 256), jnp.float32)
        for i in range(PEERS):
            turned_out += jnp.dot(
                vt[i], low[i * 128 : (i + 1) * 128], preferred_element_type=jnp.float32
            )
        turned_out = turned_out / total
        kept_out[j] = turned_out
        kept_log[j] = jnp.broadcast_to(highest + jnp.log(total), (8, 256))
        attended = turned_out.T.astype(jnp.bfloat16).reshape(2, 128, HEAD_SIZE)

        @pl.when(o == 0)
        def home():
            orecv[me] = attended

        @pl.when(o > 0)
        def away():
            osend[j] = attended
            out_copy(j, me).start()

        return carry

    lax.fori_loop(0, PEERS, block, 0)

    def collect(o, carry):
        h = (me + o) % PEERS

        @pl.when(o > 0)
        def arrived():
            out_copy(me, h).wait_recv()

        out[:, head_columns(0, 2 * h)] = orecv[h, 0]
        out[:, head_columns(0, 2 * h + 1)] = orecv[h, 1]
        return carry

    lax.fori_loop(0, PEERS, collect, 0)

    def drain(o, carry):
        r = (me + o) % PEERS
        key_copy(r, me).wait_send()
        query_copy(r, me).wait_send()
        out_copy(r, me).wait_send()
        return carry

    lax.fori_loop(1, PEERS, drain, 0)


def attend(pre, cosine, sine, gains, key_place, query_cap, collective_id):
    dma = pltpu.SemaphoreType.DMA
    low, wide = jnp.bfloat16, jnp.float32
    return pl.pallas_call(
        attend_kernel,
        out_shape=[
            jax.ShapeDtypeStruct((128, 2048), low),
            jax.ShapeDtypeStruct((PEERS, 4, 128, HEAD_SIZE), low),
            jax.ShapeDtypeStruct((PEERS, HEAD_SIZE, 256), wide),
            jax.ShapeDtypeStruct((PEERS, 8, 256), wide),
        ],
        in_specs=[pl.BlockSpec(memory_space=pltpu.VMEM)] * 6,
        out_specs=[pl.BlockSpec(memory_space=pltpu.VMEM)] * 4,
        scratch_shapes=[
            pltpu.VMEM((PEERS, 4, 128, HEAD_SIZE), low),
            pltpu.VMEM((PEERS, 2, 128, HEAD_SIZE), low),
            pltpu.VMEM((PEERS, 2, 128, HEAD_SIZE), low),
            pltpu.VMEM((PEERS, HEAD_SIZE, 128), low),
        ]
        + [dma((PEERS,))] * 6,
        compiler_params=pltpu.CompilerParams(
            collective_id=collective_id, has_side_effects=True, vmem_limit_bytes=40 * 2**20
        ),
        name="attend",
    )(pre, cosine, sine, gains, key_place, query_cap)


WORK = 12


def rms_back(values, gain, upstream):
    r = lax.rsqrt(jnp.mean(values * values, axis=-1, keepdims=True) + norm_epsilon)
    weighted = upstream * gain
    mean = jnp.mean(weighted * values, axis=-1, keepdims=True)
    grad = r * weighted - values * (r * r * r) * mean
    return grad, jnp.sum(upstream * values * r, axis=0, keepdims=True)


def stream_blocks(first, count, start, wait, body):
    start(first, 0)

    def one(i, carry):
        slot = i % 2

        @pl.when(i + 1 < count)
        def following():
            start(first + i + 1, 1 - slot)

        wait(first + i, slot)
        body(first + i, slot)
        return carry

    lax.fori_loop(0, count, one, 0)


def backward_kernel(*refs):
    count = DECODER_LAYERS
    acts = [refs[4 * n : 4 * n + 4] for n in range(count)]
    refs = refs[4 * count :]
    per_layer = [refs[7 * n : 7 * n + 7] for n in range(count)]
    refs = refs[7 * count :]
    (into_w, out_w, wide_w, down_w) = refs[:4]
    (upstream, cosine, sine, attn_gains, mlp_gains, head_gains, key_place, query_cap) = refs[4:12]
    results = refs[12:19]
    grad_stream, gain_out, held = refs[19:22]
    refs = refs[22:]
    sizes = len(reduce_scratch(count))
    reduce_refs, refs = refs[:sizes], refs[sizes:]
    gain_refs, refs = refs[:4], refs[4:]
    (down_low, both_low, out_low, pre_low, terms,
     gate_up, middle, entry, pre, kept, kept_out, kept_log, mid_grad, rows_w, wide_rows,
     dsend, drecv, qsend, qrecv, ksend, krecv, kt, key_sum, value_sum,
     load_sem, rows_sem, wide_sem, gate_sem, d_s, d_r, q_s, q_r, k_s, k_r) = refs
    reducer = Reducer(
        acts, ((down_low, 1), (both_low, 6), (out_low, 1), (pre_low, 4)), results,
        (held,) + tuple(reduce_refs), tuple(reversed(range(count))),
    )
    gain_sum = GainSum(reducer, terms, gain_out, gain_refs)
    c = lax.axis_index("ctx")
    x = lax.axis_index("fsdp")
    me = c % PEERS
    z = c // 4

    def peer(r):
        return (c - me + r, x)

    barrier = pltpu.get_barrier_semaphore()

    def greet(o, carry):
        pl.semaphore_signal(barrier, inc=1, device_id=peer((me + o) % PEERS), device_id_type=MESH)
        return carry

    lax.fori_loop(1, PEERS, greet, 0)
    pl.semaphore_signal(barrier, inc=1, device_id=reducer.across, device_id_type=MESH)
    for o in range(2):
        far = ((z // 2 * 2 + 2) % 4 + o) * 4 + c % 4
        pl.semaphore_signal(barrier, inc=1, device_id=(far, x), device_id_type=MESH)
    pl.semaphore_wait(barrier, PEERS + 2)

    grad_stream[...] = upstream[...]
    terms[...] = jnp.zeros_like(terms)
    reducer.start_acts(0, (0,))

    cos = cosine[...]
    sin = sine[...]

    def grad_copy(r, slot):
        return make_remote(dsend.at[r], drecv.at[slot], d_s.at[r], d_r.at[slot], peer(r))

    def query_copy(r, slot):
        return make_remote(qsend.at[r], qrecv.at[slot], q_s.at[r], q_r.at[slot], peer(r))

    def key_copy(r, slot):
        return make_remote(ksend.at[r], krecv.at[slot], k_s.at[r], k_r.at[slot], peer(r))

    saved = (middle, entry, pre, kept, kept_out, kept_log)

    def load(n, k):
        for layer in range(count):

            @pl.when(n == layer)
            def start(layer=layer):
                pltpu.make_async_copy(per_layer[layer][1 + k], saved[k], load_sem.at[k]).start()

    def await_load(k):
        pltpu.make_async_copy(per_layer[0][1 + k], saved[k], load_sem.at[k]).wait()

    def add_term(layer, first, term):
        for i in range(8):
            terms[pl.ds(layer * 24 + first + i, 1), :] = term[:, i * 128 : (i + 1) * 128]

    def rows_copy(ref, layer, i, slot):
        rows = pl.ds(pl.multiple_of(i * 512, 512), 512)
        return pltpu.make_async_copy(ref.at[layer, rows], rows_w.at[slot], rows_sem.at[slot])

    def wide_copy(ref, layer, i, slot):
        rows = pl.ds(pl.multiple_of(i * 128, 128), 128)
        columns = ref.shape[2]
        return pltpu.make_async_copy(
            ref.at[layer, rows], wide_rows.at[slot, :, pl.ds(0, columns)], wide_sem.at[slot]
        )

    def hidden_part(n, layer, part):
        @pl.when(part == 0)
        def opening():
            for k in range(len(saved)):
                load(n, k)
            down_low[n] = grad_stream[...].astype(jnp.bfloat16)

        @pl.when((n == 0) & (part == 0))
        def first():
            reducer.start_grad(0)
            reducer.start_acts(0, (1, 2, 3))

        def gate_copy(source, i, slot, k):
            columns = pl.ds(pl.multiple_of(k * 3072 + i * 512, 512), 512)
            return pltpu.make_async_copy(
                source.at[:, columns], gate_up.at[slot, k], gate_sem.at[slot, k]
            )

        def start(i, slot):
            rows_copy(down_w, layer, i, slot).start()
            for place in range(count):

                @pl.when(n == place)
                def gates(place=place):
                    for k in range(2):
                        gate_copy(per_layer[place][0], i, slot, k).start()

        def wait(i, slot):
            rows_copy(down_w, layer, i, slot).wait()
            for k in range(2):
                gate_copy(per_layer[0][0], i, slot, k).wait()

        def body(i, slot):
            hidden = lax.dot_general(
                down_low[n], rows_w[slot], NT, preferred_element_type=jnp.float32
            )
            gate = gate_up[slot, 0]
            up = gate_up[slot, 1]
            sigmoid = jax.nn.sigmoid(gate)
            columns = pl.multiple_of(i * 512, 512)
            both_low[n, :, pl.ds(columns, 512)] = (
                hidden * up * sigmoid * (1.0 + gate * (1.0 - sigmoid))
            ).astype(jnp.bfloat16)
            both_low[n, :, pl.ds(3072 + columns, 512)] = (hidden * gate * sigmoid).astype(
                jnp.bfloat16
            )

        stream_blocks(part * 3, 3, start, wait, body)

        @pl.when((n == 0) & (part == 1))
        def rest():
            reducer.begin_more()

    def middle_part(n, layer, part):
        def body(i, slot):
            mid_grad[:, pl.ds(pl.multiple_of(i * 128, 128), 128)] = lax.dot_general(
                both_low[n], wide_rows[slot], NT, preferred_element_type=jnp.float32
            )

        stream_blocks(
            part * 3,
            jnp.where(part == 2, 2, 3),
            lambda i, slot: wide_copy(wide_w, layer, i, slot).start(),
            lambda i, slot: wide_copy(wide_w, layer, i, slot).wait(),
            body,
        )

        @pl.when(part == 2)
        def closing():
            await_load(0)
            grad, term = rms_back(middle[...], mlp_gains[layer], mid_grad[...])
            add_term(layer, 8, term)
            total = grad_stream[...] + grad
            grad_stream[...] = total
            out_low[n] = total.astype(jnp.bfloat16)

    def out_part(n, layer):
        def place(i):
            return (i + me // 2) % 4

        def body(i, slot):
            low = lax.dot_general(
                out_low[n], rows_w[slot], NT, preferred_element_type=jnp.float32
            ).astype(jnp.bfloat16)
            for k in range(2):
                r = 2 * place(i) + k

                @pl.when(r == me)
                def home(k=k):
                    for j in range(2):
                        at = (2 * k + j) * HEAD_SIZE
                        drecv[me, j] = low[:, at : at + HEAD_SIZE]

                @pl.when(r != me)
                def away(k=k, r=r):
                    for j in range(2):
                        at = (2 * k + j) * HEAD_SIZE
                        dsend[r, j] = low[:, at : at + HEAD_SIZE]
                    grad_copy(r, me).start()

        stream_blocks(
            0,
            4,
            lambda i, slot: rows_copy(out_w, layer, place(i), slot).start(),
            lambda i, slot: rows_copy(out_w, layer, place(i), slot).wait(),
            body,
        )
        for k in range(2, len(saved)):
            await_load(k)

        def turn_keys(j, carry):
            kt[j] = kept[j, 2].astype(jnp.float32).T.astype(jnp.bfloat16)
            return carry

        lax.fori_loop(0, PEERS, turn_keys, 0)
        key_sum[...] = jnp.zeros_like(key_sum)
        value_sum[...] = jnp.zeros_like(value_sum)

    def attention_block(o):
        j = (me + o) % PEERS

        @pl.when(o > 0)
        def arrived():
            grad_copy(me, j).wait_recv()

        grads = drecv[j].reshape(2 * 128, HEAD_SIZE)
        delta = jnp.sum(grads.astype(jnp.float32).T * kept_out[j], axis=0, keepdims=True)
        queries = kept[j, 0:2].reshape(2 * 128, HEAD_SIZE)
        keys = kept[:, 2].reshape(PEERS * 128, HEAD_SIZE)
        values = kept[:, 3].reshape(PEERS * 128, HEAD_SIZE)
        scores = lax.dot_general(keys, queries, NT, preferred_element_type=jnp.float32) * SCALE
        allowed = key_place[...] <= query_cap[j]
        scores = jnp.where(allowed, scores, masked_logits)
        prob = jnp.exp(scores - kept_log[j, 0:1, :])
        dprob = lax.dot_general(values, grads, NT, preferred_element_type=jnp.float32)
        dscore = (prob * (dprob - delta)).astype(jnp.bfloat16)
        value_sum[...] += jnp.dot(
            prob.astype(jnp.bfloat16), grads, preferred_element_type=jnp.float32
        )
        key_sum[...] += jnp.dot(dscore, queries, preferred_element_type=jnp.float32)
        turned = jnp.zeros((HEAD_SIZE, 256), jnp.float32)
        for i in range(PEERS):
            turned += jnp.dot(
                kt[i], dscore[i * 128 : (i + 1) * 128], preferred_element_type=jnp.float32
            )
        query_grad = (turned * SCALE).T.astype(jnp.bfloat16).reshape(2, 128, HEAD_SIZE)

        @pl.when(o == 0)
        def home():
            qrecv[me] = query_grad

        @pl.when(o > 0)
        def away():
            qsend[j] = query_grad
            query_copy(j, me).start()

        @pl.when(o == PEERS - 1)
        def keys_done():
            lax.fori_loop(1, PEERS + 1, push_keys, 0)

    def push_keys(o, carry):
        j = (me + o) % PEERS
        rows = pl.ds(pl.multiple_of(j * 128, 128), 128)
        key = (key_sum[rows, :] * SCALE).astype(jnp.bfloat16)
        value = value_sum[rows, :].astype(jnp.bfloat16)

        @pl.when(o < PEERS)
        def away():
            ksend[j, 0] = key
            ksend[j, 1] = value
            key_copy(j, me).start()

        @pl.when(o == PEERS)
        def home():
            krecv[me, 0] = key
            krecv[me, 1] = value

        return carry

    def head_part(n, layer):
        def back(grad, first, index, gain):
            g = grad.astype(jnp.float32)
            dy = g * cos - pltpu.roll(g, HEAD_SIZE // 2, 1) * sin
            low, term = rms_back(pre[:, head_columns(first, index)], gain, dy)
            return low.astype(jnp.bfloat16), term

        def finish_queries(o, total):
            h = (me + o) % PEERS

            @pl.when(o > 0)
            def arrived():
                query_copy(me, h).wait_recv()

            for i in range(2):
                low, term = back(qrecv[h, i], 0, 2 * h + i, head_gains[layer, 0:1, :])
                pre_low[n, :, head_columns(0, 2 * h + i)] = low
                total += term
            return total

        zero = jnp.zeros((1, HEAD_SIZE), jnp.float32)
        terms[pl.ds(layer * 24 + 16, 1), :] = lax.fori_loop(0, PEERS, finish_queries, zero)

        def finish_keys(o, total):
            h = (me + o) % PEERS

            @pl.when(o > 0)
            def arrived():
                key_copy(me, h).wait_recv()

            low, term = back(krecv[h, 0], 2048, h, head_gains[layer, 1:2, :])
            pre_low[n, :, head_columns(2048, h)] = low
            pre_low[n, :, head_columns(3072, h)] = krecv[h, 1]
            return total + term

        terms[pl.ds(layer * 24 + 17, 1), :] = lax.fori_loop(0, PEERS, finish_keys, zero)

        def settle(o, carry):
            r = (me + o) % PEERS
            grad_copy(r, me).wait_send()
            query_copy(r, me).wait_send()
            key_copy(r, me).wait_send()
            return carry

        lax.fori_loop(1, PEERS, settle, 0)

    def entry_part(n, layer, part):
        def body(i, slot):
            mid_grad[:, pl.ds(pl.multiple_of(i * 128, 128), 128)] = lax.dot_general(
                pre_low[n], wide_rows[slot, :, 0:4096], NT, preferred_element_type=jnp.float32
            )

        stream_blocks(
            part * 4,
            4,
            lambda i, slot: wide_copy(into_w, layer, i, slot).start(),
            lambda i, slot: wide_copy(into_w, layer, i, slot).wait(),
            body,
        )

        @pl.when(part == 1)
        def closing():
            await_load(1)
            grad, term = rms_back(entry[...], attn_gains[layer], mid_grad[...])
            add_term(layer, 0, term)
            grad_stream[...] += grad

    def step(w, carry):
        reducer.step(w - 2)
        gain_sum.step(w, WORK * count)
        n = w // WORK
        phase = w % WORK
        layer = count - 1 - n
        busy = w < WORK * count

        @pl.when(busy & (phase < 2))
        def phase_hidden():
            hidden_part(n, layer, phase)

        @pl.when(busy & (phase >= 2) & (phase < 5))
        def phase_middle():
            middle_part(n, layer, phase - 2)

        @pl.when(busy & (phase == 5))
        def phase_out():
            out_part(n, layer)

        @pl.when(busy & (phase >= 6) & (phase < 9))
        def phase_attention():
            first = (phase - 6) * 3

            def block(i, inner):
                attention_block(first + i)
                return inner

            lax.fori_loop(0, jnp.minimum(3, PEERS - first), block, 0)

        @pl.when(busy & (phase == 9))
        def phase_heads():
            head_part(n, layer)

        @pl.when(busy & (phase >= 10))
        def phase_entry():
            entry_part(n, layer, phase - 10)

        return carry

    lax.fori_loop(0, reducer.steps() + 2, step, 0)
    reducer.drain()
    gain_sum.drain()


RESULTS = ((32, 2048), (32, 1024), (32, 1024), (64, 1024), (32, 3072), (32, 3072), (96, 1024))


def backward(acts, saved, weights, upstream, cosine, sine, gains, key_place, query_cap, number):
    count = DECODER_LAYERS
    dma = pltpu.SemaphoreType.DMA
    low, wide = jnp.bfloat16, jnp.float32
    pair = pltpu.VMEM((PEERS, 2, 128, HEAD_SIZE), low)
    anywhere = pl.BlockSpec(memory_space=pl.ANY)
    near = pl.BlockSpec(memory_space=pltpu.VMEM)
    return pl.pallas_call(
        backward_kernel,
        out_shape=[jax.ShapeDtypeStruct((count,) + shape, wide) for shape in RESULTS]
        + [
            jax.ShapeDtypeStruct((128, 1024), wide),
            jax.ShapeDtypeStruct((24 * count, 128), wide),
            jax.ShapeDtypeStruct((GRADS * count, 384, 1024), low),
        ],
        in_specs=[anywhere] * (11 * count + 4) + [near] * 8,
        out_specs=[near] * 9 + [anywhere],
        scratch_shapes=reduce_scratch(count)
        + gain_scratch(24 * count)
        + [
            pltpu.VMEM((count, 128, 1024), low),
            pltpu.VMEM((count, 128, 6144), low),
            pltpu.VMEM((count, 128, 1024), low),
            pltpu.VMEM((count, 128, 4096), low),
            pltpu.VMEM((24 * count, 128), wide),
            pltpu.VMEM((2, 2, 128, 512), wide),
            pltpu.VMEM((128, 1024), wide),
            pltpu.VMEM((128, 1024), wide),
            pltpu.VMEM((128, 4096), wide),
            pltpu.VMEM((PEERS, 4, 128, HEAD_SIZE), low),
            pltpu.VMEM((PEERS, HEAD_SIZE, 256), wide),
            pltpu.VMEM((PEERS, 8, 256), wide),
            pltpu.VMEM((128, 1024), wide),
            pltpu.VMEM((2, 512, 1024), low),
            pltpu.VMEM((2, 128, 6144), low),
        ]
        + [pair] * 6
        + [
            pltpu.VMEM((PEERS, HEAD_SIZE, 128), low),
            pltpu.VMEM((PEERS * 128, HEAD_SIZE), wide),
            pltpu.VMEM((PEERS * 128, HEAD_SIZE), wide),
            dma((6,)), dma((2,)), dma((2,)), dma((2, 2)),
        ]
        + [dma((PEERS,))] * 6,
        compiler_params=pltpu.CompilerParams(
            collective_id=number, has_side_effects=True, vmem_limit_bytes=62 * 2**20
        ),
        name="backward",
    )(*acts, *saved, *weights, upstream, cosine, sine, *gains, key_place, query_cap)


def from_partner(shard, axis, apart):
    return lax.ppermute(shard, axis, [(i, i ^ 1 << apart) for i in range(lax.axis_size(axis))])


def token_places(stretch_table, slot_lengths):
    ctx_count = stretch_table.shape[0]
    stretch_order = stretch_table.reshape(-1)
    within = jnp.arange(STRETCH, dtype=jnp.int32)
    places = (stretch_order % ctx_count * STRETCH)[:, None] + within[None, :]
    slot_ids = jnp.broadcast_to((stretch_order // ctx_count)[:, None], places.shape).reshape(-1)
    places = places.reshape(-1)
    limits = jnp.where(slot_ids == 0, slot_lengths[0], slot_lengths[1])
    return (places, slot_ids, places < limits)


def rotary_tables(places):
    half_dim = HEAD_SIZE // 2
    spread = jnp.arange(half_dim, dtype=jnp.int32).astype(jnp.float32) * (2.0 / HEAD_SIZE)
    inverse = jnp.exp(spread * -math.log(rope_base))
    angles = places.astype(jnp.float32)[:, None] * inverse[None, :]
    return (
        jnp.concatenate([jnp.cos(angles)] * 2, axis=-1),
        jnp.concatenate([jnp.sin(angles)] * 2, axis=-1),
    )


def rotate(values, cosine_table, sine_table):
    half_dim = values.shape[-1] // 2
    turned = jnp.concatenate([-values[..., half_dim:], values[..., :half_dim]], axis=-1)
    return values * cosine_table[:, None, :] + turned * sine_table[:, None, :]


def unrotate(upstream, cosine_table, sine_table):
    half_dim = upstream.shape[-1] // 2
    scaled_sine = upstream * sine_table[:, None, :]
    turned_back = jnp.concatenate(
        [scaled_sine[..., half_dim:], -scaled_sine[..., :half_dim]], axis=-1
    )
    return upstream * cosine_table[:, None, :] + turned_back


def norm_forward(values, gain_vec):
    scale_inv = lax.rsqrt(jnp.mean(values * values, axis=-1, keepdims=True) + norm_epsilon)
    return (values * scale_inv * gain_vec, scale_inv)


def norm_backward(values, scale_inv, gain_vec, upstream):
    weighted = upstream * gain_vec
    grad_input = scale_inv * weighted - values * scale_inv**3 * jnp.mean(
        weighted * values, axis=-1, keepdims=True
    )
    gain_term = jnp.sum((upstream * values * scale_inv).reshape(-1, values.shape[-1]), axis=0)
    return (grad_input, gain_term)


def upper_bit(local_index, bit_number):
    return local_index // 2**bit_number % 2 == 1


def joined_rows(mine, received, upper_side):
    first_rows = jnp.where(upper_side, received, mine)
    second_rows = jnp.where(upper_side, mine, received)
    return jnp.concatenate([first_rows, second_rows], axis=0)


def half_gather(pair, local_index):
    gathered_rows = pair
    for bit_number in range(lax.axis_size("ctx").bit_length() - 2):
        received = from_partner(gathered_rows, "ctx", bit_number)
        gathered_rows = joined_rows(gathered_rows, received, upper_bit(local_index, bit_number))
    return gathered_rows


def half_reduce(term, local_index):
    for bit_number in reversed(range(lax.axis_size("ctx").bit_length() - 2)):
        span = term.shape[0] // 2
        lower_rows = term[:span]
        upper_rows = term[span:]
        upper_side = upper_bit(local_index, bit_number)
        kept_rows = jnp.where(upper_side, upper_rows, lower_rows)
        sent_rows = jnp.where(upper_side, lower_rows, upper_rows)
        term = kept_rows + from_partner(sent_rows, "ctx", bit_number)
    return term


def over_keys(update, carried, count_rows):
    block_length = math.gcd(count_rows, 512)

    def inner_step(current, block_index):
        return (update(current, block_index * block_length, block_length), None)

    carried, unused = lax.scan(
        inner_step, carried, jnp.arange(count_rows // block_length, dtype=jnp.int32)
    )
    return carried


def allowed_mask(key_meta, query_meta, row_start, block_length):
    key_places = lax.dynamic_slice_in_dim(key_meta[0], row_start, block_length)
    key_slots = lax.dynamic_slice_in_dim(key_meta[1], row_start, block_length)
    key_live = lax.dynamic_slice_in_dim(key_meta[2], row_start, block_length)
    allowed = (
        (key_slots[None, :] == query_meta[1][:, None])
        & (key_places[None, :] <= query_meta[0][:, None])
        & key_live[None, :]
    )
    return allowed[None, None]


def forward_update(
    current, query_head_group, key_tile_block, value_tile_block, allowed, score_scale
):
    running_max, running_sum, running_acc = current
    block_length = key_tile_block.shape[0]
    key_head_list = key_tile_block.reshape(block_length, KEY_VALUE_HEADS, HEAD_SIZE)
    value_head_list = value_tile_block.reshape(block_length, KEY_VALUE_HEADS, HEAD_SIZE)
    scores = (
        jnp.einsum(
            "qhgd,khd->hgqk", query_head_group, key_head_list, preferred_element_type=jnp.float32
        )
        * score_scale
    )
    scores = jnp.where(allowed, scores, masked_logits)
    new_max = jnp.maximum(running_max, jnp.max(scores, axis=-1))
    factor = jnp.exp(running_max - new_max)
    prob_block = jnp.where(allowed, jnp.exp(scores - new_max[..., None]), 0.0)
    new_sum = running_sum * factor + jnp.sum(prob_block, axis=-1)
    new_acc = running_acc * factor[..., None] + jnp.einsum(
        "hgqk,khd->hgqd",
        prob_block.astype(jnp.bfloat16),
        value_head_list,
        preferred_element_type=jnp.float32,
    )
    return (new_max, new_sum, new_acc)


def score_parts(
    query_head_group,
    output_grad_group,
    key_tile_block,
    value_tile_block,
    allowed,
    log_total,
    row_delta,
    score_scale,
):
    block_length = key_tile_block.shape[0]
    key_head_list = key_tile_block.reshape(block_length, KEY_VALUE_HEADS, HEAD_SIZE)
    value_head_list = value_tile_block.reshape(block_length, KEY_VALUE_HEADS, HEAD_SIZE)
    scores = (
        jnp.einsum(
            "qhgd,khd->hgqk", query_head_group, key_head_list, preferred_element_type=jnp.float32
        )
        * score_scale
    )
    prob_block = jnp.where(allowed, jnp.exp(scores - log_total[..., None]), 0.0)
    dprob = jnp.einsum(
        "qhgd,khd->hgqk", output_grad_group, value_head_list, preferred_element_type=jnp.float32
    )
    dscore_low = (prob_block * (dprob - row_delta[..., None])).astype(jnp.bfloat16)
    return (prob_block, dscore_low, key_head_list)


def attention_inputs(stream, gathered, cosine_table, sine_table):
    count_rows = stream.shape[0]
    normalized, inv_attn = norm_forward(stream, gathered[7].astype(jnp.float32))
    normed_low = normalized.astype(jnp.bfloat16)
    query_heads = jnp.dot(normed_low, gathered[0], preferred_element_type=jnp.float32).reshape(
        count_rows, QUERY_HEADS, HEAD_SIZE
    )
    key_head_list = jnp.dot(normed_low, gathered[1], preferred_element_type=jnp.float32).reshape(
        count_rows, KEY_VALUE_HEADS, HEAD_SIZE
    )
    value_low = jnp.dot(normed_low, gathered[2], preferred_element_type=jnp.float32).astype(
        jnp.bfloat16
    )
    query_normed, inv_query = norm_forward(query_heads, gathered[9].astype(jnp.float32))
    key_normed, inv_key = norm_forward(key_head_list, gathered[10].astype(jnp.float32))
    query_lowered = rotate(query_normed, cosine_table, sine_table).astype(jnp.bfloat16)
    key_low = (
        rotate(key_normed, cosine_table, sine_table)
        .astype(jnp.bfloat16)
        .reshape(count_rows, KEY_VALUE_HEADS * HEAD_SIZE)
    )
    return {
        "normed_low": normed_low,
        "inv_attn": inv_attn,
        "query_heads": query_heads,
        "inv_query": inv_query,
        "key_heads": key_head_list,
        "inv_key": inv_key,
        "query_low": query_lowered,
        "key_low": key_low,
        "value_low": value_low,
    }


def block_rest(stream, gathered, attn_low):
    middle = stream + jnp.dot(attn_low, gathered[3], preferred_element_type=jnp.float32)
    normed_mid, inv_mid = norm_forward(middle, gathered[8].astype(jnp.float32))
    normed_mid_low = normed_mid.astype(jnp.bfloat16)
    gate_act = jnp.dot(normed_mid_low, gathered[4], preferred_element_type=jnp.float32)
    upward = jnp.dot(normed_mid_low, gathered[5], preferred_element_type=jnp.float32)
    hidden_low = (jax.nn.silu(gate_act) * upward).astype(jnp.bfloat16)
    result = middle + jnp.dot(hidden_low, gathered[6], preferred_element_type=jnp.float32)
    return {
        "middle": middle,
        "inv_mid": inv_mid,
        "normed_mid_low": normed_mid_low,
        "gate_act": gate_act,
        "upward": upward,
        "hidden_low": hidden_low,
        "result": result,
    }


def general_device(
    tokens,
    cotangent,
    lengths,
    stretch_ids,
    w_query,
    key_projection_weight,
    value_projection_weight,
    w_out,
    w_gate,
    w_up,
    w_down,
    g_attn,
    g_mlp,
    g_query,
    g_key,
):
    count_rows = tokens.shape[0]
    ctx_count = lax.axis_size("ctx")
    half_count = ctx_count // 2
    key_value_width = KEY_VALUE_HEADS * HEAD_SIZE
    key_meta = token_places(stretch_ids[:, 0, :], lengths[0])
    ctx_index = lax.axis_index("ctx")
    local_index = ctx_index % half_count
    base_row = ctx_index // half_count * half_count * count_rows
    half_row_set = half_count * count_rows
    offset_mine = ctx_index * count_rows
    query_meta = tuple(
        (lax.dynamic_slice_in_dim(meta_array, offset_mine, count_rows) for meta_array in key_meta)
    )
    live_mine = query_meta[2].astype(jnp.float32)[:, None]
    cosine_table, sine_table = rotary_tables(query_meta[0])
    group_count = QUERY_HEADS // KEY_VALUE_HEADS
    score_scale = HEAD_SIZE ** (-0.5)

    def attend_forward(query_head_group, key_source, value_source, current):

        def update(carried, local_row, block_length):
            key_tile_block = lax.dynamic_slice_in_dim(key_source, local_row, block_length)
            value_tile_block = lax.dynamic_slice_in_dim(value_source, local_row, block_length)
            allowed = allowed_mask(key_meta, query_meta, base_row + local_row, block_length)
            return forward_update(
                carried, query_head_group, key_tile_block, value_tile_block, allowed, score_scale
            )

        return over_keys(update, current, key_source.shape[0])

    saved = []
    stream = tokens.astype(jnp.float32)
    for layer_index in range(DECODER_LAYERS):
        gathered = (
            lax.all_gather(w_query[layer_index], "fsdp", axis=0, tiled=True),
            lax.all_gather(key_projection_weight[layer_index], "fsdp", axis=0, tiled=True),
            lax.all_gather(value_projection_weight[layer_index], "fsdp", axis=0, tiled=True),
            lax.all_gather(w_out[layer_index], "fsdp", axis=0, tiled=True),
            lax.all_gather(w_gate[layer_index], "fsdp", axis=0, tiled=True),
            lax.all_gather(w_up[layer_index], "fsdp", axis=0, tiled=True),
            lax.all_gather(w_down[layer_index], "fsdp", axis=0, tiled=True),
            lax.all_gather(g_attn[layer_index], "fsdp", axis=0, tiled=True),
            lax.all_gather(g_mlp[layer_index], "fsdp", axis=0, tiled=True),
            lax.all_gather(g_query[layer_index], "fsdp", axis=0, tiled=True),
            lax.all_gather(g_key[layer_index], "fsdp", axis=0, tiled=True),
        )
        present_inputs = attention_inputs(stream, gathered, cosine_table, sine_table)
        query_head_group = present_inputs["query_low"].reshape(
            count_rows, KEY_VALUE_HEADS, group_count, HEAD_SIZE
        )
        start_state = (
            jnp.full((KEY_VALUE_HEADS, group_count, count_rows), masked_logits, jnp.float32),
            jnp.zeros((KEY_VALUE_HEADS, group_count, count_rows), jnp.float32),
            jnp.zeros((KEY_VALUE_HEADS, group_count, count_rows, HEAD_SIZE), jnp.float32),
        )
        pair_all = half_gather(
            jnp.concatenate([present_inputs["key_low"], present_inputs["value_low"]], axis=-1),
            local_index,
        )
        key_all = pair_all[:, :key_value_width]
        value_all = pair_all[:, key_value_width:]
        final_state = attend_forward(query_head_group, key_all, value_all, start_state)
        attended = final_state[2] / final_state[1][..., None]
        log_total = final_state[0] + jnp.log(final_state[1])
        attn_low = (
            jnp.transpose(attended, (2, 0, 1, 3))
            .reshape(count_rows, QUERY_HEADS * HEAD_SIZE)
            .astype(jnp.bfloat16)
        )
        rest = block_rest(stream, gathered, attn_low)
        kept = (gathered, key_all, value_all, present_inputs, rest)
        saved.append((stream, attended, log_total, kept))
        stream = rest["result"]
    output_low = (stream * live_mine).astype(jnp.bfloat16)
    grad_stream = cotangent.astype(jnp.float32) * live_mine
    layer_grads = [None] * DECODER_LAYERS
    for layer_index in reversed(range(DECODER_LAYERS)):
        stream_in, attended, log_total, kept = saved[layer_index]
        attn_low = (
            jnp.transpose(attended, (2, 0, 1, 3))
            .reshape(count_rows, QUERY_HEADS * HEAD_SIZE)
            .astype(jnp.bfloat16)
        )
        gathered, key_all, value_all, present_inputs, rest = kept
        ffn_grad_low = grad_stream.astype(jnp.bfloat16)
        grad_down = jnp.einsum(
            "tf,td->fd", rest["hidden_low"], ffn_grad_low, preferred_element_type=jnp.float32
        )
        hidden_grad = jnp.einsum(
            "td,fd->tf", ffn_grad_low, gathered[6], preferred_element_type=jnp.float32
        )
        gate_act = rest["gate_act"]
        sigmoid_gate = jax.nn.sigmoid(gate_act)
        gate_grad_low = (
            hidden_grad * rest["upward"] * sigmoid_gate * (1.0 + gate_act * (1.0 - sigmoid_gate))
        ).astype(jnp.bfloat16)
        up_grad_low = (hidden_grad * gate_act * sigmoid_gate).astype(jnp.bfloat16)
        grad_gate = jnp.einsum(
            "td,tf->df", rest["normed_mid_low"], gate_grad_low, preferred_element_type=jnp.float32
        )
        grad_up = jnp.einsum(
            "td,tf->df", rest["normed_mid_low"], up_grad_low, preferred_element_type=jnp.float32
        )
        normed_mid_grad = jnp.einsum(
            "tf,df->td", gate_grad_low, gathered[4], preferred_element_type=jnp.float32
        ) + jnp.einsum("tf,df->td", up_grad_low, gathered[5], preferred_element_type=jnp.float32)
        mid_norm_grad, mlp_gain_term = norm_backward(
            rest["middle"], rest["inv_mid"], gathered[8].astype(jnp.float32), normed_mid_grad
        )
        middle_grad = grad_stream + mid_norm_grad
        attn_grad_low = middle_grad.astype(jnp.bfloat16)
        grad_out = jnp.einsum(
            "tq,td->qd", attn_low, attn_grad_low, preferred_element_type=jnp.float32
        )
        output_gradient_lowered = jnp.einsum(
            "td,qd->tq", attn_grad_low, gathered[3], preferred_element_type=jnp.float32
        ).astype(jnp.bfloat16)
        output_grad_group = output_gradient_lowered.reshape(
            count_rows, KEY_VALUE_HEADS, group_count, HEAD_SIZE
        )
        row_delta = jnp.sum(
            jnp.transpose(output_grad_group.astype(jnp.float32), (1, 2, 0, 3)) * attended, axis=-1
        )
        query_head_group = present_inputs["query_low"].reshape(
            count_rows, KEY_VALUE_HEADS, group_count, HEAD_SIZE
        )
        key_block_size = math.gcd(half_row_set, 512)

        def backward_step(query_acc, block_index):
            row_start = block_index * key_block_size
            key_tile_block = lax.dynamic_slice_in_dim(key_all, row_start, key_block_size)
            value_tile_block = lax.dynamic_slice_in_dim(value_all, row_start, key_block_size)
            allowed = allowed_mask(key_meta, query_meta, base_row + row_start, key_block_size)
            prob_block, dscore_low, key_head_list = score_parts(
                query_head_group,
                output_grad_group,
                key_tile_block,
                value_tile_block,
                allowed,
                log_total,
                row_delta,
                score_scale,
            )
            query_next = (query_acc, jnp.zeros((key_block_size, 2 * key_value_width), jnp.float32))[
                0
            ] + jnp.einsum(
                "hgqk,khd->qhgd", dscore_low, key_head_list, preferred_element_type=jnp.float32
            ) * score_scale
            value_grad = jnp.einsum(
                "hgqk,qhgd->khd",
                prob_block.astype(jnp.bfloat16),
                output_grad_group,
                preferred_element_type=jnp.float32,
            )
            key_grad = (
                jnp.einsum(
                    "hgqk,qhgd->khd",
                    dscore_low,
                    query_head_group,
                    preferred_element_type=jnp.float32,
                )
                * score_scale
            )
            block_rows = jnp.concatenate(
                [
                    key_grad.reshape(key_block_size, key_value_width),
                    value_grad.reshape(key_block_size, key_value_width),
                ],
                axis=-1,
            )
            return (query_next, block_rows)

        query_grad, key_value_rows = lax.scan(
            backward_step,
            jnp.zeros((count_rows, KEY_VALUE_HEADS, group_count, HEAD_SIZE), jnp.float32),
            jnp.arange(half_row_set // key_block_size, dtype=jnp.int32),
        )
        key_value_term = key_value_rows.reshape(half_row_set, 2 * key_value_width)
        key_value_gradient = half_reduce(key_value_term, local_index)
        key_gradient_rows = key_value_gradient[:, :key_value_width].reshape(
            count_rows, KEY_VALUE_HEADS, HEAD_SIZE
        )
        value_grad_low = key_value_gradient[:, key_value_width:].astype(jnp.bfloat16)
        query_pre, query_gain_term = norm_backward(
            present_inputs["query_heads"],
            present_inputs["inv_query"],
            gathered[9].astype(jnp.float32),
            unrotate(
                query_grad.reshape(count_rows, QUERY_HEADS, HEAD_SIZE), cosine_table, sine_table
            ),
        )
        key_pre, key_gain_term = norm_backward(
            present_inputs["key_heads"],
            present_inputs["inv_key"],
            gathered[10].astype(jnp.float32),
            unrotate(key_gradient_rows, cosine_table, sine_table),
        )
        query_grad_low = query_pre.reshape(count_rows, QUERY_HEADS * HEAD_SIZE).astype(jnp.bfloat16)
        key_grad_low = key_pre.reshape(count_rows, key_value_width).astype(jnp.bfloat16)
        normed_low = present_inputs["normed_low"]
        grad_query = jnp.einsum(
            "td,tq->dq", normed_low, query_grad_low, preferred_element_type=jnp.float32
        )
        grad_key = jnp.einsum(
            "td,tq->dq", normed_low, key_grad_low, preferred_element_type=jnp.float32
        )
        grad_value = jnp.einsum(
            "td,tq->dq", normed_low, value_grad_low, preferred_element_type=jnp.float32
        )
        normed_grad = jnp.einsum(
            "tq,dq->td", query_grad_low, gathered[0], preferred_element_type=jnp.float32
        )
        normed_grad = normed_grad + jnp.einsum(
            "tq,dq->td", key_grad_low, gathered[1], preferred_element_type=jnp.float32
        )
        normed_grad = normed_grad + jnp.einsum(
            "tq,dq->td", value_grad_low, gathered[2], preferred_element_type=jnp.float32
        )
        in_norm_grad, attn_gain_term = norm_backward(
            stream_in, present_inputs["inv_attn"], gathered[7].astype(jnp.float32), normed_grad
        )
        grad_stream = middle_grad + in_norm_grad
        layer_grads[layer_index] = (
            lax.psum_scatter(grad_query, ("ctx", "fsdp"), scatter_dimension=0, tiled=True),
            lax.psum_scatter(grad_key, ("ctx", "fsdp"), scatter_dimension=0, tiled=True),
            lax.psum_scatter(grad_value, ("ctx", "fsdp"), scatter_dimension=0, tiled=True),
            lax.psum_scatter(grad_out, ("ctx", "fsdp"), scatter_dimension=0, tiled=True),
            lax.psum_scatter(grad_gate, ("ctx", "fsdp"), scatter_dimension=0, tiled=True),
            lax.psum_scatter(grad_up, ("ctx", "fsdp"), scatter_dimension=0, tiled=True),
            lax.psum_scatter(grad_down, ("ctx", "fsdp"), scatter_dimension=0, tiled=True),
            lax.psum_scatter(attn_gain_term, ("ctx", "fsdp"), scatter_dimension=0, tiled=True),
            lax.psum_scatter(mlp_gain_term, ("ctx", "fsdp"), scatter_dimension=0, tiled=True),
            lax.psum_scatter(query_gain_term, ("ctx", "fsdp"), scatter_dimension=0, tiled=True),
            lax.psum_scatter(key_gain_term, ("ctx", "fsdp"), scatter_dimension=0, tiled=True),
        )
    stacked = tuple(
        (jnp.stack([layer_sums[member] for layer_sums in layer_grads]) for member in range(11))
    )
    return (output_low, grad_stream) + stacked


def act_rows(values):
    return values.T.reshape(4, 2, 2, 2, -1, 32, values.shape[0])


def product(left, right):
    return jnp.dot(left, right, preferred_element_type=jnp.float32)


def product_turned(left, right):
    return lax.dot_general(left, right, NT, preferred_element_type=jnp.float32)


def fast_device(
    tokens,
    cotangent,
    lengths,
    stretch_ids,
    w_query,
    key_projection_weight,
    value_projection_weight,
    w_out,
    w_gate,
    w_up,
    w_down,
    g_attn,
    g_mlp,
    g_query,
    g_key,
):
    count_rows, width = tokens.shape
    ctx_index = lax.axis_index("ctx")
    places, slot_ids, live = token_places(stretch_ids[:, 0, :], lengths[0])
    group_rows = PEERS * count_rows
    base_row = ctx_index // PEERS * group_rows
    my_row = ctx_index * count_rows
    slot_places = lax.dynamic_slice_in_dim(places, base_row, group_rows)
    limit = lax.dynamic_slice_in_dim(lengths[0], ctx_index // PEERS, 1)
    caps = jnp.minimum(slot_places, limit - 1).reshape(PEERS, 1, count_rows)
    query_cap = jnp.concatenate([caps, caps], axis=2)
    key_place = slot_places[:, None]
    live_mine = lax.dynamic_slice_in_dim(live, my_row, count_rows).astype(jnp.float32)[:, None]
    cosine, sine = rotary_tables(lax.dynamic_slice_in_dim(places, my_row, count_rows))
    half = HEAD_SIZE // 2
    sine = jnp.concatenate([-sine[:, :half], sine[:, half:]], axis=1)

    packed = jnp.concatenate([member.reshape(-1) for member in (g_attn, g_mlp, g_query, g_key)])
    packed = jnp.pad(packed, (0, 4096 - packed.shape[0])).reshape(32, 128)
    gathered = gather_weights(
        (w_query, key_projection_weight, value_projection_weight, w_out, w_gate, w_up, w_down),
        packed,
        tuple(range(DECODER_LAYERS)),
        1,
    )
    flat = gathered[-1].reshape(2, -1).astype(jnp.float32)
    gains = []
    offset = 0
    for member in (g_attn, g_mlp, g_query, g_key):
        span = member.shape[1]
        sides = flat[:, offset : offset + DECODER_LAYERS * span].reshape(2, DECODER_LAYERS, span)
        gains.append(sides.transpose(1, 0, 2).reshape(DECODER_LAYERS, 2 * span))
        offset += DECODER_LAYERS * span

    attn_gains, mlp_gains = gains[0][:, None, :], gains[1][:, None, :]
    head_gains = jnp.stack([gains[2], gains[3]], axis=1)
    stream = tokens.astype(jnp.float32)
    acts, saved = [], []
    for layer in range(DECODER_LAYERS):
        into, out_weight, wide_weight, down = (member[layer] for member in gathered[:4])
        normed, unused = norm_forward(stream, gains[0][layer])
        normed_low = normed.astype(jnp.bfloat16)
        pre = product(normed_low, into)
        attn_low, kept, kept_out, kept_log = attend(
            pre, cosine, sine, head_gains[layer], key_place, query_cap, 2 + layer
        )
        middle = stream + product(attn_low, out_weight)
        normed_mid, unused = norm_forward(middle, gains[1][layer])
        mid_low = normed_mid.astype(jnp.bfloat16)
        both = product(mid_low, wide_weight)
        ff = both.shape[1] // 2
        hidden_low = (jax.nn.silu(both[:, :ff]) * both[:, ff:]).astype(jnp.bfloat16)
        acts = [act_rows(member) for member in (hidden_low, mid_low, attn_low, normed_low)] + acts
        saved = [both, middle, stream, pre, kept, kept_out, kept_log] + saved
        stream = middle + product(hidden_low, down)
    output_low = (stream * live_mine).astype(jnp.bfloat16)

    place = ctx_index * 2 + lax.axis_index("fsdp")
    *weight_sums, grad_stream, sums, unused = backward(
        acts,
        saved,
        gathered[:4],
        cotangent.astype(jnp.float32) * live_mine,
        cosine,
        sine,
        (attn_gains, mlp_gains, head_gains),
        key_place,
        query_cap,
        2 + DECODER_LAYERS,
    )
    sums = sums.reshape(DECODER_LAYERS, -1)

    def share(first, span):
        return lax.dynamic_slice_in_dim(sums, first + place * span, span, axis=1)

    return (output_low, grad_stream) + tuple(weight_sums) + (
        share(0, 32), share(1024, 32), share(2048, 4), share(2176, 4)
    )


def solution(mesh):
    plain = mesh.shape["ctx"] == 2 * KEY_VALUE_HEADS and mesh.shape["fsdp"] == 2
    device = fast_device if plain else general_device
    in_specs = (
        P(("ctx", "fsdp"), None),
        P(("ctx", "fsdp"), None),
        P("fsdp", None),
        P(None, "fsdp", None),
        P(None, "fsdp", None),
        P(None, "fsdp", None),
        P(None, "fsdp", None),
        P(None, "fsdp", None),
        P(None, "fsdp", None),
        P(None, "fsdp", None),
        P(None, "fsdp", None),
        P(None, "fsdp"),
        P(None, "fsdp"),
        P(None, "fsdp"),
        P(None, "fsdp"),
    )
    out_specs = (
        P(("ctx", "fsdp"), None),
        P(("ctx", "fsdp"), None),
        P(None, ("ctx", "fsdp"), None),
        P(None, ("ctx", "fsdp"), None),
        P(None, ("ctx", "fsdp"), None),
        P(None, ("ctx", "fsdp"), None),
        P(None, ("ctx", "fsdp"), None),
        P(None, ("ctx", "fsdp"), None),
        P(None, ("ctx", "fsdp"), None),
        P(None, ("ctx", "fsdp")),
        P(None, ("ctx", "fsdp")),
        P(None, ("ctx", "fsdp")),
        P(None, ("ctx", "fsdp")),
    )
    return jax.shard_map(
        device, mesh=mesh, in_specs=in_specs, out_specs=out_specs, check_vma=False
    )
```

```python
import functools
import math

import jax
import jax.numpy as jnp
from jax import lax
from jax.experimental import pallas as pl
from jax.experimental.pallas import tpu as pltpu
from jax.sharding import PartitionSpec as P

QUERY_HEADS = 16
KEY_VALUE_HEADS = 8
HEAD_SIZE = 128
DECODER_LAYERS = 2
STRETCH = 64


norm_epsilon = 1e-06
rope_base = 1000000.0
masked_logits = -1e30

MESH = pl.DeviceIdType.MESH


TILES = 15
GRADS = 12
ACTS = 7
AHEAD = 2
SLOTS = 8
ACT_SPANS = ((0, 3), (3, 1), (4, 2), (6, 1))


def grad_index(t):
    return jnp.where(t < 3, 0, jnp.where(t < 9, t - 2, jnp.where(t < 11, 7, t - 3)))


def act_index(t):
    return jnp.where(t < 3, t, jnp.where(t < 9, 3, jnp.where(t < 11, t - 5, 6)))


def is_new(t):
    return (t == 0) | ((t >= 3) & (t < 10)) | (t >= 11)


def make_remote(src, dst, s, r, dev):
    return pltpu.make_async_remote_copy(
        src_ref=src, dst_ref=dst, send_sem=s, recv_sem=r, device_id=dev, device_id_type=MESH
    )


class Reducer:
    def __init__(self, acts, grads, results, scratch, layers):
        self.acts, self.grads, self.results, self.layers = acts, grads, results, layers
        self.count = len(layers)
        (self.gheld, self.abuf, self.afwd, self.gtile, self.ysend, self.yrecv, self.own,
         self.zsend, self.zrecv, self.zown,
         self.a_local, self.a_xs, self.a_xr, self.a_cs, self.a_cr,
         self.g_local, self.g_xs, self.g_xr, self.g_cs, self.g_cr, self.g_fs, self.g_fr,
         self.y_s, self.y_r, self.z_s, self.z_r) = scratch
        c = lax.axis_index("ctx")
        x = lax.axis_index("fsdp")
        self.c, self.x = c, x
        self.core = c % 2
        self.y = c // 2 % 2
        self.z = c // 4
        self.sibling = (c + 1 - 2 * self.core, x)
        self.across = (c, 1 - x)
        self.aside = (c + 2 - 4 * self.y, x)

    def along(self, o):
        return ((self.z + o) % 4 * 4 + self.c % 4, self.x)

    def partners(self):
        return (self.sibling, self.across, self.aside) + tuple(self.along(o) for o in (1, 2, 3))

    def act(self, n, k, what):
        first, blocks = ACT_SPANS[k]
        src = self.acts[k].at[self.layers[n]]
        span = pl.ds(first, blocks)
        x, core = self.x, self.core

        def held(place):
            return self.abuf.at[n, :, :, span, :, pl.ds(128 * place, 128)]

        if what == "local":
            return pltpu.make_async_copy(
                src.at[:, :, core, x], held(0), self.a_local.at[n, k]
            )
        if what == "across":
            return make_remote(
                src.at[:, :, core, 1 - x], held(1), self.a_xs.at[n, k, 0], self.a_xr.at[n, k, 0],
                self.across,
            )
        if what == "relay":
            return make_remote(
                src.at[:, :, 1 - core, 1 - x], self.afwd.at[n, :, :, span],
                self.a_xs.at[n, k, 1], self.a_xr.at[n, k, 1], self.across,
            )
        if what == "sibling":
            return make_remote(
                src.at[:, :, 1 - core, x], held(2), self.a_cs.at[n, k, 0], self.a_cr.at[n, k, 0],
                self.sibling,
            )
        return make_remote(
            self.afwd.at[n, :, :, span], held(3), self.a_cs.at[n, k, 1], self.a_cr.at[n, k, 1],
            self.sibling,
        )

    def start_acts(self, n, ks):
        for what in ("across", "relay", "sibling", "local"):
            for k in ks:
                self.act(n, k, what).start()

    def forward_acts(self, n, ks):
        for k in ks:
            self.act(n, k, "relay").wait_recv()
            self.act(n, k, "forward").start()

    def await_acts(self, n, ks):
        for k in ks:
            self.act(n, k, "local").wait()
            for what in ("across", "sibling", "forward"):
                self.act(n, k, what).wait_recv()

    def grad_across(self, i, src=None):
        rows = self.gheld.at[i, pl.ds(0, 128)]
        return make_remote(
            rows if src is None else src, rows, self.g_xs.at[i], self.g_xr.at[i], self.across
        )

    def grad_sibling(self, i, src=None):
        rows = self.gheld.at[i, pl.ds(128, 128)]
        return make_remote(
            rows if src is None else src, rows, self.g_cs.at[i], self.g_cr.at[i], self.sibling
        )

    def grad_forward(self, i):
        return make_remote(
            self.gheld.at[i, pl.ds(0, 128)], self.gheld.at[i, pl.ds(256, 128)],
            self.g_fs.at[i], self.g_fr.at[i], self.sibling,
        )

    def grad_own(self, i, src=None):
        rows = self.gtile.at[i % 2, pl.ds(0, 128)]
        return pltpu.make_async_copy(rows if src is None else src, rows, self.g_local.at[i % 2, 0])

    def grad_load(self, i):
        return pltpu.make_async_copy(
            self.gheld.at[i], self.gtile.at[i % 2, pl.ds(128, 384)], self.g_local.at[i % 2, 1]
        )

    def with_source(self, i, act):
        n = i // GRADS
        g = i % GRADS
        first = 0
        for ref, blocks in self.grads:

            @pl.when((g >= first) & (g < first + blocks))
            def use(ref=ref, first=first):
                act(ref.at[n, :, pl.ds(pl.multiple_of((g - first) * 1024, 1024), 1024)])

            first += blocks

    def start_grad(self, i):
        def go(src):
            self.grad_across(i, src).start()
            self.grad_sibling(i, src).start()

        self.with_source(i, go)

    def y_copy(self, t):
        return make_remote(
            self.ysend.at[t % SLOTS], self.yrecv.at[t], self.y_s.at[t], self.y_r.at[t], self.aside
        )

    def z_copy(self, t, o):
        return make_remote(
            self.zsend.at[t % SLOTS, o - 1], self.zrecv.at[t, 3 - o], self.z_s.at[t, o - 1],
            self.z_r.at[t, 3 - o], self.along(o),
        )

    def begin(self):
        self.start_acts(0, (0,))
        self.start_grad(0)
        self.start_acts(0, (1, 2, 3))

    def begin_more(self):
        for i in range(1, AHEAD):
            self.start_grad(i)

    def store(self, t, total):
        n = t // TILES
        tile = t % TILES
        query, key, value, out, gate, up, down = self.results
        by_rows = ((0, 3, down), (9, 2, out))
        by_columns = ((3, 3, gate), (6, 3, up), (11, 2, query), (13, 1, key), (14, 1, value))
        if self.count == 1:
            layer = self.layers[0]
        else:
            layer = jnp.where(n == 0, self.layers[0], self.layers[1])
        for first, blocks, ref in by_rows:

            @pl.when((tile >= first) & (tile < first + blocks))
            def rows(first=first, ref=ref):
                ref[layer, pl.ds(pl.multiple_of((tile - first) * 32, 32), 32), :] = total

        for first, blocks, ref in by_columns:

            @pl.when((tile >= first) & (tile < first + blocks))
            def columns(first=first, ref=ref):
                ref[layer, :, pl.ds(pl.multiple_of((tile - first) * 1024, 1024), 1024)] = total

    def step(self, s):
        tiles = TILES * self.count
        t = s - 6

        @pl.when((t >= 0) & (t < tiles))
        def finish():
            total = self.zown[t % 4]
            for o in (1, 2, 3):
                self.z_copy(t, o).wait_recv()
            for o in range(3):
                total += self.zrecv[t, o].astype(jnp.float32)
            self.store(t, total)

        u = s - 4

        @pl.when((u >= 0) & (u < tiles))
        def spread():
            self.y_copy(u).wait_recv()

            def part(index):
                rows = pl.ds(pl.multiple_of(index * 32, 32), 32)
                return self.own[u % 4, rows, :] + self.yrecv[u, rows, :].astype(jnp.float32)

            @pl.when(u >= SLOTS)
            def settle():
                for o in (1, 2, 3):
                    self.z_copy(u - SLOTS, o).wait_send()

            for o in (2, 1, 3):
                self.zsend[u % SLOTS, o - 1] = part((self.z + o) % 4).astype(jnp.bfloat16)
                self.z_copy(u, o).start()
            self.zown[u % 4] = part(self.z)

        v = s - 2

        @pl.when((v >= 0) & (v < tiles))
        def compute():
            n = v // TILES
            tile = v % TILES
            gi = n * GRADS + grad_index(tile)
            ai = act_index(tile)
            for layer in range(self.count):

                @pl.when(v == TILES * layer)
                def first_acts(layer=layer):
                    self.await_acts(layer, (0,))

                @pl.when(v == TILES * layer + 3)
                def second_acts(layer=layer):
                    self.await_acts(layer, (1, 2, 3))

            @pl.when(is_new(tile))
            def fresh():
                self.grad_own(gi).wait()
                self.grad_load(gi).wait()

            @pl.when(v >= SLOTS)
            def settle():
                self.y_copy(v - SLOTS).wait_send()

            left = jnp.concatenate(
                [
                    self.abuf[n, :, 1 - self.y, ai].reshape(128, 512),
                    self.abuf[n, :, self.y, ai].reshape(128, 512),
                ],
                axis=0,
            )
            for part in range(4):
                cols = pl.ds(part * 256, 256)
                result = jnp.dot(left, self.gtile[gi % 2, :, cols], preferred_element_type=jnp.float32)
                self.ysend[v % SLOTS, :, cols] = result[:128].astype(jnp.bfloat16)
                self.own[v % 4, :, cols] = result[128:]
            self.y_copy(v).start()

        w = s - 1

        @pl.when((w >= 0) & (w < tiles) & is_new(w % TILES))
        def collect():
            gi = w // TILES * GRADS + grad_index(w % TILES)
            self.with_source(gi, lambda src: self.grad_own(gi, src).start())
            self.grad_sibling(gi).wait_recv()
            self.grad_forward(gi).wait_recv()
            self.grad_load(gi).start()

        @pl.when((s >= 0) & (s < tiles) & is_new(s % TILES))
        def forward():
            i = s // TILES * GRADS + grad_index(s % TILES)
            for layer in range(self.count):

                @pl.when(s == TILES * layer)
                def first_forward(layer=layer):
                    self.forward_acts(layer, (0,))

                @pl.when(s == TILES * layer + 3)
                def second_forward(layer=layer):
                    self.forward_acts(layer, (1, 2, 3))

            self.grad_across(i).wait_recv()
            self.grad_forward(i).start()
            for layer in range(1, self.count):

                @pl.when(i == GRADS * layer - AHEAD)
                def next_acts(layer=layer):
                    self.start_acts(layer, (0,))

                @pl.when(i == GRADS * layer - AHEAD + 1)
                def other_acts(layer=layer):
                    self.start_acts(layer, (1, 2, 3))

            @pl.when(i + AHEAD < GRADS * self.count)
            def more():
                self.start_grad(i + AHEAD)

    def steps(self):
        return TILES * self.count + 6

    def drain(self):
        for n in range(self.count):
            for k in range(4):
                for what in ("across", "relay", "sibling", "forward"):
                    self.act(n, k, what).wait_send()

        def drain_grads(i, carry):
            self.grad_across(i).wait_send()
            self.grad_sibling(i).wait_send()
            self.grad_forward(i).wait_send()
            return carry

        lax.fori_loop(0, GRADS * self.count, drain_grads, 0)

        def drain_tiles(t, carry):
            self.y_copy(t).wait_send()
            for o in (1, 2, 3):
                self.z_copy(t, o).wait_send()
            return carry

        lax.fori_loop(TILES * self.count - SLOTS, TILES * self.count, drain_tiles, 0)


class GainSum:
    def __init__(self, reducer, source, out, scratch):
        self.reducer, self.source, self.out = reducer, source, out
        self.part, self.recv, self.s, self.r = scratch

    def hop(self, i):
        red = self.reducer
        return make_remote(
            self.source if i == 0 else self.part.at[i - 1], self.recv.at[i], self.s.at[i],
            self.r.at[i], (red.across, red.sibling, red.aside)[i],
        )

    def along(self, o):
        return make_remote(
            self.part.at[2], self.recv.at[6 - o], self.s.at[2 + o], self.r.at[6 - o],
            self.reducer.along(o),
        )

    def step(self, s, first):
        @pl.when(s == first)
        def begin():
            self.hop(0).start()

        for i in range(3):

            @pl.when(s == first + 1 + i)
            def stage(i=i):
                self.hop(i).wait_recv()
                self.part[i] = (self.source[...] if i == 0 else self.part[i - 1]) + self.recv[i]
                if i < 2:
                    self.hop(i + 1).start()
                else:
                    for o in (1, 2, 3):
                        self.along(o).start()

        @pl.when(s == first + 5)
        def total():
            for o in (1, 2, 3):
                self.along(o).wait_recv()
            self.out[...] = self.part[2] + self.recv[3] + self.recv[4] + self.recv[5]

    def drain(self):
        for i in range(3):
            self.hop(i).wait_send()
            self.along(i + 1).wait_send()


def reduce_scratch(count):
    dma = pltpu.SemaphoreType.DMA
    low, wide = jnp.bfloat16, jnp.float32
    tiles, grads = TILES * count, GRADS * count
    return [
        pltpu.VMEM((count, 4, 2, ACTS, 32, 512), low),
        pltpu.VMEM((count, 4, 2, ACTS, 32, 128), low),
        pltpu.VMEM((2, 512, 1024), low),
        pltpu.VMEM((SLOTS, 128, 1024), low),
        pltpu.VMEM((tiles, 128, 1024), low),
        pltpu.VMEM((4, 128, 1024), wide),
        pltpu.VMEM((SLOTS, 3, 32, 1024), low),
        pltpu.VMEM((tiles, 3, 32, 1024), low),
        pltpu.VMEM((4, 32, 1024), wide),
        dma((count, 4)), dma((count, 4, 2)), dma((count, 4, 2)), dma((count, 4, 2)),
        dma((count, 4, 2)),
        dma((2, 2)), dma((grads,)), dma((grads,)), dma((grads,)), dma((grads,)), dma((grads,)),
        dma((grads,)),
        dma((tiles,)), dma((tiles,)), dma((tiles, 3)), dma((tiles, 3)),
    ]


def gain_scratch(rows):
    dma = pltpu.SemaphoreType.DMA
    return [
        pltpu.VMEM((3, rows, 128), jnp.float32),
        pltpu.VMEM((6, rows, 128), jnp.float32),
        dma((6,)),
        dma((6,)),
    ]


RESULTS = ((32, 2048), (32, 1024), (32, 1024), (64, 1024), (32, 3072), (32, 3072), (96, 1024))


PEERS = KEY_VALUE_HEADS
SCALE = HEAD_SIZE ** (-0.5)
NT = (((1,), (1,)), ((), ()))


GATHER_PLAN = ((0, 2048), (0, 3072), (0, 0), (1, 0), (2, 0), (2, 3072), (3, 0))
MEMBERS = len(GATHER_PLAN)
LEAD = 3


class Gatherer:
    def __init__(self, sources, outs, sems, count):
        self.sources, self.outs, self.count = sources, outs, count * MEMBERS
        (self.l_s, self.l_r, self.x_s, self.x_r, self.y_s, self.y_r, self.z_s, self.z_r,
         self.yc_s, self.yc_r, self.zc_s, self.zc_r, self.c_s, self.c_r) = sems
        c = lax.axis_index("ctx")
        x = lax.axis_index("fsdp")
        self.x = x
        self.core = c % 2
        y = c // 2 % 2
        near = c // 4 % 2
        self.sibling = (c + 1 - 2 * self.core, x)
        self.across = (c, 1 - x)
        self.aside = (c + 2 - 4 * y, x)
        self.along = (c + 4 - 8 * near, x)
        self.here = near * 2 + y
        self.by_y = near * 2 + 1 - y
        self.by_z = (1 - near) * 2 + y
        self.corner = (1 - near) * 2 + 1 - y

    def partners(self):
        return (self.sibling, self.across, self.aside, self.along)

    def window(self, i, m, owner_x, piece, share=None):
        target, column = GATHER_PLAN[m]
        half, width = self.sources[m].shape[1], self.sources[m].shape[2]
        rows = half // 8
        start = owner_x * half + (piece * 2 + self.core) * rows
        if share is not None:
            rows = rows // 2
            start = start + share * rows
        return self.outs[target].at[
            i // MEMBERS, pl.ds(pl.multiple_of(start, 16), rows), pl.ds(column, width)
        ]

    def direct(self, i, m, owner_x):
        target, column = GATHER_PLAN[m]
        half, width = self.sources[m].shape[1], self.sources[m].shape[2]
        start = owner_x * half + self.core * (half // 2)
        return self.outs[target].at[
            i // MEMBERS, pl.ds(pl.multiple_of(start, 16), half // 2), pl.ds(column, width)
        ]

    def local(self, i, m):
        target, column = GATHER_PLAN[m]
        half, width = self.sources[m].shape[1], self.sources[m].shape[2]
        rows = pl.ds(pl.multiple_of(self.x * half, 16), half)
        return make_remote(
            self.sources[m].at[i // MEMBERS],
            self.outs[target].at[i // MEMBERS, rows, pl.ds(column, width)],
            self.l_s.at[i], self.l_r.at[i], self.sibling,
        )

    def x_copy(self, i, m):
        half = self.sources[m].shape[1]
        if m == MEMBERS - 1:
            rows = pl.ds(pl.multiple_of(self.core * (half // 2), 16), half // 2)
            view = self.direct(i, m, self.x)
        else:
            rows = pl.ds(pl.multiple_of((self.here * 2 + self.core) * (half // 8), 16), half // 8)
            view = self.window(i, m, self.x, self.here)
        return make_remote(
            self.sources[m].at[i // MEMBERS, rows], view, self.x_s.at[i], self.x_r.at[i],
            self.across,
        )

    def y_copy(self, i, m):
        view = self.window(i, m, 1 - self.x, self.here)
        return make_remote(view, view, self.y_s.at[i], self.y_r.at[i], self.aside)

    def z_copy(self, i, m):
        view = self.window(i, m, 1 - self.x, self.here)
        return make_remote(view, view, self.z_s.at[i], self.z_r.at[i], self.along)

    def y_corner(self, i, m):
        view = self.window(i, m, 1 - self.x, self.by_z, 1)
        return make_remote(view, view, self.yc_s.at[i], self.yc_r.at[i], self.aside)

    def z_corner(self, i, m):
        view = self.window(i, m, 1 - self.x, self.by_y, 0)
        return make_remote(view, view, self.zc_s.at[i], self.zc_r.at[i], self.along)

    def core_copy(self, i, m, which):
        if m == MEMBERS - 1:
            view = self.direct(i, m, 1 - self.x)
        else:
            piece = (self.here, self.by_y, self.by_z, self.corner)[which]
            view = self.window(i, m, 1 - self.x, piece)
        return make_remote(
            view, view, self.c_s.at[i, which], self.c_r.at[i, which], self.sibling
        )

    def each(self, i, act, members=range(MEMBERS)):
        for m in members:

            @pl.when((i >= 0) & (i < self.count) & (i % MEMBERS == m))
            def member(m=m):
                act(m)

    def send(self, i):
        def go(m):
            self.x_copy(i, m).start()
            self.local(i, m).start()

        self.each(i, go)

    def step(self, s):
        shared = range(MEMBERS - 1)

        def spread(m):
            self.x_copy(s, m).wait_recv()
            if m < MEMBERS - 1:
                self.y_copy(s, m).start()
                self.z_copy(s, m).start()
            self.core_copy(s, m, 0).start()

        self.each(s, spread)
        self.send(s + LEAD)
        i = s - 1

        def corners(m):
            self.y_copy(i, m).wait_recv()
            self.z_corner(i, m).start()
            self.core_copy(i, m, 1).start()
            self.z_copy(i, m).wait_recv()
            self.y_corner(i, m).start()
            self.core_copy(i, m, 2).start()

        self.each(i, corners, shared)
        j = s - 2

        def last(m):
            self.y_corner(j, m).wait_recv()
            self.z_corner(j, m).wait_recv()
            self.core_copy(j, m, 3).start()

        self.each(j, last, shared)

    def steps(self):
        return self.count + 2

    def ready(self, n, m):
        i = n * MEMBERS + m
        self.local(i, m).wait_recv()
        for which in range(1 if m == MEMBERS - 1 else 4):
            self.core_copy(i, m, which).wait_recv()

    def drain(self):
        def one(i, carry):
            def go(m):
                self.local(i, m).wait_send()
                self.x_copy(i, m).wait_send()
                if m < MEMBERS - 1:
                    for copy in (self.y_copy, self.z_copy, self.y_corner, self.z_corner):
                        copy(i, m).wait_send()
                for which in range(1 if m == MEMBERS - 1 else 4):
                    self.core_copy(i, m, which).wait_send()

            self.each(i, go)
            return carry

        lax.fori_loop(0, self.count, one, 0)


def gather_scratch(count):
    dma = pltpu.SemaphoreType.DMA
    return [dma((count * MEMBERS,))] * 12 + [dma((count * MEMBERS, 4))] * 2


def head_columns(first, index):
    return pl.ds(pl.multiple_of(first + index * HEAD_SIZE, HEAD_SIZE), HEAD_SIZE)


def stream_blocks(first, count, start, wait, body):
    start(first, 0)

    def one(i, carry):
        slot = i % 2

        @pl.when(i + 1 < count)
        def following():
            start(first + i + 1, 1 - slot)

        wait(first + i, slot)
        body(first + i, slot)
        return carry

    lax.fori_loop(0, count, one, 0)


def rms(values, gain):
    r = lax.rsqrt(jnp.mean(values * values, axis=-1, keepdims=True) + norm_epsilon)
    return values * r * gain


FIRST_WORK = 4
NEXT_WORK = 7


def forward_kernel(*refs):
    count = DECODER_LAYERS
    sources, refs = refs[:MEMBERS], refs[MEMBERS:]
    (packed, tokens, live, cosine, sine, key_place, query_cap), refs = refs[:7], refs[7:]
    weights, refs = refs[:4], refs[4:]
    into_w, out_w, wide_w, down_w = weights
    (both_out, middle_out, entry_out, pre_out, kept_hbm, kept_out_hbm, kept_log_hbm), refs = (
        refs[:7], refs[7:]
    )
    (hidden_t, mid_t, attn_t, normed_t, attn_gains, mlp_gains, head_gains, output), refs = (
        refs[:8], refs[8:]
    )
    sizes = len(gather_scratch(count))
    gather = Gatherer(sources, weights, refs[:sizes], count)
    (packs, stream, middle, pre, low, attn_low, hidden_low, gate_up, cols_w, rows_w,
     kept, kept_out, kept_log, send, osend, orecv, vt,
     pack_sem, cols_sem, rows_sem, gate_sem, save_sem,
     q_s, q_r, k_s, k_r, o_s, o_r) = refs[sizes:]
    c = lax.axis_index("ctx")
    x = lax.axis_index("fsdp")
    me = c % PEERS
    z = c // 4

    def peer(r):
        return (c - me + r, x)

    barrier = pltpu.get_barrier_semaphore()

    def greet(o, carry):
        pl.semaphore_signal(barrier, inc=1, device_id=peer((me + o) % PEERS), device_id_type=MESH)
        return carry

    lax.fori_loop(1, PEERS, greet, 0)
    pl.semaphore_signal(barrier, inc=1, device_id=gather.across, device_id_type=MESH)
    pl.semaphore_wait(barrier, PEERS)

    pack_copy = make_remote(packed, packs, pack_sem.at[0], pack_sem.at[1], gather.across)
    pack_copy.start()
    for i in range(LEAD):
        gather.send(i)
    stream[...] = tokens[...].astype(jnp.float32)
    pack_copy.wait_recv()

    def gain_rows(first):
        mine = [packed[first + i : first + i + 1, :] for i in range(4)]
        other = [packs[first + i : first + i + 1, :] for i in range(4)]
        a = jnp.concatenate(mine, axis=1)
        b = jnp.concatenate(other, axis=1)
        low_side = jnp.where(x == 0, a, b)
        high_side = jnp.where(x == 0, b, a)
        return jnp.concatenate([low_side, high_side], axis=1)

    for n in range(count):
        attn_gains[n] = gain_rows(4 * n)
        mlp_gains[n] = gain_rows(8 + 4 * n)
        for k in range(2):
            row = 16 + 2 * k + n
            head_gains[n, k : k + 1, :] = packed[row : row + 1, :] + packs[row : row + 1, :]

    cos = cosine[...]
    sin = sine[...]

    def cols_copy(ref, n, column, slot):
        return pltpu.make_async_copy(
            ref.at[n, :, pl.ds(pl.multiple_of(column, 512), 512)], cols_w.at[slot],
            cols_sem.at[slot],
        )

    def rows_copy(ref, n, i, slot):
        rows = pl.ds(pl.multiple_of(i * 512, 512), 512)
        return pltpu.make_async_copy(ref.at[n, rows], rows_w.at[slot], rows_sem.at[slot])

    saves = (
        (stream, entry_out), (pre, pre_out), (middle, middle_out), (kept_out, kept_out_hbm),
        (kept_log, kept_log_hbm),
    )

    def save(n, k):
        return pltpu.make_async_copy(saves[k][0], saves[k][1].at[n], save_sem.at[k])

    def save_kept(n):
        return pltpu.make_async_copy(kept.at[n], kept_hbm.at[n], save_sem.at[5])

    def turn(source, target, n, blocks):
        def one(j, carry):
            columns = pl.ds(pl.multiple_of(j * 128, 128), 128)
            target[n, columns, :] = source[:, columns].astype(jnp.float32).T.astype(jnp.bfloat16)
            return carry

        lax.fori_loop(0, blocks, one, 0)

    def key_copy(n, r, slot):
        return make_remote(
            send.at[r, pl.ds(2, 2)], kept.at[n, slot, pl.ds(2, 2)], k_s.at[r], k_r.at[slot], peer(r)
        )

    def query_copy(n, r, slot):
        return make_remote(
            send.at[r, pl.ds(0, 2)], kept.at[n, slot, pl.ds(0, 2)], q_s.at[r], q_r.at[slot], peer(r)
        )

    def out_copy(r, slot):
        return make_remote(osend.at[r], orecv.at[slot], o_s.at[r], o_r.at[slot], peer(r))

    def project(n):
        save(n, 0).start()
        low[...] = rms(stream[...], attn_gains[n]).astype(jnp.bfloat16)
        turn(low, normed_t, n, 8)
        for m in range(3):
            gather.ready(n, m)

        def column(i):
            return (i + 4) % 8 * 512

        def body(i, slot):
            pre[:, pl.ds(pl.multiple_of(column(i), 512), 512)] = jnp.dot(
                low[...], cols_w[slot], preferred_element_type=jnp.float32
            )

        stream_blocks(
            0,
            8,
            lambda i, slot: cols_copy(into_w, n, column(i), slot).start(),
            lambda i, slot: cols_copy(into_w, n, column(i), slot).wait(),
            body,
        )
        save(n, 1).start()

        def turned(first, index, gain):
            v = rms(pre[:, head_columns(first, index)], gain)
            return (v * cos + pltpu.roll(v, HEAD_SIZE // 2, 1) * sin).astype(jnp.bfloat16)

        def make_keys(o, carry):
            r = (me + o) % PEERS
            key = turned(2048, r, head_gains[n, 1:2, :])
            value = pre[:, head_columns(3072, r)].astype(jnp.bfloat16)

            @pl.when(o < PEERS)
            def away():
                send[r, 2] = key
                send[r, 3] = value
                key_copy(n, r, me).start()

            @pl.when(o == PEERS)
            def home():
                kept[n, me, 2] = key
                kept[n, me, 3] = value

            return carry

        def make_queries(o, carry):
            r = (me + o) % PEERS
            first = turned(0, 2 * r, head_gains[n, 0:1, :])
            second = turned(0, 2 * r + 1, head_gains[n, 0:1, :])

            @pl.when(o < PEERS)
            def away():
                send[r, 0] = first
                send[r, 1] = second
                query_copy(n, r, me).start()

            @pl.when(o == PEERS)
            def home():
                kept[n, me, 0] = first
                kept[n, me, 1] = second

            return carry

        lax.fori_loop(1, PEERS + 1, make_keys, 0)
        lax.fori_loop(1, PEERS + 1, make_queries, 0)

    def attention(n):
        def await_keys(o, carry):
            key_copy(n, me, (me + o) % PEERS).wait_recv()
            return carry

        lax.fori_loop(1, PEERS, await_keys, 0)

        def turn_values(j, carry):
            vt[j] = kept[n, j, 3].astype(jnp.float32).T.astype(jnp.bfloat16)
            return carry

        lax.fori_loop(0, PEERS, turn_values, 0)

        def block(o, carry):
            j = (me + o) % PEERS

            @pl.when(o > 0)
            def arrived():
                query_copy(n, me, j).wait_recv()

            queries = kept[n, j, 0:2].reshape(2 * 128, HEAD_SIZE)
            keys = kept[n, :, 2].reshape(PEERS * 128, HEAD_SIZE)
            scores = lax.dot_general(keys, queries, NT, preferred_element_type=jnp.float32) * SCALE
            allowed = key_place[...] <= query_cap[j]
            scores = jnp.where(allowed, scores, masked_logits)
            highest = jnp.max(scores, axis=0, keepdims=True)
            expo = jnp.exp(scores - highest)
            total = jnp.sum(expo, axis=0, keepdims=True)
            expo_low = expo.astype(jnp.bfloat16)
            turned_out = jnp.zeros((HEAD_SIZE, 256), jnp.float32)
            for i in range(PEERS):
                turned_out += jnp.dot(
                    vt[i], expo_low[i * 128 : (i + 1) * 128], preferred_element_type=jnp.float32
                )
            turned_out = turned_out / total
            kept_out[j] = turned_out
            kept_log[j] = jnp.broadcast_to(highest + jnp.log(total), (8, 256))
            attended = turned_out.T.astype(jnp.bfloat16).reshape(2, 128, HEAD_SIZE)

            @pl.when(o == 0)
            def home():
                orecv[me] = attended

            @pl.when(o > 0)
            def away():
                osend[j] = attended
                out_copy(j, me).start()

            return carry

        lax.fori_loop(0, PEERS, block, 0)
        save(n, 3).start()
        save(n, 4).start()
        save_kept(n).start()

    def close_attention(n):
        def collect(o, carry):
            h = (me + o) % PEERS

            @pl.when(o > 0)
            def arrived():
                out_copy(me, h).wait_recv()

            attn_low[:, head_columns(0, 2 * h)] = orecv[h, 0]
            attn_low[:, head_columns(0, 2 * h + 1)] = orecv[h, 1]
            return carry

        lax.fori_loop(0, PEERS, collect, 0)
        save(n, 0).wait()
        middle[...] = stream[...]
        gather.ready(n, 3)

        def body(i, slot):
            columns = pl.ds(pl.multiple_of(i * 512, 512), 512)
            middle[...] += jnp.dot(
                attn_low[:, columns], rows_w[slot], preferred_element_type=jnp.float32
            )

        stream_blocks(
            0,
            4,
            lambda i, slot: rows_copy(out_w, n, i, slot).start(),
            lambda i, slot: rows_copy(out_w, n, i, slot).wait(),
            body,
        )
        save(n, 2).start()
        turn(attn_low, attn_t, n, 16)
        low[...] = rms(middle[...], mlp_gains[n]).astype(jnp.bfloat16)
        turn(low, mid_t, n, 8)

        def settle(o, carry):
            r = (me + o) % PEERS
            key_copy(n, r, me).wait_send()
            query_copy(n, r, me).wait_send()
            out_copy(r, me).wait_send()
            return carry

        lax.fori_loop(1, PEERS, settle, 0)

    def gate_copy(n, i, slot, k):
        columns = pl.ds(pl.multiple_of(k * 3072 + i * 512, 512), 512)
        return pltpu.make_async_copy(
            gate_up.at[slot, k], both_out.at[n, :, columns], gate_sem.at[slot, k]
        )

    def widen(n):
        gather.ready(n, 4)
        gather.ready(n, 5)

        def column(i):
            return i % 2 * 3072 + i // 2 * 512

        def body(i, slot):
            k = i % 2
            at = i // 2
            held = at % 2

            @pl.when(i >= 4)
            def settle():
                gate_copy(n, at - 2, held, k).wait()

            gate_up[held, k] = jnp.dot(
                low[...], cols_w[slot], preferred_element_type=jnp.float32
            )
            gate_copy(n, at, held, k).start()

            @pl.when(k == 1)
            def finish():
                gate = gate_up[held, 0]
                columns = pl.ds(pl.multiple_of(at * 512, 512), 512)
                hidden_low[:, columns] = (
                    gate * jax.nn.sigmoid(gate) * gate_up[held, 1]
                ).astype(jnp.bfloat16)

        stream_blocks(
            0,
            12,
            lambda i, slot: cols_copy(wide_w, n, column(i), slot).start(),
            lambda i, slot: cols_copy(wide_w, n, column(i), slot).wait(),
            body,
        )
        for at in (4, 5):
            for k in range(2):
                gate_copy(n, at, at % 2, k).wait()

    def narrow(n):
        turn(hidden_low, hidden_t, n, 24)
        gather.ready(n, 6)
        stream[...] = middle[...]

        def body(i, slot):
            columns = pl.ds(pl.multiple_of(i * 512, 512), 512)
            stream[...] += jnp.dot(
                hidden_low[:, columns], rows_w[slot], preferred_element_type=jnp.float32
            )

        stream_blocks(
            0,
            6,
            lambda i, slot: rows_copy(down_w, n, i, slot).start(),
            lambda i, slot: rows_copy(down_w, n, i, slot).wait(),
            body,
        )
        for k in range(1, 5):
            save(n, k).wait()
        save_kept(n).wait()

    def step(w, carry):
        gather.step(w)
        n = jnp.where(w >= FIRST_WORK + NEXT_WORK, 1, 0)
        phase = w - FIRST_WORK - n * NEXT_WORK
        for at, work in enumerate((project, attention, close_attention, widen, narrow)):

            @pl.when(phase == at)
            def piece(work=work):
                work(n)

        return carry

    lax.fori_loop(0, FIRST_WORK + NEXT_WORK + 5, step, 0)
    output[...] = (stream[...] * live[...]).astype(jnp.bfloat16)
    gather.drain()
    pack_copy.wait_send()


def forward(weights, packed, tokens, live, cosine, sine, key_place, query_cap, number):
    count = DECODER_LAYERS
    dma = pltpu.SemaphoreType.DMA
    low, wide = jnp.bfloat16, jnp.float32
    pair = pltpu.VMEM((PEERS, 2, 128, HEAD_SIZE), low)
    anywhere = pl.BlockSpec(memory_space=pl.ANY)
    near = pl.BlockSpec(memory_space=pltpu.VMEM)
    gathered = [(1024, 4096), (2048, 1024), (1024, 6144), (3072, 1024)]
    saved = [
        ((128, 6144), wide), ((128, 1024), wide), ((128, 1024), wide), ((128, 4096), wide),
        ((PEERS, 4, 128, HEAD_SIZE), low), ((PEERS, HEAD_SIZE, 256), wide), ((PEERS, 8, 256), wide),
    ]
    turned = [(3072, 128), (1024, 128), (2048, 128), (1024, 128)]
    results = (
        [((count,) + s, low) for s in gathered]
        + [((count,) + s, d) for s, d in saved]
        + [((count,) + s, low) for s in turned]
        + [((count, 1, 1024), wide)] * 2
        + [((count, 2, HEAD_SIZE), wide), ((128, 1024), low)]
    )
    return pl.pallas_call(
        forward_kernel,
        out_shape=[jax.ShapeDtypeStruct(s, d) for s, d in results],
        in_specs=[anywhere] * MEMBERS + [near] * 7,
        out_specs=[anywhere] * 11 + [near] * 8,
        scratch_shapes=gather_scratch(count)
        + [
            pltpu.VMEM(packed.shape, wide),
            pltpu.VMEM((128, 1024), wide),
            pltpu.VMEM((128, 1024), wide),
            pltpu.VMEM((128, 4096), wide),
            pltpu.VMEM((128, 1024), low),
            pltpu.VMEM((128, 2048), low),
            pltpu.VMEM((128, 3072), low),
            pltpu.VMEM((2, 2, 128, 512), wide),
            pltpu.VMEM((2, 1024, 512), low),
            pltpu.VMEM((2, 512, 1024), low),
            pltpu.VMEM((count, PEERS, 4, 128, HEAD_SIZE), low),
            pltpu.VMEM((PEERS, HEAD_SIZE, 256), wide),
            pltpu.VMEM((PEERS, 8, 256), wide),
            pltpu.VMEM((PEERS, 4, 128, HEAD_SIZE), low),
            pair,
            pair,
            pltpu.VMEM((PEERS, HEAD_SIZE, 128), low),
            dma((2,)), dma((2,)), dma((2,)), dma((2, 2)), dma((6,)),
        ]
        + [dma((PEERS,))] * 6,
        compiler_params=pltpu.CompilerParams(
            collective_id=number, has_side_effects=True, vmem_limit_bytes=56 * 2**20
        ),
        name="forward",
    )(*weights, packed, tokens, live, cosine, sine, key_place, query_cap)


WORK = 12


def rms_back(values, gain, upstream):
    r = lax.rsqrt(jnp.mean(values * values, axis=-1, keepdims=True) + norm_epsilon)
    weighted = upstream * gain
    mean = jnp.mean(weighted * values, axis=-1, keepdims=True)
    grad = r * weighted - values * (r * r * r) * mean
    return grad, jnp.sum(upstream * values * r, axis=0, keepdims=True)


def backward_kernel(*refs):
    count = DECODER_LAYERS
    acts, stored, refs = refs[:4], refs[4:11], refs[11:]
    (into_w, out_w, wide_w, down_w) = refs[:4]
    (upstream, cosine, sine, attn_gains, mlp_gains, head_gains, key_place, query_cap) = refs[4:12]
    results = refs[12:19]
    grad_stream, gain_out, held = refs[19:22]
    refs = refs[22:]
    sizes = len(reduce_scratch(count))
    reduce_refs, refs = refs[:sizes], refs[sizes:]
    gain_refs, refs = refs[:4], refs[4:]
    (down_low, both_low, out_low, pre_low, terms,
     gate_up, middle, entry, pre, kept, kept_out, kept_log, mid_grad, rows_w, wide_rows,
     dsend, drecv, qsend, qrecv, ksend, krecv, kt, key_sum, value_sum,
     load_sem, rows_sem, wide_sem, gate_sem, d_s, d_r, q_s, q_r, k_s, k_r) = refs
    reducer = Reducer(
        acts, ((down_low, 1), (both_low, 6), (out_low, 1), (pre_low, 4)), results,
        (held,) + tuple(reduce_refs), tuple(reversed(range(count))),
    )
    gain_sum = GainSum(reducer, terms, gain_out, gain_refs)
    c = lax.axis_index("ctx")
    x = lax.axis_index("fsdp")
    me = c % PEERS
    z = c // 4

    def peer(r):
        return (c - me + r, x)

    barrier = pltpu.get_barrier_semaphore()

    def greet(o, carry):
        pl.semaphore_signal(barrier, inc=1, device_id=peer((me + o) % PEERS), device_id_type=MESH)
        return carry

    lax.fori_loop(1, PEERS, greet, 0)
    pl.semaphore_signal(barrier, inc=1, device_id=reducer.across, device_id_type=MESH)
    for o in range(2):
        far = ((z // 2 * 2 + 2) % 4 + o) * 4 + c % 4
        pl.semaphore_signal(barrier, inc=1, device_id=(far, x), device_id_type=MESH)
    pl.semaphore_wait(barrier, PEERS + 2)

    grad_stream[...] = upstream[...]
    terms[...] = jnp.zeros_like(terms)
    reducer.start_acts(0, (0,))

    cos = cosine[...]
    sin = sine[...]

    def grad_copy(r, slot):
        return make_remote(dsend.at[r], drecv.at[slot], d_s.at[r], d_r.at[slot], peer(r))

    def query_copy(r, slot):
        return make_remote(qsend.at[r], qrecv.at[slot], q_s.at[r], q_r.at[slot], peer(r))

    def key_copy(r, slot):
        return make_remote(ksend.at[r], krecv.at[slot], k_s.at[r], k_r.at[slot], peer(r))

    saved = (middle, entry, pre, kept, kept_out, kept_log)

    def load(layer, k):
        return pltpu.make_async_copy(stored[1 + k].at[layer], saved[k], load_sem.at[k])

    def await_load(k):
        load(0, k).wait()

    def add_term(layer, first, term):
        for i in range(8):
            terms[pl.ds(layer * 24 + first + i, 1), :] = term[:, i * 128 : (i + 1) * 128]

    def rows_copy(ref, layer, i, slot):
        rows = pl.ds(pl.multiple_of(i * 512, 512), 512)
        return pltpu.make_async_copy(ref.at[layer, rows], rows_w.at[slot], rows_sem.at[slot])

    def wide_copy(ref, layer, i, slot):
        rows = pl.ds(pl.multiple_of(i * 128, 128), 128)
        columns = ref.shape[2]
        return pltpu.make_async_copy(
            ref.at[layer, rows], wide_rows.at[slot, :, pl.ds(0, columns)], wide_sem.at[slot]
        )

    def hidden_part(n, layer, part):
        @pl.when(part == 0)
        def opening():
            for k in range(len(saved)):
                load(layer, k).start()
            down_low[n] = grad_stream[...].astype(jnp.bfloat16)

        @pl.when((n == 0) & (part == 0))
        def first():
            reducer.start_grad(0)
            reducer.start_acts(0, (1, 2, 3))

        def gate_copy(i, slot, k):
            columns = pl.ds(pl.multiple_of(k * 3072 + i * 512, 512), 512)
            return pltpu.make_async_copy(
                stored[0].at[layer, :, columns], gate_up.at[slot, k], gate_sem.at[slot, k]
            )

        def start(i, slot):
            rows_copy(down_w, layer, i, slot).start()
            for k in range(2):
                gate_copy(i, slot, k).start()

        def wait(i, slot):
            rows_copy(down_w, layer, i, slot).wait()
            for k in range(2):
                gate_copy(i, slot, k).wait()

        def body(i, slot):
            hidden = lax.dot_general(
                down_low[n], rows_w[slot], NT, preferred_element_type=jnp.float32
            )
            gate = gate_up[slot, 0]
            up = gate_up[slot, 1]
            sigmoid = jax.nn.sigmoid(gate)
            columns = pl.multiple_of(i * 512, 512)
            both_low[n, :, pl.ds(columns, 512)] = (
                hidden * up * sigmoid * (1.0 + gate * (1.0 - sigmoid))
            ).astype(jnp.bfloat16)
            both_low[n, :, pl.ds(3072 + columns, 512)] = (hidden * gate * sigmoid).astype(
                jnp.bfloat16
            )

        stream_blocks(part * 3, 3, start, wait, body)

        @pl.when((n == 0) & (part == 1))
        def rest():
            reducer.begin_more()

    def middle_part(n, layer, part):
        def body(i, slot):
            mid_grad[:, pl.ds(pl.multiple_of(i * 128, 128), 128)] = lax.dot_general(
                both_low[n], wide_rows[slot], NT, preferred_element_type=jnp.float32
            )

        stream_blocks(
            part * 3,
            jnp.where(part == 2, 2, 3),
            lambda i, slot: wide_copy(wide_w, layer, i, slot).start(),
            lambda i, slot: wide_copy(wide_w, layer, i, slot).wait(),
            body,
        )

        @pl.when(part == 2)
        def closing():
            await_load(0)
            grad, term = rms_back(middle[...], mlp_gains[layer], mid_grad[...])
            add_term(layer, 8, term)
            total = grad_stream[...] + grad
            grad_stream[...] = total
            out_low[n] = total.astype(jnp.bfloat16)

    def out_part(n, layer):
        def place(i):
            return (i + me // 2) % 4

        def body(i, slot):
            low = lax.dot_general(
                out_low[n], rows_w[slot], NT, preferred_element_type=jnp.float32
            ).astype(jnp.bfloat16)
            for k in range(2):
                r = 2 * place(i) + k

                @pl.when(r == me)
                def home(k=k):
                    for j in range(2):
                        at = (2 * k + j) * HEAD_SIZE
                        drecv[me, j] = low[:, at : at + HEAD_SIZE]

                @pl.when(r != me)
                def away(k=k, r=r):
                    for j in range(2):
                        at = (2 * k + j) * HEAD_SIZE
                        dsend[r, j] = low[:, at : at + HEAD_SIZE]
                    grad_copy(r, me).start()

        stream_blocks(
            0,
            4,
            lambda i, slot: rows_copy(out_w, layer, place(i), slot).start(),
            lambda i, slot: rows_copy(out_w, layer, place(i), slot).wait(),
            body,
        )
        for k in range(2, len(saved)):
            await_load(k)

        def turn_keys(j, carry):
            kt[j] = kept[j, 2].astype(jnp.float32).T.astype(jnp.bfloat16)
            return carry

        lax.fori_loop(0, PEERS, turn_keys, 0)
        key_sum[...] = jnp.zeros_like(key_sum)
        value_sum[...] = jnp.zeros_like(value_sum)

    def attention_block(o):
        j = (me + o) % PEERS

        @pl.when(o > 0)
        def arrived():
            grad_copy(me, j).wait_recv()

        grads = drecv[j].reshape(2 * 128, HEAD_SIZE)
        delta = jnp.sum(grads.astype(jnp.float32).T * kept_out[j], axis=0, keepdims=True)
        queries = kept[j, 0:2].reshape(2 * 128, HEAD_SIZE)
        keys = kept[:, 2].reshape(PEERS * 128, HEAD_SIZE)
        values = kept[:, 3].reshape(PEERS * 128, HEAD_SIZE)
        scores = lax.dot_general(keys, queries, NT, preferred_element_type=jnp.float32) * SCALE
        allowed = key_place[...] <= query_cap[j]
        scores = jnp.where(allowed, scores, masked_logits)
        prob = jnp.exp(scores - kept_log[j, 0:1, :])
        dprob = lax.dot_general(values, grads, NT, preferred_element_type=jnp.float32)
        dscore = (prob * (dprob - delta)).astype(jnp.bfloat16)
        value_sum[...] += jnp.dot(
            prob.astype(jnp.bfloat16), grads, preferred_element_type=jnp.float32
        )
        key_sum[...] += jnp.dot(dscore, queries, preferred_element_type=jnp.float32)
        turned = jnp.zeros((HEAD_SIZE, 256), jnp.float32)
        for i in range(PEERS):
            turned += jnp.dot(
                kt[i], dscore[i * 128 : (i + 1) * 128], preferred_element_type=jnp.float32
            )
        query_grad = (turned * SCALE).T.astype(jnp.bfloat16).reshape(2, 128, HEAD_SIZE)

        @pl.when(o == 0)
        def home():
            qrecv[me] = query_grad

        @pl.when(o > 0)
        def away():
            qsend[j] = query_grad
            query_copy(j, me).start()

        @pl.when(o == PEERS - 1)
        def keys_done():
            lax.fori_loop(1, PEERS + 1, push_keys, 0)

    def push_keys(o, carry):
        j = (me + o) % PEERS
        rows = pl.ds(pl.multiple_of(j * 128, 128), 128)
        key = (key_sum[rows, :] * SCALE).astype(jnp.bfloat16)
        value = value_sum[rows, :].astype(jnp.bfloat16)

        @pl.when(o < PEERS)
        def away():
            ksend[j, 0] = key
            ksend[j, 1] = value
            key_copy(j, me).start()

        @pl.when(o == PEERS)
        def home():
            krecv[me, 0] = key
            krecv[me, 1] = value

        return carry

    def head_part(n, layer):
        def back(grad, first, index, gain):
            g = grad.astype(jnp.float32)
            dy = g * cos - pltpu.roll(g, HEAD_SIZE // 2, 1) * sin
            low, term = rms_back(pre[:, head_columns(first, index)], gain, dy)
            return low.astype(jnp.bfloat16), term

        def finish_queries(o, total):
            h = (me + o) % PEERS

            @pl.when(o > 0)
            def arrived():
                query_copy(me, h).wait_recv()

            for i in range(2):
                low, term = back(qrecv[h, i], 0, 2 * h + i, head_gains[layer, 0:1, :])
                pre_low[n, :, head_columns(0, 2 * h + i)] = low
                total += term
            return total

        zero = jnp.zeros((1, HEAD_SIZE), jnp.float32)
        terms[pl.ds(layer * 24 + 16, 1), :] = lax.fori_loop(0, PEERS, finish_queries, zero)

        def finish_keys(o, total):
            h = (me + o) % PEERS

            @pl.when(o > 0)
            def arrived():
                key_copy(me, h).wait_recv()

            low, term = back(krecv[h, 0], 2048, h, head_gains[layer, 1:2, :])
            pre_low[n, :, head_columns(2048, h)] = low
            pre_low[n, :, head_columns(3072, h)] = krecv[h, 1]
            return total + term

        terms[pl.ds(layer * 24 + 17, 1), :] = lax.fori_loop(0, PEERS, finish_keys, zero)

        def settle(o, carry):
            r = (me + o) % PEERS
            grad_copy(r, me).wait_send()
            query_copy(r, me).wait_send()
            key_copy(r, me).wait_send()
            return carry

        lax.fori_loop(1, PEERS, settle, 0)

    def entry_part(n, layer, part):
        def body(i, slot):
            mid_grad[:, pl.ds(pl.multiple_of(i * 128, 128), 128)] = lax.dot_general(
                pre_low[n], wide_rows[slot, :, 0:4096], NT, preferred_element_type=jnp.float32
            )

        stream_blocks(
            part * 4,
            4,
            lambda i, slot: wide_copy(into_w, layer, i, slot).start(),
            lambda i, slot: wide_copy(into_w, layer, i, slot).wait(),
            body,
        )

        @pl.when(part == 1)
        def closing():
            await_load(1)
            grad, term = rms_back(entry[...], attn_gains[layer], mid_grad[...])
            add_term(layer, 0, term)
            grad_stream[...] += grad

    def step(w, carry):
        reducer.step(w - 2)
        gain_sum.step(w, WORK * count)
        n = w // WORK
        phase = w % WORK
        layer = count - 1 - n
        busy = w < WORK * count

        @pl.when(busy & (phase < 2))
        def phase_hidden():
            hidden_part(n, layer, phase)

        @pl.when(busy & (phase >= 2) & (phase < 5))
        def phase_middle():
            middle_part(n, layer, phase - 2)

        @pl.when(busy & (phase == 5))
        def phase_out():
            out_part(n, layer)

        @pl.when(busy & (phase >= 6) & (phase < 9))
        def phase_attention():
            first = (phase - 6) * 3

            def block(i, inner):
                attention_block(first + i)
                return inner

            lax.fori_loop(0, jnp.minimum(3, PEERS - first), block, 0)

        @pl.when(busy & (phase == 9))
        def phase_heads():
            head_part(n, layer)

        @pl.when(busy & (phase >= 10))
        def phase_entry():
            entry_part(n, layer, phase - 10)

        return carry

    lax.fori_loop(0, reducer.steps() + 2, step, 0)
    reducer.drain()
    gain_sum.drain()


RESULTS = ((32, 2048), (32, 1024), (32, 1024), (64, 1024), (32, 3072), (32, 3072), (96, 1024))


def backward(acts, saved, weights, upstream, cosine, sine, gains, key_place, query_cap, number):
    count = DECODER_LAYERS
    dma = pltpu.SemaphoreType.DMA
    low, wide = jnp.bfloat16, jnp.float32
    pair = pltpu.VMEM((PEERS, 2, 128, HEAD_SIZE), low)
    anywhere = pl.BlockSpec(memory_space=pl.ANY)
    near = pl.BlockSpec(memory_space=pltpu.VMEM)
    return pl.pallas_call(
        backward_kernel,
        out_shape=[jax.ShapeDtypeStruct((count,) + shape, wide) for shape in RESULTS]
        + [
            jax.ShapeDtypeStruct((128, 1024), wide),
            jax.ShapeDtypeStruct((24 * count, 128), wide),
            jax.ShapeDtypeStruct((GRADS * count, 384, 1024), low),
        ],
        in_specs=[anywhere] * 15 + [near] * 8,
        out_specs=[near] * 9 + [anywhere],
        scratch_shapes=reduce_scratch(count)
        + gain_scratch(24 * count)
        + [
            pltpu.VMEM((count, 128, 1024), low),
            pltpu.VMEM((count, 128, 6144), low),
            pltpu.VMEM((count, 128, 1024), low),
            pltpu.VMEM((count, 128, 4096), low),
            pltpu.VMEM((24 * count, 128), wide),
            pltpu.VMEM((2, 2, 128, 512), wide),
            pltpu.VMEM((128, 1024), wide),
            pltpu.VMEM((128, 1024), wide),
            pltpu.VMEM((128, 4096), wide),
            pltpu.VMEM((PEERS, 4, 128, HEAD_SIZE), low),
            pltpu.VMEM((PEERS, HEAD_SIZE, 256), wide),
            pltpu.VMEM((PEERS, 8, 256), wide),
            pltpu.VMEM((128, 1024), wide),
            pltpu.VMEM((2, 512, 1024), low),
            pltpu.VMEM((2, 128, 6144), low),
        ]
        + [pair] * 6
        + [
            pltpu.VMEM((PEERS, HEAD_SIZE, 128), low),
            pltpu.VMEM((PEERS * 128, HEAD_SIZE), wide),
            pltpu.VMEM((PEERS * 128, HEAD_SIZE), wide),
            dma((6,)), dma((2,)), dma((2,)), dma((2, 2)),
        ]
        + [dma((PEERS,))] * 6,
        compiler_params=pltpu.CompilerParams(
            collective_id=number, has_side_effects=True, vmem_limit_bytes=62 * 2**20
        ),
        name="backward",
    )(*acts, *saved, *weights, upstream, cosine, sine, *gains, key_place, query_cap)


def from_partner(shard, axis, apart):
    return lax.ppermute(shard, axis, [(i, i ^ 1 << apart) for i in range(lax.axis_size(axis))])


def token_places(stretch_table, slot_lengths):
    ctx_count = stretch_table.shape[0]
    stretch_order = stretch_table.reshape(-1)
    within = jnp.arange(STRETCH, dtype=jnp.int32)
    places = (stretch_order % ctx_count * STRETCH)[:, None] + within[None, :]
    slot_ids = jnp.broadcast_to((stretch_order // ctx_count)[:, None], places.shape).reshape(-1)
    places = places.reshape(-1)
    limits = jnp.where(slot_ids == 0, slot_lengths[0], slot_lengths[1])
    return (places, slot_ids, places < limits)


def rotary_tables(places):
    half_dim = HEAD_SIZE // 2
    spread = jnp.arange(half_dim, dtype=jnp.int32).astype(jnp.float32) * (2.0 / HEAD_SIZE)
    inverse = jnp.exp(spread * -math.log(rope_base))
    angles = places.astype(jnp.float32)[:, None] * inverse[None, :]
    return (
        jnp.concatenate([jnp.cos(angles)] * 2, axis=-1),
        jnp.concatenate([jnp.sin(angles)] * 2, axis=-1),
    )


def rotate(values, cosine_table, sine_table):
    half_dim = values.shape[-1] // 2
    turned = jnp.concatenate([-values[..., half_dim:], values[..., :half_dim]], axis=-1)
    return values * cosine_table[:, None, :] + turned * sine_table[:, None, :]


def unrotate(upstream, cosine_table, sine_table):
    half_dim = upstream.shape[-1] // 2
    scaled_sine = upstream * sine_table[:, None, :]
    turned_back = jnp.concatenate(
        [scaled_sine[..., half_dim:], -scaled_sine[..., :half_dim]], axis=-1
    )
    return upstream * cosine_table[:, None, :] + turned_back


def norm_forward(values, gain_vec):
    scale_inv = lax.rsqrt(jnp.mean(values * values, axis=-1, keepdims=True) + norm_epsilon)
    return (values * scale_inv * gain_vec, scale_inv)


def norm_backward(values, scale_inv, gain_vec, upstream):
    weighted = upstream * gain_vec
    grad_input = scale_inv * weighted - values * scale_inv**3 * jnp.mean(
        weighted * values, axis=-1, keepdims=True
    )
    gain_term = jnp.sum((upstream * values * scale_inv).reshape(-1, values.shape[-1]), axis=0)
    return (grad_input, gain_term)


def upper_bit(local_index, bit_number):
    return local_index // 2**bit_number % 2 == 1


def joined_rows(mine, received, upper_side):
    first_rows = jnp.where(upper_side, received, mine)
    second_rows = jnp.where(upper_side, mine, received)
    return jnp.concatenate([first_rows, second_rows], axis=0)


def half_gather(pair, local_index):
    gathered_rows = pair
    for bit_number in range(lax.axis_size("ctx").bit_length() - 2):
        received = from_partner(gathered_rows, "ctx", bit_number)
        gathered_rows = joined_rows(gathered_rows, received, upper_bit(local_index, bit_number))
    return gathered_rows


def half_reduce(term, local_index):
    for bit_number in reversed(range(lax.axis_size("ctx").bit_length() - 2)):
        span = term.shape[0] // 2
        lower_rows = term[:span]
        upper_rows = term[span:]
        upper_side = upper_bit(local_index, bit_number)
        kept_rows = jnp.where(upper_side, upper_rows, lower_rows)
        sent_rows = jnp.where(upper_side, lower_rows, upper_rows)
        term = kept_rows + from_partner(sent_rows, "ctx", bit_number)
    return term


def over_keys(update, carried, count_rows):
    block_length = math.gcd(count_rows, 512)

    def inner_step(current, block_index):
        return (update(current, block_index * block_length, block_length), None)

    carried, unused = lax.scan(
        inner_step, carried, jnp.arange(count_rows // block_length, dtype=jnp.int32)
    )
    return carried


def allowed_mask(key_meta, query_meta, row_start, block_length):
    key_places = lax.dynamic_slice_in_dim(key_meta[0], row_start, block_length)
    key_slots = lax.dynamic_slice_in_dim(key_meta[1], row_start, block_length)
    key_live = lax.dynamic_slice_in_dim(key_meta[2], row_start, block_length)
    allowed = (
        (key_slots[None, :] == query_meta[1][:, None])
        & (key_places[None, :] <= query_meta[0][:, None])
        & key_live[None, :]
    )
    return allowed[None, None]


def forward_update(
    current, query_head_group, key_tile_block, value_tile_block, allowed, score_scale
):
    running_max, running_sum, running_acc = current
    block_length = key_tile_block.shape[0]
    key_head_list = key_tile_block.reshape(block_length, KEY_VALUE_HEADS, HEAD_SIZE)
    value_head_list = value_tile_block.reshape(block_length, KEY_VALUE_HEADS, HEAD_SIZE)
    scores = (
        jnp.einsum(
            "qhgd,khd->hgqk", query_head_group, key_head_list, preferred_element_type=jnp.float32
        )
        * score_scale
    )
    scores = jnp.where(allowed, scores, masked_logits)
    new_max = jnp.maximum(running_max, jnp.max(scores, axis=-1))
    factor = jnp.exp(running_max - new_max)
    prob_block = jnp.where(allowed, jnp.exp(scores - new_max[..., None]), 0.0)
    new_sum = running_sum * factor + jnp.sum(prob_block, axis=-1)
    new_acc = running_acc * factor[..., None] + jnp.einsum(
        "hgqk,khd->hgqd",
        prob_block.astype(jnp.bfloat16),
        value_head_list,
        preferred_element_type=jnp.float32,
    )
    return (new_max, new_sum, new_acc)


def score_parts(
    query_head_group,
    output_grad_group,
    key_tile_block,
    value_tile_block,
    allowed,
    log_total,
    row_delta,
    score_scale,
):
    block_length = key_tile_block.shape[0]
    key_head_list = key_tile_block.reshape(block_length, KEY_VALUE_HEADS, HEAD_SIZE)
    value_head_list = value_tile_block.reshape(block_length, KEY_VALUE_HEADS, HEAD_SIZE)
    scores = (
        jnp.einsum(
            "qhgd,khd->hgqk", query_head_group, key_head_list, preferred_element_type=jnp.float32
        )
        * score_scale
    )
    prob_block = jnp.where(allowed, jnp.exp(scores - log_total[..., None]), 0.0)
    dprob = jnp.einsum(
        "qhgd,khd->hgqk", output_grad_group, value_head_list, preferred_element_type=jnp.float32
    )
    dscore_low = (prob_block * (dprob - row_delta[..., None])).astype(jnp.bfloat16)
    return (prob_block, dscore_low, key_head_list)


def attention_inputs(stream, gathered, cosine_table, sine_table):
    count_rows = stream.shape[0]
    normalized, inv_attn = norm_forward(stream, gathered[7].astype(jnp.float32))
    normed_low = normalized.astype(jnp.bfloat16)
    query_heads = jnp.dot(normed_low, gathered[0], preferred_element_type=jnp.float32).reshape(
        count_rows, QUERY_HEADS, HEAD_SIZE
    )
    key_head_list = jnp.dot(normed_low, gathered[1], preferred_element_type=jnp.float32).reshape(
        count_rows, KEY_VALUE_HEADS, HEAD_SIZE
    )
    value_low = jnp.dot(normed_low, gathered[2], preferred_element_type=jnp.float32).astype(
        jnp.bfloat16
    )
    query_normed, inv_query = norm_forward(query_heads, gathered[9].astype(jnp.float32))
    key_normed, inv_key = norm_forward(key_head_list, gathered[10].astype(jnp.float32))
    query_lowered = rotate(query_normed, cosine_table, sine_table).astype(jnp.bfloat16)
    key_low = (
        rotate(key_normed, cosine_table, sine_table)
        .astype(jnp.bfloat16)
        .reshape(count_rows, KEY_VALUE_HEADS * HEAD_SIZE)
    )
    return {
        "normed_low": normed_low,
        "inv_attn": inv_attn,
        "query_heads": query_heads,
        "inv_query": inv_query,
        "key_heads": key_head_list,
        "inv_key": inv_key,
        "query_low": query_lowered,
        "key_low": key_low,
        "value_low": value_low,
    }


def block_rest(stream, gathered, attn_low):
    middle = stream + jnp.dot(attn_low, gathered[3], preferred_element_type=jnp.float32)
    normed_mid, inv_mid = norm_forward(middle, gathered[8].astype(jnp.float32))
    normed_mid_low = normed_mid.astype(jnp.bfloat16)
    gate_act = jnp.dot(normed_mid_low, gathered[4], preferred_element_type=jnp.float32)
    upward = jnp.dot(normed_mid_low, gathered[5], preferred_element_type=jnp.float32)
    hidden_low = (jax.nn.silu(gate_act) * upward).astype(jnp.bfloat16)
    result = middle + jnp.dot(hidden_low, gathered[6], preferred_element_type=jnp.float32)
    return {
        "middle": middle,
        "inv_mid": inv_mid,
        "normed_mid_low": normed_mid_low,
        "gate_act": gate_act,
        "upward": upward,
        "hidden_low": hidden_low,
        "result": result,
    }


def general_device(
    tokens,
    cotangent,
    lengths,
    stretch_ids,
    w_query,
    key_projection_weight,
    value_projection_weight,
    w_out,
    w_gate,
    w_up,
    w_down,
    g_attn,
    g_mlp,
    g_query,
    g_key,
):
    count_rows = tokens.shape[0]
    ctx_count = lax.axis_size("ctx")
    half_count = ctx_count // 2
    key_value_width = KEY_VALUE_HEADS * HEAD_SIZE
    key_meta = token_places(stretch_ids[:, 0, :], lengths[0])
    ctx_index = lax.axis_index("ctx")
    local_index = ctx_index % half_count
    base_row = ctx_index // half_count * half_count * count_rows
    half_row_set = half_count * count_rows
    offset_mine = ctx_index * count_rows
    query_meta = tuple(
        (lax.dynamic_slice_in_dim(meta_array, offset_mine, count_rows) for meta_array in key_meta)
    )
    live_mine = query_meta[2].astype(jnp.float32)[:, None]
    cosine_table, sine_table = rotary_tables(query_meta[0])
    group_count = QUERY_HEADS // KEY_VALUE_HEADS
    score_scale = HEAD_SIZE ** (-0.5)

    def attend_forward(query_head_group, key_source, value_source, current):

        def update(carried, local_row, block_length):
            key_tile_block = lax.dynamic_slice_in_dim(key_source, local_row, block_length)
            value_tile_block = lax.dynamic_slice_in_dim(value_source, local_row, block_length)
            allowed = allowed_mask(key_meta, query_meta, base_row + local_row, block_length)
            return forward_update(
                carried, query_head_group, key_tile_block, value_tile_block, allowed, score_scale
            )

        return over_keys(update, current, key_source.shape[0])

    saved = []
    stream = tokens.astype(jnp.float32)
    for layer_index in range(DECODER_LAYERS):
        gathered = (
            lax.all_gather(w_query[layer_index], "fsdp", axis=0, tiled=True),
            lax.all_gather(key_projection_weight[layer_index], "fsdp", axis=0, tiled=True),
            lax.all_gather(value_projection_weight[layer_index], "fsdp", axis=0, tiled=True),
            lax.all_gather(w_out[layer_index], "fsdp", axis=0, tiled=True),
            lax.all_gather(w_gate[layer_index], "fsdp", axis=0, tiled=True),
            lax.all_gather(w_up[layer_index], "fsdp", axis=0, tiled=True),
            lax.all_gather(w_down[layer_index], "fsdp", axis=0, tiled=True),
            lax.all_gather(g_attn[layer_index], "fsdp", axis=0, tiled=True),
            lax.all_gather(g_mlp[layer_index], "fsdp", axis=0, tiled=True),
            lax.all_gather(g_query[layer_index], "fsdp", axis=0, tiled=True),
            lax.all_gather(g_key[layer_index], "fsdp", axis=0, tiled=True),
        )
        present_inputs = attention_inputs(stream, gathered, cosine_table, sine_table)
        query_head_group = present_inputs["query_low"].reshape(
            count_rows, KEY_VALUE_HEADS, group_count, HEAD_SIZE
        )
        start_state = (
            jnp.full((KEY_VALUE_HEADS, group_count, count_rows), masked_logits, jnp.float32),
            jnp.zeros((KEY_VALUE_HEADS, group_count, count_rows), jnp.float32),
            jnp.zeros((KEY_VALUE_HEADS, group_count, count_rows, HEAD_SIZE), jnp.float32),
        )
        pair_all = half_gather(
            jnp.concatenate([present_inputs["key_low"], present_inputs["value_low"]], axis=-1),
            local_index,
        )
        key_all = pair_all[:, :key_value_width]
        value_all = pair_all[:, key_value_width:]
        final_state = attend_forward(query_head_group, key_all, value_all, start_state)
        attended = final_state[2] / final_state[1][..., None]
        log_total = final_state[0] + jnp.log(final_state[1])
        attn_low = (
            jnp.transpose(attended, (2, 0, 1, 3))
            .reshape(count_rows, QUERY_HEADS * HEAD_SIZE)
            .astype(jnp.bfloat16)
        )
        rest = block_rest(stream, gathered, attn_low)
        kept = (gathered, key_all, value_all, present_inputs, rest)
        saved.append((stream, attended, log_total, kept))
        stream = rest["result"]
    output_low = (stream * live_mine).astype(jnp.bfloat16)
    grad_stream = cotangent.astype(jnp.float32) * live_mine
    layer_grads = [None] * DECODER_LAYERS
    for layer_index in reversed(range(DECODER_LAYERS)):
        stream_in, attended, log_total, kept = saved[layer_index]
        attn_low = (
            jnp.transpose(attended, (2, 0, 1, 3))
            .reshape(count_rows, QUERY_HEADS * HEAD_SIZE)
            .astype(jnp.bfloat16)
        )
        gathered, key_all, value_all, present_inputs, rest = kept
        ffn_grad_low = grad_stream.astype(jnp.bfloat16)
        grad_down = jnp.einsum(
            "tf,td->fd", rest["hidden_low"], ffn_grad_low, preferred_element_type=jnp.float32
        )
        hidden_grad = jnp.einsum(
            "td,fd->tf", ffn_grad_low, gathered[6], preferred_element_type=jnp.float32
        )
        gate_act = rest["gate_act"]
        sigmoid_gate = jax.nn.sigmoid(gate_act)
        gate_grad_low = (
            hidden_grad * rest["upward"] * sigmoid_gate * (1.0 + gate_act * (1.0 - sigmoid_gate))
        ).astype(jnp.bfloat16)
        up_grad_low = (hidden_grad * gate_act * sigmoid_gate).astype(jnp.bfloat16)
        grad_gate = jnp.einsum(
            "td,tf->df", rest["normed_mid_low"], gate_grad_low, preferred_element_type=jnp.float32
        )
        grad_up = jnp.einsum(
            "td,tf->df", rest["normed_mid_low"], up_grad_low, preferred_element_type=jnp.float32
        )
        normed_mid_grad = jnp.einsum(
            "tf,df->td", gate_grad_low, gathered[4], preferred_element_type=jnp.float32
        ) + jnp.einsum("tf,df->td", up_grad_low, gathered[5], preferred_element_type=jnp.float32)
        mid_norm_grad, mlp_gain_term = norm_backward(
            rest["middle"], rest["inv_mid"], gathered[8].astype(jnp.float32), normed_mid_grad
        )
        middle_grad = grad_stream + mid_norm_grad
        attn_grad_low = middle_grad.astype(jnp.bfloat16)
        grad_out = jnp.einsum(
            "tq,td->qd", attn_low, attn_grad_low, preferred_element_type=jnp.float32
        )
        output_gradient_lowered = jnp.einsum(
            "td,qd->tq", attn_grad_low, gathered[3], preferred_element_type=jnp.float32
        ).astype(jnp.bfloat16)
        output_grad_group = output_gradient_lowered.reshape(
            count_rows, KEY_VALUE_HEADS, group_count, HEAD_SIZE
        )
        row_delta = jnp.sum(
            jnp.transpose(output_grad_group.astype(jnp.float32), (1, 2, 0, 3)) * attended, axis=-1
        )
        query_head_group = present_inputs["query_low"].reshape(
            count_rows, KEY_VALUE_HEADS, group_count, HEAD_SIZE
        )
        key_block_size = math.gcd(half_row_set, 512)

        def backward_step(query_acc, block_index):
            row_start = block_index * key_block_size
            key_tile_block = lax.dynamic_slice_in_dim(key_all, row_start, key_block_size)
            value_tile_block = lax.dynamic_slice_in_dim(value_all, row_start, key_block_size)
            allowed = allowed_mask(key_meta, query_meta, base_row + row_start, key_block_size)
            prob_block, dscore_low, key_head_list = score_parts(
                query_head_group,
                output_grad_group,
                key_tile_block,
                value_tile_block,
                allowed,
                log_total,
                row_delta,
                score_scale,
            )
            query_next = (query_acc, jnp.zeros((key_block_size, 2 * key_value_width), jnp.float32))[
                0
            ] + jnp.einsum(
                "hgqk,khd->qhgd", dscore_low, key_head_list, preferred_element_type=jnp.float32
            ) * score_scale
            value_grad = jnp.einsum(
                "hgqk,qhgd->khd",
                prob_block.astype(jnp.bfloat16),
                output_grad_group,
                preferred_element_type=jnp.float32,
            )
            key_grad = (
                jnp.einsum(
                    "hgqk,qhgd->khd",
                    dscore_low,
                    query_head_group,
                    preferred_element_type=jnp.float32,
                )
                * score_scale
            )
            block_rows = jnp.concatenate(
                [
                    key_grad.reshape(key_block_size, key_value_width),
                    value_grad.reshape(key_block_size, key_value_width),
                ],
                axis=-1,
            )
            return (query_next, block_rows)

        query_grad, key_value_rows = lax.scan(
            backward_step,
            jnp.zeros((count_rows, KEY_VALUE_HEADS, group_count, HEAD_SIZE), jnp.float32),
            jnp.arange(half_row_set // key_block_size, dtype=jnp.int32),
        )
        key_value_term = key_value_rows.reshape(half_row_set, 2 * key_value_width)
        key_value_gradient = half_reduce(key_value_term, local_index)
        key_gradient_rows = key_value_gradient[:, :key_value_width].reshape(
            count_rows, KEY_VALUE_HEADS, HEAD_SIZE
        )
        value_grad_low = key_value_gradient[:, key_value_width:].astype(jnp.bfloat16)
        query_pre, query_gain_term = norm_backward(
            present_inputs["query_heads"],
            present_inputs["inv_query"],
            gathered[9].astype(jnp.float32),
            unrotate(
                query_grad.reshape(count_rows, QUERY_HEADS, HEAD_SIZE), cosine_table, sine_table
            ),
        )
        key_pre, key_gain_term = norm_backward(
            present_inputs["key_heads"],
            present_inputs["inv_key"],
            gathered[10].astype(jnp.float32),
            unrotate(key_gradient_rows, cosine_table, sine_table),
        )
        query_grad_low = query_pre.reshape(count_rows, QUERY_HEADS * HEAD_SIZE).astype(jnp.bfloat16)
        key_grad_low = key_pre.reshape(count_rows, key_value_width).astype(jnp.bfloat16)
        normed_low = present_inputs["normed_low"]
        grad_query = jnp.einsum(
            "td,tq->dq", normed_low, query_grad_low, preferred_element_type=jnp.float32
        )
        grad_key = jnp.einsum(
            "td,tq->dq", normed_low, key_grad_low, preferred_element_type=jnp.float32
        )
        grad_value = jnp.einsum(
            "td,tq->dq", normed_low, value_grad_low, preferred_element_type=jnp.float32
        )
        normed_grad = jnp.einsum(
            "tq,dq->td", query_grad_low, gathered[0], preferred_element_type=jnp.float32
        )
        normed_grad = normed_grad + jnp.einsum(
            "tq,dq->td", key_grad_low, gathered[1], preferred_element_type=jnp.float32
        )
        normed_grad = normed_grad + jnp.einsum(
            "tq,dq->td", value_grad_low, gathered[2], preferred_element_type=jnp.float32
        )
        in_norm_grad, attn_gain_term = norm_backward(
            stream_in, present_inputs["inv_attn"], gathered[7].astype(jnp.float32), normed_grad
        )
        grad_stream = middle_grad + in_norm_grad
        layer_grads[layer_index] = (
            lax.psum_scatter(grad_query, ("ctx", "fsdp"), scatter_dimension=0, tiled=True),
            lax.psum_scatter(grad_key, ("ctx", "fsdp"), scatter_dimension=0, tiled=True),
            lax.psum_scatter(grad_value, ("ctx", "fsdp"), scatter_dimension=0, tiled=True),
            lax.psum_scatter(grad_out, ("ctx", "fsdp"), scatter_dimension=0, tiled=True),
            lax.psum_scatter(grad_gate, ("ctx", "fsdp"), scatter_dimension=0, tiled=True),
            lax.psum_scatter(grad_up, ("ctx", "fsdp"), scatter_dimension=0, tiled=True),
            lax.psum_scatter(grad_down, ("ctx", "fsdp"), scatter_dimension=0, tiled=True),
            lax.psum_scatter(attn_gain_term, ("ctx", "fsdp"), scatter_dimension=0, tiled=True),
            lax.psum_scatter(mlp_gain_term, ("ctx", "fsdp"), scatter_dimension=0, tiled=True),
            lax.psum_scatter(query_gain_term, ("ctx", "fsdp"), scatter_dimension=0, tiled=True),
            lax.psum_scatter(key_gain_term, ("ctx", "fsdp"), scatter_dimension=0, tiled=True),
        )
    stacked = tuple(
        (jnp.stack([layer_sums[member] for layer_sums in layer_grads]) for member in range(11))
    )
    return (output_low, grad_stream) + stacked


def fast_device(
    tokens,
    cotangent,
    lengths,
    stretch_ids,
    w_query,
    key_projection_weight,
    value_projection_weight,
    w_out,
    w_gate,
    w_up,
    w_down,
    g_attn,
    g_mlp,
    g_query,
    g_key,
):
    count_rows, width = tokens.shape
    ctx_index = lax.axis_index("ctx")
    places, slot_ids, live = token_places(stretch_ids[:, 0, :], lengths[0])
    group_rows = PEERS * count_rows
    base_row = ctx_index // PEERS * group_rows
    my_row = ctx_index * count_rows
    slot_places = lax.dynamic_slice_in_dim(places, base_row, group_rows)
    limit = lax.dynamic_slice_in_dim(lengths[0], ctx_index // PEERS, 1)
    caps = jnp.minimum(slot_places, limit - 1).reshape(PEERS, 1, count_rows)
    query_cap = jnp.concatenate([caps, caps], axis=2)
    key_place = slot_places[:, None]
    live_mine = lax.dynamic_slice_in_dim(live, my_row, count_rows).astype(jnp.float32)[:, None]
    cosine, sine = rotary_tables(lax.dynamic_slice_in_dim(places, my_row, count_rows))
    half = HEAD_SIZE // 2
    sine = jnp.concatenate([-sine[:, :half], sine[:, half:]], axis=1)

    mesh_x = lax.axis_index("fsdp")
    rows = [member.reshape(-1, 128) for member in (g_attn, g_mlp)]
    for member in (g_query, g_key):
        zero = jnp.zeros_like(member)
        rows.append(
            jnp.concatenate(
                [jnp.where(mesh_x == 0, member, zero), jnp.where(mesh_x == 0, zero, member)], axis=1
            )
        )
    packed = jnp.pad(jnp.concatenate(rows, axis=0).astype(jnp.float32), ((0, 4), (0, 0)))
    results = forward(
        (key_projection_weight, value_projection_weight, w_query, w_out, w_gate, w_up, w_down),
        packed,
        tokens,
        live_mine,
        cosine,
        sine,
        key_place,
        query_cap,
        1,
    )
    gathered, saved, turned, gains, output_low = (
        results[:4], results[4:11], results[11:15], results[15:18], results[18]
    )
    acts = [
        member.reshape(DECODER_LAYERS, 4, 2, 2, 2, -1, 32, count_rows) for member in turned
    ]

    place = ctx_index * 2 + mesh_x
    *weight_sums, grad_stream, sums, unused = backward(
        acts,
        saved,
        gathered,
        cotangent.astype(jnp.float32) * live_mine,
        cosine,
        sine,
        gains,
        key_place,
        query_cap,
        2,
    )
    sums = sums.reshape(DECODER_LAYERS, -1)

    def share(first, span):
        return lax.dynamic_slice_in_dim(sums, first + place * span, span, axis=1)

    return (output_low, grad_stream) + tuple(weight_sums) + (
        share(0, 32), share(1024, 32), share(2048, 4), share(2176, 4)
    )


def solution(mesh):
    plain = mesh.shape["ctx"] == 2 * KEY_VALUE_HEADS and mesh.shape["fsdp"] == 2
    device = fast_device if plain else general_device
    in_specs = (
        P(("ctx", "fsdp"), None),
        P(("ctx", "fsdp"), None),
        P("fsdp", None),
        P(None, "fsdp", None),
        P(None, "fsdp", None),
        P(None, "fsdp", None),
        P(None, "fsdp", None),
        P(None, "fsdp", None),
        P(None, "fsdp", None),
        P(None, "fsdp", None),
        P(None, "fsdp", None),
        P(None, "fsdp"),
        P(None, "fsdp"),
        P(None, "fsdp"),
        P(None, "fsdp"),
    )
    out_specs = (
        P(("ctx", "fsdp"), None),
        P(("ctx", "fsdp"), None),
        P(None, ("ctx", "fsdp"), None),
        P(None, ("ctx", "fsdp"), None),
        P(None, ("ctx", "fsdp"), None),
        P(None, ("ctx", "fsdp"), None),
        P(None, ("ctx", "fsdp"), None),
        P(None, ("ctx", "fsdp"), None),
        P(None, ("ctx", "fsdp"), None),
        P(None, ("ctx", "fsdp")),
        P(None, ("ctx", "fsdp")),
        P(None, ("ctx", "fsdp")),
        P(None, ("ctx", "fsdp")),
    )
    return jax.shard_map(
        device, mesh=mesh, in_specs=in_specs, out_specs=out_specs, check_vma=False
    )
```

```python
import functools
import math

import jax
import jax.numpy as jnp
from jax import lax
from jax.experimental import pallas as pl
from jax.experimental.pallas import tpu as pltpu
from jax.sharding import PartitionSpec as P

QUERY_HEADS = 16
KEY_VALUE_HEADS = 8
HEAD_SIZE = 128
DECODER_LAYERS = 2
STRETCH = 64


norm_epsilon = 1e-06
rope_base = 1000000.0
masked_logits = -1e30

MESH = pl.DeviceIdType.MESH


TILES = 15
GRADS = 12
ACTS = 7
AHEAD = 2
SLOTS = 8
ACT_SPANS = ((0, 3), (3, 1), (4, 2), (6, 1))


def grad_index(t):
    return jnp.where(t < 3, 0, jnp.where(t < 9, t - 2, jnp.where(t < 11, 7, t - 3)))


def act_index(t):
    return jnp.where(t < 3, t, jnp.where(t < 9, 3, jnp.where(t < 11, t - 5, 6)))


def is_new(t):
    return (t == 0) | ((t >= 3) & (t < 10)) | (t >= 11)


def make_remote(src, dst, s, r, dev):
    return pltpu.make_async_remote_copy(
        src_ref=src, dst_ref=dst, send_sem=s, recv_sem=r, device_id=dev, device_id_type=MESH
    )


class Reducer:
    def __init__(self, acts, grads, results, scratch, layers):
        self.acts, self.grads, self.results, self.layers = acts, grads, results, layers
        self.count = len(layers)
        (self.gheld, self.abuf, self.afwd, self.gtile, self.ysend, self.yrecv, self.own,
         self.zsend, self.zrecv, self.zown,
         self.a_local, self.a_xs, self.a_xr, self.a_cs, self.a_cr,
         self.g_local, self.g_xs, self.g_xr, self.g_cs, self.g_cr, self.g_fs, self.g_fr,
         self.y_s, self.y_r, self.z_s, self.z_r) = scratch
        c = lax.axis_index("ctx")
        x = lax.axis_index("fsdp")
        self.c, self.x = c, x
        self.core = c % 2
        self.y = c // 2 % 2
        self.z = c // 4
        self.sibling = (c + 1 - 2 * self.core, x)
        self.across = (c, 1 - x)
        self.aside = (c + 2 - 4 * self.y, x)

    def along(self, o):
        return ((self.z + o) % 4 * 4 + self.c % 4, self.x)

    def partners(self):
        return (self.sibling, self.across, self.aside) + tuple(self.along(o) for o in (1, 2, 3))

    def act(self, n, k, what):
        first, blocks = ACT_SPANS[k]
        src = self.acts[k].at[self.layers[n]]
        span = pl.ds(first, blocks)
        x, core = self.x, self.core

        def held(place):
            return self.abuf.at[n, :, :, span, :, pl.ds(128 * place, 128)]

        if what == "local":
            return pltpu.make_async_copy(
                src.at[:, :, core, x], held(0), self.a_local.at[n, k]
            )
        if what == "across":
            return make_remote(
                src.at[:, :, core, 1 - x], held(1), self.a_xs.at[n, k, 0], self.a_xr.at[n, k, 0],
                self.across,
            )
        if what == "relay":
            return make_remote(
                src.at[:, :, 1 - core, 1 - x], self.afwd.at[n, :, :, span],
                self.a_xs.at[n, k, 1], self.a_xr.at[n, k, 1], self.across,
            )
        if what == "sibling":
            return make_remote(
                src.at[:, :, 1 - core, x], held(2), self.a_cs.at[n, k, 0], self.a_cr.at[n, k, 0],
                self.sibling,
            )
        return make_remote(
            self.afwd.at[n, :, :, span], held(3), self.a_cs.at[n, k, 1], self.a_cr.at[n, k, 1],
            self.sibling,
        )

    def start_acts(self, n, ks):
        for what in ("across", "relay", "sibling", "local"):
            for k in ks:
                self.act(n, k, what).start()

    def forward_acts(self, n, ks):
        for k in ks:
            self.act(n, k, "relay").wait_recv()
            self.act(n, k, "forward").start()

    def await_acts(self, n, ks):
        for k in ks:
            self.act(n, k, "local").wait()
            for what in ("across", "sibling", "forward"):
                self.act(n, k, what).wait_recv()

    def grad_across(self, i, src=None):
        rows = self.gheld.at[i, pl.ds(0, 128)]
        return make_remote(
            rows if src is None else src, rows, self.g_xs.at[i], self.g_xr.at[i], self.across
        )

    def grad_sibling(self, i, src=None):
        rows = self.gheld.at[i, pl.ds(128, 128)]
        return make_remote(
            rows if src is None else src, rows, self.g_cs.at[i], self.g_cr.at[i], self.sibling
        )

    def grad_forward(self, i):
        return make_remote(
            self.gheld.at[i, pl.ds(0, 128)], self.gheld.at[i, pl.ds(256, 128)],
            self.g_fs.at[i], self.g_fr.at[i], self.sibling,
        )

    def grad_own(self, i, src=None):
        rows = self.gtile.at[i % 2, pl.ds(0, 128)]
        return pltpu.make_async_copy(rows if src is None else src, rows, self.g_local.at[i % 2, 0])

    def grad_load(self, i):
        return pltpu.make_async_copy(
            self.gheld.at[i], self.gtile.at[i % 2, pl.ds(128, 384)], self.g_local.at[i % 2, 1]
        )

    def with_source(self, i, act):
        n = i // GRADS
        g = i % GRADS
        first = 0
        for ref, blocks in self.grads:

            @pl.when((g >= first) & (g < first + blocks))
            def use(ref=ref, first=first):
                act(ref.at[n, :, pl.ds(pl.multiple_of((g - first) * 1024, 1024), 1024)])

            first += blocks

    def start_grad(self, i):
        def go(src):
            self.grad_across(i, src).start()
            self.grad_sibling(i, src).start()

        self.with_source(i, go)

    def y_copy(self, t):
        return make_remote(
            self.ysend.at[t % SLOTS], self.yrecv.at[t], self.y_s.at[t], self.y_r.at[t], self.aside
        )

    def z_copy(self, t, o):
        return make_remote(
            self.zsend.at[t % SLOTS, o - 1], self.zrecv.at[t, 3 - o], self.z_s.at[t, o - 1],
            self.z_r.at[t, 3 - o], self.along(o),
        )

    def begin(self):
        self.start_acts(0, (0,))
        self.start_grad(0)
        self.start_acts(0, (1, 2, 3))

    def begin_more(self):
        for i in range(1, AHEAD):
            self.start_grad(i)

    def store(self, t, total):
        n = t // TILES
        tile = t % TILES
        query, key, value, out, gate, up, down = self.results
        by_rows = ((0, 3, down), (9, 2, out))
        by_columns = ((3, 3, gate), (6, 3, up), (11, 2, query), (13, 1, key), (14, 1, value))
        if self.count == 1:
            layer = self.layers[0]
        else:
            layer = jnp.where(n == 0, self.layers[0], self.layers[1])
        for first, blocks, ref in by_rows:

            @pl.when((tile >= first) & (tile < first + blocks))
            def rows(first=first, ref=ref):
                ref[layer, pl.ds(pl.multiple_of((tile - first) * 32, 32), 32), :] = total

        for first, blocks, ref in by_columns:

            @pl.when((tile >= first) & (tile < first + blocks))
            def columns(first=first, ref=ref):
                ref[layer, :, pl.ds(pl.multiple_of((tile - first) * 1024, 1024), 1024)] = total

    def step(self, s):
        tiles = TILES * self.count
        t = s - 6

        @pl.when((t >= 0) & (t < tiles))
        def finish():
            total = self.zown[t % 4]
            for o in (1, 2, 3):
                self.z_copy(t, o).wait_recv()
            for o in range(3):
                total += self.zrecv[t, o].astype(jnp.float32)
            self.store(t, total)

        u = s - 4

        @pl.when((u >= 0) & (u < tiles))
        def spread():
            self.y_copy(u).wait_recv()

            def part(index):
                rows = pl.ds(pl.multiple_of(index * 32, 32), 32)
                return self.own[u % 4, rows, :] + self.yrecv[u, rows, :].astype(jnp.float32)

            @pl.when(u >= SLOTS)
            def settle():
                for o in (1, 2, 3):
                    self.z_copy(u - SLOTS, o).wait_send()

            for o in (2, 1, 3):
                self.zsend[u % SLOTS, o - 1] = part((self.z + o) % 4).astype(jnp.bfloat16)
                self.z_copy(u, o).start()
            self.zown[u % 4] = part(self.z)

        v = s - 2

        @pl.when((v >= 0) & (v < tiles))
        def compute():
            n = v // TILES
            tile = v % TILES
            gi = n * GRADS + grad_index(tile)
            ai = act_index(tile)
            for layer in range(self.count):

                @pl.when(v == TILES * layer)
                def first_acts(layer=layer):
                    self.await_acts(layer, (0,))

                @pl.when(v == TILES * layer + 3)
                def second_acts(layer=layer):
                    self.await_acts(layer, (1, 2, 3))

            @pl.when(is_new(tile))
            def fresh():
                self.grad_own(gi).wait()
                self.grad_load(gi).wait()

            @pl.when(v >= SLOTS)
            def settle():
                self.y_copy(v - SLOTS).wait_send()

            left = jnp.concatenate(
                [
                    self.abuf[n, :, 1 - self.y, ai].reshape(128, 512),
                    self.abuf[n, :, self.y, ai].reshape(128, 512),
                ],
                axis=0,
            )
            for part in range(4):
                cols = pl.ds(part * 256, 256)
                result = jnp.dot(left, self.gtile[gi % 2, :, cols], preferred_element_type=jnp.float32)
                self.ysend[v % SLOTS, :, cols] = result[:128].astype(jnp.bfloat16)
                self.own[v % 4, :, cols] = result[128:]
            self.y_copy(v).start()

        w = s - 1

        @pl.when((w >= 0) & (w < tiles) & is_new(w % TILES))
        def collect():
            gi = w // TILES * GRADS + grad_index(w % TILES)
            self.with_source(gi, lambda src: self.grad_own(gi, src).start())
            self.grad_sibling(gi).wait_recv()
            self.grad_forward(gi).wait_recv()
            self.grad_load(gi).start()

        @pl.when((s >= 0) & (s < tiles) & is_new(s % TILES))
        def forward():
            i = s // TILES * GRADS + grad_index(s % TILES)
            for layer in range(self.count):

                @pl.when(s == TILES * layer)
                def first_forward(layer=layer):
                    self.forward_acts(layer, (0,))

                @pl.when(s == TILES * layer + 3)
                def second_forward(layer=layer):
                    self.forward_acts(layer, (1, 2, 3))

            self.grad_across(i).wait_recv()
            self.grad_forward(i).start()
            for layer in range(1, self.count):

                @pl.when(i == GRADS * layer - AHEAD)
                def next_acts(layer=layer):
                    self.start_acts(layer, (0,))

                @pl.when(i == GRADS * layer - AHEAD + 1)
                def other_acts(layer=layer):
                    self.start_acts(layer, (1, 2, 3))

            @pl.when(i + AHEAD < GRADS * self.count)
            def more():
                self.start_grad(i + AHEAD)

    def steps(self):
        return TILES * self.count + 6

    def drain(self):
        for n in range(self.count):
            for k in range(4):
                for what in ("across", "relay", "sibling", "forward"):
                    self.act(n, k, what).wait_send()

        def drain_grads(i, carry):
            self.grad_across(i).wait_send()
            self.grad_sibling(i).wait_send()
            self.grad_forward(i).wait_send()
            return carry

        lax.fori_loop(0, GRADS * self.count, drain_grads, 0)

        def drain_tiles(t, carry):
            self.y_copy(t).wait_send()
            for o in (1, 2, 3):
                self.z_copy(t, o).wait_send()
            return carry

        lax.fori_loop(TILES * self.count - SLOTS, TILES * self.count, drain_tiles, 0)


class GainSum:
    def __init__(self, reducer, source, out, scratch):
        self.reducer, self.source, self.out = reducer, source, out
        self.part, self.recv, self.s, self.r = scratch

    def hop(self, i):
        red = self.reducer
        return make_remote(
            self.source if i == 0 else self.part.at[i - 1], self.recv.at[i], self.s.at[i],
            self.r.at[i], (red.across, red.sibling, red.aside)[i],
        )

    def along(self, o):
        return make_remote(
            self.part.at[2], self.recv.at[6 - o], self.s.at[2 + o], self.r.at[6 - o],
            self.reducer.along(o),
        )

    def step(self, s, first):
        @pl.when(s == first)
        def begin():
            self.hop(0).start()

        for i in range(3):

            @pl.when(s == first + 1 + i)
            def stage(i=i):
                self.hop(i).wait_recv()
                self.part[i] = (self.source[...] if i == 0 else self.part[i - 1]) + self.recv[i]
                if i < 2:
                    self.hop(i + 1).start()
                else:
                    for o in (1, 2, 3):
                        self.along(o).start()

        @pl.when(s == first + 5)
        def total():
            for o in (1, 2, 3):
                self.along(o).wait_recv()
            self.out[...] = self.part[2] + self.recv[3] + self.recv[4] + self.recv[5]

    def drain(self):
        for i in range(3):
            self.hop(i).wait_send()
            self.along(i + 1).wait_send()


def reduce_scratch(count):
    dma = pltpu.SemaphoreType.DMA
    low, wide = jnp.bfloat16, jnp.float32
    tiles, grads = TILES * count, GRADS * count
    return [
        pltpu.VMEM((count, 4, 2, ACTS, 32, 512), low),
        pltpu.VMEM((count, 4, 2, ACTS, 32, 128), low),
        pltpu.VMEM((2, 512, 1024), low),
        pltpu.VMEM((SLOTS, 128, 1024), low),
        pltpu.VMEM((tiles, 128, 1024), low),
        pltpu.VMEM((4, 128, 1024), wide),
        pltpu.VMEM((SLOTS, 3, 32, 1024), low),
        pltpu.VMEM((tiles, 3, 32, 1024), low),
        pltpu.VMEM((4, 32, 1024), wide),
        dma((count, 4)), dma((count, 4, 2)), dma((count, 4, 2)), dma((count, 4, 2)),
        dma((count, 4, 2)),
        dma((2, 2)), dma((grads,)), dma((grads,)), dma((grads,)), dma((grads,)), dma((grads,)),
        dma((grads,)),
        dma((tiles,)), dma((tiles,)), dma((tiles, 3)), dma((tiles, 3)),
    ]


def gain_scratch(rows):
    dma = pltpu.SemaphoreType.DMA
    return [
        pltpu.VMEM((3, rows, 128), jnp.float32),
        pltpu.VMEM((6, rows, 128), jnp.float32),
        dma((6,)),
        dma((6,)),
    ]


RESULTS = ((32, 2048), (32, 1024), (32, 1024), (64, 1024), (32, 3072), (32, 3072), (96, 1024))


PEERS = KEY_VALUE_HEADS
SCALE = HEAD_SIZE ** (-0.5)
NT = (((1,), (1,)), ((), ()))


GATHER_PLAN = ((0, 2048), (0, 3072), (0, 0), (1, 0), (2, 0), (2, 3072), (3, 0))
MEMBERS = len(GATHER_PLAN)
LEAD = 3


class Gatherer:
    def __init__(self, sources, outs, sems, count):
        self.sources, self.outs, self.count = sources, outs, count * MEMBERS
        (self.l_s, self.l_r, self.x_s, self.x_r, self.y_s, self.y_r, self.z_s, self.z_r,
         self.yc_s, self.yc_r, self.zc_s, self.zc_r, self.c_s, self.c_r) = sems
        c = lax.axis_index("ctx")
        x = lax.axis_index("fsdp")
        self.x = x
        self.core = c % 2
        y = c // 2 % 2
        near = c // 4 % 2
        self.sibling = (c + 1 - 2 * self.core, x)
        self.across = (c, 1 - x)
        self.aside = (c + 2 - 4 * y, x)
        self.along = (c + 4 - 8 * near, x)
        self.here = near * 2 + y
        self.by_y = near * 2 + 1 - y
        self.by_z = (1 - near) * 2 + y
        self.corner = (1 - near) * 2 + 1 - y

    def partners(self):
        return (self.sibling, self.across, self.aside, self.along)

    def window(self, i, m, owner_x, piece, share=None):
        target, column = GATHER_PLAN[m]
        half, width = self.sources[m].shape[1], self.sources[m].shape[2]
        rows = half // 8
        start = owner_x * half + (piece * 2 + self.core) * rows
        if share is not None:
            rows = rows // 2
            start = start + share * rows
        return self.outs[target].at[
            i // MEMBERS, pl.ds(pl.multiple_of(start, 16), rows), pl.ds(column, width)
        ]

    def direct(self, i, m, owner_x):
        target, column = GATHER_PLAN[m]
        half, width = self.sources[m].shape[1], self.sources[m].shape[2]
        start = owner_x * half + self.core * (half // 2)
        return self.outs[target].at[
            i // MEMBERS, pl.ds(pl.multiple_of(start, 16), half // 2), pl.ds(column, width)
        ]

    def local(self, i, m):
        target, column = GATHER_PLAN[m]
        half, width = self.sources[m].shape[1], self.sources[m].shape[2]
        rows = pl.ds(pl.multiple_of(self.x * half, 16), half)
        return make_remote(
            self.sources[m].at[i // MEMBERS],
            self.outs[target].at[i // MEMBERS, rows, pl.ds(column, width)],
            self.l_s.at[i], self.l_r.at[i], self.sibling,
        )

    def x_copy(self, i, m):
        half = self.sources[m].shape[1]
        if m == MEMBERS - 1:
            rows = pl.ds(pl.multiple_of(self.core * (half // 2), 16), half // 2)
            view = self.direct(i, m, self.x)
        else:
            rows = pl.ds(pl.multiple_of((self.here * 2 + self.core) * (half // 8), 16), half // 8)
            view = self.window(i, m, self.x, self.here)
        return make_remote(
            self.sources[m].at[i // MEMBERS, rows], view, self.x_s.at[i], self.x_r.at[i],
            self.across,
        )

    def y_copy(self, i, m):
        view = self.window(i, m, 1 - self.x, self.here)
        return make_remote(view, view, self.y_s.at[i], self.y_r.at[i], self.aside)

    def z_copy(self, i, m):
        view = self.window(i, m, 1 - self.x, self.here)
        return make_remote(view, view, self.z_s.at[i], self.z_r.at[i], self.along)

    def y_corner(self, i, m):
        view = self.window(i, m, 1 - self.x, self.by_z, 1)
        return make_remote(view, view, self.yc_s.at[i], self.yc_r.at[i], self.aside)

    def z_corner(self, i, m):
        view = self.window(i, m, 1 - self.x, self.by_y, 0)
        return make_remote(view, view, self.zc_s.at[i], self.zc_r.at[i], self.along)

    def core_copy(self, i, m, which):
        if m == MEMBERS - 1:
            view = self.direct(i, m, 1 - self.x)
        else:
            piece = (self.here, self.by_y, self.by_z, self.corner)[which]
            view = self.window(i, m, 1 - self.x, piece)
        return make_remote(
            view, view, self.c_s.at[i, which], self.c_r.at[i, which], self.sibling
        )

    def each(self, i, act, members=range(MEMBERS)):
        for m in members:

            @pl.when((i >= 0) & (i < self.count) & (i % MEMBERS == m))
            def member(m=m):
                act(m)

    def send(self, i):
        def go(m):
            self.x_copy(i, m).start()
            self.local(i, m).start()

        self.each(i, go)

    def step(self, u):
        s = u // 3
        stage = u % 3

        @pl.when(stage == 0)
        def first():
            def spread(m):
                self.x_copy(s, m).wait_recv()
                if m < MEMBERS - 1:
                    self.y_copy(s, m).start()
                    self.z_copy(s, m).start()
                self.core_copy(s, m, 0).start()

            self.each(s, spread)
            self.send(s + LEAD)

        @pl.when(stage == 1)
        def second():
            i = s - 1

            def corners(m):
                self.y_copy(i, m).wait_recv()
                self.z_corner(i, m).start()
                self.core_copy(i, m, 1).start()
                self.z_copy(i, m).wait_recv()
                self.y_corner(i, m).start()
                self.core_copy(i, m, 2).start()

            self.each(i, corners, range(MEMBERS - 1))

        @pl.when(stage == 2)
        def third():
            j = s - 2

            def last(m):
                self.y_corner(j, m).wait_recv()
                self.z_corner(j, m).wait_recv()
                self.core_copy(j, m, 3).start()

            self.each(j, last, range(MEMBERS - 1))

    def steps(self):
        return 3 * (self.count + 2)

    def ready(self, n, m):
        i = n * MEMBERS + m
        self.local(i, m).wait_recv()
        for which in range(1 if m == MEMBERS - 1 else 4):
            self.core_copy(i, m, which).wait_recv()

    def drain(self):
        def one(i, carry):
            def go(m):
                self.local(i, m).wait_send()
                self.x_copy(i, m).wait_send()
                if m < MEMBERS - 1:
                    for copy in (self.y_copy, self.z_copy, self.y_corner, self.z_corner):
                        copy(i, m).wait_send()
                for which in range(1 if m == MEMBERS - 1 else 4):
                    self.core_copy(i, m, which).wait_send()

            self.each(i, go)
            return carry

        lax.fori_loop(0, self.count, one, 0)


def gather_scratch(count):
    dma = pltpu.SemaphoreType.DMA
    return [dma((count * MEMBERS,))] * 12 + [dma((count * MEMBERS, 4))] * 2


def head_columns(first, index):
    return pl.ds(pl.multiple_of(first + index * HEAD_SIZE, HEAD_SIZE), HEAD_SIZE)


def stream_blocks(first, count, slots, start, wait, body):
    def fill(i, carry):
        start(first + i, i)
        return carry

    lax.fori_loop(0, jnp.minimum(slots - 1, count), fill, 0)

    def one(i, carry):
        slot = i % slots

        @pl.when(i + slots - 1 < count)
        def following():
            start(first + i + slots - 1, (i + slots - 1) % slots)

        wait(first + i, slot)
        body(first + i, slot)
        return carry

    lax.fori_loop(0, count, one, 0)


def rms(values, gain):
    r = lax.rsqrt(jnp.mean(values * values, axis=-1, keepdims=True) + norm_epsilon)
    return values * r * gain


BUFFERS = 4
SCHEDULE = (
    (9, 12, 15, 16, 18, 19, 20, 21, 23, 24, 25, 26, 27, 28, 29),
    (30, 33, 36, 37, 39, 40, 41, 42, 43, 44, 45, 46, 47, 47, 48),
)


def forward_kernel(*refs):
    count = DECODER_LAYERS
    sources, refs = refs[:MEMBERS], refs[MEMBERS:]
    (g_attn, g_mlp, g_query, g_key, tokens, stretch_ids, lengths), refs = refs[:7], refs[7:]
    weights, refs = refs[:4], refs[4:]
    into_w, out_w, wide_w, down_w = weights
    (both_out, middle_out, entry_out, pre_out, kept_hbm, kept_out_hbm, kept_log_hbm), refs = (
        refs[:7], refs[7:]
    )
    (hidden_t, mid_t, attn_t, normed_t, attn_gains, mlp_gains, head_gains), refs = (
        refs[:7], refs[7:]
    )
    (output, live, cosine, sine, key_place, query_cap), refs = refs[:6], refs[6:]
    sizes = len(gather_scratch(count))
    gather = Gatherer(sources, weights, refs[:sizes], count)
    (wide_mine, wide_other, head_mine, head_other, stream, middle, pre, low, attn_low, hidden_low, gate_up, cols_w, rows_w,
     kept, kept_out, kept_log, send, osend, orecv, vt,
     pack_sem, cols_sem, rows_sem, gate_sem, save_sem,
     q_s, q_r, k_s, k_r, o_s, o_r) = refs[sizes:]
    c = lax.axis_index("ctx")
    x = lax.axis_index("fsdp")
    me = c % PEERS
    z = c // 4

    def peer(r):
        return (c - me + r, x)

    barrier = pltpu.get_barrier_semaphore()

    def greet(o, carry):
        pl.semaphore_signal(barrier, inc=1, device_id=peer((me + o) % PEERS), device_id_type=MESH)
        return carry

    lax.fori_loop(1, PEERS, greet, 0)
    pl.semaphore_signal(barrier, inc=1, device_id=gather.across, device_id_type=MESH)
    pl.semaphore_wait(barrier, PEERS)

    for k, member in enumerate((g_attn, g_mlp)):
        wide_mine[k] = member[...].astype(jnp.float32)
    for k, member in enumerate((g_query, g_key)):
        head_mine[k] = member[...].astype(jnp.float32)
    gain_copies = (
        make_remote(wide_mine, wide_other, pack_sem.at[0], pack_sem.at[1], gather.across),
        make_remote(head_mine, head_other, pack_sem.at[2], pack_sem.at[3], gather.across),
    )
    for copy in gain_copies:
        copy.start()
    for i in range(LEAD):
        gather.send(i)
    stream[...] = tokens[...].astype(jnp.float32)

    slot = c // PEERS
    limit = lengths[0, slot]
    stretches = 2 * PEERS
    lane = lax.broadcasted_iota(jnp.int32, (1, 256), 1) % 128
    row = lax.broadcasted_iota(jnp.int32, (128, 1), 0)

    def spots(r, along):
        first = stretch_ids[slot * PEERS + r, 0, 0] % stretches * STRETCH
        second = stretch_ids[slot * PEERS + r, 0, 1] % stretches * STRETCH
        return jnp.where(along < STRETCH, first, second - STRETCH) + along

    for r in range(PEERS):
        key_place[r * 128 : (r + 1) * 128, :] = spots(r, row)
        query_cap[r] = jnp.minimum(spots(r, lane), limit - 1)
    mine = spots(me, row)
    live[...] = jnp.where(mine < limit, 1.0, 0.0)
    half = HEAD_SIZE // 2
    column = lax.broadcasted_iota(jnp.int32, (1, HEAD_SIZE), 1)
    spread = (column % half).astype(jnp.float32) * (2.0 / HEAD_SIZE)
    angles = mine.astype(jnp.float32) * jnp.exp(spread * -math.log(rope_base))
    cosine[...] = jnp.cos(angles)
    sine[...] = jnp.where(column < half, -jnp.sin(angles), jnp.sin(angles))

    for copy in gain_copies:
        copy.wait_recv()
    low_side = jnp.where(x == 0, 0, 1)

    def pick(first, second, flip):
        return jnp.where(low_side == flip, first, second)

    for k, target in enumerate((attn_gains, mlp_gains)):
        sides = [pick(wide_mine[k], wide_other[k], flip) for flip in range(2)]
        for n in range(count):
            target[n] = jnp.concatenate([side[n : n + 1] for side in sides], axis=1)
    for k in range(2):
        for flip in range(2):
            side = pick(head_mine[k], head_other[k], flip)
            for n in range(count):
                head_gains[n, k : k + 1, flip * half : (flip + 1) * half] = side[n : n + 1]

    cos = cosine[...]
    sin = sine[...]

    def cols_copy(ref, n, column, slot):
        return pltpu.make_async_copy(
            ref.at[n, :, pl.ds(pl.multiple_of(column, 512), 512)], cols_w.at[slot],
            cols_sem.at[slot],
        )

    def rows_copy(ref, n, i, slot):
        rows = pl.ds(pl.multiple_of(i * 512, 512), 512)
        return pltpu.make_async_copy(ref.at[n, rows], rows_w.at[slot], rows_sem.at[slot])

    saves = (
        (stream, entry_out), (pre, pre_out), (middle, middle_out), (kept_out, kept_out_hbm),
        (kept_log, kept_log_hbm),
    )

    def save(n, k):
        return pltpu.make_async_copy(saves[k][0], saves[k][1].at[n], save_sem.at[k])

    def save_kept(n):
        return pltpu.make_async_copy(kept.at[n], kept_hbm.at[n], save_sem.at[5])

    def turn(source, target, n, blocks):
        def one(j, carry):
            columns = pl.ds(pl.multiple_of(j * 128, 128), 128)
            target[n, columns, :] = source[:, columns].astype(jnp.float32).T.astype(jnp.bfloat16)
            return carry

        lax.fori_loop(0, blocks, one, 0)

    def key_copy(n, r, slot):
        return make_remote(
            send.at[r, pl.ds(2, 2)], kept.at[n, slot, pl.ds(2, 2)], k_s.at[r], k_r.at[slot], peer(r)
        )

    def query_copy(n, r, slot):
        return make_remote(
            send.at[r, pl.ds(0, 2)], kept.at[n, slot, pl.ds(0, 2)], q_s.at[r], q_r.at[slot], peer(r)
        )

    def out_copy(r, slot):
        return make_remote(osend.at[r], orecv.at[slot], o_s.at[r], o_r.at[slot], peer(r))

    def project(n, first, blocks):
        def body(i, slot):
            pre[:, pl.ds(pl.multiple_of(i * 512, 512), 512)] = jnp.dot(
                low[...], cols_w[slot], preferred_element_type=jnp.float32
            )

        stream_blocks(
            first,
            blocks,
            BUFFERS,
            lambda i, slot: cols_copy(into_w, n, i * 512, slot).start(),
            lambda i, slot: cols_copy(into_w, n, i * 512, slot).wait(),
            body,
        )

    def turned(n, first, index, k):
        v = rms(pre[:, head_columns(first, index)], head_gains[n, k : k + 1, :])
        return (v * cos + pltpu.roll(v, HEAD_SIZE // 2, 1) * sin).astype(jnp.bfloat16)

    def keys_part(n):
        save(n, 0).start()
        low[...] = rms(stream[...], attn_gains[n]).astype(jnp.bfloat16)
        turn(low, normed_t, n, 8)
        gather.ready(n, 0)
        project(n, 4, 2)

    def values_part(n):
        gather.ready(n, 1)
        project(n, 6, 2)

        def make_keys(o, carry):
            r = (me + o) % PEERS
            key = turned(n, 2048, r, 1)
            value = pre[:, head_columns(3072, r)].astype(jnp.bfloat16)

            @pl.when(o < PEERS)
            def away():
                send[r, 2] = key
                send[r, 3] = value
                key_copy(n, r, me).start()

            @pl.when(o == PEERS)
            def home():
                kept[n, me, 2] = key
                kept[n, me, 3] = value

            return carry

        lax.fori_loop(1, PEERS + 1, make_keys, 0)

    def queries_part(n):
        gather.ready(n, 2)
        project(n, 0, 4)
        save(n, 1).start()

    def spread_queries(n):
        def make_queries(o, carry):
            r = (me + o) % PEERS
            first = turned(n, 0, 2 * r, 0)
            second = turned(n, 0, 2 * r + 1, 0)

            @pl.when(o < PEERS)
            def away():
                send[r, 0] = first
                send[r, 1] = second
                query_copy(n, r, me).start()

            @pl.when(o == PEERS)
            def home():
                kept[n, me, 0] = first
                kept[n, me, 1] = second

            return carry

        lax.fori_loop(1, PEERS + 1, make_queries, 0)

    def attention(n, part):
        def await_keys(o, carry):
            key_copy(n, me, (me + o) % PEERS).wait_recv()
            return carry

        def turn_values(j, carry):
            vt[j] = kept[n, j, 3].astype(jnp.float32).T.astype(jnp.bfloat16)
            return carry

        @pl.when(part == 0)
        def opening():
            lax.fori_loop(1, PEERS, await_keys, 0)
            lax.fori_loop(0, PEERS, turn_values, 0)

        def block(o, carry):
            j = (me + o) % PEERS

            @pl.when(o > 0)
            def arrived():
                query_copy(n, me, j).wait_recv()

            queries = kept[n, j, 0:2].reshape(2 * 128, HEAD_SIZE)
            keys = kept[n, :, 2].reshape(PEERS * 128, HEAD_SIZE)
            scores = lax.dot_general(keys, queries, NT, preferred_element_type=jnp.float32) * SCALE
            allowed = key_place[...] <= query_cap[j]
            scores = jnp.where(allowed, scores, masked_logits)
            highest = jnp.max(scores, axis=0, keepdims=True)
            expo = jnp.exp(scores - highest)
            total = jnp.sum(expo, axis=0, keepdims=True)
            expo_low = expo.astype(jnp.bfloat16)
            turned_out = jnp.zeros((HEAD_SIZE, 256), jnp.float32)
            for i in range(PEERS):
                turned_out += jnp.dot(
                    vt[i], expo_low[i * 128 : (i + 1) * 128], preferred_element_type=jnp.float32
                )
            turned_out = turned_out / total
            kept_out[j] = turned_out
            kept_log[j] = jnp.broadcast_to(highest + jnp.log(total), (8, 256))
            attended = turned_out.T.astype(jnp.bfloat16).reshape(2, 128, HEAD_SIZE)

            @pl.when(o == 0)
            def home():
                orecv[me] = attended

            @pl.when(o > 0)
            def away():
                osend[j] = attended
                out_copy(j, me).start()

            return carry

        lax.fori_loop(2 * part, 2 * part + 2, block, 0)

        @pl.when(part == 3)
        def closing():
            save(n, 3).start()
            save(n, 4).start()
            save_kept(n).start()

    def close_attention(n):
        def collect(o, carry):
            h = (me + o) % PEERS

            @pl.when(o > 0)
            def arrived():
                out_copy(me, h).wait_recv()

            attn_low[:, head_columns(0, 2 * h)] = orecv[h, 0]
            attn_low[:, head_columns(0, 2 * h + 1)] = orecv[h, 1]
            return carry

        lax.fori_loop(0, PEERS, collect, 0)
        save(n, 0).wait()
        middle[...] = stream[...]
        gather.ready(n, 3)

        def body(i, slot):
            columns = pl.ds(pl.multiple_of(i * 512, 512), 512)
            middle[...] += jnp.dot(
                attn_low[:, columns], rows_w[slot], preferred_element_type=jnp.float32
            )

        stream_blocks(
            0,
            4,
            BUFFERS,
            lambda i, slot: rows_copy(out_w, n, i, slot).start(),
            lambda i, slot: rows_copy(out_w, n, i, slot).wait(),
            body,
        )
        save(n, 2).start()

    def middle_norm(n):
        turn(attn_low, attn_t, n, 16)
        low[...] = rms(middle[...], mlp_gains[n]).astype(jnp.bfloat16)
        turn(low, mid_t, n, 8)

        def settle(o, carry):
            r = (me + o) % PEERS
            key_copy(n, r, me).wait_send()
            query_copy(n, r, me).wait_send()
            out_copy(r, me).wait_send()
            return carry

        lax.fori_loop(1, PEERS, settle, 0)

    def gate_copy(n, i, slot, k):
        columns = pl.ds(pl.multiple_of(k * 3072 + i * 512, 512), 512)
        return pltpu.make_async_copy(
            gate_up.at[slot, k], both_out.at[n, :, columns], gate_sem.at[slot, k]
        )

    def widen(n, part):
        @pl.when(part == 0)
        def opening():
            gather.ready(n, 4)
            gather.ready(n, 5)

        def column(i):
            return i % 2 * 3072 + i // 2 * 512

        def body(i, slot):
            k = i % 2
            at = i // 2
            held = at % 2

            @pl.when(i >= 4)
            def settle():
                gate_copy(n, at - 2, held, k).wait()

            gate_up[held, k] = jnp.dot(
                low[...], cols_w[slot], preferred_element_type=jnp.float32
            )
            gate_copy(n, at, held, k).start()

            @pl.when(k == 1)
            def finish():
                gate = gate_up[held, 0]
                columns = pl.ds(pl.multiple_of(at * 512, 512), 512)
                hidden_low[:, columns] = (
                    gate * jax.nn.sigmoid(gate) * gate_up[held, 1]
                ).astype(jnp.bfloat16)

        stream_blocks(
            4 * part,
            4,
            BUFFERS,
            lambda i, slot: cols_copy(wide_w, n, column(i), slot).start(),
            lambda i, slot: cols_copy(wide_w, n, column(i), slot).wait(),
            body,
        )
        @pl.when(part == 2)
        def closing():
            for at in (4, 5):
                for k in range(2):
                    gate_copy(n, at, at % 2, k).wait()

    def turn_hidden(n):
        turn(hidden_low, hidden_t, n, 24)

    def narrow(n):
        gather.ready(n, 6)
        stream[...] = middle[...]

        def body(i, slot):
            columns = pl.ds(pl.multiple_of(i * 512, 512), 512)
            stream[...] += jnp.dot(
                hidden_low[:, columns], rows_w[slot], preferred_element_type=jnp.float32
            )

        stream_blocks(
            0,
            6,
            BUFFERS,
            lambda i, slot: rows_copy(down_w, n, i, slot).start(),
            lambda i, slot: rows_copy(down_w, n, i, slot).wait(),
            body,
        )
        for k in range(1, 5):
            save(n, k).wait()
        save_kept(n).wait()

    def when_at(u, index):
        return (u == SCHEDULE[0][index]) | (u == SCHEDULE[1][index])

    def at_among(u, first, blocks):
        part = jnp.zeros((), jnp.int32)
        for k in range(blocks):
            part = jnp.where(when_at(u, first + k), k, part)
        chosen = functools.reduce(jnp.logical_or, [when_at(u, first + k) for k in range(blocks)])
        return chosen, part

    def step(u, carry):
        gather.step(u)
        n = jnp.where(u >= SCHEDULE[1][0], 1, 0)
        pieces = (
            (1, keys_part), (1, values_part), (1, queries_part), (1, spread_queries),
            (4, attention), (1, close_attention), (1, middle_norm), (3, widen), (1, turn_hidden),
            (1, narrow),
        )
        index = 0
        for blocks, work in pieces:
            chosen, part = at_among(u, index, blocks)

            @pl.when(chosen)
            def piece(blocks=blocks, work=work, part=part):
                if blocks == 1:
                    work(n)
                else:
                    work(n, part)

            index += blocks
        return carry

    lax.fori_loop(0, SCHEDULE[1][-1] + 1, step, 0)
    output[...] = (stream[...] * live[...]).astype(jnp.bfloat16)
    gather.drain()
    for copy in gain_copies:
        copy.wait_send()


def forward(weights, gains, tokens, stretch_ids, lengths, number):
    count = DECODER_LAYERS
    dma = pltpu.SemaphoreType.DMA
    low, wide = jnp.bfloat16, jnp.float32
    pair = pltpu.VMEM((PEERS, 2, 128, HEAD_SIZE), low)
    anywhere = pl.BlockSpec(memory_space=pl.ANY)
    near = pl.BlockSpec(memory_space=pltpu.VMEM)
    gathered = [(1024, 4096), (2048, 1024), (1024, 6144), (3072, 1024)]
    saved = [
        ((128, 6144), wide), ((128, 1024), wide), ((128, 1024), wide), ((128, 4096), wide),
        ((PEERS, 4, 128, HEAD_SIZE), low), ((PEERS, HEAD_SIZE, 256), wide), ((PEERS, 8, 256), wide),
    ]
    turned = [(3072, 128), (1024, 128), (2048, 128), (1024, 128)]
    results = (
        [((count,) + s, low) for s in gathered]
        + [((count,) + s, d) for s, d in saved]
        + [((count,) + s, low) for s in turned]
        + [((count, 1, 1024), wide)] * 2
        + [((count, 2, HEAD_SIZE), wide), ((128, 1024), low), ((128, 1), wide)]
        + [((128, HEAD_SIZE), wide)] * 2
        + [((PEERS * 128, 1), jnp.int32), ((PEERS, 1, 256), jnp.int32)]
    )
    return pl.pallas_call(
        forward_kernel,
        out_shape=[jax.ShapeDtypeStruct(s, d) for s, d in results],
        in_specs=[anywhere] * MEMBERS + [near] * 5 + [pl.BlockSpec(memory_space=pltpu.SMEM)] * 2,
        out_specs=[anywhere] * 11 + [near] * 13,
        scratch_shapes=gather_scratch(count)
        + [
            pltpu.VMEM((2, count, 512), wide),
            pltpu.VMEM((2, count, 512), wide),
            pltpu.VMEM((2, count, 64), wide),
            pltpu.VMEM((2, count, 64), wide),
            pltpu.VMEM((128, 1024), wide),
            pltpu.VMEM((128, 1024), wide),
            pltpu.VMEM((128, 4096), wide),
            pltpu.VMEM((128, 1024), low),
            pltpu.VMEM((128, 2048), low),
            pltpu.VMEM((128, 3072), low),
            pltpu.VMEM((2, 2, 128, 512), wide),
            pltpu.VMEM((BUFFERS, 1024, 512), low),
            pltpu.VMEM((BUFFERS, 512, 1024), low),
            pltpu.VMEM((count, PEERS, 4, 128, HEAD_SIZE), low),
            pltpu.VMEM((PEERS, HEAD_SIZE, 256), wide),
            pltpu.VMEM((PEERS, 8, 256), wide),
            pltpu.VMEM((PEERS, 4, 128, HEAD_SIZE), low),
            pair,
            pair,
            pltpu.VMEM((PEERS, HEAD_SIZE, 128), low),
            dma((4,)), dma((BUFFERS,)), dma((BUFFERS,)), dma((2, 2)), dma((6,)),
        ]
        + [dma((PEERS,))] * 6,
        compiler_params=pltpu.CompilerParams(
            collective_id=number, has_side_effects=True, vmem_limit_bytes=56 * 2**20
        ),
        name="forward",
    )(*weights, *gains, tokens, stretch_ids, lengths)


WORK = 12


def rms_back(values, gain, upstream):
    r = lax.rsqrt(jnp.mean(values * values, axis=-1, keepdims=True) + norm_epsilon)
    weighted = upstream * gain
    mean = jnp.mean(weighted * values, axis=-1, keepdims=True)
    grad = r * weighted - values * (r * r * r) * mean
    return grad, jnp.sum(upstream * values * r, axis=0, keepdims=True)


def backward_kernel(*refs):
    count = DECODER_LAYERS
    acts, stored, refs = refs[:4], refs[4:11], refs[11:]
    (into_w, out_w, wide_w, down_w) = refs[:4]
    (cotangent, attn_gains, mlp_gains, head_gains, live, cosine, sine, key_place, query_cap) = (
        refs[4:13]
    )
    results = refs[13:20]
    grad_stream, gain_out, held = refs[20:23]
    refs = refs[23:]
    sizes = len(reduce_scratch(count))
    reduce_refs, refs = refs[:sizes], refs[sizes:]
    gain_refs, refs = refs[:4], refs[4:]
    (down_low, both_low, out_low, pre_low, terms,
     gate_up, middle, entry, pre, kept, kept_out, kept_log, mid_grad, rows_w, wide_rows,
     dsend, drecv, qsend, qrecv, ksend, krecv, kt, key_sum, value_sum,
     load_sem, rows_sem, wide_sem, gate_sem, d_s, d_r, q_s, q_r, k_s, k_r) = refs
    reducer = Reducer(
        acts, ((down_low, 1), (both_low, 6), (out_low, 1), (pre_low, 4)), results,
        (held,) + tuple(reduce_refs), tuple(reversed(range(count))),
    )
    gain_sum = GainSum(reducer, terms, gain_out, gain_refs)
    c = lax.axis_index("ctx")
    x = lax.axis_index("fsdp")
    me = c % PEERS
    z = c // 4

    def peer(r):
        return (c - me + r, x)

    barrier = pltpu.get_barrier_semaphore()

    def greet(o, carry):
        pl.semaphore_signal(barrier, inc=1, device_id=peer((me + o) % PEERS), device_id_type=MESH)
        return carry

    lax.fori_loop(1, PEERS, greet, 0)
    pl.semaphore_signal(barrier, inc=1, device_id=reducer.across, device_id_type=MESH)
    for o in range(2):
        far = ((z // 2 * 2 + 2) % 4 + o) * 4 + c % 4
        pl.semaphore_signal(barrier, inc=1, device_id=(far, x), device_id_type=MESH)
    pl.semaphore_wait(barrier, PEERS + 2)

    grad_stream[...] = cotangent[...].astype(jnp.float32) * live[...]
    terms[...] = jnp.zeros_like(terms)
    reducer.start_acts(0, (0,))

    cos = cosine[...]
    sin = sine[...]

    def grad_copy(r, slot):
        return make_remote(dsend.at[r], drecv.at[slot], d_s.at[r], d_r.at[slot], peer(r))

    def query_copy(r, slot):
        return make_remote(qsend.at[r], qrecv.at[slot], q_s.at[r], q_r.at[slot], peer(r))

    def key_copy(r, slot):
        return make_remote(ksend.at[r], krecv.at[slot], k_s.at[r], k_r.at[slot], peer(r))

    saved = (middle, entry, pre, kept, kept_out, kept_log)

    def load(layer, k):
        return pltpu.make_async_copy(stored[1 + k].at[layer], saved[k], load_sem.at[k])

    def await_load(k):
        load(0, k).wait()

    def add_term(layer, first, term):
        for i in range(8):
            terms[pl.ds(layer * 24 + first + i, 1), :] = term[:, i * 128 : (i + 1) * 128]

    def rows_copy(ref, layer, i, slot):
        rows = pl.ds(pl.multiple_of(i * 512, 512), 512)
        return pltpu.make_async_copy(ref.at[layer, rows], rows_w.at[slot], rows_sem.at[slot])

    def wide_copy(ref, layer, i, slot):
        rows = pl.ds(pl.multiple_of(i * 128, 128), 128)
        columns = ref.shape[2]
        return pltpu.make_async_copy(
            ref.at[layer, rows], wide_rows.at[slot, :, pl.ds(0, columns)], wide_sem.at[slot]
        )

    def hidden_part(n, layer, part):
        @pl.when(part == 0)
        def opening():
            for k in range(len(saved)):
                load(layer, k).start()
            down_low[n] = grad_stream[...].astype(jnp.bfloat16)

        @pl.when((n == 0) & (part == 0))
        def first():
            reducer.start_grad(0)
            reducer.start_acts(0, (1, 2, 3))

        def gate_copy(i, slot, k):
            columns = pl.ds(pl.multiple_of(k * 3072 + i * 512, 512), 512)
            return pltpu.make_async_copy(
                stored[0].at[layer, :, columns], gate_up.at[slot, k], gate_sem.at[slot, k]
            )

        def start(i, slot):
            rows_copy(down_w, layer, i, slot).start()
            for k in range(2):
                gate_copy(i, slot, k).start()

        def wait(i, slot):
            rows_copy(down_w, layer, i, slot).wait()
            for k in range(2):
                gate_copy(i, slot, k).wait()

        def body(i, slot):
            hidden = lax.dot_general(
                down_low[n], rows_w[slot], NT, preferred_element_type=jnp.float32
            )
            gate = gate_up[slot, 0]
            up = gate_up[slot, 1]
            sigmoid = jax.nn.sigmoid(gate)
            columns = pl.multiple_of(i * 512, 512)
            both_low[n, :, pl.ds(columns, 512)] = (
                hidden * up * sigmoid * (1.0 + gate * (1.0 - sigmoid))
            ).astype(jnp.bfloat16)
            both_low[n, :, pl.ds(3072 + columns, 512)] = (hidden * gate * sigmoid).astype(
                jnp.bfloat16
            )

        stream_blocks(part * 3, 3, 2, start, wait, body)

        @pl.when((n == 0) & (part == 1))
        def rest():
            reducer.begin_more()

    def middle_part(n, layer, part):
        def body(i, slot):
            mid_grad[:, pl.ds(pl.multiple_of(i * 128, 128), 128)] = lax.dot_general(
                both_low[n], wide_rows[slot], NT, preferred_element_type=jnp.float32
            )

        stream_blocks(
            part * 3,
            jnp.where(part == 2, 2, 3),
            2,
            lambda i, slot: wide_copy(wide_w, layer, i, slot).start(),
            lambda i, slot: wide_copy(wide_w, layer, i, slot).wait(),
            body,
        )

        @pl.when(part == 2)
        def closing():
            await_load(0)
            grad, term = rms_back(middle[...], mlp_gains[layer], mid_grad[...])
            add_term(layer, 8, term)
            total = grad_stream[...] + grad
            grad_stream[...] = total
            out_low[n] = total.astype(jnp.bfloat16)

    def out_part(n, layer):
        def place(i):
            return (i + me // 2) % 4

        def body(i, slot):
            low = lax.dot_general(
                out_low[n], rows_w[slot], NT, preferred_element_type=jnp.float32
            ).astype(jnp.bfloat16)
            for k in range(2):
                r = 2 * place(i) + k

                @pl.when(r == me)
                def home(k=k):
                    for j in range(2):
                        at = (2 * k + j) * HEAD_SIZE
                        drecv[me, j] = low[:, at : at + HEAD_SIZE]

                @pl.when(r != me)
                def away(k=k, r=r):
                    for j in range(2):
                        at = (2 * k + j) * HEAD_SIZE
                        dsend[r, j] = low[:, at : at + HEAD_SIZE]
                    grad_copy(r, me).start()

        stream_blocks(
            0,
            4,
            2,
            lambda i, slot: rows_copy(out_w, layer, place(i), slot).start(),
            lambda i, slot: rows_copy(out_w, layer, place(i), slot).wait(),
            body,
        )
        for k in range(2, len(saved)):
            await_load(k)

        def turn_keys(j, carry):
            kt[j] = kept[j, 2].astype(jnp.float32).T.astype(jnp.bfloat16)
            return carry

        lax.fori_loop(0, PEERS, turn_keys, 0)
        key_sum[...] = jnp.zeros_like(key_sum)
        value_sum[...] = jnp.zeros_like(value_sum)

    def attention_block(o):
        j = (me + o) % PEERS

        @pl.when(o > 0)
        def arrived():
            grad_copy(me, j).wait_recv()

        grads = drecv[j].reshape(2 * 128, HEAD_SIZE)
        delta = jnp.sum(grads.astype(jnp.float32).T * kept_out[j], axis=0, keepdims=True)
        queries = kept[j, 0:2].reshape(2 * 128, HEAD_SIZE)
        keys = kept[:, 2].reshape(PEERS * 128, HEAD_SIZE)
        values = kept[:, 3].reshape(PEERS * 128, HEAD_SIZE)
        scores = lax.dot_general(keys, queries, NT, preferred_element_type=jnp.float32) * SCALE
        allowed = key_place[...] <= query_cap[j]
        scores = jnp.where(allowed, scores, masked_logits)
        prob = jnp.exp(scores - kept_log[j, 0:1, :])
        dprob = lax.dot_general(values, grads, NT, preferred_element_type=jnp.float32)
        dscore = (prob * (dprob - delta)).astype(jnp.bfloat16)
        value_sum[...] += jnp.dot(
            prob.astype(jnp.bfloat16), grads, preferred_element_type=jnp.float32
        )
        key_sum[...] += jnp.dot(dscore, queries, preferred_element_type=jnp.float32)
        turned = jnp.zeros((HEAD_SIZE, 256), jnp.float32)
        for i in range(PEERS):
            turned += jnp.dot(
                kt[i], dscore[i * 128 : (i + 1) * 128], preferred_element_type=jnp.float32
            )
        query_grad = (turned * SCALE).T.astype(jnp.bfloat16).reshape(2, 128, HEAD_SIZE)

        @pl.when(o == 0)
        def home():
            qrecv[me] = query_grad

        @pl.when(o > 0)
        def away():
            qsend[j] = query_grad
            query_copy(j, me).start()

        @pl.when(o == PEERS - 1)
        def keys_done():
            lax.fori_loop(1, PEERS + 1, push_keys, 0)

    def push_keys(o, carry):
        j = (me + o) % PEERS
        rows = pl.ds(pl.multiple_of(j * 128, 128), 128)
        key = (key_sum[rows, :] * SCALE).astype(jnp.bfloat16)
        value = value_sum[rows, :].astype(jnp.bfloat16)

        @pl.when(o < PEERS)
        def away():
            ksend[j, 0] = key
            ksend[j, 1] = value
            key_copy(j, me).start()

        @pl.when(o == PEERS)
        def home():
            krecv[me, 0] = key
            krecv[me, 1] = value

        return carry

    def head_part(n, layer):
        def back(grad, first, index, gain):
            g = grad.astype(jnp.float32)
            dy = g * cos - pltpu.roll(g, HEAD_SIZE // 2, 1) * sin
            low, term = rms_back(pre[:, head_columns(first, index)], gain, dy)
            return low.astype(jnp.bfloat16), term

        def finish_queries(o, total):
            h = (me + o) % PEERS

            @pl.when(o > 0)
            def arrived():
                query_copy(me, h).wait_recv()

            for i in range(2):
                low, term = back(qrecv[h, i], 0, 2 * h + i, head_gains[layer, 0:1, :])
                pre_low[n, :, head_columns(0, 2 * h + i)] = low
                total += term
            return total

        zero = jnp.zeros((1, HEAD_SIZE), jnp.float32)
        terms[pl.ds(layer * 24 + 16, 1), :] = lax.fori_loop(0, PEERS, finish_queries, zero)

        def finish_keys(o, total):
            h = (me + o) % PEERS

            @pl.when(o > 0)
            def arrived():
                key_copy(me, h).wait_recv()

            low, term = back(krecv[h, 0], 2048, h, head_gains[layer, 1:2, :])
            pre_low[n, :, head_columns(2048, h)] = low
            pre_low[n, :, head_columns(3072, h)] = krecv[h, 1]
            return total + term

        terms[pl.ds(layer * 24 + 17, 1), :] = lax.fori_loop(0, PEERS, finish_keys, zero)

        def settle(o, carry):
            r = (me + o) % PEERS
            grad_copy(r, me).wait_send()
            query_copy(r, me).wait_send()
            key_copy(r, me).wait_send()
            return carry

        lax.fori_loop(1, PEERS, settle, 0)

    def entry_part(n, layer, part):
        def body(i, slot):
            mid_grad[:, pl.ds(pl.multiple_of(i * 128, 128), 128)] = lax.dot_general(
                pre_low[n], wide_rows[slot, :, 0:4096], NT, preferred_element_type=jnp.float32
            )

        stream_blocks(
            part * 4,
            4,
            2,
            lambda i, slot: wide_copy(into_w, layer, i, slot).start(),
            lambda i, slot: wide_copy(into_w, layer, i, slot).wait(),
            body,
        )

        @pl.when(part == 1)
        def closing():
            await_load(1)
            grad, term = rms_back(entry[...], attn_gains[layer], mid_grad[...])
            add_term(layer, 0, term)
            grad_stream[...] += grad

    def step(w, carry):
        reducer.step(w - 2)
        gain_sum.step(w, WORK * count)
        n = w // WORK
        phase = w % WORK
        layer = count - 1 - n
        busy = w < WORK * count

        @pl.when(busy & (phase < 2))
        def phase_hidden():
            hidden_part(n, layer, phase)

        @pl.when(busy & (phase >= 2) & (phase < 5))
        def phase_middle():
            middle_part(n, layer, phase - 2)

        @pl.when(busy & (phase == 5))
        def phase_out():
            out_part(n, layer)

        @pl.when(busy & (phase >= 6) & (phase < 9))
        def phase_attention():
            first = (phase - 6) * 3

            def block(i, inner):
                attention_block(first + i)
                return inner

            lax.fori_loop(0, jnp.minimum(3, PEERS - first), block, 0)

        @pl.when(busy & (phase == 9))
        def phase_heads():
            head_part(n, layer)

        @pl.when(busy & (phase >= 10))
        def phase_entry():
            entry_part(n, layer, phase - 10)

        return carry

    lax.fori_loop(0, reducer.steps() + 2, step, 0)
    reducer.drain()
    gain_sum.drain()


RESULTS = ((32, 2048), (32, 1024), (32, 1024), (64, 1024), (32, 3072), (32, 3072), (96, 1024))


def backward(acts, saved, weights, cotangent, gains, tables, number):
    count = DECODER_LAYERS
    dma = pltpu.SemaphoreType.DMA
    low, wide = jnp.bfloat16, jnp.float32
    pair = pltpu.VMEM((PEERS, 2, 128, HEAD_SIZE), low)
    anywhere = pl.BlockSpec(memory_space=pl.ANY)
    near = pl.BlockSpec(memory_space=pltpu.VMEM)
    return pl.pallas_call(
        backward_kernel,
        out_shape=[jax.ShapeDtypeStruct((count,) + shape, wide) for shape in RESULTS]
        + [
            jax.ShapeDtypeStruct((128, 1024), wide),
            jax.ShapeDtypeStruct((24 * count, 128), wide),
            jax.ShapeDtypeStruct((GRADS * count, 384, 1024), low),
        ],
        in_specs=[anywhere] * 15 + [near] * 9,
        out_specs=[near] * 9 + [anywhere],
        scratch_shapes=reduce_scratch(count)
        + gain_scratch(24 * count)
        + [
            pltpu.VMEM((count, 128, 1024), low),
            pltpu.VMEM((count, 128, 6144), low),
            pltpu.VMEM((count, 128, 1024), low),
            pltpu.VMEM((count, 128, 4096), low),
            pltpu.VMEM((24 * count, 128), wide),
            pltpu.VMEM((2, 2, 128, 512), wide),
            pltpu.VMEM((128, 1024), wide),
            pltpu.VMEM((128, 1024), wide),
            pltpu.VMEM((128, 4096), wide),
            pltpu.VMEM((PEERS, 4, 128, HEAD_SIZE), low),
            pltpu.VMEM((PEERS, HEAD_SIZE, 256), wide),
            pltpu.VMEM((PEERS, 8, 256), wide),
            pltpu.VMEM((128, 1024), wide),
            pltpu.VMEM((2, 512, 1024), low),
            pltpu.VMEM((2, 128, 6144), low),
        ]
        + [pair] * 6
        + [
            pltpu.VMEM((PEERS, HEAD_SIZE, 128), low),
            pltpu.VMEM((PEERS * 128, HEAD_SIZE), wide),
            pltpu.VMEM((PEERS * 128, HEAD_SIZE), wide),
            dma((6,)), dma((2,)), dma((2,)), dma((2, 2)),
        ]
        + [dma((PEERS,))] * 6,
        compiler_params=pltpu.CompilerParams(
            collective_id=number, has_side_effects=True, vmem_limit_bytes=62 * 2**20
        ),
        name="backward",
    )(*acts, *saved, *weights, cotangent, *gains, *tables)


def finish_kernel(*refs):
    count = DECODER_LAYERS
    moved, sums = refs[:9], refs[9]
    outs, gain_outs = refs[10:19], refs[19:23]
    held, sems = refs[23:32], refs[32]

    def into(k):
        return pltpu.make_async_copy(moved[k], held[k], sems.at[0, k])

    def onward(k):
        return pltpu.make_async_copy(held[k], outs[k], sems.at[1, k])

    for k in range(9):
        into(k).start()
    for k in range(9):
        into(k).wait()
        onward(k).start()
    place = lax.axis_index("ctx") * 2 + lax.axis_index("fsdp")

    def cut(row, offset, span):
        values = sums[pl.ds(row, 1), :]
        return pltpu.roll(values, (128 - offset) % 128, 1)[:, :span]

    for n in range(count):
        first = 24 * n
        for k in range(2):
            gain_outs[k][n : n + 1, :] = cut(first + 8 * k + place // 4, place % 4 * 32, 32)
            gain_outs[2 + k][n : n + 1, :] = cut(first + 16 + k, place * 4, 4)
    for k in range(9):
        onward(k).wait()


def finish(moved, sums):
    count = DECODER_LAYERS
    anywhere = pl.BlockSpec(memory_space=pl.ANY)
    near = pl.BlockSpec(memory_space=pltpu.VMEM)
    return pl.pallas_call(
        finish_kernel,
        out_shape=[jax.ShapeDtypeStruct(member.shape, member.dtype) for member in moved]
        + [jax.ShapeDtypeStruct((count, span), jnp.float32) for span in (32, 32, 4, 4)],
        in_specs=[anywhere] * 9 + [near],
        out_specs=[anywhere] * 9 + [near] * 4,
        scratch_shapes=[pltpu.VMEM(member.shape, member.dtype) for member in moved]
        + [pltpu.SemaphoreType.DMA((2, 9))],
        compiler_params=pltpu.CompilerParams(vmem_limit_bytes=60 * 2**20),
        name="finish",
    )(*moved, sums)


def from_partner(shard, axis, apart):
    return lax.ppermute(shard, axis, [(i, i ^ 1 << apart) for i in range(lax.axis_size(axis))])


def token_places(stretch_table, slot_lengths):
    ctx_count = stretch_table.shape[0]
    stretch_order = stretch_table.reshape(-1)
    within = jnp.arange(STRETCH, dtype=jnp.int32)
    places = (stretch_order % ctx_count * STRETCH)[:, None] + within[None, :]
    slot_ids = jnp.broadcast_to((stretch_order // ctx_count)[:, None], places.shape).reshape(-1)
    places = places.reshape(-1)
    limits = jnp.where(slot_ids == 0, slot_lengths[0], slot_lengths[1])
    return (places, slot_ids, places < limits)


def rotary_tables(places):
    half_dim = HEAD_SIZE // 2
    spread = jnp.arange(half_dim, dtype=jnp.int32).astype(jnp.float32) * (2.0 / HEAD_SIZE)
    inverse = jnp.exp(spread * -math.log(rope_base))
    angles = places.astype(jnp.float32)[:, None] * inverse[None, :]
    return (
        jnp.concatenate([jnp.cos(angles)] * 2, axis=-1),
        jnp.concatenate([jnp.sin(angles)] * 2, axis=-1),
    )


def rotate(values, cosine_table, sine_table):
    half_dim = values.shape[-1] // 2
    turned = jnp.concatenate([-values[..., half_dim:], values[..., :half_dim]], axis=-1)
    return values * cosine_table[:, None, :] + turned * sine_table[:, None, :]


def unrotate(upstream, cosine_table, sine_table):
    half_dim = upstream.shape[-1] // 2
    scaled_sine = upstream * sine_table[:, None, :]
    turned_back = jnp.concatenate(
        [scaled_sine[..., half_dim:], -scaled_sine[..., :half_dim]], axis=-1
    )
    return upstream * cosine_table[:, None, :] + turned_back


def norm_forward(values, gain_vec):
    scale_inv = lax.rsqrt(jnp.mean(values * values, axis=-1, keepdims=True) + norm_epsilon)
    return (values * scale_inv * gain_vec, scale_inv)


def norm_backward(values, scale_inv, gain_vec, upstream):
    weighted = upstream * gain_vec
    grad_input = scale_inv * weighted - values * scale_inv**3 * jnp.mean(
        weighted * values, axis=-1, keepdims=True
    )
    gain_term = jnp.sum((upstream * values * scale_inv).reshape(-1, values.shape[-1]), axis=0)
    return (grad_input, gain_term)


def upper_bit(local_index, bit_number):
    return local_index // 2**bit_number % 2 == 1


def joined_rows(mine, received, upper_side):
    first_rows = jnp.where(upper_side, received, mine)
    second_rows = jnp.where(upper_side, mine, received)
    return jnp.concatenate([first_rows, second_rows], axis=0)


def half_gather(pair, local_index):
    gathered_rows = pair
    for bit_number in range(lax.axis_size("ctx").bit_length() - 2):
        received = from_partner(gathered_rows, "ctx", bit_number)
        gathered_rows = joined_rows(gathered_rows, received, upper_bit(local_index, bit_number))
    return gathered_rows


def half_reduce(term, local_index):
    for bit_number in reversed(range(lax.axis_size("ctx").bit_length() - 2)):
        span = term.shape[0] // 2
        lower_rows = term[:span]
        upper_rows = term[span:]
        upper_side = upper_bit(local_index, bit_number)
        kept_rows = jnp.where(upper_side, upper_rows, lower_rows)
        sent_rows = jnp.where(upper_side, lower_rows, upper_rows)
        term = kept_rows + from_partner(sent_rows, "ctx", bit_number)
    return term


def over_keys(update, carried, count_rows):
    block_length = math.gcd(count_rows, 512)

    def inner_step(current, block_index):
        return (update(current, block_index * block_length, block_length), None)

    carried, unused = lax.scan(
        inner_step, carried, jnp.arange(count_rows // block_length, dtype=jnp.int32)
    )
    return carried


def allowed_mask(key_meta, query_meta, row_start, block_length):
    key_places = lax.dynamic_slice_in_dim(key_meta[0], row_start, block_length)
    key_slots = lax.dynamic_slice_in_dim(key_meta[1], row_start, block_length)
    key_live = lax.dynamic_slice_in_dim(key_meta[2], row_start, block_length)
    allowed = (
        (key_slots[None, :] == query_meta[1][:, None])
        & (key_places[None, :] <= query_meta[0][:, None])
        & key_live[None, :]
    )
    return allowed[None, None]


def forward_update(
    current, query_head_group, key_tile_block, value_tile_block, allowed, score_scale
):
    running_max, running_sum, running_acc = current
    block_length = key_tile_block.shape[0]
    key_head_list = key_tile_block.reshape(block_length, KEY_VALUE_HEADS, HEAD_SIZE)
    value_head_list = value_tile_block.reshape(block_length, KEY_VALUE_HEADS, HEAD_SIZE)
    scores = (
        jnp.einsum(
            "qhgd,khd->hgqk", query_head_group, key_head_list, preferred_element_type=jnp.float32
        )
        * score_scale
    )
    scores = jnp.where(allowed, scores, masked_logits)
    new_max = jnp.maximum(running_max, jnp.max(scores, axis=-1))
    factor = jnp.exp(running_max - new_max)
    prob_block = jnp.where(allowed, jnp.exp(scores - new_max[..., None]), 0.0)
    new_sum = running_sum * factor + jnp.sum(prob_block, axis=-1)
    new_acc = running_acc * factor[..., None] + jnp.einsum(
        "hgqk,khd->hgqd",
        prob_block.astype(jnp.bfloat16),
        value_head_list,
        preferred_element_type=jnp.float32,
    )
    return (new_max, new_sum, new_acc)


def score_parts(
    query_head_group,
    output_grad_group,
    key_tile_block,
    value_tile_block,
    allowed,
    log_total,
    row_delta,
    score_scale,
):
    block_length = key_tile_block.shape[0]
    key_head_list = key_tile_block.reshape(block_length, KEY_VALUE_HEADS, HEAD_SIZE)
    value_head_list = value_tile_block.reshape(block_length, KEY_VALUE_HEADS, HEAD_SIZE)
    scores = (
        jnp.einsum(
            "qhgd,khd->hgqk", query_head_group, key_head_list, preferred_element_type=jnp.float32
        )
        * score_scale
    )
    prob_block = jnp.where(allowed, jnp.exp(scores - log_total[..., None]), 0.0)
    dprob = jnp.einsum(
        "qhgd,khd->hgqk", output_grad_group, value_head_list, preferred_element_type=jnp.float32
    )
    dscore_low = (prob_block * (dprob - row_delta[..., None])).astype(jnp.bfloat16)
    return (prob_block, dscore_low, key_head_list)


def attention_inputs(stream, gathered, cosine_table, sine_table):
    count_rows = stream.shape[0]
    normalized, inv_attn = norm_forward(stream, gathered[7].astype(jnp.float32))
    normed_low = normalized.astype(jnp.bfloat16)
    query_heads = jnp.dot(normed_low, gathered[0], preferred_element_type=jnp.float32).reshape(
        count_rows, QUERY_HEADS, HEAD_SIZE
    )
    key_head_list = jnp.dot(normed_low, gathered[1], preferred_element_type=jnp.float32).reshape(
        count_rows, KEY_VALUE_HEADS, HEAD_SIZE
    )
    value_low = jnp.dot(normed_low, gathered[2], preferred_element_type=jnp.float32).astype(
        jnp.bfloat16
    )
    query_normed, inv_query = norm_forward(query_heads, gathered[9].astype(jnp.float32))
    key_normed, inv_key = norm_forward(key_head_list, gathered[10].astype(jnp.float32))
    query_lowered = rotate(query_normed, cosine_table, sine_table).astype(jnp.bfloat16)
    key_low = (
        rotate(key_normed, cosine_table, sine_table)
        .astype(jnp.bfloat16)
        .reshape(count_rows, KEY_VALUE_HEADS * HEAD_SIZE)
    )
    return {
        "normed_low": normed_low,
        "inv_attn": inv_attn,
        "query_heads": query_heads,
        "inv_query": inv_query,
        "key_heads": key_head_list,
        "inv_key": inv_key,
        "query_low": query_lowered,
        "key_low": key_low,
        "value_low": value_low,
    }


def block_rest(stream, gathered, attn_low):
    middle = stream + jnp.dot(attn_low, gathered[3], preferred_element_type=jnp.float32)
    normed_mid, inv_mid = norm_forward(middle, gathered[8].astype(jnp.float32))
    normed_mid_low = normed_mid.astype(jnp.bfloat16)
    gate_act = jnp.dot(normed_mid_low, gathered[4], preferred_element_type=jnp.float32)
    upward = jnp.dot(normed_mid_low, gathered[5], preferred_element_type=jnp.float32)
    hidden_low = (jax.nn.silu(gate_act) * upward).astype(jnp.bfloat16)
    result = middle + jnp.dot(hidden_low, gathered[6], preferred_element_type=jnp.float32)
    return {
        "middle": middle,
        "inv_mid": inv_mid,
        "normed_mid_low": normed_mid_low,
        "gate_act": gate_act,
        "upward": upward,
        "hidden_low": hidden_low,
        "result": result,
    }


def general_device(
    tokens,
    cotangent,
    lengths,
    stretch_ids,
    w_query,
    key_projection_weight,
    value_projection_weight,
    w_out,
    w_gate,
    w_up,
    w_down,
    g_attn,
    g_mlp,
    g_query,
    g_key,
):
    count_rows = tokens.shape[0]
    ctx_count = lax.axis_size("ctx")
    half_count = ctx_count // 2
    key_value_width = KEY_VALUE_HEADS * HEAD_SIZE
    key_meta = token_places(stretch_ids[:, 0, :], lengths[0])
    ctx_index = lax.axis_index("ctx")
    local_index = ctx_index % half_count
    base_row = ctx_index // half_count * half_count * count_rows
    half_row_set = half_count * count_rows
    offset_mine = ctx_index * count_rows
    query_meta = tuple(
        (lax.dynamic_slice_in_dim(meta_array, offset_mine, count_rows) for meta_array in key_meta)
    )
    live_mine = query_meta[2].astype(jnp.float32)[:, None]
    cosine_table, sine_table = rotary_tables(query_meta[0])
    group_count = QUERY_HEADS // KEY_VALUE_HEADS
    score_scale = HEAD_SIZE ** (-0.5)

    def attend_forward(query_head_group, key_source, value_source, current):

        def update(carried, local_row, block_length):
            key_tile_block = lax.dynamic_slice_in_dim(key_source, local_row, block_length)
            value_tile_block = lax.dynamic_slice_in_dim(value_source, local_row, block_length)
            allowed = allowed_mask(key_meta, query_meta, base_row + local_row, block_length)
            return forward_update(
                carried, query_head_group, key_tile_block, value_tile_block, allowed, score_scale
            )

        return over_keys(update, current, key_source.shape[0])

    saved = []
    stream = tokens.astype(jnp.float32)
    for layer_index in range(DECODER_LAYERS):
        gathered = (
            lax.all_gather(w_query[layer_index], "fsdp", axis=0, tiled=True),
            lax.all_gather(key_projection_weight[layer_index], "fsdp", axis=0, tiled=True),
            lax.all_gather(value_projection_weight[layer_index], "fsdp", axis=0, tiled=True),
            lax.all_gather(w_out[layer_index], "fsdp", axis=0, tiled=True),
            lax.all_gather(w_gate[layer_index], "fsdp", axis=0, tiled=True),
            lax.all_gather(w_up[layer_index], "fsdp", axis=0, tiled=True),
            lax.all_gather(w_down[layer_index], "fsdp", axis=0, tiled=True),
            lax.all_gather(g_attn[layer_index], "fsdp", axis=0, tiled=True),
            lax.all_gather(g_mlp[layer_index], "fsdp", axis=0, tiled=True),
            lax.all_gather(g_query[layer_index], "fsdp", axis=0, tiled=True),
            lax.all_gather(g_key[layer_index], "fsdp", axis=0, tiled=True),
        )
        present_inputs = attention_inputs(stream, gathered, cosine_table, sine_table)
        query_head_group = present_inputs["query_low"].reshape(
            count_rows, KEY_VALUE_HEADS, group_count, HEAD_SIZE
        )
        start_state = (
            jnp.full((KEY_VALUE_HEADS, group_count, count_rows), masked_logits, jnp.float32),
            jnp.zeros((KEY_VALUE_HEADS, group_count, count_rows), jnp.float32),
            jnp.zeros((KEY_VALUE_HEADS, group_count, count_rows, HEAD_SIZE), jnp.float32),
        )
        pair_all = half_gather(
            jnp.concatenate([present_inputs["key_low"], present_inputs["value_low"]], axis=-1),
            local_index,
        )
        key_all = pair_all[:, :key_value_width]
        value_all = pair_all[:, key_value_width:]
        final_state = attend_forward(query_head_group, key_all, value_all, start_state)
        attended = final_state[2] / final_state[1][..., None]
        log_total = final_state[0] + jnp.log(final_state[1])
        attn_low = (
            jnp.transpose(attended, (2, 0, 1, 3))
            .reshape(count_rows, QUERY_HEADS * HEAD_SIZE)
            .astype(jnp.bfloat16)
        )
        rest = block_rest(stream, gathered, attn_low)
        kept = (gathered, key_all, value_all, present_inputs, rest)
        saved.append((stream, attended, log_total, kept))
        stream = rest["result"]
    output_low = (stream * live_mine).astype(jnp.bfloat16)
    grad_stream = cotangent.astype(jnp.float32) * live_mine
    layer_grads = [None] * DECODER_LAYERS
    for layer_index in reversed(range(DECODER_LAYERS)):
        stream_in, attended, log_total, kept = saved[layer_index]
        attn_low = (
            jnp.transpose(attended, (2, 0, 1, 3))
            .reshape(count_rows, QUERY_HEADS * HEAD_SIZE)
            .astype(jnp.bfloat16)
        )
        gathered, key_all, value_all, present_inputs, rest = kept
        ffn_grad_low = grad_stream.astype(jnp.bfloat16)
        grad_down = jnp.einsum(
            "tf,td->fd", rest["hidden_low"], ffn_grad_low, preferred_element_type=jnp.float32
        )
        hidden_grad = jnp.einsum(
            "td,fd->tf", ffn_grad_low, gathered[6], preferred_element_type=jnp.float32
        )
        gate_act = rest["gate_act"]
        sigmoid_gate = jax.nn.sigmoid(gate_act)
        gate_grad_low = (
            hidden_grad * rest["upward"] * sigmoid_gate * (1.0 + gate_act * (1.0 - sigmoid_gate))
        ).astype(jnp.bfloat16)
        up_grad_low = (hidden_grad * gate_act * sigmoid_gate).astype(jnp.bfloat16)
        grad_gate = jnp.einsum(
            "td,tf->df", rest["normed_mid_low"], gate_grad_low, preferred_element_type=jnp.float32
        )
        grad_up = jnp.einsum(
            "td,tf->df", rest["normed_mid_low"], up_grad_low, preferred_element_type=jnp.float32
        )
        normed_mid_grad = jnp.einsum(
            "tf,df->td", gate_grad_low, gathered[4], preferred_element_type=jnp.float32
        ) + jnp.einsum("tf,df->td", up_grad_low, gathered[5], preferred_element_type=jnp.float32)
        mid_norm_grad, mlp_gain_term = norm_backward(
            rest["middle"], rest["inv_mid"], gathered[8].astype(jnp.float32), normed_mid_grad
        )
        middle_grad = grad_stream + mid_norm_grad
        attn_grad_low = middle_grad.astype(jnp.bfloat16)
        grad_out = jnp.einsum(
            "tq,td->qd", attn_low, attn_grad_low, preferred_element_type=jnp.float32
        )
        output_gradient_lowered = jnp.einsum(
            "td,qd->tq", attn_grad_low, gathered[3], preferred_element_type=jnp.float32
        ).astype(jnp.bfloat16)
        output_grad_group = output_gradient_lowered.reshape(
            count_rows, KEY_VALUE_HEADS, group_count, HEAD_SIZE
        )
        row_delta = jnp.sum(
            jnp.transpose(output_grad_group.astype(jnp.float32), (1, 2, 0, 3)) * attended, axis=-1
        )
        query_head_group = present_inputs["query_low"].reshape(
            count_rows, KEY_VALUE_HEADS, group_count, HEAD_SIZE
        )
        key_block_size = math.gcd(half_row_set, 512)

        def backward_step(query_acc, block_index):
            row_start = block_index * key_block_size
            key_tile_block = lax.dynamic_slice_in_dim(key_all, row_start, key_block_size)
            value_tile_block = lax.dynamic_slice_in_dim(value_all, row_start, key_block_size)
            allowed = allowed_mask(key_meta, query_meta, base_row + row_start, key_block_size)
            prob_block, dscore_low, key_head_list = score_parts(
                query_head_group,
                output_grad_group,
                key_tile_block,
                value_tile_block,
                allowed,
                log_total,
                row_delta,
                score_scale,
            )
            query_next = (query_acc, jnp.zeros((key_block_size, 2 * key_value_width), jnp.float32))[
                0
            ] + jnp.einsum(
                "hgqk,khd->qhgd", dscore_low, key_head_list, preferred_element_type=jnp.float32
            ) * score_scale
            value_grad = jnp.einsum(
                "hgqk,qhgd->khd",
                prob_block.astype(jnp.bfloat16),
                output_grad_group,
                preferred_element_type=jnp.float32,
            )
            key_grad = (
                jnp.einsum(
                    "hgqk,qhgd->khd",
                    dscore_low,
                    query_head_group,
                    preferred_element_type=jnp.float32,
                )
                * score_scale
            )
            block_rows = jnp.concatenate(
                [
                    key_grad.reshape(key_block_size, key_value_width),
                    value_grad.reshape(key_block_size, key_value_width),
                ],
                axis=-1,
            )
            return (query_next, block_rows)

        query_grad, key_value_rows = lax.scan(
            backward_step,
            jnp.zeros((count_rows, KEY_VALUE_HEADS, group_count, HEAD_SIZE), jnp.float32),
            jnp.arange(half_row_set // key_block_size, dtype=jnp.int32),
        )
        key_value_term = key_value_rows.reshape(half_row_set, 2 * key_value_width)
        key_value_gradient = half_reduce(key_value_term, local_index)
        key_gradient_rows = key_value_gradient[:, :key_value_width].reshape(
            count_rows, KEY_VALUE_HEADS, HEAD_SIZE
        )
        value_grad_low = key_value_gradient[:, key_value_width:].astype(jnp.bfloat16)
        query_pre, query_gain_term = norm_backward(
            present_inputs["query_heads"],
            present_inputs["inv_query"],
            gathered[9].astype(jnp.float32),
            unrotate(
                query_grad.reshape(count_rows, QUERY_HEADS, HEAD_SIZE), cosine_table, sine_table
            ),
        )
        key_pre, key_gain_term = norm_backward(
            present_inputs["key_heads"],
            present_inputs["inv_key"],
            gathered[10].astype(jnp.float32),
            unrotate(key_gradient_rows, cosine_table, sine_table),
        )
        query_grad_low = query_pre.reshape(count_rows, QUERY_HEADS * HEAD_SIZE).astype(jnp.bfloat16)
        key_grad_low = key_pre.reshape(count_rows, key_value_width).astype(jnp.bfloat16)
        normed_low = present_inputs["normed_low"]
        grad_query = jnp.einsum(
            "td,tq->dq", normed_low, query_grad_low, preferred_element_type=jnp.float32
        )
        grad_key = jnp.einsum(
            "td,tq->dq", normed_low, key_grad_low, preferred_element_type=jnp.float32
        )
        grad_value = jnp.einsum(
            "td,tq->dq", normed_low, value_grad_low, preferred_element_type=jnp.float32
        )
        normed_grad = jnp.einsum(
            "tq,dq->td", query_grad_low, gathered[0], preferred_element_type=jnp.float32
        )
        normed_grad = normed_grad + jnp.einsum(
            "tq,dq->td", key_grad_low, gathered[1], preferred_element_type=jnp.float32
        )
        normed_grad = normed_grad + jnp.einsum(
            "tq,dq->td", value_grad_low, gathered[2], preferred_element_type=jnp.float32
        )
        in_norm_grad, attn_gain_term = norm_backward(
            stream_in, present_inputs["inv_attn"], gathered[7].astype(jnp.float32), normed_grad
        )
        grad_stream = middle_grad + in_norm_grad
        layer_grads[layer_index] = (
            lax.psum_scatter(grad_query, ("ctx", "fsdp"), scatter_dimension=0, tiled=True),
            lax.psum_scatter(grad_key, ("ctx", "fsdp"), scatter_dimension=0, tiled=True),
            lax.psum_scatter(grad_value, ("ctx", "fsdp"), scatter_dimension=0, tiled=True),
            lax.psum_scatter(grad_out, ("ctx", "fsdp"), scatter_dimension=0, tiled=True),
            lax.psum_scatter(grad_gate, ("ctx", "fsdp"), scatter_dimension=0, tiled=True),
            lax.psum_scatter(grad_up, ("ctx", "fsdp"), scatter_dimension=0, tiled=True),
            lax.psum_scatter(grad_down, ("ctx", "fsdp"), scatter_dimension=0, tiled=True),
            lax.psum_scatter(attn_gain_term, ("ctx", "fsdp"), scatter_dimension=0, tiled=True),
            lax.psum_scatter(mlp_gain_term, ("ctx", "fsdp"), scatter_dimension=0, tiled=True),
            lax.psum_scatter(query_gain_term, ("ctx", "fsdp"), scatter_dimension=0, tiled=True),
            lax.psum_scatter(key_gain_term, ("ctx", "fsdp"), scatter_dimension=0, tiled=True),
        )
    stacked = tuple(
        (jnp.stack([layer_sums[member] for layer_sums in layer_grads]) for member in range(11))
    )
    return (output_low, grad_stream) + stacked


def fast_device(
    tokens,
    cotangent,
    lengths,
    stretch_ids,
    w_query,
    key_projection_weight,
    value_projection_weight,
    w_out,
    w_gate,
    w_up,
    w_down,
    g_attn,
    g_mlp,
    g_query,
    g_key,
):
    results = forward(
        (key_projection_weight, value_projection_weight, w_query, w_out, w_gate, w_up, w_down),
        (g_attn, g_mlp, g_query, g_key),
        tokens,
        stretch_ids,
        lengths,
        1,
    )
    gathered, saved, turned, gains, output_low, tables = (
        results[:4], results[4:11], results[11:15], results[15:18], results[18], results[19:]
    )
    acts = [
        member.reshape(DECODER_LAYERS, 4, 2, 2, 2, -1, 32, tokens.shape[0]) for member in turned
    ]
    *weight_sums, grad_stream, sums, unused = backward(
        acts, saved, gathered, cotangent, gains, tables, 2
    )
    return tuple(finish((output_low, grad_stream, *weight_sums), sums))


def solution(mesh):
    plain = mesh.shape["ctx"] == 2 * KEY_VALUE_HEADS and mesh.shape["fsdp"] == 2
    device = fast_device if plain else general_device
    in_specs = (
        P(("ctx", "fsdp"), None),
        P(("ctx", "fsdp"), None),
        P("fsdp", None),
        P(None, "fsdp", None),
        P(None, "fsdp", None),
        P(None, "fsdp", None),
        P(None, "fsdp", None),
        P(None, "fsdp", None),
        P(None, "fsdp", None),
        P(None, "fsdp", None),
        P(None, "fsdp", None),
        P(None, "fsdp"),
        P(None, "fsdp"),
        P(None, "fsdp"),
        P(None, "fsdp"),
    )
    out_specs = (
        P(("ctx", "fsdp"), None),
        P(("ctx", "fsdp"), None),
        P(None, ("ctx", "fsdp"), None),
        P(None, ("ctx", "fsdp"), None),
        P(None, ("ctx", "fsdp"), None),
        P(None, ("ctx", "fsdp"), None),
        P(None, ("ctx", "fsdp"), None),
        P(None, ("ctx", "fsdp"), None),
        P(None, ("ctx", "fsdp"), None),
        P(None, ("ctx", "fsdp")),
        P(None, ("ctx", "fsdp")),
        P(None, ("ctx", "fsdp")),
        P(None, ("ctx", "fsdp")),
    )
    return jax.shard_map(
        device, mesh=mesh, in_specs=in_specs, out_specs=out_specs, check_vma=False
    )
```

```python
import functools
import math

import jax
import jax.numpy as jnp
from jax import lax
from jax.experimental import pallas as pl
from jax.experimental.pallas import tpu as pltpu
from jax.sharding import PartitionSpec as P

QUERY_HEADS = 16
KEY_VALUE_HEADS = 8
HEAD_SIZE = 128
DECODER_LAYERS = 2
STRETCH = 64


norm_epsilon = 1e-06
rope_base = 1000000.0
masked_logits = -1e30

MESH = pl.DeviceIdType.MESH


TILES = 15
GRADS = 12
ACTS = 7
AHEAD = 2
SLOTS = 8
ACT_SPANS = ((0, 3), (3, 1), (4, 2), (6, 1))


def grad_index(t):
    return jnp.where(t < 3, 0, jnp.where(t < 9, t - 2, jnp.where(t < 11, 7, t - 3)))


def act_index(t):
    return jnp.where(t < 3, t, jnp.where(t < 9, 3, jnp.where(t < 11, t - 5, 6)))


def is_new(t):
    return (t == 0) | ((t >= 3) & (t < 10)) | (t >= 11)


def make_remote(src, dst, s, r, dev):
    return pltpu.make_async_remote_copy(
        src_ref=src, dst_ref=dst, send_sem=s, recv_sem=r, device_id=dev, device_id_type=MESH
    )


class Reducer:
    def __init__(self, acts, grads, results, scratch, layers):
        self.acts, self.grads, self.results, self.layers = acts, grads, results, layers
        self.count = len(layers)
        (self.gheld, self.abuf, self.afwd, self.gtile, self.ysend, self.yrecv, self.own,
         self.zsend, self.zrecv, self.zown,
         self.a_local, self.a_xs, self.a_xr, self.a_cs, self.a_cr,
         self.g_local, self.g_xs, self.g_xr, self.g_cs, self.g_cr, self.g_fs, self.g_fr,
         self.y_s, self.y_r, self.z_s, self.z_r) = scratch
        c = lax.axis_index("ctx")
        x = lax.axis_index("fsdp")
        self.c, self.x = c, x
        self.core = c % 2
        self.y = c // 2 % 2
        self.z = c // 4
        self.sibling = (c + 1 - 2 * self.core, x)
        self.across = (c, 1 - x)
        self.aside = (c + 2 - 4 * self.y, x)

    def along(self, o):
        return ((self.z + o) % 4 * 4 + self.c % 4, self.x)

    def partners(self):
        return (self.sibling, self.across, self.aside) + tuple(self.along(o) for o in (1, 2, 3))

    def act(self, n, k, what):
        first, blocks = ACT_SPANS[k]
        src = self.acts[k].at[self.layers[n]]
        span = pl.ds(first, blocks)
        x, core = self.x, self.core

        def held(place):
            return self.abuf.at[n, :, :, span, :, pl.ds(128 * place, 128)]

        if what == "local":
            return pltpu.make_async_copy(
                src.at[:, :, core, x], held(0), self.a_local.at[n, k]
            )
        if what == "across":
            return make_remote(
                src.at[:, :, core, 1 - x], held(1), self.a_xs.at[n, k, 0], self.a_xr.at[n, k, 0],
                self.across,
            )
        if what == "relay":
            return make_remote(
                src.at[:, :, 1 - core, 1 - x], self.afwd.at[n, :, :, span],
                self.a_xs.at[n, k, 1], self.a_xr.at[n, k, 1], self.across,
            )
        if what == "sibling":
            return make_remote(
                src.at[:, :, 1 - core, x], held(2), self.a_cs.at[n, k, 0], self.a_cr.at[n, k, 0],
                self.sibling,
            )
        return make_remote(
            self.afwd.at[n, :, :, span], held(3), self.a_cs.at[n, k, 1], self.a_cr.at[n, k, 1],
            self.sibling,
        )

    def start_acts(self, n, ks):
        for what in ("across", "relay", "sibling", "local"):
            for k in ks:
                self.act(n, k, what).start()

    def forward_acts(self, n, ks):
        for k in ks:
            self.act(n, k, "relay").wait_recv()
            self.act(n, k, "forward").start()

    def await_acts(self, n, ks):
        for k in ks:
            self.act(n, k, "local").wait()
            for what in ("across", "sibling", "forward"):
                self.act(n, k, what).wait_recv()

    def grad_across(self, i, src=None):
        rows = self.gheld.at[i, pl.ds(0, 128)]
        return make_remote(
            rows if src is None else src, rows, self.g_xs.at[i], self.g_xr.at[i], self.across
        )

    def grad_sibling(self, i, src=None):
        rows = self.gheld.at[i, pl.ds(128, 128)]
        return make_remote(
            rows if src is None else src, rows, self.g_cs.at[i], self.g_cr.at[i], self.sibling
        )

    def grad_forward(self, i):
        return make_remote(
            self.gheld.at[i, pl.ds(0, 128)], self.gheld.at[i, pl.ds(256, 128)],
            self.g_fs.at[i], self.g_fr.at[i], self.sibling,
        )

    def grad_own(self, i, src=None):
        rows = self.gtile.at[i % 2, pl.ds(0, 128)]
        return pltpu.make_async_copy(rows if src is None else src, rows, self.g_local.at[i % 2, 0])

    def grad_load(self, i):
        return pltpu.make_async_copy(
            self.gheld.at[i], self.gtile.at[i % 2, pl.ds(128, 384)], self.g_local.at[i % 2, 1]
        )

    def with_source(self, i, act):
        n = i // GRADS
        g = i % GRADS
        first = 0
        for ref, blocks in self.grads:

            @pl.when((g >= first) & (g < first + blocks))
            def use(ref=ref, first=first):
                act(ref.at[n, :, pl.ds(pl.multiple_of((g - first) * 1024, 1024), 1024)])

            first += blocks

    def start_grad(self, i):
        def go(src):
            self.grad_across(i, src).start()
            self.grad_sibling(i, src).start()

        self.with_source(i, go)

    def y_copy(self, t):
        return make_remote(
            self.ysend.at[t % SLOTS], self.yrecv.at[t], self.y_s.at[t], self.y_r.at[t], self.aside
        )

    def z_copy(self, t, o):
        return make_remote(
            self.zsend.at[t % SLOTS, o - 1], self.zrecv.at[t, 3 - o], self.z_s.at[t, o - 1],
            self.z_r.at[t, 3 - o], self.along(o),
        )

    def begin(self):
        self.start_acts(0, (0,))
        self.start_grad(0)
        self.start_acts(0, (1, 2, 3))

    def begin_more(self):
        for i in range(1, AHEAD):
            self.start_grad(i)

    def store(self, t, total):
        n = t // TILES
        tile = t % TILES
        query, key, value, out, gate, up, down = self.results
        by_rows = ((0, 3, down), (9, 2, out))
        by_columns = ((3, 3, gate), (6, 3, up), (11, 2, query), (13, 1, key), (14, 1, value))
        if self.count == 1:
            layer = self.layers[0]
        else:
            layer = jnp.where(n == 0, self.layers[0], self.layers[1])
        for first, blocks, ref in by_rows:

            @pl.when((tile >= first) & (tile < first + blocks))
            def rows(first=first, ref=ref):
                ref[layer, pl.ds(pl.multiple_of((tile - first) * 32, 32), 32), :] = total

        for first, blocks, ref in by_columns:

            @pl.when((tile >= first) & (tile < first + blocks))
            def columns(first=first, ref=ref):
                ref[layer, :, pl.ds(pl.multiple_of((tile - first) * 1024, 1024), 1024)] = total

    def step(self, s):
        tiles = TILES * self.count
        t = s - 6

        @pl.when((t >= 0) & (t < tiles))
        def finish():
            total = self.zown[t % 4]
            for o in (1, 2, 3):
                self.z_copy(t, o).wait_recv()
            for o in range(3):
                total += self.zrecv[t, o].astype(jnp.float32)
            self.store(t, total)

        u = s - 4

        @pl.when((u >= 0) & (u < tiles))
        def spread():
            self.y_copy(u).wait_recv()

            def part(index):
                rows = pl.ds(pl.multiple_of(index * 32, 32), 32)
                return self.own[u % 4, rows, :] + self.yrecv[u, rows, :].astype(jnp.float32)

            @pl.when(u >= SLOTS)
            def settle():
                for o in (1, 2, 3):
                    self.z_copy(u - SLOTS, o).wait_send()

            for o in (2, 1, 3):
                self.zsend[u % SLOTS, o - 1] = part((self.z + o) % 4).astype(jnp.bfloat16)
                self.z_copy(u, o).start()
            self.zown[u % 4] = part(self.z)

        v = s - 2

        @pl.when((v >= 0) & (v < tiles))
        def compute():
            n = v // TILES
            tile = v % TILES
            gi = n * GRADS + grad_index(tile)
            ai = act_index(tile)
            for layer in range(self.count):

                @pl.when(v == TILES * layer)
                def first_acts(layer=layer):
                    self.await_acts(layer, (0,))

                @pl.when(v == TILES * layer + 3)
                def second_acts(layer=layer):
                    self.await_acts(layer, (1, 2, 3))

            @pl.when(is_new(tile))
            def fresh():
                self.grad_own(gi).wait()
                self.grad_load(gi).wait()

            @pl.when(v >= SLOTS)
            def settle():
                self.y_copy(v - SLOTS).wait_send()

            left = jnp.concatenate(
                [
                    self.abuf[n, :, 1 - self.y, ai].reshape(128, 512),
                    self.abuf[n, :, self.y, ai].reshape(128, 512),
                ],
                axis=0,
            )
            for part in range(4):
                cols = pl.ds(part * 256, 256)
                result = jnp.dot(left, self.gtile[gi % 2, :, cols], preferred_element_type=jnp.float32)
                self.ysend[v % SLOTS, :, cols] = result[:128].astype(jnp.bfloat16)
                self.own[v % 4, :, cols] = result[128:]
            self.y_copy(v).start()

        w = s - 1

        @pl.when((w >= 0) & (w < tiles) & is_new(w % TILES))
        def collect():
            gi = w // TILES * GRADS + grad_index(w % TILES)
            self.with_source(gi, lambda src: self.grad_own(gi, src).start())
            self.grad_sibling(gi).wait_recv()
            self.grad_forward(gi).wait_recv()
            self.grad_load(gi).start()

        @pl.when((s >= 0) & (s < tiles) & is_new(s % TILES))
        def forward():
            i = s // TILES * GRADS + grad_index(s % TILES)
            for layer in range(self.count):

                @pl.when(s == TILES * layer)
                def first_forward(layer=layer):
                    self.forward_acts(layer, (0,))

                @pl.when(s == TILES * layer + 3)
                def second_forward(layer=layer):
                    self.forward_acts(layer, (1, 2, 3))

            self.grad_across(i).wait_recv()
            self.grad_forward(i).start()
            for layer in range(1, self.count):

                @pl.when(i == GRADS * layer - AHEAD)
                def next_acts(layer=layer):
                    self.start_acts(layer, (0,))

                @pl.when(i == GRADS * layer - AHEAD + 1)
                def other_acts(layer=layer):
                    self.start_acts(layer, (1, 2, 3))

            @pl.when(i + AHEAD < GRADS * self.count)
            def more():
                self.start_grad(i + AHEAD)

    def steps(self):
        return TILES * self.count + 6

    def drain(self):
        for n in range(self.count):
            for k in range(4):
                for what in ("across", "relay", "sibling", "forward"):
                    self.act(n, k, what).wait_send()

        def drain_grads(i, carry):
            self.grad_across(i).wait_send()
            self.grad_sibling(i).wait_send()
            self.grad_forward(i).wait_send()
            return carry

        lax.fori_loop(0, GRADS * self.count, drain_grads, 0)

        def drain_tiles(t, carry):
            self.y_copy(t).wait_send()
            for o in (1, 2, 3):
                self.z_copy(t, o).wait_send()
            return carry

        lax.fori_loop(TILES * self.count - SLOTS, TILES * self.count, drain_tiles, 0)


class GainSum:
    def __init__(self, reducer, source, out, scratch):
        self.reducer, self.source, self.out = reducer, source, out
        self.part, self.recv, self.s, self.r = scratch

    def hop(self, i):
        red = self.reducer
        return make_remote(
            self.source if i == 0 else self.part.at[i - 1], self.recv.at[i], self.s.at[i],
            self.r.at[i], (red.across, red.sibling, red.aside)[i],
        )

    def along(self, o):
        return make_remote(
            self.part.at[2], self.recv.at[6 - o], self.s.at[2 + o], self.r.at[6 - o],
            self.reducer.along(o),
        )

    def step(self, s, first):
        @pl.when(s == first)
        def begin():
            self.hop(0).start()

        for i in range(3):

            @pl.when(s == first + 1 + i)
            def stage(i=i):
                self.hop(i).wait_recv()
                self.part[i] = (self.source[...] if i == 0 else self.part[i - 1]) + self.recv[i]
                if i < 2:
                    self.hop(i + 1).start()
                else:
                    for o in (1, 2, 3):
                        self.along(o).start()

        @pl.when(s == first + 5)
        def total():
            for o in (1, 2, 3):
                self.along(o).wait_recv()
            self.out[...] = self.part[2] + self.recv[3] + self.recv[4] + self.recv[5]

    def drain(self):
        for i in range(3):
            self.hop(i).wait_send()
            self.along(i + 1).wait_send()


def reduce_scratch(count):
    dma = pltpu.SemaphoreType.DMA
    low, wide = jnp.bfloat16, jnp.float32
    tiles, grads = TILES * count, GRADS * count
    return [
        pltpu.VMEM((count, 4, 2, ACTS, 32, 512), low),
        pltpu.VMEM((count, 4, 2, ACTS, 32, 128), low),
        pltpu.VMEM((2, 512, 1024), low),
        pltpu.VMEM((SLOTS, 128, 1024), low),
        pltpu.VMEM((tiles, 128, 1024), low),
        pltpu.VMEM((4, 128, 1024), wide),
        pltpu.VMEM((SLOTS, 3, 32, 1024), low),
        pltpu.VMEM((tiles, 3, 32, 1024), low),
        pltpu.VMEM((4, 32, 1024), wide),
        dma((count, 4)), dma((count, 4, 2)), dma((count, 4, 2)), dma((count, 4, 2)),
        dma((count, 4, 2)),
        dma((2, 2)), dma((grads,)), dma((grads,)), dma((grads,)), dma((grads,)), dma((grads,)),
        dma((grads,)),
        dma((tiles,)), dma((tiles,)), dma((tiles, 3)), dma((tiles, 3)),
    ]


def gain_scratch(rows):
    dma = pltpu.SemaphoreType.DMA
    return [
        pltpu.VMEM((3, rows, 128), jnp.float32),
        pltpu.VMEM((6, rows, 128), jnp.float32),
        dma((6,)),
        dma((6,)),
    ]


RESULTS = ((32, 2048), (32, 1024), (32, 1024), (64, 1024), (32, 3072), (32, 3072), (96, 1024))


PEERS = KEY_VALUE_HEADS
SCALE = HEAD_SIZE ** (-0.5)
NT = (((1,), (1,)), ((), ()))


GATHER_PLAN = ((0, 2048), (0, 3072), (0, 0), (1, 0), (2, 0), (2, 3072), (3, 0))
MEMBERS = len(GATHER_PLAN)
ORDER = tuple((n, m) for n in range(2) for m in range(MEMBERS))
ALONE = tuple(i for i, member in enumerate(ORDER) if member[1] == MEMBERS - 1)
LEAD = 4


class Gatherer:
    def __init__(self, sources, outs, sems):
        self.sources, self.outs = sources, outs
        (self.l_s, self.l_r, self.x_s, self.x_r, self.y_s, self.y_r, self.z_s, self.z_r,
         self.yc_s, self.yc_r, self.zc_s, self.zc_r, self.c_s, self.c_r) = sems
        c = lax.axis_index("ctx")
        x = lax.axis_index("fsdp")
        self.x = x
        self.core = c % 2
        y = c // 2 % 2
        near = c // 4 % 2
        self.sibling = (c + 1 - 2 * self.core, x)
        self.across = (c, 1 - x)
        self.aside = (c + 2 - 4 * y, x)
        self.along = (c + 4 - 8 * near, x)
        self.here = near * 2 + y
        self.by_y = near * 2 + 1 - y
        self.by_z = (1 - near) * 2 + y
        self.corner = (1 - near) * 2 + 1 - y

    def rows(self, i, owner_x, start, rows):
        n, m = ORDER[i]
        target, column = GATHER_PLAN[m]
        half, width = self.sources[m].shape[1], self.sources[m].shape[2]
        return self.outs[target].at[
            n, pl.ds(pl.multiple_of(owner_x * half + start, 16), rows), pl.ds(column, width)
        ]

    def window(self, i, owner_x, piece, share=None):
        half = self.sources[ORDER[i][1]].shape[1]
        if i in ALONE:
            return self.rows(i, owner_x, self.core * (half // 2), half // 2)
        rows = half // 8
        start = (piece * 2 + self.core) * rows
        if share is not None:
            rows = rows // 2
            start = start + share * rows
        return self.rows(i, owner_x, start, rows)

    def local(self, i):
        n, m = ORDER[i]
        half = self.sources[m].shape[1]
        return make_remote(
            self.sources[m].at[n], self.rows(i, self.x, 0, half), self.l_s.at[i], self.l_r.at[i],
            self.sibling,
        )

    def x_copy(self, i):
        n, m = ORDER[i]
        half = self.sources[m].shape[1]
        if i in ALONE:
            rows = pl.ds(pl.multiple_of(self.core * (half // 2), 16), half // 2)
        else:
            rows = pl.ds(pl.multiple_of((self.here * 2 + self.core) * (half // 8), 16), half // 8)
        return make_remote(
            self.sources[m].at[n, rows], self.window(i, self.x, self.here), self.x_s.at[i],
            self.x_r.at[i], self.across,
        )

    def y_copy(self, i):
        view = self.window(i, 1 - self.x, self.here)
        return make_remote(view, view, self.y_s.at[i], self.y_r.at[i], self.aside)

    def z_copy(self, i):
        view = self.window(i, 1 - self.x, self.here)
        return make_remote(view, view, self.z_s.at[i], self.z_r.at[i], self.along)

    def y_corner(self, i):
        view = self.window(i, 1 - self.x, self.by_z, 1)
        return make_remote(view, view, self.yc_s.at[i], self.yc_r.at[i], self.aside)

    def z_corner(self, i):
        view = self.window(i, 1 - self.x, self.by_y, 0)
        return make_remote(view, view, self.zc_s.at[i], self.zc_r.at[i], self.along)

    def core_copy(self, i, which):
        piece = (self.here, self.by_y, self.by_z, self.corner)[which]
        view = self.window(i, 1 - self.x, piece)
        return make_remote(
            view, view, self.c_s.at[i, which], self.c_r.at[i, which], self.sibling
        )

    def each(self, i, act, alone=False):
        for place in range(len(ORDER)):
            if place in ALONE and not alone:
                continue

            @pl.when(i == place)
            def member(place=place):
                act(place)

    def send(self, i):
        def go(i):
            self.x_copy(i).start()
            self.local(i).start()

        self.each(i, go, True)

    def step(self, u):
        s = u // 3
        stage = u % 3

        @pl.when(stage == 0)
        def first():
            def spread(i):
                self.x_copy(i).wait_recv()
                self.y_copy(i).start()
                self.z_copy(i).start()
                self.core_copy(i, 0).start()

            self.each(s, spread)
            self.send(s + LEAD)

        @pl.when(stage == 1)
        def second():
            def corners(i):
                self.y_copy(i).wait_recv()
                self.z_corner(i).start()
                self.core_copy(i, 1).start()
                self.z_copy(i).wait_recv()
                self.y_corner(i).start()
                self.core_copy(i, 2).start()

            self.each(s - 1, corners)

        @pl.when(stage == 2)
        def third():
            def last(i):
                self.y_corner(i).wait_recv()
                self.z_corner(i).wait_recv()
                self.core_copy(i, 3).start()

            self.each(s - 2, last)

    def pass_on(self, n, m):
        for i in ALONE:
            if ORDER[i][1] == m:

                @pl.when(n == ORDER[i][0])
                def member(i=i):
                    self.x_copy(i).wait_recv()
                    self.core_copy(i, 0).start()

    def ready(self, n, m):
        for i in range(len(ORDER)):
            if ORDER[i][1] == m:

                @pl.when(n == ORDER[i][0])
                def member(i=i):
                    self.local(i).wait_recv()
                    for which in range(4 if i not in ALONE else 1):
                        self.core_copy(i, which).wait_recv()

    def drain(self):
        for i in range(len(ORDER)):
            self.local(i).wait_send()
            self.x_copy(i).wait_send()
            if i not in ALONE:
                for copy in (self.y_copy, self.z_copy, self.y_corner, self.z_corner):
                    copy(i).wait_send()
            for which in range(4 if i not in ALONE else 1):
                self.core_copy(i, which).wait_send()


def gather_scratch():
    dma = pltpu.SemaphoreType.DMA
    return [dma((len(ORDER),))] * 12 + [dma((len(ORDER), 4))] * 2


def head_columns(first, index):
    return pl.ds(pl.multiple_of(first + index * HEAD_SIZE, HEAD_SIZE), HEAD_SIZE)


def stream_blocks(first, count, slots, start, wait, body):
    def fill(i, carry):
        start(first + i, i)
        return carry

    lax.fori_loop(0, jnp.minimum(slots - 1, count), fill, 0)

    def one(i, carry):
        slot = i % slots

        @pl.when(i + slots - 1 < count)
        def following():
            start(first + i + slots - 1, (i + slots - 1) % slots)

        wait(first + i, slot)
        body(first + i, slot)
        return carry

    lax.fori_loop(0, count, one, 0)


def rms(values, gain):
    r = lax.rsqrt(jnp.mean(values * values, axis=-1, keepdims=True) + norm_epsilon)
    return values * r * gain


BUFFERS = 4
SCHEDULE = (
    (9, 12, 15, 16, 20, 21, 22, 23, 28, 29, 31, 32, 33, 34, 35, 36),
    (37, 37, 38, 38, 42, 43, 44, 45, 46, 46, 46, 47, 48, 49, 49, 50),
)


def forward_kernel(*refs):
    count = DECODER_LAYERS
    sources, refs = refs[:MEMBERS], refs[MEMBERS:]
    (g_attn, g_mlp, g_query, g_key, tokens, stretch_ids, lengths), refs = refs[:7], refs[7:]
    weights, refs = refs[:4], refs[4:]
    into_w, out_w, wide_w, down_w = weights
    (both_out, middle_out, entry_out, pre_out, kept_hbm, kept_out_hbm, kept_log_hbm), refs = (
        refs[:7], refs[7:]
    )
    (hidden_t, mid_t, attn_t, normed_t, attn_gains, mlp_gains, head_gains), refs = (
        refs[:7], refs[7:]
    )
    (output, live, cosine, sine, key_place, query_cap), refs = refs[:6], refs[6:]
    sizes = len(gather_scratch())
    gather = Gatherer(sources, weights, refs[:sizes])
    (wide_mine, wide_other, head_mine, head_other, stream, middle, pre, low, attn_low, hidden_low, both, cols_w, rows_w,
     kept, kept_out, kept_log, send, osend, orecv, vt,
     pack_sem, cols_sem, rows_sem, save_sem,
     q_s, q_r, k_s, k_r, o_s, o_r) = refs[sizes:]
    c = lax.axis_index("ctx")
    x = lax.axis_index("fsdp")
    me = c % PEERS
    z = c // 4

    def peer(r):
        return (c - me + r, x)

    barrier = pltpu.get_barrier_semaphore()

    def greet(o, carry):
        pl.semaphore_signal(barrier, inc=1, device_id=peer((me + o) % PEERS), device_id_type=MESH)
        return carry

    lax.fori_loop(1, PEERS, greet, 0)
    pl.semaphore_signal(barrier, inc=1, device_id=gather.across, device_id_type=MESH)
    pl.semaphore_wait(barrier, PEERS)

    for k, member in enumerate((g_attn, g_mlp)):
        wide_mine[k] = member[...].astype(jnp.float32)
    for k, member in enumerate((g_query, g_key)):
        head_mine[k] = member[...].astype(jnp.float32)
    gain_copies = (
        make_remote(wide_mine, wide_other, pack_sem.at[0], pack_sem.at[1], gather.across),
        make_remote(head_mine, head_other, pack_sem.at[2], pack_sem.at[3], gather.across),
    )
    for copy in gain_copies:
        copy.start()
    for i in range(LEAD):
        gather.send(i)
    stream[...] = tokens[...].astype(jnp.float32)

    slot = c // PEERS
    limit = lengths[0, slot]
    stretches = 2 * PEERS
    lane = lax.broadcasted_iota(jnp.int32, (1, 256), 1) % 128
    row = lax.broadcasted_iota(jnp.int32, (128, 1), 0)

    def spots(r, along):
        first = stretch_ids[slot * PEERS + r, 0, 0] % stretches * STRETCH
        second = stretch_ids[slot * PEERS + r, 0, 1] % stretches * STRETCH
        return jnp.where(along < STRETCH, first, second - STRETCH) + along

    for r in range(PEERS):
        key_place[r * 128 : (r + 1) * 128, :] = spots(r, row)
        query_cap[r] = jnp.minimum(spots(r, lane), limit - 1)
    mine = spots(me, row)
    live[...] = jnp.where(mine < limit, 1.0, 0.0)
    half = HEAD_SIZE // 2
    column = lax.broadcasted_iota(jnp.int32, (1, HEAD_SIZE), 1)
    spread = (column % half).astype(jnp.float32) * (2.0 / HEAD_SIZE)
    angles = mine.astype(jnp.float32) * jnp.exp(spread * -math.log(rope_base))
    cosine[...] = jnp.cos(angles)
    sine[...] = jnp.where(column < half, -jnp.sin(angles), jnp.sin(angles))

    for copy in gain_copies:
        copy.wait_recv()
    low_side = jnp.where(x == 0, 0, 1)

    def pick(first, second, flip):
        return jnp.where(low_side == flip, first, second)

    for k, target in enumerate((attn_gains, mlp_gains)):
        sides = [pick(wide_mine[k], wide_other[k], flip) for flip in range(2)]
        for n in range(count):
            target[n] = jnp.concatenate([side[n : n + 1] for side in sides], axis=1)
    for k in range(2):
        for flip in range(2):
            side = pick(head_mine[k], head_other[k], flip)
            for n in range(count):
                head_gains[n, k : k + 1, flip * half : (flip + 1) * half] = side[n : n + 1]

    cos = cosine[...]
    sin = sine[...]

    def cols_copy(ref, n, column, slot):
        return pltpu.make_async_copy(
            ref.at[n, :, pl.ds(pl.multiple_of(column, 512), 512)], cols_w.at[slot],
            cols_sem.at[slot],
        )

    def rows_copy(ref, n, i, slot):
        rows = pl.ds(pl.multiple_of(i * 512, 512), 512)
        return pltpu.make_async_copy(ref.at[n, rows], rows_w.at[slot], rows_sem.at[slot])

    saves = (
        (stream, entry_out), (pre, pre_out), (middle, middle_out), (kept_out, kept_out_hbm),
        (kept_log, kept_log_hbm), (both, both_out),
    )

    def save(n, k):
        return pltpu.make_async_copy(saves[k][0], saves[k][1].at[n], save_sem.at[k])

    def save_kept(n):
        return pltpu.make_async_copy(kept.at[n], kept_hbm.at[n], save_sem.at[6])

    def turn(source, target, n, blocks):
        def one(j, carry):
            columns = pl.ds(pl.multiple_of(j * 128, 128), 128)
            target[n, columns, :] = source[:, columns].astype(jnp.float32).T.astype(jnp.bfloat16)
            return carry

        lax.fori_loop(0, blocks, one, 0)

    def key_copy(n, r, slot):
        return make_remote(
            send.at[r, pl.ds(2, 2)], kept.at[n, slot, pl.ds(2, 2)], k_s.at[r], k_r.at[slot], peer(r)
        )

    def query_copy(n, r, slot):
        return make_remote(
            send.at[r, pl.ds(0, 2)], kept.at[n, slot, pl.ds(0, 2)], q_s.at[r], q_r.at[slot], peer(r)
        )

    def out_copy(r, slot):
        return make_remote(osend.at[r], orecv.at[slot], o_s.at[r], o_r.at[slot], peer(r))

    def project(n, first, blocks):
        def body(i, slot):
            pre[:, pl.ds(pl.multiple_of(i * 512, 512), 512)] = jnp.dot(
                low[...], cols_w[slot], preferred_element_type=jnp.float32
            )

        stream_blocks(
            first,
            blocks,
            BUFFERS,
            lambda i, slot: cols_copy(into_w, n, i * 512, slot).start(),
            lambda i, slot: cols_copy(into_w, n, i * 512, slot).wait(),
            body,
        )

    def turned(n, first, index, k):
        v = rms(pre[:, head_columns(first, index)], head_gains[n, k : k + 1, :])
        return (v * cos + pltpu.roll(v, HEAD_SIZE // 2, 1) * sin).astype(jnp.bfloat16)

    def keys_part(n):
        save(n, 0).start()
        low[...] = rms(stream[...], attn_gains[n]).astype(jnp.bfloat16)
        turn(low, normed_t, n, 8)
        gather.ready(n, 0)
        project(n, 4, 2)

    def values_part(n):
        gather.ready(n, 1)
        project(n, 6, 2)

        def make_keys(o, carry):
            r = (me + o) % PEERS
            key = turned(n, 2048, r, 1)
            value = pre[:, head_columns(3072, r)].astype(jnp.bfloat16)

            @pl.when(o < PEERS)
            def away():
                send[r, 2] = key
                send[r, 3] = value
                key_copy(n, r, me).start()

            @pl.when(o == PEERS)
            def home():
                kept[n, me, 2] = key
                kept[n, me, 3] = value

            return carry

        lax.fori_loop(1, PEERS + 1, make_keys, 0)

    def queries_part(n):
        gather.ready(n, 2)
        project(n, 0, 4)
        save(n, 1).start()

    def spread_queries(n):
        def make_queries(o, carry):
            r = (me + o) % PEERS
            first = turned(n, 0, 2 * r, 0)
            second = turned(n, 0, 2 * r + 1, 0)

            @pl.when(o < PEERS)
            def away():
                send[r, 0] = first
                send[r, 1] = second
                query_copy(n, r, me).start()

            @pl.when(o == PEERS)
            def home():
                kept[n, me, 0] = first
                kept[n, me, 1] = second

            return carry

        lax.fori_loop(1, PEERS + 1, make_queries, 0)

    def attention(n, part):
        def await_keys(o, carry):
            key_copy(n, me, (me + o) % PEERS).wait_recv()
            return carry

        def turn_values(j, carry):
            vt[j] = kept[n, j, 3].astype(jnp.float32).T.astype(jnp.bfloat16)
            return carry

        @pl.when(part == 0)
        def opening():
            lax.fori_loop(1, PEERS, await_keys, 0)
            lax.fori_loop(0, PEERS, turn_values, 0)

        def block(o, carry):
            j = (me + o) % PEERS

            @pl.when(o > 0)
            def arrived():
                query_copy(n, me, j).wait_recv()

            queries = kept[n, j, 0:2].reshape(2 * 128, HEAD_SIZE)
            keys = kept[n, :, 2].reshape(PEERS * 128, HEAD_SIZE)
            scores = lax.dot_general(keys, queries, NT, preferred_element_type=jnp.float32) * SCALE
            allowed = key_place[...] <= query_cap[j]
            scores = jnp.where(allowed, scores, masked_logits)
            highest = jnp.max(scores, axis=0, keepdims=True)
            expo = jnp.exp(scores - highest)
            total = jnp.sum(expo, axis=0, keepdims=True)
            expo_low = expo.astype(jnp.bfloat16)
            turned_out = jnp.zeros((HEAD_SIZE, 256), jnp.float32)
            for i in range(PEERS):
                turned_out += jnp.dot(
                    vt[i], expo_low[i * 128 : (i + 1) * 128], preferred_element_type=jnp.float32
                )
            turned_out = turned_out / total
            kept_out[j] = turned_out
            kept_log[j] = jnp.broadcast_to(highest + jnp.log(total), (8, 256))
            attended = turned_out.T.astype(jnp.bfloat16).reshape(2, 128, HEAD_SIZE)

            @pl.when(o == 0)
            def home():
                orecv[me] = attended

            @pl.when(o > 0)
            def away():
                osend[j] = attended
                out_copy(j, me).start()

            return carry

        lax.fori_loop(2 * part, 2 * part + 2, block, 0)

        @pl.when(part == 3)
        def closing():
            save(n, 3).start()
            save(n, 4).start()
            save_kept(n).start()

    def close_attention(n):
        def collect(o, carry):
            h = (me + o) % PEERS

            @pl.when(o > 0)
            def arrived():
                out_copy(me, h).wait_recv()

            attn_low[:, head_columns(0, 2 * h)] = orecv[h, 0]
            attn_low[:, head_columns(0, 2 * h + 1)] = orecv[h, 1]
            return carry

        lax.fori_loop(0, PEERS, collect, 0)
        save(n, 0).wait()
        middle[...] = stream[...]
        gather.ready(n, 3)

        def body(i, slot):
            columns = pl.ds(pl.multiple_of(i * 512, 512), 512)
            middle[...] += jnp.dot(
                attn_low[:, columns], rows_w[slot], preferred_element_type=jnp.float32
            )

        stream_blocks(
            0,
            4,
            BUFFERS,
            lambda i, slot: rows_copy(out_w, n, i, slot).start(),
            lambda i, slot: rows_copy(out_w, n, i, slot).wait(),
            body,
        )
        save(n, 2).start()

    def middle_norm(n):
        turn(attn_low, attn_t, n, 16)
        low[...] = rms(middle[...], mlp_gains[n]).astype(jnp.bfloat16)
        turn(low, mid_t, n, 8)

        def settle(o, carry):
            r = (me + o) % PEERS
            key_copy(n, r, me).wait_send()
            query_copy(n, r, me).wait_send()
            out_copy(r, me).wait_send()
            return carry

        lax.fori_loop(1, PEERS, settle, 0)

    def widen(n, base, part):
        def body(i, slot):
            columns = pl.ds(pl.multiple_of(base + i * 512, 512), 512)
            result = jnp.dot(low[...], cols_w[slot], preferred_element_type=jnp.float32)
            both[:, columns] = result
            if base > 0:
                inner = pl.ds(pl.multiple_of(i * 512, 512), 512)
                gate = both[:, inner]
                hidden_low[:, inner] = (gate * jax.nn.sigmoid(gate) * result).astype(jnp.bfloat16)

        stream_blocks(
            3 * part,
            3,
            BUFFERS,
            lambda i, slot: cols_copy(wide_w, n, base + i * 512, slot).start(),
            lambda i, slot: cols_copy(wide_w, n, base + i * 512, slot).wait(),
            body,
        )

    def gate_part(n, part):
        @pl.when(part == 0)
        def opening():
            gather.ready(n, 4)

        widen(n, 0, part)

    def up_part(n, part):
        @pl.when(part == 0)
        def opening():
            gather.ready(n, 5)

        widen(n, 3072, part)

        @pl.when(part == 1)
        def closing():
            save(n, 5).start()

    def turn_hidden(n):
        gather.pass_on(n, 6)
        turn(hidden_low, hidden_t, n, 24)

    def narrow(n):
        gather.ready(n, 6)
        stream[...] = middle[...]

        def body(i, slot):
            columns = pl.ds(pl.multiple_of(i * 512, 512), 512)
            stream[...] += jnp.dot(
                hidden_low[:, columns], rows_w[slot], preferred_element_type=jnp.float32
            )

        stream_blocks(
            0,
            6,
            BUFFERS,
            lambda i, slot: rows_copy(down_w, n, i, slot).start(),
            lambda i, slot: rows_copy(down_w, n, i, slot).wait(),
            body,
        )
        for k in range(1, 6):
            save(n, k).wait()
        save_kept(n).wait()

    def when_at(u, index):
        return (u == SCHEDULE[0][index]) | (u == SCHEDULE[1][index])

    def at_among(u, first, blocks):
        part = jnp.zeros((), jnp.int32)
        for k in range(blocks):
            part = jnp.where(when_at(u, first + k), k, part)
        chosen = functools.reduce(jnp.logical_or, [when_at(u, first + k) for k in range(blocks)])
        return chosen, part

    def step(u, carry):
        gather.step(u)
        n = jnp.where(u >= SCHEDULE[1][0], 1, 0)
        pieces = (
            (1, keys_part), (1, values_part), (1, queries_part), (1, spread_queries),
            (4, attention), (1, close_attention), (1, middle_norm), (2, gate_part),
            (2, up_part), (1, turn_hidden), (1, narrow),
        )
        index = 0
        for blocks, work in pieces:
            chosen, part = at_among(u, index, blocks)

            @pl.when(chosen)
            def piece(blocks=blocks, work=work, part=part):
                if blocks == 1:
                    work(n)
                else:
                    work(n, part)

            index += blocks
        return carry

    lax.fori_loop(0, SCHEDULE[1][-1] + 1, step, 0)
    output[...] = (stream[...] * live[...]).astype(jnp.bfloat16)
    gather.drain()
    for copy in gain_copies:
        copy.wait_send()


def forward(weights, gains, tokens, stretch_ids, lengths, number):
    count = DECODER_LAYERS
    dma = pltpu.SemaphoreType.DMA
    low, wide = jnp.bfloat16, jnp.float32
    pair = pltpu.VMEM((PEERS, 2, 128, HEAD_SIZE), low)
    anywhere = pl.BlockSpec(memory_space=pl.ANY)
    near = pl.BlockSpec(memory_space=pltpu.VMEM)
    gathered = [(1024, 4096), (2048, 1024), (1024, 6144), (3072, 1024)]
    saved = [
        ((128, 6144), wide), ((128, 1024), wide), ((128, 1024), wide), ((128, 4096), wide),
        ((PEERS, 4, 128, HEAD_SIZE), low), ((PEERS, HEAD_SIZE, 256), wide), ((PEERS, 8, 256), wide),
    ]
    turned = [(3072, 128), (1024, 128), (2048, 128), (1024, 128)]
    results = (
        [((count,) + s, low) for s in gathered]
        + [((count,) + s, d) for s, d in saved]
        + [((count,) + s, low) for s in turned]
        + [((count, 1, 1024), wide)] * 2
        + [((count, 2, HEAD_SIZE), wide), ((128, 1024), low), ((128, 1), wide)]
        + [((128, HEAD_SIZE), wide)] * 2
        + [((PEERS * 128, 1), jnp.int32), ((PEERS, 1, 256), jnp.int32)]
    )
    return pl.pallas_call(
        forward_kernel,
        out_shape=[jax.ShapeDtypeStruct(s, d) for s, d in results],
        in_specs=[anywhere] * MEMBERS + [near] * 5 + [pl.BlockSpec(memory_space=pltpu.SMEM)] * 2,
        out_specs=[anywhere] * 11 + [near] * 13,
        scratch_shapes=gather_scratch()
        + [
            pltpu.VMEM((2, count, 512), wide),
            pltpu.VMEM((2, count, 512), wide),
            pltpu.VMEM((2, count, 64), wide),
            pltpu.VMEM((2, count, 64), wide),
            pltpu.VMEM((128, 1024), wide),
            pltpu.VMEM((128, 1024), wide),
            pltpu.VMEM((128, 4096), wide),
            pltpu.VMEM((128, 1024), low),
            pltpu.VMEM((128, 2048), low),
            pltpu.VMEM((128, 3072), low),
            pltpu.VMEM((128, 6144), wide),
            pltpu.VMEM((BUFFERS, 1024, 512), low),
            pltpu.VMEM((BUFFERS, 512, 1024), low),
            pltpu.VMEM((count, PEERS, 4, 128, HEAD_SIZE), low),
            pltpu.VMEM((PEERS, HEAD_SIZE, 256), wide),
            pltpu.VMEM((PEERS, 8, 256), wide),
            pltpu.VMEM((PEERS, 4, 128, HEAD_SIZE), low),
            pair,
            pair,
            pltpu.VMEM((PEERS, HEAD_SIZE, 128), low),
            dma((4,)), dma((BUFFERS,)), dma((BUFFERS,)), dma((7,)),
        ]
        + [dma((PEERS,))] * 6,
        compiler_params=pltpu.CompilerParams(
            collective_id=number, has_side_effects=True, vmem_limit_bytes=56 * 2**20
        ),
        name="forward",
    )(*weights, *gains, tokens, stretch_ids, lengths)


WORK = 12


def rms_back(values, gain, upstream):
    r = lax.rsqrt(jnp.mean(values * values, axis=-1, keepdims=True) + norm_epsilon)
    weighted = upstream * gain
    mean = jnp.mean(weighted * values, axis=-1, keepdims=True)
    grad = r * weighted - values * (r * r * r) * mean
    return grad, jnp.sum(upstream * values * r, axis=0, keepdims=True)


def backward_kernel(*refs):
    count = DECODER_LAYERS
    acts, stored, refs = refs[:4], refs[4:11], refs[11:]
    (into_w, out_w, wide_w, down_w) = refs[:4]
    (cotangent, attn_gains, mlp_gains, head_gains, live, cosine, sine, key_place, query_cap) = (
        refs[4:13]
    )
    results = refs[13:20]
    grad_stream, gain_out, held = refs[20:23]
    refs = refs[23:]
    sizes = len(reduce_scratch(count))
    reduce_refs, refs = refs[:sizes], refs[sizes:]
    gain_refs, refs = refs[:4], refs[4:]
    (down_low, both_low, out_low, pre_low, terms,
     gate_up, middle, entry, pre, kept, kept_out, kept_log, mid_grad, rows_w, wide_rows,
     dsend, drecv, qsend, qrecv, ksend, krecv, kt, key_sum, value_sum,
     load_sem, rows_sem, wide_sem, gate_sem, d_s, d_r, q_s, q_r, k_s, k_r) = refs
    reducer = Reducer(
        acts, ((down_low, 1), (both_low, 6), (out_low, 1), (pre_low, 4)), results,
        (held,) + tuple(reduce_refs), tuple(reversed(range(count))),
    )
    gain_sum = GainSum(reducer, terms, gain_out, gain_refs)
    c = lax.axis_index("ctx")
    x = lax.axis_index("fsdp")
    me = c % PEERS
    z = c // 4

    def peer(r):
        return (c - me + r, x)

    barrier = pltpu.get_barrier_semaphore()

    def greet(o, carry):
        pl.semaphore_signal(barrier, inc=1, device_id=peer((me + o) % PEERS), device_id_type=MESH)
        return carry

    lax.fori_loop(1, PEERS, greet, 0)
    pl.semaphore_signal(barrier, inc=1, device_id=reducer.across, device_id_type=MESH)
    for o in range(2):
        far = ((z // 2 * 2 + 2) % 4 + o) * 4 + c % 4
        pl.semaphore_signal(barrier, inc=1, device_id=(far, x), device_id_type=MESH)
    pl.semaphore_wait(barrier, PEERS + 2)

    grad_stream[...] = cotangent[...].astype(jnp.float32) * live[...]
    terms[...] = jnp.zeros_like(terms)
    reducer.start_acts(0, (0,))

    cos = cosine[...]
    sin = sine[...]

    def grad_copy(r, slot):
        return make_remote(dsend.at[r], drecv.at[slot], d_s.at[r], d_r.at[slot], peer(r))

    def query_copy(r, slot):
        return make_remote(qsend.at[r], qrecv.at[slot], q_s.at[r], q_r.at[slot], peer(r))

    def key_copy(r, slot):
        return make_remote(ksend.at[r], krecv.at[slot], k_s.at[r], k_r.at[slot], peer(r))

    saved = (middle, entry, pre, kept, kept_out, kept_log)

    def load(layer, k):
        return pltpu.make_async_copy(stored[1 + k].at[layer], saved[k], load_sem.at[k])

    def await_load(k):
        load(0, k).wait()

    def add_term(layer, first, term):
        for i in range(8):
            terms[pl.ds(layer * 24 + first + i, 1), :] = term[:, i * 128 : (i + 1) * 128]

    def rows_copy(ref, layer, i, slot):
        rows = pl.ds(pl.multiple_of(i * 512, 512), 512)
        return pltpu.make_async_copy(ref.at[layer, rows], rows_w.at[slot], rows_sem.at[slot])

    def wide_copy(ref, layer, i, slot):
        rows = pl.ds(pl.multiple_of(i * 128, 128), 128)
        columns = ref.shape[2]
        return pltpu.make_async_copy(
            ref.at[layer, rows], wide_rows.at[slot, :, pl.ds(0, columns)], wide_sem.at[slot]
        )

    def hidden_part(n, layer, part):
        @pl.when(part == 0)
        def opening():
            for k in range(len(saved)):
                load(layer, k).start()
            down_low[n] = grad_stream[...].astype(jnp.bfloat16)

        @pl.when((n == 0) & (part == 0))
        def first():
            reducer.start_grad(0)
            reducer.start_acts(0, (1, 2, 3))

        def gate_copy(i, slot, k):
            columns = pl.ds(pl.multiple_of(k * 3072 + i * 512, 512), 512)
            return pltpu.make_async_copy(
                stored[0].at[layer, :, columns], gate_up.at[slot, k], gate_sem.at[slot, k]
            )

        def start(i, slot):
            rows_copy(down_w, layer, i, slot).start()
            for k in range(2):
                gate_copy(i, slot, k).start()

        def wait(i, slot):
            rows_copy(down_w, layer, i, slot).wait()
            for k in range(2):
                gate_copy(i, slot, k).wait()

        def body(i, slot):
            hidden = lax.dot_general(
                down_low[n], rows_w[slot], NT, preferred_element_type=jnp.float32
            )
            gate = gate_up[slot, 0]
            up = gate_up[slot, 1]
            sigmoid = jax.nn.sigmoid(gate)
            columns = pl.multiple_of(i * 512, 512)
            both_low[n, :, pl.ds(columns, 512)] = (
                hidden * up * sigmoid * (1.0 + gate * (1.0 - sigmoid))
            ).astype(jnp.bfloat16)
            both_low[n, :, pl.ds(3072 + columns, 512)] = (hidden * gate * sigmoid).astype(
                jnp.bfloat16
            )

        stream_blocks(part * 3, 3, 2, start, wait, body)

        @pl.when((n == 0) & (part == 1))
        def rest():
            reducer.begin_more()

    def middle_part(n, layer, part):
        def body(i, slot):
            mid_grad[:, pl.ds(pl.multiple_of(i * 128, 128), 128)] = lax.dot_general(
                both_low[n], wide_rows[slot], NT, preferred_element_type=jnp.float32
            )

        stream_blocks(
            part * 3,
            jnp.where(part == 2, 2, 3),
            2,
            lambda i, slot: wide_copy(wide_w, layer, i, slot).start(),
            lambda i, slot: wide_copy(wide_w, layer, i, slot).wait(),
            body,
        )

        @pl.when(part == 2)
        def closing():
            await_load(0)
            grad, term = rms_back(middle[...], mlp_gains[layer], mid_grad[...])
            add_term(layer, 8, term)
            total = grad_stream[...] + grad
            grad_stream[...] = total
            out_low[n] = total.astype(jnp.bfloat16)

    def out_part(n, layer):
        def place(i):
            return (i + me // 2) % 4

        def body(i, slot):
            low = lax.dot_general(
                out_low[n], rows_w[slot], NT, preferred_element_type=jnp.float32
            ).astype(jnp.bfloat16)
            for k in range(2):
                r = 2 * place(i) + k

                @pl.when(r == me)
                def home(k=k):
                    for j in range(2):
                        at = (2 * k + j) * HEAD_SIZE
                        drecv[me, j] = low[:, at : at + HEAD_SIZE]

                @pl.when(r != me)
                def away(k=k, r=r):
                    for j in range(2):
                        at = (2 * k + j) * HEAD_SIZE
                        dsend[r, j] = low[:, at : at + HEAD_SIZE]
                    grad_copy(r, me).start()

        stream_blocks(
            0,
            4,
            2,
            lambda i, slot: rows_copy(out_w, layer, place(i), slot).start(),
            lambda i, slot: rows_copy(out_w, layer, place(i), slot).wait(),
            body,
        )
        for k in range(2, len(saved)):
            await_load(k)

        def turn_keys(j, carry):
            kt[j] = kept[j, 2].astype(jnp.float32).T.astype(jnp.bfloat16)
            return carry

        lax.fori_loop(0, PEERS, turn_keys, 0)
        key_sum[...] = jnp.zeros_like(key_sum)
        value_sum[...] = jnp.zeros_like(value_sum)

    def attention_block(o):
        j = (me + o) % PEERS

        @pl.when(o > 0)
        def arrived():
            grad_copy(me, j).wait_recv()

        grads = drecv[j].reshape(2 * 128, HEAD_SIZE)
        delta = jnp.sum(grads.astype(jnp.float32).T * kept_out[j], axis=0, keepdims=True)
        queries = kept[j, 0:2].reshape(2 * 128, HEAD_SIZE)
        keys = kept[:, 2].reshape(PEERS * 128, HEAD_SIZE)
        values = kept[:, 3].reshape(PEERS * 128, HEAD_SIZE)
        scores = lax.dot_general(keys, queries, NT, preferred_element_type=jnp.float32) * SCALE
        allowed = key_place[...] <= query_cap[j]
        scores = jnp.where(allowed, scores, masked_logits)
        prob = jnp.exp(scores - kept_log[j, 0:1, :])
        dprob = lax.dot_general(values, grads, NT, preferred_element_type=jnp.float32)
        dscore = (prob * (dprob - delta)).astype(jnp.bfloat16)
        value_sum[...] += jnp.dot(
            prob.astype(jnp.bfloat16), grads, preferred_element_type=jnp.float32
        )
        key_sum[...] += jnp.dot(dscore, queries, preferred_element_type=jnp.float32)
        turned = jnp.zeros((HEAD_SIZE, 256), jnp.float32)
        for i in range(PEERS):
            turned += jnp.dot(
                kt[i], dscore[i * 128 : (i + 1) * 128], preferred_element_type=jnp.float32
            )
        query_grad = (turned * SCALE).T.astype(jnp.bfloat16).reshape(2, 128, HEAD_SIZE)

        @pl.when(o == 0)
        def home():
            qrecv[me] = query_grad

        @pl.when(o > 0)
        def away():
            qsend[j] = query_grad
            query_copy(j, me).start()

        @pl.when(o == PEERS - 1)
        def keys_done():
            lax.fori_loop(1, PEERS + 1, push_keys, 0)

    def push_keys(o, carry):
        j = (me + o) % PEERS
        rows = pl.ds(pl.multiple_of(j * 128, 128), 128)
        key = (key_sum[rows, :] * SCALE).astype(jnp.bfloat16)
        value = value_sum[rows, :].astype(jnp.bfloat16)

        @pl.when(o < PEERS)
        def away():
            ksend[j, 0] = key
            ksend[j, 1] = value
            key_copy(j, me).start()

        @pl.when(o == PEERS)
        def home():
            krecv[me, 0] = key
            krecv[me, 1] = value

        return carry

    def head_part(n, layer):
        def back(grad, first, index, gain):
            g = grad.astype(jnp.float32)
            dy = g * cos - pltpu.roll(g, HEAD_SIZE // 2, 1) * sin
            low, term = rms_back(pre[:, head_columns(first, index)], gain, dy)
            return low.astype(jnp.bfloat16), term

        def finish_queries(o, total):
            h = (me + o) % PEERS

            @pl.when(o > 0)
            def arrived():
                query_copy(me, h).wait_recv()

            for i in range(2):
                low, term = back(qrecv[h, i], 0, 2 * h + i, head_gains[layer, 0:1, :])
                pre_low[n, :, head_columns(0, 2 * h + i)] = low
                total += term
            return total

        zero = jnp.zeros((1, HEAD_SIZE), jnp.float32)
        terms[pl.ds(layer * 24 + 16, 1), :] = lax.fori_loop(0, PEERS, finish_queries, zero)

        def finish_keys(o, total):
            h = (me + o) % PEERS

            @pl.when(o > 0)
            def arrived():
                key_copy(me, h).wait_recv()

            low, term = back(krecv[h, 0], 2048, h, head_gains[layer, 1:2, :])
            pre_low[n, :, head_columns(2048, h)] = low
            pre_low[n, :, head_columns(3072, h)] = krecv[h, 1]
            return total + term

        terms[pl.ds(layer * 24 + 17, 1), :] = lax.fori_loop(0, PEERS, finish_keys, zero)

        def settle(o, carry):
            r = (me + o) % PEERS
            grad_copy(r, me).wait_send()
            query_copy(r, me).wait_send()
            key_copy(r, me).wait_send()
            return carry

        lax.fori_loop(1, PEERS, settle, 0)

    def entry_part(n, layer, part):
        def body(i, slot):
            mid_grad[:, pl.ds(pl.multiple_of(i * 128, 128), 128)] = lax.dot_general(
                pre_low[n], wide_rows[slot, :, 0:4096], NT, preferred_element_type=jnp.float32
            )

        stream_blocks(
            part * 4,
            4,
            2,
            lambda i, slot: wide_copy(into_w, layer, i, slot).start(),
            lambda i, slot: wide_copy(into_w, layer, i, slot).wait(),
            body,
        )

        @pl.when(part == 1)
        def closing():
            await_load(1)
            grad, term = rms_back(entry[...], attn_gains[layer], mid_grad[...])
            add_term(layer, 0, term)
            grad_stream[...] += grad

    def step(w, carry):
        reducer.step(w - 2)
        gain_sum.step(w, WORK * count)
        n = w // WORK
        phase = w % WORK
        layer = count - 1 - n
        busy = w < WORK * count

        @pl.when(busy & (phase < 2))
        def phase_hidden():
            hidden_part(n, layer, phase)

        @pl.when(busy & (phase >= 2) & (phase < 5))
        def phase_middle():
            middle_part(n, layer, phase - 2)

        @pl.when(busy & (phase == 5))
        def phase_out():
            out_part(n, layer)

        @pl.when(busy & (phase >= 6) & (phase < 9))
        def phase_attention():
            first = (phase - 6) * 3

            def block(i, inner):
                attention_block(first + i)
                return inner

            lax.fori_loop(0, jnp.minimum(3, PEERS - first), block, 0)

        @pl.when(busy & (phase == 9))
        def phase_heads():
            head_part(n, layer)

        @pl.when(busy & (phase >= 10))
        def phase_entry():
            entry_part(n, layer, phase - 10)

        return carry

    lax.fori_loop(0, reducer.steps() + 2, step, 0)
    reducer.drain()
    gain_sum.drain()


RESULTS = ((32, 2048), (32, 1024), (32, 1024), (64, 1024), (32, 3072), (32, 3072), (96, 1024))


def backward(acts, saved, weights, cotangent, gains, tables, number):
    count = DECODER_LAYERS
    dma = pltpu.SemaphoreType.DMA
    low, wide = jnp.bfloat16, jnp.float32
    pair = pltpu.VMEM((PEERS, 2, 128, HEAD_SIZE), low)
    anywhere = pl.BlockSpec(memory_space=pl.ANY)
    near = pl.BlockSpec(memory_space=pltpu.VMEM)
    return pl.pallas_call(
        backward_kernel,
        out_shape=[jax.ShapeDtypeStruct((count,) + shape, wide) for shape in RESULTS]
        + [
            jax.ShapeDtypeStruct((128, 1024), wide),
            jax.ShapeDtypeStruct((24 * count, 128), wide),
            jax.ShapeDtypeStruct((GRADS * count, 384, 1024), low),
        ],
        in_specs=[anywhere] * 15 + [near] * 9,
        out_specs=[near] * 9 + [anywhere],
        scratch_shapes=reduce_scratch(count)
        + gain_scratch(24 * count)
        + [
            pltpu.VMEM((count, 128, 1024), low),
            pltpu.VMEM((count, 128, 6144), low),
            pltpu.VMEM((count, 128, 1024), low),
            pltpu.VMEM((count, 128, 4096), low),
            pltpu.VMEM((24 * count, 128), wide),
            pltpu.VMEM((2, 2, 128, 512), wide),
            pltpu.VMEM((128, 1024), wide),
            pltpu.VMEM((128, 1024), wide),
            pltpu.VMEM((128, 4096), wide),
            pltpu.VMEM((PEERS, 4, 128, HEAD_SIZE), low),
            pltpu.VMEM((PEERS, HEAD_SIZE, 256), wide),
            pltpu.VMEM((PEERS, 8, 256), wide),
            pltpu.VMEM((128, 1024), wide),
            pltpu.VMEM((2, 512, 1024), low),
            pltpu.VMEM((2, 128, 6144), low),
        ]
        + [pair] * 6
        + [
            pltpu.VMEM((PEERS, HEAD_SIZE, 128), low),
            pltpu.VMEM((PEERS * 128, HEAD_SIZE), wide),
            pltpu.VMEM((PEERS * 128, HEAD_SIZE), wide),
            dma((6,)), dma((2,)), dma((2,)), dma((2, 2)),
        ]
        + [dma((PEERS,))] * 6,
        compiler_params=pltpu.CompilerParams(
            collective_id=number, has_side_effects=True, vmem_limit_bytes=62 * 2**20
        ),
        name="backward",
    )(*acts, *saved, *weights, cotangent, *gains, *tables)


def finish_kernel(*refs):
    count = DECODER_LAYERS
    moved, sums = refs[:9], refs[9]
    outs, gain_outs = refs[10:19], refs[19:23]
    held, sems = refs[23:32], refs[32]

    def into(k):
        return pltpu.make_async_copy(moved[k], held[k], sems.at[0, k])

    def onward(k):
        return pltpu.make_async_copy(held[k], outs[k], sems.at[1, k])

    for k in range(9):
        into(k).start()
    for k in range(9):
        into(k).wait()
        onward(k).start()
    place = lax.axis_index("ctx") * 2 + lax.axis_index("fsdp")

    def cut(row, offset, span):
        values = sums[pl.ds(row, 1), :]
        return pltpu.roll(values, (128 - offset) % 128, 1)[:, :span]

    for n in range(count):
        first = 24 * n
        for k in range(2):
            gain_outs[k][n : n + 1, :] = cut(first + 8 * k + place // 4, place % 4 * 32, 32)
            gain_outs[2 + k][n : n + 1, :] = cut(first + 16 + k, place * 4, 4)
    for k in range(9):
        onward(k).wait()


def finish(moved, sums):
    count = DECODER_LAYERS
    anywhere = pl.BlockSpec(memory_space=pl.ANY)
    near = pl.BlockSpec(memory_space=pltpu.VMEM)
    return pl.pallas_call(
        finish_kernel,
        out_shape=[jax.ShapeDtypeStruct(member.shape, member.dtype) for member in moved]
        + [jax.ShapeDtypeStruct((count, span), jnp.float32) for span in (32, 32, 4, 4)],
        in_specs=[anywhere] * 9 + [near],
        out_specs=[anywhere] * 9 + [near] * 4,
        scratch_shapes=[pltpu.VMEM(member.shape, member.dtype) for member in moved]
        + [pltpu.SemaphoreType.DMA((2, 9))],
        compiler_params=pltpu.CompilerParams(vmem_limit_bytes=60 * 2**20),
        name="finish",
    )(*moved, sums)


def from_partner(shard, axis, apart):
    return lax.ppermute(shard, axis, [(i, i ^ 1 << apart) for i in range(lax.axis_size(axis))])


def token_places(stretch_table, slot_lengths):
    ctx_count = stretch_table.shape[0]
    stretch_order = stretch_table.reshape(-1)
    within = jnp.arange(STRETCH, dtype=jnp.int32)
    places = (stretch_order % ctx_count * STRETCH)[:, None] + within[None, :]
    slot_ids = jnp.broadcast_to((stretch_order // ctx_count)[:, None], places.shape).reshape(-1)
    places = places.reshape(-1)
    limits = jnp.where(slot_ids == 0, slot_lengths[0], slot_lengths[1])
    return (places, slot_ids, places < limits)


def rotary_tables(places):
    half_dim = HEAD_SIZE // 2
    spread = jnp.arange(half_dim, dtype=jnp.int32).astype(jnp.float32) * (2.0 / HEAD_SIZE)
    inverse = jnp.exp(spread * -math.log(rope_base))
    angles = places.astype(jnp.float32)[:, None] * inverse[None, :]
    return (
        jnp.concatenate([jnp.cos(angles)] * 2, axis=-1),
        jnp.concatenate([jnp.sin(angles)] * 2, axis=-1),
    )


def rotate(values, cosine_table, sine_table):
    half_dim = values.shape[-1] // 2
    turned = jnp.concatenate([-values[..., half_dim:], values[..., :half_dim]], axis=-1)
    return values * cosine_table[:, None, :] + turned * sine_table[:, None, :]


def unrotate(upstream, cosine_table, sine_table):
    half_dim = upstream.shape[-1] // 2
    scaled_sine = upstream * sine_table[:, None, :]
    turned_back = jnp.concatenate(
        [scaled_sine[..., half_dim:], -scaled_sine[..., :half_dim]], axis=-1
    )
    return upstream * cosine_table[:, None, :] + turned_back


def norm_forward(values, gain_vec):
    scale_inv = lax.rsqrt(jnp.mean(values * values, axis=-1, keepdims=True) + norm_epsilon)
    return (values * scale_inv * gain_vec, scale_inv)


def norm_backward(values, scale_inv, gain_vec, upstream):
    weighted = upstream * gain_vec
    grad_input = scale_inv * weighted - values * scale_inv**3 * jnp.mean(
        weighted * values, axis=-1, keepdims=True
    )
    gain_term = jnp.sum((upstream * values * scale_inv).reshape(-1, values.shape[-1]), axis=0)
    return (grad_input, gain_term)


def upper_bit(local_index, bit_number):
    return local_index // 2**bit_number % 2 == 1


def joined_rows(mine, received, upper_side):
    first_rows = jnp.where(upper_side, received, mine)
    second_rows = jnp.where(upper_side, mine, received)
    return jnp.concatenate([first_rows, second_rows], axis=0)


def half_gather(pair, local_index):
    gathered_rows = pair
    for bit_number in range(lax.axis_size("ctx").bit_length() - 2):
        received = from_partner(gathered_rows, "ctx", bit_number)
        gathered_rows = joined_rows(gathered_rows, received, upper_bit(local_index, bit_number))
    return gathered_rows


def half_reduce(term, local_index):
    for bit_number in reversed(range(lax.axis_size("ctx").bit_length() - 2)):
        span = term.shape[0] // 2
        lower_rows = term[:span]
        upper_rows = term[span:]
        upper_side = upper_bit(local_index, bit_number)
        kept_rows = jnp.where(upper_side, upper_rows, lower_rows)
        sent_rows = jnp.where(upper_side, lower_rows, upper_rows)
        term = kept_rows + from_partner(sent_rows, "ctx", bit_number)
    return term


def over_keys(update, carried, count_rows):
    block_length = math.gcd(count_rows, 512)

    def inner_step(current, block_index):
        return (update(current, block_index * block_length, block_length), None)

    carried, unused = lax.scan(
        inner_step, carried, jnp.arange(count_rows // block_length, dtype=jnp.int32)
    )
    return carried


def allowed_mask(key_meta, query_meta, row_start, block_length):
    key_places = lax.dynamic_slice_in_dim(key_meta[0], row_start, block_length)
    key_slots = lax.dynamic_slice_in_dim(key_meta[1], row_start, block_length)
    key_live = lax.dynamic_slice_in_dim(key_meta[2], row_start, block_length)
    allowed = (
        (key_slots[None, :] == query_meta[1][:, None])
        & (key_places[None, :] <= query_meta[0][:, None])
        & key_live[None, :]
    )
    return allowed[None, None]


def forward_update(
    current, query_head_group, key_tile_block, value_tile_block, allowed, score_scale
):
    running_max, running_sum, running_acc = current
    block_length = key_tile_block.shape[0]
    key_head_list = key_tile_block.reshape(block_length, KEY_VALUE_HEADS, HEAD_SIZE)
    value_head_list = value_tile_block.reshape(block_length, KEY_VALUE_HEADS, HEAD_SIZE)
    scores = (
        jnp.einsum(
            "qhgd,khd->hgqk", query_head_group, key_head_list, preferred_element_type=jnp.float32
        )
        * score_scale
    )
    scores = jnp.where(allowed, scores, masked_logits)
    new_max = jnp.maximum(running_max, jnp.max(scores, axis=-1))
    factor = jnp.exp(running_max - new_max)
    prob_block = jnp.where(allowed, jnp.exp(scores - new_max[..., None]), 0.0)
    new_sum = running_sum * factor + jnp.sum(prob_block, axis=-1)
    new_acc = running_acc * factor[..., None] + jnp.einsum(
        "hgqk,khd->hgqd",
        prob_block.astype(jnp.bfloat16),
        value_head_list,
        preferred_element_type=jnp.float32,
    )
    return (new_max, new_sum, new_acc)


def score_parts(
    query_head_group,
    output_grad_group,
    key_tile_block,
    value_tile_block,
    allowed,
    log_total,
    row_delta,
    score_scale,
):
    block_length = key_tile_block.shape[0]
    key_head_list = key_tile_block.reshape(block_length, KEY_VALUE_HEADS, HEAD_SIZE)
    value_head_list = value_tile_block.reshape(block_length, KEY_VALUE_HEADS, HEAD_SIZE)
    scores = (
        jnp.einsum(
            "qhgd,khd->hgqk", query_head_group, key_head_list, preferred_element_type=jnp.float32
        )
        * score_scale
    )
    prob_block = jnp.where(allowed, jnp.exp(scores - log_total[..., None]), 0.0)
    dprob = jnp.einsum(
        "qhgd,khd->hgqk", output_grad_group, value_head_list, preferred_element_type=jnp.float32
    )
    dscore_low = (prob_block * (dprob - row_delta[..., None])).astype(jnp.bfloat16)
    return (prob_block, dscore_low, key_head_list)


def attention_inputs(stream, gathered, cosine_table, sine_table):
    count_rows = stream.shape[0]
    normalized, inv_attn = norm_forward(stream, gathered[7].astype(jnp.float32))
    normed_low = normalized.astype(jnp.bfloat16)
    query_heads = jnp.dot(normed_low, gathered[0], preferred_element_type=jnp.float32).reshape(
        count_rows, QUERY_HEADS, HEAD_SIZE
    )
    key_head_list = jnp.dot(normed_low, gathered[1], preferred_element_type=jnp.float32).reshape(
        count_rows, KEY_VALUE_HEADS, HEAD_SIZE
    )
    value_low = jnp.dot(normed_low, gathered[2], preferred_element_type=jnp.float32).astype(
        jnp.bfloat16
    )
    query_normed, inv_query = norm_forward(query_heads, gathered[9].astype(jnp.float32))
    key_normed, inv_key = norm_forward(key_head_list, gathered[10].astype(jnp.float32))
    query_lowered = rotate(query_normed, cosine_table, sine_table).astype(jnp.bfloat16)
    key_low = (
        rotate(key_normed, cosine_table, sine_table)
        .astype(jnp.bfloat16)
        .reshape(count_rows, KEY_VALUE_HEADS * HEAD_SIZE)
    )
    return {
        "normed_low": normed_low,
        "inv_attn": inv_attn,
        "query_heads": query_heads,
        "inv_query": inv_query,
        "key_heads": key_head_list,
        "inv_key": inv_key,
        "query_low": query_lowered,
        "key_low": key_low,
        "value_low": value_low,
    }


def block_rest(stream, gathered, attn_low):
    middle = stream + jnp.dot(attn_low, gathered[3], preferred_element_type=jnp.float32)
    normed_mid, inv_mid = norm_forward(middle, gathered[8].astype(jnp.float32))
    normed_mid_low = normed_mid.astype(jnp.bfloat16)
    gate_act = jnp.dot(normed_mid_low, gathered[4], preferred_element_type=jnp.float32)
    upward = jnp.dot(normed_mid_low, gathered[5], preferred_element_type=jnp.float32)
    hidden_low = (jax.nn.silu(gate_act) * upward).astype(jnp.bfloat16)
    result = middle + jnp.dot(hidden_low, gathered[6], preferred_element_type=jnp.float32)
    return {
        "middle": middle,
        "inv_mid": inv_mid,
        "normed_mid_low": normed_mid_low,
        "gate_act": gate_act,
        "upward": upward,
        "hidden_low": hidden_low,
        "result": result,
    }


def general_device(
    tokens,
    cotangent,
    lengths,
    stretch_ids,
    w_query,
    key_projection_weight,
    value_projection_weight,
    w_out,
    w_gate,
    w_up,
    w_down,
    g_attn,
    g_mlp,
    g_query,
    g_key,
):
    count_rows = tokens.shape[0]
    ctx_count = lax.axis_size("ctx")
    half_count = ctx_count // 2
    key_value_width = KEY_VALUE_HEADS * HEAD_SIZE
    key_meta = token_places(stretch_ids[:, 0, :], lengths[0])
    ctx_index = lax.axis_index("ctx")
    local_index = ctx_index % half_count
    base_row = ctx_index // half_count * half_count * count_rows
    half_row_set = half_count * count_rows
    offset_mine = ctx_index * count_rows
    query_meta = tuple(
        (lax.dynamic_slice_in_dim(meta_array, offset_mine, count_rows) for meta_array in key_meta)
    )
    live_mine = query_meta[2].astype(jnp.float32)[:, None]
    cosine_table, sine_table = rotary_tables(query_meta[0])
    group_count = QUERY_HEADS // KEY_VALUE_HEADS
    score_scale = HEAD_SIZE ** (-0.5)

    def attend_forward(query_head_group, key_source, value_source, current):

        def update(carried, local_row, block_length):
            key_tile_block = lax.dynamic_slice_in_dim(key_source, local_row, block_length)
            value_tile_block = lax.dynamic_slice_in_dim(value_source, local_row, block_length)
            allowed = allowed_mask(key_meta, query_meta, base_row + local_row, block_length)
            return forward_update(
                carried, query_head_group, key_tile_block, value_tile_block, allowed, score_scale
            )

        return over_keys(update, current, key_source.shape[0])

    saved = []
    stream = tokens.astype(jnp.float32)
    for layer_index in range(DECODER_LAYERS):
        gathered = (
            lax.all_gather(w_query[layer_index], "fsdp", axis=0, tiled=True),
            lax.all_gather(key_projection_weight[layer_index], "fsdp", axis=0, tiled=True),
            lax.all_gather(value_projection_weight[layer_index], "fsdp", axis=0, tiled=True),
            lax.all_gather(w_out[layer_index], "fsdp", axis=0, tiled=True),
            lax.all_gather(w_gate[layer_index], "fsdp", axis=0, tiled=True),
            lax.all_gather(w_up[layer_index], "fsdp", axis=0, tiled=True),
            lax.all_gather(w_down[layer_index], "fsdp", axis=0, tiled=True),
            lax.all_gather(g_attn[layer_index], "fsdp", axis=0, tiled=True),
            lax.all_gather(g_mlp[layer_index], "fsdp", axis=0, tiled=True),
            lax.all_gather(g_query[layer_index], "fsdp", axis=0, tiled=True),
            lax.all_gather(g_key[layer_index], "fsdp", axis=0, tiled=True),
        )
        present_inputs = attention_inputs(stream, gathered, cosine_table, sine_table)
        query_head_group = present_inputs["query_low"].reshape(
            count_rows, KEY_VALUE_HEADS, group_count, HEAD_SIZE
        )
        start_state = (
            jnp.full((KEY_VALUE_HEADS, group_count, count_rows), masked_logits, jnp.float32),
            jnp.zeros((KEY_VALUE_HEADS, group_count, count_rows), jnp.float32),
            jnp.zeros((KEY_VALUE_HEADS, group_count, count_rows, HEAD_SIZE), jnp.float32),
        )
        pair_all = half_gather(
            jnp.concatenate([present_inputs["key_low"], present_inputs["value_low"]], axis=-1),
            local_index,
        )
        key_all = pair_all[:, :key_value_width]
        value_all = pair_all[:, key_value_width:]
        final_state = attend_forward(query_head_group, key_all, value_all, start_state)
        attended = final_state[2] / final_state[1][..., None]
        log_total = final_state[0] + jnp.log(final_state[1])
        attn_low = (
            jnp.transpose(attended, (2, 0, 1, 3))
            .reshape(count_rows, QUERY_HEADS * HEAD_SIZE)
            .astype(jnp.bfloat16)
        )
        rest = block_rest(stream, gathered, attn_low)
        kept = (gathered, key_all, value_all, present_inputs, rest)
        saved.append((stream, attended, log_total, kept))
        stream = rest["result"]
    output_low = (stream * live_mine).astype(jnp.bfloat16)
    grad_stream = cotangent.astype(jnp.float32) * live_mine
    layer_grads = [None] * DECODER_LAYERS
    for layer_index in reversed(range(DECODER_LAYERS)):
        stream_in, attended, log_total, kept = saved[layer_index]
        attn_low = (
            jnp.transpose(attended, (2, 0, 1, 3))
            .reshape(count_rows, QUERY_HEADS * HEAD_SIZE)
            .astype(jnp.bfloat16)
        )
        gathered, key_all, value_all, present_inputs, rest = kept
        ffn_grad_low = grad_stream.astype(jnp.bfloat16)
        grad_down = jnp.einsum(
            "tf,td->fd", rest["hidden_low"], ffn_grad_low, preferred_element_type=jnp.float32
        )
        hidden_grad = jnp.einsum(
            "td,fd->tf", ffn_grad_low, gathered[6], preferred_element_type=jnp.float32
        )
        gate_act = rest["gate_act"]
        sigmoid_gate = jax.nn.sigmoid(gate_act)
        gate_grad_low = (
            hidden_grad * rest["upward"] * sigmoid_gate * (1.0 + gate_act * (1.0 - sigmoid_gate))
        ).astype(jnp.bfloat16)
        up_grad_low = (hidden_grad * gate_act * sigmoid_gate).astype(jnp.bfloat16)
        grad_gate = jnp.einsum(
            "td,tf->df", rest["normed_mid_low"], gate_grad_low, preferred_element_type=jnp.float32
        )
        grad_up = jnp.einsum(
            "td,tf->df", rest["normed_mid_low"], up_grad_low, preferred_element_type=jnp.float32
        )
        normed_mid_grad = jnp.einsum(
            "tf,df->td", gate_grad_low, gathered[4], preferred_element_type=jnp.float32
        ) + jnp.einsum("tf,df->td", up_grad_low, gathered[5], preferred_element_type=jnp.float32)
        mid_norm_grad, mlp_gain_term = norm_backward(
            rest["middle"], rest["inv_mid"], gathered[8].astype(jnp.float32), normed_mid_grad
        )
        middle_grad = grad_stream + mid_norm_grad
        attn_grad_low = middle_grad.astype(jnp.bfloat16)
        grad_out = jnp.einsum(
            "tq,td->qd", attn_low, attn_grad_low, preferred_element_type=jnp.float32
        )
        output_gradient_lowered = jnp.einsum(
            "td,qd->tq", attn_grad_low, gathered[3], preferred_element_type=jnp.float32
        ).astype(jnp.bfloat16)
        output_grad_group = output_gradient_lowered.reshape(
            count_rows, KEY_VALUE_HEADS, group_count, HEAD_SIZE
        )
        row_delta = jnp.sum(
            jnp.transpose(output_grad_group.astype(jnp.float32), (1, 2, 0, 3)) * attended, axis=-1
        )
        query_head_group = present_inputs["query_low"].reshape(
            count_rows, KEY_VALUE_HEADS, group_count, HEAD_SIZE
        )
        key_block_size = math.gcd(half_row_set, 512)

        def backward_step(query_acc, block_index):
            row_start = block_index * key_block_size
            key_tile_block = lax.dynamic_slice_in_dim(key_all, row_start, key_block_size)
            value_tile_block = lax.dynamic_slice_in_dim(value_all, row_start, key_block_size)
            allowed = allowed_mask(key_meta, query_meta, base_row + row_start, key_block_size)
            prob_block, dscore_low, key_head_list = score_parts(
                query_head_group,
                output_grad_group,
                key_tile_block,
                value_tile_block,
                allowed,
                log_total,
                row_delta,
                score_scale,
            )
            query_next = (query_acc, jnp.zeros((key_block_size, 2 * key_value_width), jnp.float32))[
                0
            ] + jnp.einsum(
                "hgqk,khd->qhgd", dscore_low, key_head_list, preferred_element_type=jnp.float32
            ) * score_scale
            value_grad = jnp.einsum(
                "hgqk,qhgd->khd",
                prob_block.astype(jnp.bfloat16),
                output_grad_group,
                preferred_element_type=jnp.float32,
            )
            key_grad = (
                jnp.einsum(
                    "hgqk,qhgd->khd",
                    dscore_low,
                    query_head_group,
                    preferred_element_type=jnp.float32,
                )
                * score_scale
            )
            block_rows = jnp.concatenate(
                [
                    key_grad.reshape(key_block_size, key_value_width),
                    value_grad.reshape(key_block_size, key_value_width),
                ],
                axis=-1,
            )
            return (query_next, block_rows)

        query_grad, key_value_rows = lax.scan(
            backward_step,
            jnp.zeros((count_rows, KEY_VALUE_HEADS, group_count, HEAD_SIZE), jnp.float32),
            jnp.arange(half_row_set // key_block_size, dtype=jnp.int32),
        )
        key_value_term = key_value_rows.reshape(half_row_set, 2 * key_value_width)
        key_value_gradient = half_reduce(key_value_term, local_index)
        key_gradient_rows = key_value_gradient[:, :key_value_width].reshape(
            count_rows, KEY_VALUE_HEADS, HEAD_SIZE
        )
        value_grad_low = key_value_gradient[:, key_value_width:].astype(jnp.bfloat16)
        query_pre, query_gain_term = norm_backward(
            present_inputs["query_heads"],
            present_inputs["inv_query"],
            gathered[9].astype(jnp.float32),
            unrotate(
                query_grad.reshape(count_rows, QUERY_HEADS, HEAD_SIZE), cosine_table, sine_table
            ),
        )
        key_pre, key_gain_term = norm_backward(
            present_inputs["key_heads"],
            present_inputs["inv_key"],
            gathered[10].astype(jnp.float32),
            unrotate(key_gradient_rows, cosine_table, sine_table),
        )
        query_grad_low = query_pre.reshape(count_rows, QUERY_HEADS * HEAD_SIZE).astype(jnp.bfloat16)
        key_grad_low = key_pre.reshape(count_rows, key_value_width).astype(jnp.bfloat16)
        normed_low = present_inputs["normed_low"]
        grad_query = jnp.einsum(
            "td,tq->dq", normed_low, query_grad_low, preferred_element_type=jnp.float32
        )
        grad_key = jnp.einsum(
            "td,tq->dq", normed_low, key_grad_low, preferred_element_type=jnp.float32
        )
        grad_value = jnp.einsum(
            "td,tq->dq", normed_low, value_grad_low, preferred_element_type=jnp.float32
        )
        normed_grad = jnp.einsum(
            "tq,dq->td", query_grad_low, gathered[0], preferred_element_type=jnp.float32
        )
        normed_grad = normed_grad + jnp.einsum(
            "tq,dq->td", key_grad_low, gathered[1], preferred_element_type=jnp.float32
        )
        normed_grad = normed_grad + jnp.einsum(
            "tq,dq->td", value_grad_low, gathered[2], preferred_element_type=jnp.float32
        )
        in_norm_grad, attn_gain_term = norm_backward(
            stream_in, present_inputs["inv_attn"], gathered[7].astype(jnp.float32), normed_grad
        )
        grad_stream = middle_grad + in_norm_grad
        layer_grads[layer_index] = (
            lax.psum_scatter(grad_query, ("ctx", "fsdp"), scatter_dimension=0, tiled=True),
            lax.psum_scatter(grad_key, ("ctx", "fsdp"), scatter_dimension=0, tiled=True),
            lax.psum_scatter(grad_value, ("ctx", "fsdp"), scatter_dimension=0, tiled=True),
            lax.psum_scatter(grad_out, ("ctx", "fsdp"), scatter_dimension=0, tiled=True),
            lax.psum_scatter(grad_gate, ("ctx", "fsdp"), scatter_dimension=0, tiled=True),
            lax.psum_scatter(grad_up, ("ctx", "fsdp"), scatter_dimension=0, tiled=True),
            lax.psum_scatter(grad_down, ("ctx", "fsdp"), scatter_dimension=0, tiled=True),
            lax.psum_scatter(attn_gain_term, ("ctx", "fsdp"), scatter_dimension=0, tiled=True),
            lax.psum_scatter(mlp_gain_term, ("ctx", "fsdp"), scatter_dimension=0, tiled=True),
            lax.psum_scatter(query_gain_term, ("ctx", "fsdp"), scatter_dimension=0, tiled=True),
            lax.psum_scatter(key_gain_term, ("ctx", "fsdp"), scatter_dimension=0, tiled=True),
        )
    stacked = tuple(
        (jnp.stack([layer_sums[member] for layer_sums in layer_grads]) for member in range(11))
    )
    return (output_low, grad_stream) + stacked


def fast_device(
    tokens,
    cotangent,
    lengths,
    stretch_ids,
    w_query,
    key_projection_weight,
    value_projection_weight,
    w_out,
    w_gate,
    w_up,
    w_down,
    g_attn,
    g_mlp,
    g_query,
    g_key,
):
    results = forward(
        (key_projection_weight, value_projection_weight, w_query, w_out, w_gate, w_up, w_down),
        (g_attn, g_mlp, g_query, g_key),
        tokens,
        stretch_ids,
        lengths,
        1,
    )
    gathered, saved, turned, gains, output_low, tables = (
        results[:4], results[4:11], results[11:15], results[15:18], results[18], results[19:]
    )
    acts = [
        member.reshape(DECODER_LAYERS, 4, 2, 2, 2, -1, 32, tokens.shape[0]) for member in turned
    ]
    *weight_sums, grad_stream, sums, unused = backward(
        acts, saved, gathered, cotangent, gains, tables, 2
    )
    return tuple(finish((output_low, grad_stream, *weight_sums), sums))


def solution(mesh):
    plain = mesh.shape["ctx"] == 2 * KEY_VALUE_HEADS and mesh.shape["fsdp"] == 2
    device = fast_device if plain else general_device
    in_specs = (
        P(("ctx", "fsdp"), None),
        P(("ctx", "fsdp"), None),
        P("fsdp", None),
        P(None, "fsdp", None),
        P(None, "fsdp", None),
        P(None, "fsdp", None),
        P(None, "fsdp", None),
        P(None, "fsdp", None),
        P(None, "fsdp", None),
        P(None, "fsdp", None),
        P(None, "fsdp", None),
        P(None, "fsdp"),
        P(None, "fsdp"),
        P(None, "fsdp"),
        P(None, "fsdp"),
    )
    out_specs = (
        P(("ctx", "fsdp"), None),
        P(("ctx", "fsdp"), None),
        P(None, ("ctx", "fsdp"), None),
        P(None, ("ctx", "fsdp"), None),
        P(None, ("ctx", "fsdp"), None),
        P(None, ("ctx", "fsdp"), None),
        P(None, ("ctx", "fsdp"), None),
        P(None, ("ctx", "fsdp"), None),
        P(None, ("ctx", "fsdp"), None),
        P(None, ("ctx", "fsdp")),
        P(None, ("ctx", "fsdp")),
        P(None, ("ctx", "fsdp")),
        P(None, ("ctx", "fsdp")),
    )
    return jax.shard_map(
        device, mesh=mesh, in_specs=in_specs, out_specs=out_specs, check_vma=False
    )
```

```python
import functools
import math

import jax
import jax.numpy as jnp
from jax import lax
from jax.experimental import pallas as pl
from jax.experimental.pallas import tpu as pltpu
from jax.sharding import PartitionSpec as P

QUERY_HEADS = 16
KEY_VALUE_HEADS = 8
HEAD_SIZE = 128
DECODER_LAYERS = 2
STRETCH = 64


norm_epsilon = 1e-06
rope_base = 1000000.0
masked_logits = -1e30

MESH = pl.DeviceIdType.MESH


TILES = 15
GRADS = 12
ACTS = 7
AHEAD = 2
SLOTS = 8
ACT_SPANS = ((0, 3), (3, 1), (4, 2), (6, 1))


def grad_index(t):
    return jnp.where(t < 3, 0, jnp.where(t < 9, t - 2, jnp.where(t < 11, 7, t - 3)))


def act_index(t):
    return jnp.where(t < 3, t, jnp.where(t < 9, 3, jnp.where(t < 11, t - 5, 6)))


def is_new(t):
    return (t == 0) | ((t >= 3) & (t < 10)) | (t >= 11)


def make_remote(src, dst, s, r, dev):
    return pltpu.make_async_remote_copy(
        src_ref=src, dst_ref=dst, send_sem=s, recv_sem=r, device_id=dev, device_id_type=MESH
    )


class Reducer:
    def __init__(self, acts, grads, results, scratch, layers):
        self.acts, self.grads, self.results, self.layers = acts, grads, results, layers
        self.count = len(layers)
        (self.gheld, self.abuf, self.afwd, self.gtile, self.ysend, self.yrecv, self.own,
         self.zsend, self.zrecv, self.zown,
         self.a_local, self.a_xs, self.a_xr, self.a_cs, self.a_cr,
         self.g_local, self.g_xs, self.g_xr, self.g_cs, self.g_cr, self.g_fs, self.g_fr,
         self.y_s, self.y_r, self.z_s, self.z_r) = scratch
        c = lax.axis_index("ctx")
        x = lax.axis_index("fsdp")
        self.c, self.x = c, x
        self.core = c % 2
        self.y = c // 2 % 2
        self.z = c // 4
        self.sibling = (c + 1 - 2 * self.core, x)
        self.across = (c, 1 - x)
        self.aside = (c + 2 - 4 * self.y, x)

    def along(self, o):
        return ((self.z + o) % 4 * 4 + self.c % 4, self.x)

    def partners(self):
        return (self.sibling, self.across, self.aside) + tuple(self.along(o) for o in (1, 2, 3))

    def act(self, n, k, what):
        first, blocks = ACT_SPANS[k]
        src = self.acts[k].at[self.layers[n]]
        span = pl.ds(first, blocks)
        x, core = self.x, self.core

        def held(place):
            return self.abuf.at[n, :, :, span, :, pl.ds(128 * place, 128)]

        if what == "local":
            return pltpu.make_async_copy(
                src.at[:, :, core, x], held(0), self.a_local.at[n, k]
            )
        if what == "across":
            return make_remote(
                src.at[:, :, core, 1 - x], held(1), self.a_xs.at[n, k, 0], self.a_xr.at[n, k, 0],
                self.across,
            )
        if what == "relay":
            return make_remote(
                src.at[:, :, 1 - core, 1 - x], self.afwd.at[n, :, :, span],
                self.a_xs.at[n, k, 1], self.a_xr.at[n, k, 1], self.across,
            )
        if what == "sibling":
            return make_remote(
                src.at[:, :, 1 - core, x], held(2), self.a_cs.at[n, k, 0], self.a_cr.at[n, k, 0],
                self.sibling,
            )
        return make_remote(
            self.afwd.at[n, :, :, span], held(3), self.a_cs.at[n, k, 1], self.a_cr.at[n, k, 1],
            self.sibling,
        )

    def start_acts(self, n, ks):
        for what in ("across", "relay", "sibling", "local"):
            for k in ks:
                self.act(n, k, what).start()

    def forward_acts(self, n, ks):
        for k in ks:
            self.act(n, k, "relay").wait_recv()
            self.act(n, k, "forward").start()

    def await_acts(self, n, ks):
        for k in ks:
            self.act(n, k, "local").wait()
            for what in ("across", "sibling", "forward"):
                self.act(n, k, what).wait_recv()

    def grad_across(self, i, src=None):
        rows = self.gheld.at[i, pl.ds(0, 128)]
        return make_remote(
            rows if src is None else src, rows, self.g_xs.at[i], self.g_xr.at[i], self.across
        )

    def grad_sibling(self, i, src=None):
        rows = self.gheld.at[i, pl.ds(128, 128)]
        return make_remote(
            rows if src is None else src, rows, self.g_cs.at[i], self.g_cr.at[i], self.sibling
        )

    def grad_forward(self, i):
        return make_remote(
            self.gheld.at[i, pl.ds(0, 128)], self.gheld.at[i, pl.ds(256, 128)],
            self.g_fs.at[i], self.g_fr.at[i], self.sibling,
        )

    def grad_own(self, i, src=None):
        rows = self.gtile.at[i % 2, pl.ds(0, 128)]
        return pltpu.make_async_copy(rows if src is None else src, rows, self.g_local.at[i % 2, 0])

    def grad_load(self, i):
        return pltpu.make_async_copy(
            self.gheld.at[i], self.gtile.at[i % 2, pl.ds(128, 384)], self.g_local.at[i % 2, 1]
        )

    def with_source(self, i, act):
        n = i // GRADS
        g = i % GRADS
        first = 0
        for ref, blocks in self.grads:

            @pl.when((g >= first) & (g < first + blocks))
            def use(ref=ref, first=first):
                act(ref.at[n, :, pl.ds(pl.multiple_of((g - first) * 1024, 1024), 1024)])

            first += blocks

    def start_grad(self, i):
        def go(src):
            self.grad_across(i, src).start()
            self.grad_sibling(i, src).start()

        self.with_source(i, go)

    def y_copy(self, t):
        return make_remote(
            self.ysend.at[t % SLOTS], self.yrecv.at[t], self.y_s.at[t], self.y_r.at[t], self.aside
        )

    def z_copy(self, t, o):
        return make_remote(
            self.zsend.at[t % SLOTS, o - 1], self.zrecv.at[t, 3 - o], self.z_s.at[t, o - 1],
            self.z_r.at[t, 3 - o], self.along(o),
        )

    def begin(self):
        self.start_acts(0, (0,))
        self.start_grad(0)
        self.start_acts(0, (1, 2, 3))

    def begin_more(self):
        for i in range(1, AHEAD):
            self.start_grad(i)

    def store(self, t, total):
        n = t // TILES
        tile = t % TILES
        query, key, value, out, gate, up, down = self.results
        by_rows = ((0, 3, down), (9, 2, out))
        by_columns = ((3, 3, gate), (6, 3, up), (11, 2, query), (13, 1, key), (14, 1, value))
        if self.count == 1:
            layer = self.layers[0]
        else:
            layer = jnp.where(n == 0, self.layers[0], self.layers[1])
        for first, blocks, ref in by_rows:

            @pl.when((tile >= first) & (tile < first + blocks))
            def rows(first=first, ref=ref):
                ref[layer, pl.ds(pl.multiple_of((tile - first) * 32, 32), 32), :] = total

        for first, blocks, ref in by_columns:

            @pl.when((tile >= first) & (tile < first + blocks))
            def columns(first=first, ref=ref):
                ref[layer, :, pl.ds(pl.multiple_of((tile - first) * 1024, 1024), 1024)] = total

    def step(self, s):
        tiles = TILES * self.count
        t = s - 6

        @pl.when((t >= 0) & (t < tiles))
        def finish():
            total = self.zown[t % 4]
            for o in (1, 2, 3):
                self.z_copy(t, o).wait_recv()
            for o in range(3):
                total += self.zrecv[t, o].astype(jnp.float32)
            self.store(t, total)

        u = s - 4

        @pl.when((u >= 0) & (u < tiles))
        def spread():
            self.y_copy(u).wait_recv()

            def part(index):
                rows = pl.ds(pl.multiple_of(index * 32, 32), 32)
                return self.own[u % 4, rows, :] + self.yrecv[u, rows, :].astype(jnp.float32)

            @pl.when(u >= SLOTS)
            def settle():
                for o in (1, 2, 3):
                    self.z_copy(u - SLOTS, o).wait_send()

            for o in (2, 1, 3):
                self.zsend[u % SLOTS, o - 1] = part((self.z + o) % 4).astype(jnp.bfloat16)
                self.z_copy(u, o).start()
            self.zown[u % 4] = part(self.z)

        v = s - 2

        @pl.when((v >= 0) & (v < tiles))
        def compute():
            n = v // TILES
            tile = v % TILES
            gi = n * GRADS + grad_index(tile)
            ai = act_index(tile)
            for layer in range(self.count):

                @pl.when(v == TILES * layer)
                def first_acts(layer=layer):
                    self.await_acts(layer, (0,))

                @pl.when(v == TILES * layer + 3)
                def second_acts(layer=layer):
                    self.await_acts(layer, (1, 2, 3))

            @pl.when(is_new(tile))
            def fresh():
                self.grad_own(gi).wait()
                self.grad_load(gi).wait()

            @pl.when(v >= SLOTS)
            def settle():
                self.y_copy(v - SLOTS).wait_send()

            left = jnp.concatenate(
                [
                    self.abuf[n, :, 1 - self.y, ai].reshape(128, 512),
                    self.abuf[n, :, self.y, ai].reshape(128, 512),
                ],
                axis=0,
            )
            for part in range(4):
                cols = pl.ds(part * 256, 256)
                result = jnp.dot(left, self.gtile[gi % 2, :, cols], preferred_element_type=jnp.float32)
                self.ysend[v % SLOTS, :, cols] = result[:128].astype(jnp.bfloat16)
                self.own[v % 4, :, cols] = result[128:]
            self.y_copy(v).start()

        w = s - 1

        @pl.when((w >= 0) & (w < tiles) & is_new(w % TILES))
        def collect():
            gi = w // TILES * GRADS + grad_index(w % TILES)
            self.with_source(gi, lambda src: self.grad_own(gi, src).start())
            self.grad_sibling(gi).wait_recv()
            self.grad_forward(gi).wait_recv()
            self.grad_load(gi).start()

        @pl.when((s >= 0) & (s < tiles) & is_new(s % TILES))
        def forward():
            i = s // TILES * GRADS + grad_index(s % TILES)
            for layer in range(self.count):

                @pl.when(s == TILES * layer)
                def first_forward(layer=layer):
                    self.forward_acts(layer, (0,))

                @pl.when(s == TILES * layer + 3)
                def second_forward(layer=layer):
                    self.forward_acts(layer, (1, 2, 3))

            self.grad_across(i).wait_recv()
            self.grad_forward(i).start()
            for layer in range(1, self.count):

                @pl.when(i == GRADS * layer - AHEAD)
                def next_acts(layer=layer):
                    self.start_acts(layer, (0,))

                @pl.when(i == GRADS * layer - AHEAD + 1)
                def other_acts(layer=layer):
                    self.start_acts(layer, (1, 2, 3))

            @pl.when(i + AHEAD < GRADS * self.count)
            def more():
                self.start_grad(i + AHEAD)

    def steps(self):
        return TILES * self.count + 6

    def drain(self):
        for n in range(self.count):
            for k in range(4):
                for what in ("across", "relay", "sibling", "forward"):
                    self.act(n, k, what).wait_send()

        def drain_grads(i, carry):
            self.grad_across(i).wait_send()
            self.grad_sibling(i).wait_send()
            self.grad_forward(i).wait_send()
            return carry

        lax.fori_loop(0, GRADS * self.count, drain_grads, 0)

        def drain_tiles(t, carry):
            self.y_copy(t).wait_send()
            for o in (1, 2, 3):
                self.z_copy(t, o).wait_send()
            return carry

        lax.fori_loop(TILES * self.count - SLOTS, TILES * self.count, drain_tiles, 0)


class GainSum:
    def __init__(self, reducer, source, out, scratch):
        self.reducer, self.source, self.out = reducer, source, out
        self.part, self.recv, self.s, self.r = scratch

    def hop(self, i):
        red = self.reducer
        return make_remote(
            self.source if i == 0 else self.part.at[i - 1], self.recv.at[i], self.s.at[i],
            self.r.at[i], (red.across, red.sibling, red.aside)[i],
        )

    def along(self, o):
        return make_remote(
            self.part.at[2], self.recv.at[6 - o], self.s.at[2 + o], self.r.at[6 - o],
            self.reducer.along(o),
        )

    def step(self, s, first):
        @pl.when(s == first)
        def begin():
            self.hop(0).start()

        for i in range(3):

            @pl.when(s == first + 1 + i)
            def stage(i=i):
                self.hop(i).wait_recv()
                self.part[i] = (self.source[...] if i == 0 else self.part[i - 1]) + self.recv[i]
                if i < 2:
                    self.hop(i + 1).start()
                else:
                    for o in (1, 2, 3):
                        self.along(o).start()

        @pl.when(s == first + 5)
        def total():
            for o in (1, 2, 3):
                self.along(o).wait_recv()
            self.out[...] = self.part[2] + self.recv[3] + self.recv[4] + self.recv[5]

    def drain(self):
        for i in range(3):
            self.hop(i).wait_send()
            self.along(i + 1).wait_send()


def reduce_scratch(count):
    dma = pltpu.SemaphoreType.DMA
    low, wide = jnp.bfloat16, jnp.float32
    tiles, grads = TILES * count, GRADS * count
    return [
        pltpu.VMEM((count, 4, 2, ACTS, 32, 512), low),
        pltpu.VMEM((count, 4, 2, ACTS, 32, 128), low),
        pltpu.VMEM((2, 512, 1024), low),
        pltpu.VMEM((SLOTS, 128, 1024), low),
        pltpu.VMEM((tiles, 128, 1024), low),
        pltpu.VMEM((4, 128, 1024), wide),
        pltpu.VMEM((SLOTS, 3, 32, 1024), low),
        pltpu.VMEM((tiles, 3, 32, 1024), low),
        pltpu.VMEM((4, 32, 1024), wide),
        dma((count, 4)), dma((count, 4, 2)), dma((count, 4, 2)), dma((count, 4, 2)),
        dma((count, 4, 2)),
        dma((2, 2)), dma((grads,)), dma((grads,)), dma((grads,)), dma((grads,)), dma((grads,)),
        dma((grads,)),
        dma((tiles,)), dma((tiles,)), dma((tiles, 3)), dma((tiles, 3)),
    ]


def gain_scratch(rows):
    dma = pltpu.SemaphoreType.DMA
    return [
        pltpu.VMEM((3, rows, 128), jnp.float32),
        pltpu.VMEM((6, rows, 128), jnp.float32),
        dma((6,)),
        dma((6,)),
    ]


RESULTS = ((32, 2048), (32, 1024), (32, 1024), (64, 1024), (32, 3072), (32, 3072), (96, 1024))


PEERS = KEY_VALUE_HEADS
SCALE = HEAD_SIZE ** (-0.5)
NT = (((1,), (1,)), ((), ()))


GATHER_PLAN = ((0, 2048), (0, 3072), (0, 0), (1, 0), (2, 0), (2, 3072), (3, 0))
MEMBERS = len(GATHER_PLAN)
ORDER = tuple((n, m) for n in range(2) for m in range(MEMBERS))
ALONE = tuple(i for i, member in enumerate(ORDER) if member[1] == MEMBERS - 1)
LEAD = 4


class Gatherer:
    def __init__(self, sources, outs, sems):
        self.sources, self.outs = sources, outs
        (self.l_s, self.l_r, self.x_s, self.x_r, self.y_s, self.y_r, self.z_s, self.z_r,
         self.yc_s, self.yc_r, self.zc_s, self.zc_r, self.c_s, self.c_r) = sems
        c = lax.axis_index("ctx")
        x = lax.axis_index("fsdp")
        self.x = x
        self.core = c % 2
        y = c // 2 % 2
        near = c // 4 % 2
        self.sibling = (c + 1 - 2 * self.core, x)
        self.across = (c, 1 - x)
        self.aside = (c + 2 - 4 * y, x)
        self.along = (c + 4 - 8 * near, x)
        self.here = near * 2 + y
        self.by_y = near * 2 + 1 - y
        self.by_z = (1 - near) * 2 + y
        self.corner = (1 - near) * 2 + 1 - y

    def rows(self, i, owner_x, start, rows):
        n, m = ORDER[i]
        target, column = GATHER_PLAN[m]
        half, width = self.sources[m].shape[1], self.sources[m].shape[2]
        return self.outs[target].at[
            n, pl.ds(pl.multiple_of(owner_x * half + start, 16), rows), pl.ds(column, width)
        ]

    def window(self, i, owner_x, piece, share=None):
        half = self.sources[ORDER[i][1]].shape[1]
        if i in ALONE:
            return self.rows(i, owner_x, self.core * (half // 2), half // 2)
        rows = half // 8
        start = (piece * 2 + self.core) * rows
        if share is not None:
            rows = rows // 2
            start = start + share * rows
        return self.rows(i, owner_x, start, rows)

    def local(self, i):
        n, m = ORDER[i]
        half = self.sources[m].shape[1]
        return make_remote(
            self.sources[m].at[n], self.rows(i, self.x, 0, half), self.l_s.at[i], self.l_r.at[i],
            self.sibling,
        )

    def x_copy(self, i):
        n, m = ORDER[i]
        half = self.sources[m].shape[1]
        if i in ALONE:
            rows = pl.ds(pl.multiple_of(self.core * (half // 2), 16), half // 2)
        else:
            rows = pl.ds(pl.multiple_of((self.here * 2 + self.core) * (half // 8), 16), half // 8)
        return make_remote(
            self.sources[m].at[n, rows], self.window(i, self.x, self.here), self.x_s.at[i],
            self.x_r.at[i], self.across,
        )

    def y_copy(self, i):
        view = self.window(i, 1 - self.x, self.here)
        return make_remote(view, view, self.y_s.at[i], self.y_r.at[i], self.aside)

    def z_copy(self, i):
        view = self.window(i, 1 - self.x, self.here)
        return make_remote(view, view, self.z_s.at[i], self.z_r.at[i], self.along)

    def y_corner(self, i):
        view = self.window(i, 1 - self.x, self.by_z, 1)
        return make_remote(view, view, self.yc_s.at[i], self.yc_r.at[i], self.aside)

    def z_corner(self, i):
        view = self.window(i, 1 - self.x, self.by_y, 0)
        return make_remote(view, view, self.zc_s.at[i], self.zc_r.at[i], self.along)

    def core_copy(self, i, which):
        piece = (self.here, self.by_y, self.by_z, self.corner)[which]
        view = self.window(i, 1 - self.x, piece)
        return make_remote(
            view, view, self.c_s.at[i, which], self.c_r.at[i, which], self.sibling
        )

    def each(self, i, act, alone=False):
        for place in range(len(ORDER)):
            if place in ALONE and not alone:
                continue

            @pl.when(i == place)
            def member(place=place):
                act(place)

    def send(self, i):
        def go(i):
            self.x_copy(i).start()
            self.local(i).start()

        self.each(i, go, True)

    def step(self, u):
        s = u // 3
        stage = u % 3

        @pl.when(stage == 0)
        def first():
            def spread(i):
                self.x_copy(i).wait_recv()
                self.y_copy(i).start()
                self.z_copy(i).start()
                self.core_copy(i, 0).start()

            self.each(s, spread)
            self.send(s + LEAD)

        @pl.when(stage == 1)
        def second():
            def corners(i):
                self.y_copy(i).wait_recv()
                self.z_corner(i).start()
                self.core_copy(i, 1).start()
                self.z_copy(i).wait_recv()
                self.y_corner(i).start()
                self.core_copy(i, 2).start()

            self.each(s - 1, corners)

        @pl.when(stage == 2)
        def third():
            def last(i):
                self.y_corner(i).wait_recv()
                self.z_corner(i).wait_recv()
                self.core_copy(i, 3).start()

            self.each(s - 2, last)

    def pass_on(self, n, m):
        for i in ALONE:
            if ORDER[i][1] == m:

                @pl.when(n == ORDER[i][0])
                def member(i=i):
                    self.x_copy(i).wait_recv()
                    self.core_copy(i, 0).start()

    def ready(self, n, m):
        for i in range(len(ORDER)):
            if ORDER[i][1] == m:

                @pl.when(n == ORDER[i][0])
                def member(i=i):
                    self.local(i).wait_recv()
                    for which in range(4 if i not in ALONE else 1):
                        self.core_copy(i, which).wait_recv()

    def drain(self):
        for i in range(len(ORDER)):
            self.local(i).wait_send()
            self.x_copy(i).wait_send()
            if i not in ALONE:
                for copy in (self.y_copy, self.z_copy, self.y_corner, self.z_corner):
                    copy(i).wait_send()
            for which in range(4 if i not in ALONE else 1):
                self.core_copy(i, which).wait_send()


def gather_scratch():
    dma = pltpu.SemaphoreType.DMA
    return [dma((len(ORDER),))] * 12 + [dma((len(ORDER), 4))] * 2


def head_columns(first, index):
    return pl.ds(pl.multiple_of(first + index * HEAD_SIZE, HEAD_SIZE), HEAD_SIZE)


def stream_blocks(first, count, slots, start, wait, body):
    def fill(i, carry):
        start(first + i, i)
        return carry

    lax.fori_loop(0, jnp.minimum(slots - 1, count), fill, 0)

    def one(i, carry):
        slot = i % slots

        @pl.when(i + slots - 1 < count)
        def following():
            start(first + i + slots - 1, (i + slots - 1) % slots)

        wait(first + i, slot)
        body(first + i, slot)
        return carry

    lax.fori_loop(0, count, one, 0)


def rms(values, gain):
    r = lax.rsqrt(jnp.mean(values * values, axis=-1, keepdims=True) + norm_epsilon)
    return values * r * gain


BUFFERS = 4
SCHEDULE = (
    (9, 12, 15, 16, 20, 21, 22, 23, 28, 29, 31, 32, 33, 34, 35, 36),
    (37, 37, 38, 38, 41, 42, 43, 44, 45, 45, 45, 46, 47, 48, 48, 49),
)


def forward_kernel(*refs):
    count = DECODER_LAYERS
    sources, refs = refs[:MEMBERS], refs[MEMBERS:]
    (g_attn, g_mlp, g_query, g_key, tokens, stretch_ids, lengths), refs = refs[:7], refs[7:]
    weights, refs = refs[:4], refs[4:]
    into_w, out_w, wide_w, down_w = weights
    (both_out, middle_out, entry_out, pre_out, kept_hbm, kept_out_hbm, kept_log_hbm), refs = (
        refs[:7], refs[7:]
    )
    (hidden_t, mid_t, attn_t, normed_t, attn_gains, mlp_gains, head_gains), refs = (
        refs[:7], refs[7:]
    )
    (output, live, cosine, sine, key_place, query_cap), refs = refs[:6], refs[6:]
    sizes = len(gather_scratch())
    gather = Gatherer(sources, weights, refs[:sizes])
    (wide_mine, wide_other, head_mine, head_other, stream, middle, pre, low, attn_low, hidden_low, both, cols_w, rows_w,
     kept, kept_out, kept_log, send, osend, orecv, vt,
     pack_sem, cols_sem, rows_sem, save_sem,
     q_s, q_r, k_s, k_r, o_s, o_r) = refs[sizes:]
    c = lax.axis_index("ctx")
    x = lax.axis_index("fsdp")
    me = c % PEERS
    z = c // 4

    def peer(r):
        return (c - me + r, x)

    barrier = pltpu.get_barrier_semaphore()

    def greet(o, carry):
        pl.semaphore_signal(barrier, inc=1, device_id=peer((me + o) % PEERS), device_id_type=MESH)
        return carry

    lax.fori_loop(1, PEERS, greet, 0)
    pl.semaphore_signal(barrier, inc=1, device_id=gather.across, device_id_type=MESH)
    pl.semaphore_wait(barrier, PEERS)

    for k, member in enumerate((g_attn, g_mlp)):
        wide_mine[k] = member[...].astype(jnp.float32)
    for k, member in enumerate((g_query, g_key)):
        head_mine[k] = member[...].astype(jnp.float32)
    gain_copies = (
        make_remote(wide_mine, wide_other, pack_sem.at[0], pack_sem.at[1], gather.across),
        make_remote(head_mine, head_other, pack_sem.at[2], pack_sem.at[3], gather.across),
    )
    for copy in gain_copies:
        copy.start()
    for i in range(LEAD):
        gather.send(i)
    stream[...] = tokens[...].astype(jnp.float32)

    slot = c // PEERS
    limit = lengths[0, slot]
    stretches = 2 * PEERS
    lane = lax.broadcasted_iota(jnp.int32, (1, 256), 1) % 128
    row = lax.broadcasted_iota(jnp.int32, (128, 1), 0)

    def spots(r, along):
        first = stretch_ids[slot * PEERS + r, 0, 0] % stretches * STRETCH
        second = stretch_ids[slot * PEERS + r, 0, 1] % stretches * STRETCH
        return jnp.where(along < STRETCH, first, second - STRETCH) + along

    for r in range(PEERS):
        key_place[r * 128 : (r + 1) * 128, :] = spots(r, row)
        query_cap[r] = jnp.minimum(spots(r, lane), limit - 1)
    mine = spots(me, row)
    live[...] = jnp.where(mine < limit, 1.0, 0.0)
    half = HEAD_SIZE // 2
    column = lax.broadcasted_iota(jnp.int32, (1, HEAD_SIZE), 1)
    spread = (column % half).astype(jnp.float32) * (2.0 / HEAD_SIZE)
    angles = mine.astype(jnp.float32) * jnp.exp(spread * -math.log(rope_base))
    cosine[...] = jnp.cos(angles)
    sine[...] = jnp.where(column < half, -jnp.sin(angles), jnp.sin(angles))

    for copy in gain_copies:
        copy.wait_recv()
    low_side = jnp.where(x == 0, 0, 1)

    def pick(first, second, flip):
        return jnp.where(low_side == flip, first, second)

    for k, target in enumerate((attn_gains, mlp_gains)):
        sides = [pick(wide_mine[k], wide_other[k], flip) for flip in range(2)]
        for n in range(count):
            target[n] = jnp.concatenate([side[n : n + 1] for side in sides], axis=1)
    for k in range(2):
        for flip in range(2):
            side = pick(head_mine[k], head_other[k], flip)
            for n in range(count):
                head_gains[n, k : k + 1, flip * half : (flip + 1) * half] = side[n : n + 1]

    cos = cosine[...]
    sin = sine[...]

    def cols_copy(ref, n, column, slot):
        return pltpu.make_async_copy(
            ref.at[n, :, pl.ds(pl.multiple_of(column, 512), 512)], cols_w.at[slot],
            cols_sem.at[slot],
        )

    def rows_copy(ref, n, i, slot):
        rows = pl.ds(pl.multiple_of(i * 512, 512), 512)
        return pltpu.make_async_copy(ref.at[n, rows], rows_w.at[slot], rows_sem.at[slot])

    saves = (
        (stream, entry_out), (pre, pre_out), (middle, middle_out), (kept_out, kept_out_hbm),
        (kept_log, kept_log_hbm), (both, both_out),
    )

    def save(n, k):
        return pltpu.make_async_copy(saves[k][0], saves[k][1].at[n], save_sem.at[k])

    def save_kept(n):
        return pltpu.make_async_copy(kept.at[n], kept_hbm.at[n], save_sem.at[6])

    def turn(source, target, n, blocks):
        def one(j, carry):
            columns = pl.ds(pl.multiple_of(j * 128, 128), 128)
            target[n, columns, :] = source[:, columns].astype(jnp.float32).T.astype(jnp.bfloat16)
            return carry

        lax.fori_loop(0, blocks, one, 0)

    def key_copy(n, r, slot):
        return make_remote(
            send.at[r, pl.ds(2, 2)], kept.at[n, slot, pl.ds(2, 2)], k_s.at[r], k_r.at[slot], peer(r)
        )

    def query_copy(n, r, slot):
        return make_remote(
            send.at[r, pl.ds(0, 2)], kept.at[n, slot, pl.ds(0, 2)], q_s.at[r], q_r.at[slot], peer(r)
        )

    def out_copy(r, slot):
        return make_remote(osend.at[r], orecv.at[slot], o_s.at[r], o_r.at[slot], peer(r))

    def project(n, first, blocks):
        def body(i, slot):
            pre[:, pl.ds(pl.multiple_of(i * 512, 512), 512)] = jnp.dot(
                low[...], cols_w[slot], preferred_element_type=jnp.float32
            )

        stream_blocks(
            first,
            blocks,
            BUFFERS,
            lambda i, slot: cols_copy(into_w, n, i * 512, slot).start(),
            lambda i, slot: cols_copy(into_w, n, i * 512, slot).wait(),
            body,
        )

    def turned(n, first, index, k):
        v = rms(pre[:, head_columns(first, index)], head_gains[n, k : k + 1, :])
        return (v * cos + pltpu.roll(v, HEAD_SIZE // 2, 1) * sin).astype(jnp.bfloat16)

    def keys_part(n):
        save(n, 0).start()
        low[...] = rms(stream[...], attn_gains[n]).astype(jnp.bfloat16)
        turn(low, normed_t, n, 8)
        gather.ready(n, 0)
        project(n, 4, 2)

    def values_part(n):
        gather.ready(n, 1)
        project(n, 6, 2)

        def make_keys(o, carry):
            r = (me + o) % PEERS
            key = turned(n, 2048, r, 1)
            value = pre[:, head_columns(3072, r)].astype(jnp.bfloat16)

            @pl.when(o < PEERS)
            def away():
                send[r, 2] = key
                send[r, 3] = value
                key_copy(n, r, me).start()

            @pl.when(o == PEERS)
            def home():
                kept[n, me, 2] = key
                kept[n, me, 3] = value

            return carry

        lax.fori_loop(1, PEERS + 1, make_keys, 0)

    def queries_part(n):
        gather.ready(n, 2)
        project(n, 0, 4)
        save(n, 1).start()

    def spread_queries(n):
        def make_queries(o, carry):
            r = (me + o) % PEERS
            first = turned(n, 0, 2 * r, 0)
            second = turned(n, 0, 2 * r + 1, 0)

            @pl.when(o < PEERS)
            def away():
                send[r, 0] = first
                send[r, 1] = second
                query_copy(n, r, me).start()

            @pl.when(o == PEERS)
            def home():
                kept[n, me, 0] = first
                kept[n, me, 1] = second

            return carry

        lax.fori_loop(1, PEERS + 1, make_queries, 0)

    def attention(n, part):
        def await_keys(o, carry):
            key_copy(n, me, (me + o) % PEERS).wait_recv()
            return carry

        def turn_values(j, carry):
            vt[j] = kept[n, j, 3].astype(jnp.float32).T.astype(jnp.bfloat16)
            return carry

        @pl.when(part == 0)
        def opening():
            lax.fori_loop(1, PEERS, await_keys, 0)
            lax.fori_loop(0, PEERS, turn_values, 0)

        def block(o, carry):
            j = (me + o) % PEERS

            @pl.when(o > 0)
            def arrived():
                query_copy(n, me, j).wait_recv()

            queries = kept[n, j, 0:2].reshape(2 * 128, HEAD_SIZE)
            keys = kept[n, :, 2].reshape(PEERS * 128, HEAD_SIZE)
            scores = lax.dot_general(keys, queries, NT, preferred_element_type=jnp.float32) * SCALE
            allowed = key_place[...] <= query_cap[j]
            scores = jnp.where(allowed, scores, masked_logits)
            highest = jnp.max(scores, axis=0, keepdims=True)
            expo = jnp.exp(scores - highest)
            total = jnp.sum(expo, axis=0, keepdims=True)
            expo_low = expo.astype(jnp.bfloat16)
            turned_out = jnp.zeros((HEAD_SIZE, 256), jnp.float32)
            for i in range(PEERS):
                turned_out += jnp.dot(
                    vt[i], expo_low[i * 128 : (i + 1) * 128], preferred_element_type=jnp.float32
                )
            turned_out = turned_out / total
            kept_out[j] = turned_out
            kept_log[j] = jnp.broadcast_to(highest + jnp.log(total), (8, 256))
            attended = turned_out.T.astype(jnp.bfloat16).reshape(2, 128, HEAD_SIZE)

            @pl.when(o == 0)
            def home():
                orecv[me] = attended

            @pl.when(o > 0)
            def away():
                osend[j] = attended
                out_copy(j, me).start()

            return carry

        lax.fori_loop(2 * part, 2 * part + 2, block, 0)

        @pl.when(part == 3)
        def closing():
            save(n, 3).start()
            save(n, 4).start()
            save_kept(n).start()

    def close_attention(n):
        def collect(o, carry):
            h = (me + o) % PEERS

            @pl.when(o > 0)
            def arrived():
                out_copy(me, h).wait_recv()

            attn_low[:, head_columns(0, 2 * h)] = orecv[h, 0]
            attn_low[:, head_columns(0, 2 * h + 1)] = orecv[h, 1]
            return carry

        lax.fori_loop(0, PEERS, collect, 0)
        save(n, 0).wait()
        middle[...] = stream[...]
        gather.ready(n, 3)

        def body(i, slot):
            columns = pl.ds(pl.multiple_of(i * 512, 512), 512)
            middle[...] += jnp.dot(
                attn_low[:, columns], rows_w[slot], preferred_element_type=jnp.float32
            )

        stream_blocks(
            0,
            4,
            BUFFERS,
            lambda i, slot: rows_copy(out_w, n, i, slot).start(),
            lambda i, slot: rows_copy(out_w, n, i, slot).wait(),
            body,
        )
        save(n, 2).start()

    def middle_norm(n):
        turn(attn_low, attn_t, n, 16)
        low[...] = rms(middle[...], mlp_gains[n]).astype(jnp.bfloat16)
        turn(low, mid_t, n, 8)

        def settle(o, carry):
            r = (me + o) % PEERS
            key_copy(n, r, me).wait_send()
            query_copy(n, r, me).wait_send()
            out_copy(r, me).wait_send()
            return carry

        lax.fori_loop(1, PEERS, settle, 0)

    def widen(n, base, part):
        def body(i, slot):
            columns = pl.ds(pl.multiple_of(base + i * 512, 512), 512)
            result = jnp.dot(low[...], cols_w[slot], preferred_element_type=jnp.float32)
            both[:, columns] = result
            if base > 0:
                inner = pl.ds(pl.multiple_of(i * 512, 512), 512)
                gate = both[:, inner]
                hidden_low[:, inner] = (gate * jax.nn.sigmoid(gate) * result).astype(jnp.bfloat16)

        stream_blocks(
            3 * part,
            3,
            BUFFERS,
            lambda i, slot: cols_copy(wide_w, n, base + i * 512, slot).start(),
            lambda i, slot: cols_copy(wide_w, n, base + i * 512, slot).wait(),
            body,
        )

    def gate_part(n, part):
        @pl.when(part == 0)
        def opening():
            gather.ready(n, 4)

        widen(n, 0, part)

    def up_part(n, part):
        @pl.when(part == 0)
        def opening():
            gather.ready(n, 5)

        widen(n, 3072, part)

        @pl.when(part == 1)
        def closing():
            save(n, 5).start()

    def turn_hidden(n):
        gather.pass_on(n, 6)
        turn(hidden_low, hidden_t, n, 24)

    def narrow(n):
        gather.ready(n, 6)
        stream[...] = middle[...]

        def body(i, slot):
            columns = pl.ds(pl.multiple_of(i * 512, 512), 512)
            stream[...] += jnp.dot(
                hidden_low[:, columns], rows_w[slot], preferred_element_type=jnp.float32
            )

        stream_blocks(
            0,
            6,
            BUFFERS,
            lambda i, slot: rows_copy(down_w, n, i, slot).start(),
            lambda i, slot: rows_copy(down_w, n, i, slot).wait(),
            body,
        )
        for k in range(1, 6):
            save(n, k).wait()
        save_kept(n).wait()

    def when_at(u, index):
        return (u == SCHEDULE[0][index]) | (u == SCHEDULE[1][index])

    def at_among(u, first, blocks):
        part = jnp.zeros((), jnp.int32)
        for k in range(blocks):
            part = jnp.where(when_at(u, first + k), k, part)
        chosen = functools.reduce(jnp.logical_or, [when_at(u, first + k) for k in range(blocks)])
        return chosen, part

    def step(u, carry):
        gather.step(u)
        n = jnp.where(u >= SCHEDULE[1][0], 1, 0)
        pieces = (
            (1, keys_part), (1, values_part), (1, queries_part), (1, spread_queries),
            (4, attention), (1, close_attention), (1, middle_norm), (2, gate_part),
            (2, up_part), (1, turn_hidden), (1, narrow),
        )
        index = 0
        for blocks, work in pieces:
            chosen, part = at_among(u, index, blocks)

            @pl.when(chosen)
            def piece(blocks=blocks, work=work, part=part):
                if blocks == 1:
                    work(n)
                else:
                    work(n, part)

            index += blocks
        return carry

    lax.fori_loop(0, SCHEDULE[1][-1] + 1, step, 0)
    output[...] = (stream[...] * live[...]).astype(jnp.bfloat16)
    gather.drain()
    for copy in gain_copies:
        copy.wait_send()


def forward(weights, gains, tokens, stretch_ids, lengths, number):
    count = DECODER_LAYERS
    dma = pltpu.SemaphoreType.DMA
    low, wide = jnp.bfloat16, jnp.float32
    pair = pltpu.VMEM((PEERS, 2, 128, HEAD_SIZE), low)
    anywhere = pl.BlockSpec(memory_space=pl.ANY)
    near = pl.BlockSpec(memory_space=pltpu.VMEM)
    gathered = [(1024, 4096), (2048, 1024), (1024, 6144), (3072, 1024)]
    saved = [
        ((128, 6144), wide), ((128, 1024), wide), ((128, 1024), wide), ((128, 4096), wide),
        ((PEERS, 4, 128, HEAD_SIZE), low), ((PEERS, HEAD_SIZE, 256), wide), ((PEERS, 8, 256), wide),
    ]
    turned = [(3072, 128), (1024, 128), (2048, 128), (1024, 128)]
    results = (
        [((count,) + s, low) for s in gathered]
        + [((count,) + s, d) for s, d in saved]
        + [((count,) + s, low) for s in turned]
        + [((count, 1, 1024), wide)] * 2
        + [((count, 2, HEAD_SIZE), wide), ((128, 1024), low), ((128, 1), wide)]
        + [((128, HEAD_SIZE), wide)] * 2
        + [((PEERS * 128, 1), jnp.int32), ((PEERS, 1, 256), jnp.int32)]
    )
    return pl.pallas_call(
        forward_kernel,
        out_shape=[jax.ShapeDtypeStruct(s, d) for s, d in results],
        in_specs=[anywhere] * MEMBERS + [near] * 5 + [pl.BlockSpec(memory_space=pltpu.SMEM)] * 2,
        out_specs=[anywhere] * 11 + [near] * 13,
        scratch_shapes=gather_scratch()
        + [
            pltpu.VMEM((2, count, 512), wide),
            pltpu.VMEM((2, count, 512), wide),
            pltpu.VMEM((2, count, 64), wide),
            pltpu.VMEM((2, count, 64), wide),
            pltpu.VMEM((128, 1024), wide),
            pltpu.VMEM((128, 1024), wide),
            pltpu.VMEM((128, 4096), wide),
            pltpu.VMEM((128, 1024), low),
            pltpu.VMEM((128, 2048), low),
            pltpu.VMEM((128, 3072), low),
            pltpu.VMEM((128, 6144), wide),
            pltpu.VMEM((BUFFERS, 1024, 512), low),
            pltpu.VMEM((BUFFERS, 512, 1024), low),
            pltpu.VMEM((count, PEERS, 4, 128, HEAD_SIZE), low),
            pltpu.VMEM((PEERS, HEAD_SIZE, 256), wide),
            pltpu.VMEM((PEERS, 8, 256), wide),
            pltpu.VMEM((PEERS, 4, 128, HEAD_SIZE), low),
            pair,
            pair,
            pltpu.VMEM((PEERS, HEAD_SIZE, 128), low),
            dma((4,)), dma((BUFFERS,)), dma((BUFFERS,)), dma((7,)),
        ]
        + [dma((PEERS,))] * 6,
        compiler_params=pltpu.CompilerParams(
            collective_id=number, has_side_effects=True, vmem_limit_bytes=56 * 2**20
        ),
        name="forward",
    )(*weights, *gains, tokens, stretch_ids, lengths)


WORK = 12


def rms_back(values, gain, upstream):
    r = lax.rsqrt(jnp.mean(values * values, axis=-1, keepdims=True) + norm_epsilon)
    weighted = upstream * gain
    mean = jnp.mean(weighted * values, axis=-1, keepdims=True)
    grad = r * weighted - values * (r * r * r) * mean
    return grad, jnp.sum(upstream * values * r, axis=0, keepdims=True)


def backward_kernel(*refs):
    count = DECODER_LAYERS
    acts, stored, refs = refs[:4], refs[4:11], refs[11:]
    (into_w, out_w, wide_w, down_w) = refs[:4]
    (cotangent, attn_gains, mlp_gains, head_gains, live, cosine, sine, key_place, query_cap) = (
        refs[4:13]
    )
    results = refs[13:20]
    grad_stream, gain_out, held = refs[20:23]
    refs = refs[23:]
    sizes = len(reduce_scratch(count))
    reduce_refs, refs = refs[:sizes], refs[sizes:]
    gain_refs, refs = refs[:4], refs[4:]
    (down_low, both_low, out_low, pre_low, terms,
     gate_up, middle, entry, pre, kept, kept_out, kept_log, mid_grad, rows_w, wide_rows,
     dsend, drecv, qsend, qrecv, ksend, krecv, kt, key_sum, value_sum,
     load_sem, rows_sem, wide_sem, gate_sem, d_s, d_r, q_s, q_r, k_s, k_r) = refs
    reducer = Reducer(
        acts, ((down_low, 1), (both_low, 6), (out_low, 1), (pre_low, 4)), results,
        (held,) + tuple(reduce_refs), tuple(reversed(range(count))),
    )
    gain_sum = GainSum(reducer, terms, gain_out, gain_refs)
    c = lax.axis_index("ctx")
    x = lax.axis_index("fsdp")
    me = c % PEERS
    z = c // 4

    def peer(r):
        return (c - me + r, x)

    barrier = pltpu.get_barrier_semaphore()

    def greet(o, carry):
        pl.semaphore_signal(barrier, inc=1, device_id=peer((me + o) % PEERS), device_id_type=MESH)
        return carry

    lax.fori_loop(1, PEERS, greet, 0)
    pl.semaphore_signal(barrier, inc=1, device_id=reducer.across, device_id_type=MESH)
    for o in range(2):
        far = ((z // 2 * 2 + 2) % 4 + o) * 4 + c % 4
        pl.semaphore_signal(barrier, inc=1, device_id=(far, x), device_id_type=MESH)
    pl.semaphore_wait(barrier, PEERS + 2)

    grad_stream[...] = cotangent[...].astype(jnp.float32) * live[...]
    terms[...] = jnp.zeros_like(terms)
    reducer.start_acts(0, (0,))

    cos = cosine[...]
    sin = sine[...]

    def grad_copy(r, slot):
        return make_remote(dsend.at[r], drecv.at[slot], d_s.at[r], d_r.at[slot], peer(r))

    def query_copy(r, slot):
        return make_remote(qsend.at[r], qrecv.at[slot], q_s.at[r], q_r.at[slot], peer(r))

    def key_copy(r, slot):
        return make_remote(ksend.at[r], krecv.at[slot], k_s.at[r], k_r.at[slot], peer(r))

    saved = (middle, entry, pre, kept, kept_out, kept_log)

    def load(layer, k):
        return pltpu.make_async_copy(stored[1 + k].at[layer], saved[k], load_sem.at[k])

    def await_load(k):
        load(0, k).wait()

    def add_term(layer, first, term):
        for i in range(8):
            terms[pl.ds(layer * 24 + first + i, 1), :] = term[:, i * 128 : (i + 1) * 128]

    def rows_copy(ref, layer, i, slot):
        rows = pl.ds(pl.multiple_of(i * 512, 512), 512)
        return pltpu.make_async_copy(ref.at[layer, rows], rows_w.at[slot], rows_sem.at[slot])

    def wide_copy(ref, layer, i, slot):
        rows = pl.ds(pl.multiple_of(i * 128, 128), 128)
        columns = ref.shape[2]
        return pltpu.make_async_copy(
            ref.at[layer, rows], wide_rows.at[slot, :, pl.ds(0, columns)], wide_sem.at[slot]
        )

    def hidden_part(n, layer, part):
        @pl.when(part == 0)
        def opening():
            for k in range(len(saved)):
                load(layer, k).start()
            down_low[n] = grad_stream[...].astype(jnp.bfloat16)

        @pl.when((n == 0) & (part == 0))
        def first():
            reducer.start_grad(0)
            reducer.start_acts(0, (1, 2, 3))

        def gate_copy(i, slot, k):
            columns = pl.ds(pl.multiple_of(k * 3072 + i * 512, 512), 512)
            return pltpu.make_async_copy(
                stored[0].at[layer, :, columns], gate_up.at[slot, k], gate_sem.at[slot, k]
            )

        def start(i, slot):
            rows_copy(down_w, layer, i, slot).start()
            for k in range(2):
                gate_copy(i, slot, k).start()

        def wait(i, slot):
            rows_copy(down_w, layer, i, slot).wait()
            for k in range(2):
                gate_copy(i, slot, k).wait()

        def body(i, slot):
            hidden = lax.dot_general(
                down_low[n], rows_w[slot], NT, preferred_element_type=jnp.float32
            )
            gate = gate_up[slot, 0]
            up = gate_up[slot, 1]
            sigmoid = jax.nn.sigmoid(gate)
            columns = pl.multiple_of(i * 512, 512)
            both_low[n, :, pl.ds(columns, 512)] = (
                hidden * up * sigmoid * (1.0 + gate * (1.0 - sigmoid))
            ).astype(jnp.bfloat16)
            both_low[n, :, pl.ds(3072 + columns, 512)] = (hidden * gate * sigmoid).astype(
                jnp.bfloat16
            )

        stream_blocks(part * 3, 3, 2, start, wait, body)

        @pl.when((n == 0) & (part == 1))
        def rest():
            reducer.begin_more()

    def middle_part(n, layer, part):
        def body(i, slot):
            mid_grad[:, pl.ds(pl.multiple_of(i * 128, 128), 128)] = lax.dot_general(
                both_low[n], wide_rows[slot], NT, preferred_element_type=jnp.float32
            )

        stream_blocks(
            part * 3,
            jnp.where(part == 2, 2, 3),
            2,
            lambda i, slot: wide_copy(wide_w, layer, i, slot).start(),
            lambda i, slot: wide_copy(wide_w, layer, i, slot).wait(),
            body,
        )

        @pl.when(part == 2)
        def closing():
            await_load(0)
            grad, term = rms_back(middle[...], mlp_gains[layer], mid_grad[...])
            add_term(layer, 8, term)
            total = grad_stream[...] + grad
            grad_stream[...] = total
            out_low[n] = total.astype(jnp.bfloat16)

    def out_part(n, layer):
        def place(i):
            return (i + me // 2) % 4

        def body(i, slot):
            low = lax.dot_general(
                out_low[n], rows_w[slot], NT, preferred_element_type=jnp.float32
            ).astype(jnp.bfloat16)
            for k in range(2):
                r = 2 * place(i) + k

                @pl.when(r == me)
                def home(k=k):
                    for j in range(2):
                        at = (2 * k + j) * HEAD_SIZE
                        drecv[me, j] = low[:, at : at + HEAD_SIZE]

                @pl.when(r != me)
                def away(k=k, r=r):
                    for j in range(2):
                        at = (2 * k + j) * HEAD_SIZE
                        dsend[r, j] = low[:, at : at + HEAD_SIZE]
                    grad_copy(r, me).start()

        stream_blocks(
            0,
            4,
            2,
            lambda i, slot: rows_copy(out_w, layer, place(i), slot).start(),
            lambda i, slot: rows_copy(out_w, layer, place(i), slot).wait(),
            body,
        )
        for k in range(2, len(saved)):
            await_load(k)

        def turn_keys(j, carry):
            kt[j] = kept[j, 2].astype(jnp.float32).T.astype(jnp.bfloat16)
            return carry

        lax.fori_loop(0, PEERS, turn_keys, 0)
        key_sum[...] = jnp.zeros_like(key_sum)
        value_sum[...] = jnp.zeros_like(value_sum)

    def attention_block(o):
        j = (me + o) % PEERS

        @pl.when(o > 0)
        def arrived():
            grad_copy(me, j).wait_recv()

        grads = drecv[j].reshape(2 * 128, HEAD_SIZE)
        delta = jnp.sum(grads.astype(jnp.float32).T * kept_out[j], axis=0, keepdims=True)
        queries = kept[j, 0:2].reshape(2 * 128, HEAD_SIZE)
        keys = kept[:, 2].reshape(PEERS * 128, HEAD_SIZE)
        values = kept[:, 3].reshape(PEERS * 128, HEAD_SIZE)
        scores = lax.dot_general(keys, queries, NT, preferred_element_type=jnp.float32) * SCALE
        allowed = key_place[...] <= query_cap[j]
        scores = jnp.where(allowed, scores, masked_logits)
        prob = jnp.exp(scores - kept_log[j, 0:1, :])
        dprob = lax.dot_general(values, grads, NT, preferred_element_type=jnp.float32)
        dscore = (prob * (dprob - delta)).astype(jnp.bfloat16)
        value_sum[...] += jnp.dot(
            prob.astype(jnp.bfloat16), grads, preferred_element_type=jnp.float32
        )
        key_sum[...] += jnp.dot(dscore, queries, preferred_element_type=jnp.float32)
        turned = jnp.zeros((HEAD_SIZE, 256), jnp.float32)
        for i in range(PEERS):
            turned += jnp.dot(
                kt[i], dscore[i * 128 : (i + 1) * 128], preferred_element_type=jnp.float32
            )
        query_grad = (turned * SCALE).T.astype(jnp.bfloat16).reshape(2, 128, HEAD_SIZE)

        @pl.when(o == 0)
        def home():
            qrecv[me] = query_grad

        @pl.when(o > 0)
        def away():
            qsend[j] = query_grad
            query_copy(j, me).start()

        @pl.when(o == PEERS - 1)
        def keys_done():
            lax.fori_loop(1, PEERS + 1, push_keys, 0)

    def push_keys(o, carry):
        j = (me + o) % PEERS
        rows = pl.ds(pl.multiple_of(j * 128, 128), 128)
        key = (key_sum[rows, :] * SCALE).astype(jnp.bfloat16)
        value = value_sum[rows, :].astype(jnp.bfloat16)

        @pl.when(o < PEERS)
        def away():
            ksend[j, 0] = key
            ksend[j, 1] = value
            key_copy(j, me).start()

        @pl.when(o == PEERS)
        def home():
            krecv[me, 0] = key
            krecv[me, 1] = value

        return carry

    def head_part(n, layer):
        def back(grad, first, index, gain):
            g = grad.astype(jnp.float32)
            dy = g * cos - pltpu.roll(g, HEAD_SIZE // 2, 1) * sin
            low, term = rms_back(pre[:, head_columns(first, index)], gain, dy)
            return low.astype(jnp.bfloat16), term

        def finish_queries(o, total):
            h = (me + o) % PEERS

            @pl.when(o > 0)
            def arrived():
                query_copy(me, h).wait_recv()

            for i in range(2):
                low, term = back(qrecv[h, i], 0, 2 * h + i, head_gains[layer, 0:1, :])
                pre_low[n, :, head_columns(0, 2 * h + i)] = low
                total += term
            return total

        zero = jnp.zeros((1, HEAD_SIZE), jnp.float32)
        terms[pl.ds(layer * 24 + 16, 1), :] = lax.fori_loop(0, PEERS, finish_queries, zero)

        def finish_keys(o, total):
            h = (me + o) % PEERS

            @pl.when(o > 0)
            def arrived():
                key_copy(me, h).wait_recv()

            low, term = back(krecv[h, 0], 2048, h, head_gains[layer, 1:2, :])
            pre_low[n, :, head_columns(2048, h)] = low
            pre_low[n, :, head_columns(3072, h)] = krecv[h, 1]
            return total + term

        terms[pl.ds(layer * 24 + 17, 1), :] = lax.fori_loop(0, PEERS, finish_keys, zero)

        def settle(o, carry):
            r = (me + o) % PEERS
            grad_copy(r, me).wait_send()
            query_copy(r, me).wait_send()
            key_copy(r, me).wait_send()
            return carry

        lax.fori_loop(1, PEERS, settle, 0)

    def entry_part(n, layer, part):
        def body(i, slot):
            mid_grad[:, pl.ds(pl.multiple_of(i * 128, 128), 128)] = lax.dot_general(
                pre_low[n], wide_rows[slot, :, 0:4096], NT, preferred_element_type=jnp.float32
            )

        stream_blocks(
            part * 4,
            4,
            2,
            lambda i, slot: wide_copy(into_w, layer, i, slot).start(),
            lambda i, slot: wide_copy(into_w, layer, i, slot).wait(),
            body,
        )

        @pl.when(part == 1)
        def closing():
            await_load(1)
            grad, term = rms_back(entry[...], attn_gains[layer], mid_grad[...])
            add_term(layer, 0, term)
            grad_stream[...] += grad

    def step(w, carry):
        reducer.step(w - 2)
        gain_sum.step(w, WORK * count)
        n = w // WORK
        phase = w % WORK
        layer = count - 1 - n
        busy = w < WORK * count

        @pl.when(busy & (phase < 2))
        def phase_hidden():
            hidden_part(n, layer, phase)

        @pl.when(busy & (phase >= 2) & (phase < 5))
        def phase_middle():
            middle_part(n, layer, phase - 2)

        @pl.when(busy & (phase == 5))
        def phase_out():
            out_part(n, layer)

        @pl.when(busy & (phase >= 6) & (phase < 9))
        def phase_attention():
            first = (phase - 6) * 3

            def block(i, inner):
                attention_block(first + i)
                return inner

            lax.fori_loop(0, jnp.minimum(3, PEERS - first), block, 0)

        @pl.when(busy & (phase == 9))
        def phase_heads():
            head_part(n, layer)

        @pl.when(busy & (phase >= 10))
        def phase_entry():
            entry_part(n, layer, phase - 10)

        return carry

    lax.fori_loop(0, reducer.steps() + 2, step, 0)
    reducer.drain()
    gain_sum.drain()


RESULTS = ((32, 2048), (32, 1024), (32, 1024), (64, 1024), (32, 3072), (32, 3072), (96, 1024))


def backward(acts, saved, weights, cotangent, gains, tables, number):
    count = DECODER_LAYERS
    dma = pltpu.SemaphoreType.DMA
    low, wide = jnp.bfloat16, jnp.float32
    pair = pltpu.VMEM((PEERS, 2, 128, HEAD_SIZE), low)
    anywhere = pl.BlockSpec(memory_space=pl.ANY)
    near = pl.BlockSpec(memory_space=pltpu.VMEM)
    return pl.pallas_call(
        backward_kernel,
        out_shape=[jax.ShapeDtypeStruct((count,) + shape, wide) for shape in RESULTS]
        + [
            jax.ShapeDtypeStruct((128, 1024), wide),
            jax.ShapeDtypeStruct((24 * count, 128), wide),
            jax.ShapeDtypeStruct((GRADS * count, 384, 1024), low),
        ],
        in_specs=[anywhere] * 15 + [near] * 9,
        out_specs=[near] * 9 + [anywhere],
        scratch_shapes=reduce_scratch(count)
        + gain_scratch(24 * count)
        + [
            pltpu.VMEM((count, 128, 1024), low),
            pltpu.VMEM((count, 128, 6144), low),
            pltpu.VMEM((count, 128, 1024), low),
            pltpu.VMEM((count, 128, 4096), low),
            pltpu.VMEM((24 * count, 128), wide),
            pltpu.VMEM((2, 2, 128, 512), wide),
            pltpu.VMEM((128, 1024), wide),
            pltpu.VMEM((128, 1024), wide),
            pltpu.VMEM((128, 4096), wide),
            pltpu.VMEM((PEERS, 4, 128, HEAD_SIZE), low),
            pltpu.VMEM((PEERS, HEAD_SIZE, 256), wide),
            pltpu.VMEM((PEERS, 8, 256), wide),
            pltpu.VMEM((128, 1024), wide),
            pltpu.VMEM((2, 512, 1024), low),
            pltpu.VMEM((2, 128, 6144), low),
        ]
        + [pair] * 6
        + [
            pltpu.VMEM((PEERS, HEAD_SIZE, 128), low),
            pltpu.VMEM((PEERS * 128, HEAD_SIZE), wide),
            pltpu.VMEM((PEERS * 128, HEAD_SIZE), wide),
            dma((6,)), dma((2,)), dma((2,)), dma((2, 2)),
        ]
        + [dma((PEERS,))] * 6,
        compiler_params=pltpu.CompilerParams(
            collective_id=number, has_side_effects=True, vmem_limit_bytes=62 * 2**20
        ),
        name="backward",
    )(*acts, *saved, *weights, cotangent, *gains, *tables)


def finish_kernel(*refs):
    count = DECODER_LAYERS
    moved, sums = refs[:9], refs[9]
    outs, gain_outs = refs[10:19], refs[19:23]
    held, sems = refs[23:32], refs[32]

    def into(k):
        return pltpu.make_async_copy(moved[k], held[k], sems.at[0, k])

    def onward(k):
        return pltpu.make_async_copy(held[k], outs[k], sems.at[1, k])

    for k in range(9):
        into(k).start()
    for k in range(9):
        into(k).wait()
        onward(k).start()
    place = lax.axis_index("ctx") * 2 + lax.axis_index("fsdp")

    def cut(row, offset, span):
        values = sums[pl.ds(row, 1), :]
        return pltpu.roll(values, (128 - offset) % 128, 1)[:, :span]

    for n in range(count):
        first = 24 * n
        for k in range(2):
            gain_outs[k][n : n + 1, :] = cut(first + 8 * k + place // 4, place % 4 * 32, 32)
            gain_outs[2 + k][n : n + 1, :] = cut(first + 16 + k, place * 4, 4)
    for k in range(9):
        onward(k).wait()


def finish(moved, sums):
    count = DECODER_LAYERS
    anywhere = pl.BlockSpec(memory_space=pl.ANY)
    near = pl.BlockSpec(memory_space=pltpu.VMEM)
    return pl.pallas_call(
        finish_kernel,
        out_shape=[jax.ShapeDtypeStruct(member.shape, member.dtype) for member in moved]
        + [jax.ShapeDtypeStruct((count, span), jnp.float32) for span in (32, 32, 4, 4)],
        in_specs=[anywhere] * 9 + [near],
        out_specs=[anywhere] * 9 + [near] * 4,
        scratch_shapes=[pltpu.VMEM(member.shape, member.dtype) for member in moved]
        + [pltpu.SemaphoreType.DMA((2, 9))],
        compiler_params=pltpu.CompilerParams(vmem_limit_bytes=60 * 2**20),
        name="finish",
    )(*moved, sums)


def from_partner(shard, axis, apart):
    return lax.ppermute(shard, axis, [(i, i ^ 1 << apart) for i in range(lax.axis_size(axis))])


def token_places(stretch_table, slot_lengths):
    ctx_count = stretch_table.shape[0]
    stretch_order = stretch_table.reshape(-1)
    within = jnp.arange(STRETCH, dtype=jnp.int32)
    places = (stretch_order % ctx_count * STRETCH)[:, None] + within[None, :]
    slot_ids = jnp.broadcast_to((stretch_order // ctx_count)[:, None], places.shape).reshape(-1)
    places = places.reshape(-1)
    limits = jnp.where(slot_ids == 0, slot_lengths[0], slot_lengths[1])
    return (places, slot_ids, places < limits)


def rotary_tables(places):
    half_dim = HEAD_SIZE // 2
    spread = jnp.arange(half_dim, dtype=jnp.int32).astype(jnp.float32) * (2.0 / HEAD_SIZE)
    inverse = jnp.exp(spread * -math.log(rope_base))
    angles = places.astype(jnp.float32)[:, None] * inverse[None, :]
    return (
        jnp.concatenate([jnp.cos(angles)] * 2, axis=-1),
        jnp.concatenate([jnp.sin(angles)] * 2, axis=-1),
    )


def rotate(values, cosine_table, sine_table):
    half_dim = values.shape[-1] // 2
    turned = jnp.concatenate([-values[..., half_dim:], values[..., :half_dim]], axis=-1)
    return values * cosine_table[:, None, :] + turned * sine_table[:, None, :]


def unrotate(upstream, cosine_table, sine_table):
    half_dim = upstream.shape[-1] // 2
    scaled_sine = upstream * sine_table[:, None, :]
    turned_back = jnp.concatenate(
        [scaled_sine[..., half_dim:], -scaled_sine[..., :half_dim]], axis=-1
    )
    return upstream * cosine_table[:, None, :] + turned_back


def norm_forward(values, gain_vec):
    scale_inv = lax.rsqrt(jnp.mean(values * values, axis=-1, keepdims=True) + norm_epsilon)
    return (values * scale_inv * gain_vec, scale_inv)


def norm_backward(values, scale_inv, gain_vec, upstream):
    weighted = upstream * gain_vec
    grad_input = scale_inv * weighted - values * scale_inv**3 * jnp.mean(
        weighted * values, axis=-1, keepdims=True
    )
    gain_term = jnp.sum((upstream * values * scale_inv).reshape(-1, values.shape[-1]), axis=0)
    return (grad_input, gain_term)


def upper_bit(local_index, bit_number):
    return local_index // 2**bit_number % 2 == 1


def joined_rows(mine, received, upper_side):
    first_rows = jnp.where(upper_side, received, mine)
    second_rows = jnp.where(upper_side, mine, received)
    return jnp.concatenate([first_rows, second_rows], axis=0)


def half_gather(pair, local_index):
    gathered_rows = pair
    for bit_number in range(lax.axis_size("ctx").bit_length() - 2):
        received = from_partner(gathered_rows, "ctx", bit_number)
        gathered_rows = joined_rows(gathered_rows, received, upper_bit(local_index, bit_number))
    return gathered_rows


def half_reduce(term, local_index):
    for bit_number in reversed(range(lax.axis_size("ctx").bit_length() - 2)):
        span = term.shape[0] // 2
        lower_rows = term[:span]
        upper_rows = term[span:]
        upper_side = upper_bit(local_index, bit_number)
        kept_rows = jnp.where(upper_side, upper_rows, lower_rows)
        sent_rows = jnp.where(upper_side, lower_rows, upper_rows)
        term = kept_rows + from_partner(sent_rows, "ctx", bit_number)
    return term


def over_keys(update, carried, count_rows):
    block_length = math.gcd(count_rows, 512)

    def inner_step(current, block_index):
        return (update(current, block_index * block_length, block_length), None)

    carried, unused = lax.scan(
        inner_step, carried, jnp.arange(count_rows // block_length, dtype=jnp.int32)
    )
    return carried


def allowed_mask(key_meta, query_meta, row_start, block_length):
    key_places = lax.dynamic_slice_in_dim(key_meta[0], row_start, block_length)
    key_slots = lax.dynamic_slice_in_dim(key_meta[1], row_start, block_length)
    key_live = lax.dynamic_slice_in_dim(key_meta[2], row_start, block_length)
    allowed = (
        (key_slots[None, :] == query_meta[1][:, None])
        & (key_places[None, :] <= query_meta[0][:, None])
        & key_live[None, :]
    )
    return allowed[None, None]


def forward_update(
    current, query_head_group, key_tile_block, value_tile_block, allowed, score_scale
):
    running_max, running_sum, running_acc = current
    block_length = key_tile_block.shape[0]
    key_head_list = key_tile_block.reshape(block_length, KEY_VALUE_HEADS, HEAD_SIZE)
    value_head_list = value_tile_block.reshape(block_length, KEY_VALUE_HEADS, HEAD_SIZE)
    scores = (
        jnp.einsum(
            "qhgd,khd->hgqk", query_head_group, key_head_list, preferred_element_type=jnp.float32
        )
        * score_scale
    )
    scores = jnp.where(allowed, scores, masked_logits)
    new_max = jnp.maximum(running_max, jnp.max(scores, axis=-1))
    factor = jnp.exp(running_max - new_max)
    prob_block = jnp.where(allowed, jnp.exp(scores - new_max[..., None]), 0.0)
    new_sum = running_sum * factor + jnp.sum(prob_block, axis=-1)
    new_acc = running_acc * factor[..., None] + jnp.einsum(
        "hgqk,khd->hgqd",
        prob_block.astype(jnp.bfloat16),
        value_head_list,
        preferred_element_type=jnp.float32,
    )
    return (new_max, new_sum, new_acc)


def score_parts(
    query_head_group,
    output_grad_group,
    key_tile_block,
    value_tile_block,
    allowed,
    log_total,
    row_delta,
    score_scale,
):
    block_length = key_tile_block.shape[0]
    key_head_list = key_tile_block.reshape(block_length, KEY_VALUE_HEADS, HEAD_SIZE)
    value_head_list = value_tile_block.reshape(block_length, KEY_VALUE_HEADS, HEAD_SIZE)
    scores = (
        jnp.einsum(
            "qhgd,khd->hgqk", query_head_group, key_head_list, preferred_element_type=jnp.float32
        )
        * score_scale
    )
    prob_block = jnp.where(allowed, jnp.exp(scores - log_total[..., None]), 0.0)
    dprob = jnp.einsum(
        "qhgd,khd->hgqk", output_grad_group, value_head_list, preferred_element_type=jnp.float32
    )
    dscore_low = (prob_block * (dprob - row_delta[..., None])).astype(jnp.bfloat16)
    return (prob_block, dscore_low, key_head_list)


def attention_inputs(stream, gathered, cosine_table, sine_table):
    count_rows = stream.shape[0]
    normalized, inv_attn = norm_forward(stream, gathered[7].astype(jnp.float32))
    normed_low = normalized.astype(jnp.bfloat16)
    query_heads = jnp.dot(normed_low, gathered[0], preferred_element_type=jnp.float32).reshape(
        count_rows, QUERY_HEADS, HEAD_SIZE
    )
    key_head_list = jnp.dot(normed_low, gathered[1], preferred_element_type=jnp.float32).reshape(
        count_rows, KEY_VALUE_HEADS, HEAD_SIZE
    )
    value_low = jnp.dot(normed_low, gathered[2], preferred_element_type=jnp.float32).astype(
        jnp.bfloat16
    )
    query_normed, inv_query = norm_forward(query_heads, gathered[9].astype(jnp.float32))
    key_normed, inv_key = norm_forward(key_head_list, gathered[10].astype(jnp.float32))
    query_lowered = rotate(query_normed, cosine_table, sine_table).astype(jnp.bfloat16)
    key_low = (
        rotate(key_normed, cosine_table, sine_table)
        .astype(jnp.bfloat16)
        .reshape(count_rows, KEY_VALUE_HEADS * HEAD_SIZE)
    )
    return {
        "normed_low": normed_low,
        "inv_attn": inv_attn,
        "query_heads": query_heads,
        "inv_query": inv_query,
        "key_heads": key_head_list,
        "inv_key": inv_key,
        "query_low": query_lowered,
        "key_low": key_low,
        "value_low": value_low,
    }


def block_rest(stream, gathered, attn_low):
    middle = stream + jnp.dot(attn_low, gathered[3], preferred_element_type=jnp.float32)
    normed_mid, inv_mid = norm_forward(middle, gathered[8].astype(jnp.float32))
    normed_mid_low = normed_mid.astype(jnp.bfloat16)
    gate_act = jnp.dot(normed_mid_low, gathered[4], preferred_element_type=jnp.float32)
    upward = jnp.dot(normed_mid_low, gathered[5], preferred_element_type=jnp.float32)
    hidden_low = (jax.nn.silu(gate_act) * upward).astype(jnp.bfloat16)
    result = middle + jnp.dot(hidden_low, gathered[6], preferred_element_type=jnp.float32)
    return {
        "middle": middle,
        "inv_mid": inv_mid,
        "normed_mid_low": normed_mid_low,
        "gate_act": gate_act,
        "upward": upward,
        "hidden_low": hidden_low,
        "result": result,
    }


def general_device(
    tokens,
    cotangent,
    lengths,
    stretch_ids,
    w_query,
    key_projection_weight,
    value_projection_weight,
    w_out,
    w_gate,
    w_up,
    w_down,
    g_attn,
    g_mlp,
    g_query,
    g_key,
):
    count_rows = tokens.shape[0]
    ctx_count = lax.axis_size("ctx")
    half_count = ctx_count // 2
    key_value_width = KEY_VALUE_HEADS * HEAD_SIZE
    key_meta = token_places(stretch_ids[:, 0, :], lengths[0])
    ctx_index = lax.axis_index("ctx")
    local_index = ctx_index % half_count
    base_row = ctx_index // half_count * half_count * count_rows
    half_row_set = half_count * count_rows
    offset_mine = ctx_index * count_rows
    query_meta = tuple(
        (lax.dynamic_slice_in_dim(meta_array, offset_mine, count_rows) for meta_array in key_meta)
    )
    live_mine = query_meta[2].astype(jnp.float32)[:, None]
    cosine_table, sine_table = rotary_tables(query_meta[0])
    group_count = QUERY_HEADS // KEY_VALUE_HEADS
    score_scale = HEAD_SIZE ** (-0.5)

    def attend_forward(query_head_group, key_source, value_source, current):

        def update(carried, local_row, block_length):
            key_tile_block = lax.dynamic_slice_in_dim(key_source, local_row, block_length)
            value_tile_block = lax.dynamic_slice_in_dim(value_source, local_row, block_length)
            allowed = allowed_mask(key_meta, query_meta, base_row + local_row, block_length)
            return forward_update(
                carried, query_head_group, key_tile_block, value_tile_block, allowed, score_scale
            )

        return over_keys(update, current, key_source.shape[0])

    saved = []
    stream = tokens.astype(jnp.float32)
    for layer_index in range(DECODER_LAYERS):
        gathered = (
            lax.all_gather(w_query[layer_index], "fsdp", axis=0, tiled=True),
            lax.all_gather(key_projection_weight[layer_index], "fsdp", axis=0, tiled=True),
            lax.all_gather(value_projection_weight[layer_index], "fsdp", axis=0, tiled=True),
            lax.all_gather(w_out[layer_index], "fsdp", axis=0, tiled=True),
            lax.all_gather(w_gate[layer_index], "fsdp", axis=0, tiled=True),
            lax.all_gather(w_up[layer_index], "fsdp", axis=0, tiled=True),
            lax.all_gather(w_down[layer_index], "fsdp", axis=0, tiled=True),
            lax.all_gather(g_attn[layer_index], "fsdp", axis=0, tiled=True),
            lax.all_gather(g_mlp[layer_index], "fsdp", axis=0, tiled=True),
            lax.all_gather(g_query[layer_index], "fsdp", axis=0, tiled=True),
            lax.all_gather(g_key[layer_index], "fsdp", axis=0, tiled=True),
        )
        present_inputs = attention_inputs(stream, gathered, cosine_table, sine_table)
        query_head_group = present_inputs["query_low"].reshape(
            count_rows, KEY_VALUE_HEADS, group_count, HEAD_SIZE
        )
        start_state = (
            jnp.full((KEY_VALUE_HEADS, group_count, count_rows), masked_logits, jnp.float32),
            jnp.zeros((KEY_VALUE_HEADS, group_count, count_rows), jnp.float32),
            jnp.zeros((KEY_VALUE_HEADS, group_count, count_rows, HEAD_SIZE), jnp.float32),
        )
        pair_all = half_gather(
            jnp.concatenate([present_inputs["key_low"], present_inputs["value_low"]], axis=-1),
            local_index,
        )
        key_all = pair_all[:, :key_value_width]
        value_all = pair_all[:, key_value_width:]
        final_state = attend_forward(query_head_group, key_all, value_all, start_state)
        attended = final_state[2] / final_state[1][..., None]
        log_total = final_state[0] + jnp.log(final_state[1])
        attn_low = (
            jnp.transpose(attended, (2, 0, 1, 3))
            .reshape(count_rows, QUERY_HEADS * HEAD_SIZE)
            .astype(jnp.bfloat16)
        )
        rest = block_rest(stream, gathered, attn_low)
        kept = (gathered, key_all, value_all, present_inputs, rest)
        saved.append((stream, attended, log_total, kept))
        stream = rest["result"]
    output_low = (stream * live_mine).astype(jnp.bfloat16)
    grad_stream = cotangent.astype(jnp.float32) * live_mine
    layer_grads = [None] * DECODER_LAYERS
    for layer_index in reversed(range(DECODER_LAYERS)):
        stream_in, attended, log_total, kept = saved[layer_index]
        attn_low = (
            jnp.transpose(attended, (2, 0, 1, 3))
            .reshape(count_rows, QUERY_HEADS * HEAD_SIZE)
            .astype(jnp.bfloat16)
        )
        gathered, key_all, value_all, present_inputs, rest = kept
        ffn_grad_low = grad_stream.astype(jnp.bfloat16)
        grad_down = jnp.einsum(
            "tf,td->fd", rest["hidden_low"], ffn_grad_low, preferred_element_type=jnp.float32
        )
        hidden_grad = jnp.einsum(
            "td,fd->tf", ffn_grad_low, gathered[6], preferred_element_type=jnp.float32
        )
        gate_act = rest["gate_act"]
        sigmoid_gate = jax.nn.sigmoid(gate_act)
        gate_grad_low = (
            hidden_grad * rest["upward"] * sigmoid_gate * (1.0 + gate_act * (1.0 - sigmoid_gate))
        ).astype(jnp.bfloat16)
        up_grad_low = (hidden_grad * gate_act * sigmoid_gate).astype(jnp.bfloat16)
        grad_gate = jnp.einsum(
            "td,tf->df", rest["normed_mid_low"], gate_grad_low, preferred_element_type=jnp.float32
        )
        grad_up = jnp.einsum(
            "td,tf->df", rest["normed_mid_low"], up_grad_low, preferred_element_type=jnp.float32
        )
        normed_mid_grad = jnp.einsum(
            "tf,df->td", gate_grad_low, gathered[4], preferred_element_type=jnp.float32
        ) + jnp.einsum("tf,df->td", up_grad_low, gathered[5], preferred_element_type=jnp.float32)
        mid_norm_grad, mlp_gain_term = norm_backward(
            rest["middle"], rest["inv_mid"], gathered[8].astype(jnp.float32), normed_mid_grad
        )
        middle_grad = grad_stream + mid_norm_grad
        attn_grad_low = middle_grad.astype(jnp.bfloat16)
        grad_out = jnp.einsum(
            "tq,td->qd", attn_low, attn_grad_low, preferred_element_type=jnp.float32
        )
        output_gradient_lowered = jnp.einsum(
            "td,qd->tq", attn_grad_low, gathered[3], preferred_element_type=jnp.float32
        ).astype(jnp.bfloat16)
        output_grad_group = output_gradient_lowered.reshape(
            count_rows, KEY_VALUE_HEADS, group_count, HEAD_SIZE
        )
        row_delta = jnp.sum(
            jnp.transpose(output_grad_group.astype(jnp.float32), (1, 2, 0, 3)) * attended, axis=-1
        )
        query_head_group = present_inputs["query_low"].reshape(
            count_rows, KEY_VALUE_HEADS, group_count, HEAD_SIZE
        )
        key_block_size = math.gcd(half_row_set, 512)

        def backward_step(query_acc, block_index):
            row_start = block_index * key_block_size
            key_tile_block = lax.dynamic_slice_in_dim(key_all, row_start, key_block_size)
            value_tile_block = lax.dynamic_slice_in_dim(value_all, row_start, key_block_size)
            allowed = allowed_mask(key_meta, query_meta, base_row + row_start, key_block_size)
            prob_block, dscore_low, key_head_list = score_parts(
                query_head_group,
                output_grad_group,
                key_tile_block,
                value_tile_block,
                allowed,
                log_total,
                row_delta,
                score_scale,
            )
            query_next = (query_acc, jnp.zeros((key_block_size, 2 * key_value_width), jnp.float32))[
                0
            ] + jnp.einsum(
                "hgqk,khd->qhgd", dscore_low, key_head_list, preferred_element_type=jnp.float32
            ) * score_scale
            value_grad = jnp.einsum(
                "hgqk,qhgd->khd",
                prob_block.astype(jnp.bfloat16),
                output_grad_group,
                preferred_element_type=jnp.float32,
            )
            key_grad = (
                jnp.einsum(
                    "hgqk,qhgd->khd",
                    dscore_low,
                    query_head_group,
                    preferred_element_type=jnp.float32,
                )
                * score_scale
            )
            block_rows = jnp.concatenate(
                [
                    key_grad.reshape(key_block_size, key_value_width),
                    value_grad.reshape(key_block_size, key_value_width),
                ],
                axis=-1,
            )
            return (query_next, block_rows)

        query_grad, key_value_rows = lax.scan(
            backward_step,
            jnp.zeros((count_rows, KEY_VALUE_HEADS, group_count, HEAD_SIZE), jnp.float32),
            jnp.arange(half_row_set // key_block_size, dtype=jnp.int32),
        )
        key_value_term = key_value_rows.reshape(half_row_set, 2 * key_value_width)
        key_value_gradient = half_reduce(key_value_term, local_index)
        key_gradient_rows = key_value_gradient[:, :key_value_width].reshape(
            count_rows, KEY_VALUE_HEADS, HEAD_SIZE
        )
        value_grad_low = key_value_gradient[:, key_value_width:].astype(jnp.bfloat16)
        query_pre, query_gain_term = norm_backward(
            present_inputs["query_heads"],
            present_inputs["inv_query"],
            gathered[9].astype(jnp.float32),
            unrotate(
                query_grad.reshape(count_rows, QUERY_HEADS, HEAD_SIZE), cosine_table, sine_table
            ),
        )
        key_pre, key_gain_term = norm_backward(
            present_inputs["key_heads"],
            present_inputs["inv_key"],
            gathered[10].astype(jnp.float32),
            unrotate(key_gradient_rows, cosine_table, sine_table),
        )
        query_grad_low = query_pre.reshape(count_rows, QUERY_HEADS * HEAD_SIZE).astype(jnp.bfloat16)
        key_grad_low = key_pre.reshape(count_rows, key_value_width).astype(jnp.bfloat16)
        normed_low = present_inputs["normed_low"]
        grad_query = jnp.einsum(
            "td,tq->dq", normed_low, query_grad_low, preferred_element_type=jnp.float32
        )
        grad_key = jnp.einsum(
            "td,tq->dq", normed_low, key_grad_low, preferred_element_type=jnp.float32
        )
        grad_value = jnp.einsum(
            "td,tq->dq", normed_low, value_grad_low, preferred_element_type=jnp.float32
        )
        normed_grad = jnp.einsum(
            "tq,dq->td", query_grad_low, gathered[0], preferred_element_type=jnp.float32
        )
        normed_grad = normed_grad + jnp.einsum(
            "tq,dq->td", key_grad_low, gathered[1], preferred_element_type=jnp.float32
        )
        normed_grad = normed_grad + jnp.einsum(
            "tq,dq->td", value_grad_low, gathered[2], preferred_element_type=jnp.float32
        )
        in_norm_grad, attn_gain_term = norm_backward(
            stream_in, present_inputs["inv_attn"], gathered[7].astype(jnp.float32), normed_grad
        )
        grad_stream = middle_grad + in_norm_grad
        layer_grads[layer_index] = (
            lax.psum_scatter(grad_query, ("ctx", "fsdp"), scatter_dimension=0, tiled=True),
            lax.psum_scatter(grad_key, ("ctx", "fsdp"), scatter_dimension=0, tiled=True),
            lax.psum_scatter(grad_value, ("ctx", "fsdp"), scatter_dimension=0, tiled=True),
            lax.psum_scatter(grad_out, ("ctx", "fsdp"), scatter_dimension=0, tiled=True),
            lax.psum_scatter(grad_gate, ("ctx", "fsdp"), scatter_dimension=0, tiled=True),
            lax.psum_scatter(grad_up, ("ctx", "fsdp"), scatter_dimension=0, tiled=True),
            lax.psum_scatter(grad_down, ("ctx", "fsdp"), scatter_dimension=0, tiled=True),
            lax.psum_scatter(attn_gain_term, ("ctx", "fsdp"), scatter_dimension=0, tiled=True),
            lax.psum_scatter(mlp_gain_term, ("ctx", "fsdp"), scatter_dimension=0, tiled=True),
            lax.psum_scatter(query_gain_term, ("ctx", "fsdp"), scatter_dimension=0, tiled=True),
            lax.psum_scatter(key_gain_term, ("ctx", "fsdp"), scatter_dimension=0, tiled=True),
        )
    stacked = tuple(
        (jnp.stack([layer_sums[member] for layer_sums in layer_grads]) for member in range(11))
    )
    return (output_low, grad_stream) + stacked


def fast_device(
    tokens,
    cotangent,
    lengths,
    stretch_ids,
    w_query,
    key_projection_weight,
    value_projection_weight,
    w_out,
    w_gate,
    w_up,
    w_down,
    g_attn,
    g_mlp,
    g_query,
    g_key,
):
    results = forward(
        (key_projection_weight, value_projection_weight, w_query, w_out, w_gate, w_up, w_down),
        (g_attn, g_mlp, g_query, g_key),
        tokens,
        stretch_ids,
        lengths,
        1,
    )
    gathered, saved, turned, gains, output_low, tables = (
        results[:4], results[4:11], results[11:15], results[15:18], results[18], results[19:]
    )
    acts = [
        member.reshape(DECODER_LAYERS, 4, 2, 2, 2, -1, 32, tokens.shape[0]) for member in turned
    ]
    *weight_sums, grad_stream, sums, unused = backward(
        acts, saved, gathered, cotangent, gains, tables, 2
    )
    return tuple(finish((output_low, grad_stream, *weight_sums), sums))


def solution(mesh):
    plain = mesh.shape["ctx"] == 2 * KEY_VALUE_HEADS and mesh.shape["fsdp"] == 2
    device = fast_device if plain else general_device
    in_specs = (
        P(("ctx", "fsdp"), None),
        P(("ctx", "fsdp"), None),
        P("fsdp", None),
        P(None, "fsdp", None),
        P(None, "fsdp", None),
        P(None, "fsdp", None),
        P(None, "fsdp", None),
        P(None, "fsdp", None),
        P(None, "fsdp", None),
        P(None, "fsdp", None),
        P(None, "fsdp", None),
        P(None, "fsdp"),
        P(None, "fsdp"),
        P(None, "fsdp"),
        P(None, "fsdp"),
    )
    out_specs = (
        P(("ctx", "fsdp"), None),
        P(("ctx", "fsdp"), None),
        P(None, ("ctx", "fsdp"), None),
        P(None, ("ctx", "fsdp"), None),
        P(None, ("ctx", "fsdp"), None),
        P(None, ("ctx", "fsdp"), None),
        P(None, ("ctx", "fsdp"), None),
        P(None, ("ctx", "fsdp"), None),
        P(None, ("ctx", "fsdp"), None),
        P(None, ("ctx", "fsdp")),
        P(None, ("ctx", "fsdp")),
        P(None, ("ctx", "fsdp")),
        P(None, ("ctx", "fsdp")),
    )
    return jax.shard_map(
        device, mesh=mesh, in_specs=in_specs, out_specs=out_specs, check_vma=False
    )
```
